32 devices in a mesh: wide: 16 (over z, y, core), narrow: 2 (over x).
Axes of the slice: x: 2, y: 2, z: 4, core: 2. Of those that a mesh axis runs over, the one named last changes fastest.
Arguments:
- layer_input: bfloat16 [32, 384, 768], P(('wide', 'narrow')), may hold values from -6 to 6
- memory: bfloat16 [32, 256, 768], P(('wide', 'narrow')), may hold values from -6 to 6
- cotangent: bfloat16 [32, 384, 768], P(('wide', 'narrow')), may hold values from -6 to 6
- segment_ids: int32 [32, 384], P(('wide', 'narrow')), may hold values from 0 to 7, never falling along the last dimension, each value on 1 to 96 neighbouring positions
- padding: int32 [32, 384], P(('wide', 'narrow')), may hold values 0 or 1
- image_of_row: int32 [32], replicated, may hold values from 0 to 9, as said below
- self_weights: bfloat16 [4, 768, 768], P(None, 'wide'), as said below
- cross_weights: bfloat16 [4, 768, 768], P(None, 'wide'), as said below
- mlp_in: bfloat16 [2, 768, 2048], P(None, 'wide'), may hold values from -0.21875 to 0.21875
- mlp_out: bfloat16 [2048, 768], P('wide'), may hold values from -0.125 to 0.125
- gains: bfloat16 [3, 768], P(None, 'wide'), may hold values from 0.25 to 1.75
Outputs:
- layer_output: bfloat16 [32, 384, 768], P(('wide', 'narrow'))
- x_grad: float32 [32, 384, 768], P(('wide', 'narrow'))
- memory_grad: float32 [32, 256, 768], P(('wide', 'narrow'))
- self_grad: float32 [4, 768, 768], P(None, 'wide')
- cross_grad: float32 [4, 768, 768], P(None, 'wide')
- mlp_in_grad: float32 [2, 768, 2048], P(None, 'wide')
- mlp_out_grad: float32 [2048, 768], P('wide')
- gains_grad: float32 [3, 768], P(None, 'wide')
The draws below stay inside these ranges and needn't reach their ends.
Inputs may be any that keep to these rules, and one draw needn't show every extreme that they name: `image_of_row`: image numbers never fall along the rows; each of the 10 images has a run of 2 to 4 consecutive rows; some image has 4 rows and some has 2. `self_weights`: each layer matrix has independent entries. `cross_weights`: each layer matrix has independent entries.
All inputs are finite; a program needn't handle non-finite values. No bound on the sum of `padding` on one device may be relied on, other than what follows from the above.
Results may differ from the reference program's by a relative error of at most 0.018.
Values may be sent and summed in bfloat16 or wider, within the bound.
A program may use at most 256 MiB of HBM per device.

```python
import math
import jax
import jax.numpy as jnp
import numpy as np
from jax import lax

D = 768
HEAD_DIM = 64
FF = 2048
TOK_DEV = 384
PATCH = 256
SEGS = 8
ROWS = 32
IMAGES = 10


def draw_image_of_row(key, part):
    key = jax.random.fold_in(key, 7)
    key_count, key_order = jax.random.split(key)
    surplus = ROWS - 3 * IMAGES
    pairs = jax.random.randint(key_count, (), 1, 3)
    ordinal = jnp.arange(IMAGES)
    run_lengths = jnp.where(ordinal < pairs + surplus, 4, jnp.where(ordinal < 2 * pairs + surplus, 2, 3))
    shuffle = jax.random.permutation(key_order, IMAGES)
    run_lengths = run_lengths[shuffle]
    run_ends = jnp.cumsum(run_lengths)
    row_ids = jnp.arange(ROWS)
    return jnp.sum(row_ids[:, None] >= run_ends[None, :], axis=1).astype(jnp.int32)


def draw_self_weights(key, part):
    key = jax.random.fold_in(key, 11)
    normal_draw = jax.random.normal(key, (4, D, D), jnp.float32)
    out_fan = max(2, D // 16)
    factors = jnp.where(jnp.arange(4) == 3, out_fan ** (-0.5), D ** (-0.5))
    return (normal_draw * factors[:, None, None]).astype(jnp.bfloat16)


def draw_cross_weights(key, part):
    key = jax.random.fold_in(key, 13)
    normal_draw = jax.random.normal(key, (4, D, D), jnp.float32)
    out_fan = max(2, 4096 // PATCH)
    factors = jnp.where(jnp.arange(4) == 3, out_fan ** (-0.5), D ** (-0.5))
    return (normal_draw * factors[:, None, None]).astype(jnp.bfloat16)


def plant(drawn, stream_key, smallest, high):
    longest = drawn.shape.index(max(drawn.shape))
    spots = []
    for shift in (0, 1):
        where = [jax.random.randint(jax.random.fold_in(stream_key, axis), (), 0, length) for axis, length in enumerate(drawn.shape)]
        where[longest] = (where[longest] + shift) % drawn.shape[longest]
        spots.append(tuple(where))
    return drawn.at[spots[0]].set(smallest).at[spots[1]].set(high)


def block_levels(key, extent, shards, smallest, top_value):
    def one(dim, parts):
        heights = jax.random.uniform(jax.random.fold_in(jax.random.fold_in(key, 6), dim), (parts,), jnp.float32, smallest / len(shards), top_value / len(shards))
        return jnp.repeat(jnp.exp(heights), extent[dim] // parts).reshape((-1,) + (1,) * (len(extent) - dim - 1))

    level = one(*shards[0])
    for cut in shards[1:]:
        level = level * one(*cut)
    return level


def profile(amount, total, bound, skew):
    loads = [(1 << 20) // math.isqrt(grade ** skew) + 1 for grade in range(2, amount + 1)]
    spare, given = total - bound - (amount - 1), [1] * (amount - 1)
    while spare > 0:
        candidates = [i for i in range(amount - 1) if given[i] < bound]
        whole, left = sum([loads[i] for i in candidates]), spare
        for i in candidates:
            extra = min(bound - given[i], max(1, left * loads[i] // whole), spare)
            given[i] = given[i] + extra
            spare = spare - extra
    return np.array([bound] + given)


def ragged(stream_key, amount, total, limit, slope):
    if amount == 2:
        one = jax.random.randint(stream_key, (), max(1, total - limit), min(limit, total - 1) + 1)
        return jnp.stack([one, total - one])
    lengths = jnp.asarray(profile(amount, total, limit, slope), jnp.int32)
    twos = (amount - 1) // 2
    donor, sink = lengths[1:1 + 2 * twos:2], lengths[2:2 + 2 * twos:2]
    margin = jnp.minimum(donor - 1, limit - sink)
    passed = jax.random.randint(jax.random.fold_in(stream_key, 1), (twos,), 0, 1 << 20) % (margin + 1)
    lengths = lengths.at[1:1 + 2 * twos:2].set(donor - passed).at[2:2 + 2 * twos:2].set(sink + passed)
    return lengths[jax.random.permutation(jax.random.fold_in(stream_key, 2), amount)]


def scatter_about(stream_key, extent, spread, bound, pieces=(), dtype=jnp.bfloat16):
    values = jax.random.normal(stream_key, extent, jnp.float32) * spread
    if len(pieces) > 0:
        values = block_levels(stream_key, extent, pieces, -0.22, 0.18) * values
    return jnp.clip(values, min=-bound, max=bound).astype(dtype)


def setup_inputs(seed: int = 0) -> dict:
    seeds = jax.random.split(jax.random.key(seed), 12)
    layer_input = scatter_about(seeds[0], (ROWS, TOK_DEV, D), 1.0, 6.0, ((0, 32),))
    memory = scatter_about(seeds[1], (ROWS, PATCH, D), 1.0, 6.0, ((0, 32),))
    cotangent = scatter_about(seeds[2], (ROWS, TOK_DEV, D), 1.0, 6.0, ((0, 32),))
    segment_ids = jax.vmap(lambda own: jnp.searchsorted(jnp.cumsum(ragged(own, SEGS, TOK_DEV, TOK_DEV // 4, 1)), jnp.arange(TOK_DEV), side="right"))(jax.random.split(seeds[3], ROWS)).reshape((ROWS, TOK_DEV)).astype(jnp.int32)
    padding = plant((jax.random.randint(seeds[4], (ROWS, TOK_DEV), 0, 8) < 7).astype(jnp.int32), jax.random.fold_in(seeds[4], 1), 0, 1)
    image_of_row = draw_image_of_row(jax.random.fold_in(seeds[11], 71), 0)
    self_weights = draw_self_weights(jax.random.fold_in(seeds[11], 71), 0)
    cross_weights = draw_cross_weights(jax.random.fold_in(seeds[11], 71), 0)
    mlp_in = scatter_about(seeds[8], (2, D, FF), D ** -0.5, 0.21875, ((1, 16),))
    mlp_out = scatter_about(seeds[9], (FF, D), FF ** -0.5, 0.125, ((0, 16),))
    gains = jnp.clip(1.0 + 0.15 * jax.random.normal(seeds[10], (3, D), jnp.float32), 0.25, 1.75).astype(jnp.bfloat16)
    return {"layer_input": layer_input, "memory": memory, "cotangent": cotangent, "segment_ids": segment_ids, "padding": padding, "image_of_row": image_of_row, "self_weights": self_weights, "cross_weights": cross_weights, "mlp_in": mlp_in, "mlp_out": mlp_out, "gains": gains}


@jax.custom_vjp
def low(v):
    return lax.optimization_barrier(v.astype(jnp.bfloat16)).astype(jnp.float32)

@jax.custom_vjp
def low_back(v):
    return v

def low_keep(v):
    return (low(v), None)

def low_pass(kept, grad):
    return (grad,)

def back_keep(v):
    return (v, None)

def back_low(kept, grad):
    return (low(grad),)
low.defvjp(low_keep, low_pass)
low_back.defvjp(back_keep, back_low)
EPSILON = 1e-06

def matmul_exact(a, b):
    return jnp.dot(a, b, precision=lax.Precision.HIGHEST)

def rms_norm(v, g):
    return v * lax.rsqrt(lax.optimization_barrier(jnp.mean(v * v, axis=-1, keepdims=True)) + EPSILON) * g

def project(a, w):
    return low(low_back(matmul_exact(a, w)))

def attend(q, k, v, allowed):
    score_scale = HEAD_DIM ** (-0.5)
    q_part = q.reshape(q.shape[0], -1, HEAD_DIM)
    k_part = k.reshape(k.shape[0], -1, HEAD_DIM)
    v_part = v.reshape(v.shape[0], -1, HEAD_DIM)
    scores = jnp.einsum('qhd,khd->hqk', q_part, k_part, precision=lax.Precision.HIGHEST) * score_scale
    if allowed is not None:
        scores = jnp.where(allowed[None], scores, -1e+30)
    scores = low_back(scores)
    highest = lax.optimization_barrier(jnp.max(scores, axis=-1, keepdims=True))
    powers = jnp.exp(scores - highest)
    shares = low(powers / lax.optimization_barrier(jnp.sum(powers, axis=-1, keepdims=True)))
    mixed = jnp.einsum('hqk,khd->qhd', shares, v_part, precision=lax.Precision.HIGHEST)
    return low(low_back(mixed.reshape(q.shape[0], -1)))

def row_layer(x_row, seg_row, pad_row, mem_row, self_w, cross_w, in_w, out_w, g):
    seq_len = x_row.shape[0]
    position = jnp.arange(seq_len)
    allowed = (seg_row[:, None] == seg_row[None, :]) & (position[None, :] <= position[:, None]) & ((pad_row[None, :] == 1) | (position[:, None] == position[None, :]))
    h_one = low(rms_norm(x_row, g[0]))
    mixed = attend(project(h_one, self_w[0]), project(h_one, self_w[1]), project(h_one, self_w[2]), allowed)
    x_one = x_row + low_back(matmul_exact(mixed, self_w[3]))
    h_two = low(rms_norm(x_one, g[1]))
    cross_mix = attend(project(h_two, cross_w[0]), project(mem_row, cross_w[1]), project(mem_row, cross_w[2]), None)
    x_two = x_one + low_back(matmul_exact(cross_mix, cross_w[3]))
    h_three = low(rms_norm(x_two, g[2]))
    gate_act = low_back(matmul_exact(h_three, in_w[0]))
    up_act = low_back(matmul_exact(h_three, in_w[1]))
    hidden = low(jax.nn.gelu(gate_act, approximate=True) * up_act)
    return x_two + low_back(matmul_exact(hidden, out_w))

def reference(layer_input, memory, cotangent, segment_ids, padding, image_of_row, self_weights, cross_weights, mlp_in, mlp_out, gains):
    starts = lax.optimization_barrier(jnp.sum(image_of_row[None, :] < image_of_row[:, None], axis=1)).astype(jnp.int32)

    def decoder(x_float, mem_float, self_w, cross_w, in_w, out_w, g):

        def one_row(row_items):
            x_row, seg_row, pad_row, start = row_items
            mem_row = lax.dynamic_index_in_dim(mem_float, start, 0, keepdims=False)
            return row_layer(x_row, seg_row, pad_row, mem_row, self_w, cross_w, in_w, out_w, g)
        return lax.map(jax.checkpoint(one_row), (x_float, segment_ids, padding, starts))
    result, pullback = jax.vjp(decoder, layer_input.astype(jnp.float32), memory.astype(jnp.float32), self_weights.astype(jnp.float32), cross_weights.astype(jnp.float32), mlp_in.astype(jnp.float32), mlp_out.astype(jnp.float32), gains.astype(jnp.float32))
    grads = pullback(cotangent.astype(jnp.float32))
    return (result.astype(jnp.bfloat16), grads[0], grads[1], grads[2], grads[3], grads[4], grads[5], grads[6])
```

```python
import functools

import jax
import jax.numpy as jnp
from jax import lax
from jax.experimental import pallas as pl
from jax.experimental.pallas import tpu as pltpu
from jax.sharding import PartitionSpec as P

HEAD_DIM = 64


EPSILON = 1e-06


def shifted(value, axis, steps):
    count = lax.axis_size(axis)
    first, last = (max(0, -steps), min(count, count - steps))
    return lax.ppermute(value, axis, [(source, source + steps) for source in range(first, last)])


def rms_norm(v, g):
    return v * lax.rsqrt(jnp.mean(v * v, axis=-1, keepdims=True) + EPSILON) * g


def contract_rows(a, b):
    return lax.dot_general(a, b, (((0,), (0,)), ((), ())), preferred_element_type=jnp.float32)


def times_transposed(a, w):
    return lax.dot_general(a, w, (((1,), (1,)), ((), ())), preferred_element_type=jnp.float32)


def linear(a, w):
    return jnp.dot(a, w, preferred_element_type=jnp.float32)


def head_scores(q_part, k_part, allowed):
    scores = jnp.einsum(
        "qhd,khd->hqk", q_part, k_part, preferred_element_type=jnp.float32
    ) * HEAD_DIM ** (-0.5)
    if allowed is not None:
        scores = jnp.where(allowed[None], scores, -1e30)
    return scores


def split_heads(a, head_start):
    return a[:, head_start * HEAD_DIM : (head_start + 4) * HEAD_DIM].reshape(
        a.shape[0], 4, HEAD_DIM
    )


def forward_heads(q, k, v, allowed):
    seq_len = q.shape[0]
    head_count = q.shape[1] // HEAD_DIM
    pieces = []
    log_sums = []
    for head_start in range(0, head_count, 4):
        q_part = split_heads(q, head_start)
        k_part = split_heads(k, head_start)
        v_part = split_heads(v, head_start)
        scores = head_scores(q_part, k_part, allowed)
        highest = jnp.max(scores, axis=-1, keepdims=True)
        powers = jnp.exp(scores - highest)
        summed = jnp.sum(powers, axis=-1, keepdims=True)
        shares = (powers / summed).astype(jnp.bfloat16)
        mixed = jnp.einsum("hqk,khd->qhd", shares, v_part, preferred_element_type=jnp.float32)
        pieces.append(mixed.reshape(seq_len, -1))
        log_sums.append(highest + jnp.log(summed))
    return (jnp.concatenate(pieces, axis=1).astype(jnp.bfloat16), jnp.concatenate(log_sums, axis=0))


def backward_heads(q, k, v, mix_grad, log_sum, allowed):
    seq_len = q.shape[0]
    head_count = q.shape[1] // HEAD_DIM
    q_pieces = []
    k_pieces = []
    v_pieces = []
    for head_start in range(0, head_count, 4):
        q_part = split_heads(q, head_start)
        k_part = split_heads(k, head_start)
        v_part = split_heads(v, head_start)
        o_part = split_heads(mix_grad, head_start)
        scores = head_scores(q_part, k_part, allowed)
        shares = jnp.exp(scores - log_sum[head_start : head_start + 4])
        v_grad = jnp.einsum(
            "hqk,qhd->khd", shares.astype(jnp.bfloat16), o_part, preferred_element_type=jnp.float32
        )
        p_grad = jnp.einsum("qhd,khd->hqk", o_part, v_part, preferred_element_type=jnp.float32)
        s_grad = shares * (p_grad - jnp.sum(shares * p_grad, axis=-1, keepdims=True))
        s_low = s_grad.astype(jnp.bfloat16)
        q_grad = jnp.einsum(
            "hqk,khd->qhd", s_low, k_part, preferred_element_type=jnp.float32
        ) * HEAD_DIM ** (-0.5)
        k_grad = jnp.einsum(
            "hqk,qhd->khd", s_low, q_part, preferred_element_type=jnp.float32
        ) * HEAD_DIM ** (-0.5)
        q_pieces.append(q_grad.reshape(seq_len, -1))
        k_pieces.append(k_grad.reshape(k.shape[0], -1))
        v_pieces.append(v_grad.reshape(k.shape[0], -1))
    return (
        jnp.concatenate(q_pieces, axis=1).astype(jnp.bfloat16),
        jnp.concatenate(k_pieces, axis=1).astype(jnp.bfloat16),
        jnp.concatenate(v_pieces, axis=1).astype(jnp.bfloat16),
    )


def gated_product(gate_act, up_act):
    return jax.nn.gelu(gate_act, approximate=True) * up_act


MESH = pl.DeviceIdType.MESH


class Place:
    def __init__(self, depth):
        self.depth = depth
        self.wide = lax.axis_index("wide")
        self.x = lax.axis_index("narrow")
        self.core = self.wide % 2
        self.y = (self.wide // 2) % 2
        self.z = self.wide // 4

    def shard(self, z, y, core):
        return z * 4 + y * 2 + core

    def z_ahead(self, step):
        return (self.shard((self.z + step) % self.depth, self.y, self.core), self.x)

    def z_behind(self, step):
        return (self.z + self.depth - step) % self.depth

    @property
    def across_x(self):
        return (self.wide, 1 - self.x)

    @property
    def across_y(self):
        return (self.shard(self.z, 1 - self.y, self.core), self.x)

    @property
    def across_core(self):
        return (self.shard(self.z, self.y, 1 - self.core), self.x)

    def greet(self):
        barrier = pltpu.get_barrier_semaphore()
        others = [self.across_x, self.across_y, self.across_core]
        others += [self.z_ahead(step) for step in range(1, self.depth)]
        for other in others:
            pl.semaphore_signal(barrier, inc=1, device_id=other, device_id_type=MESH)
        pl.semaphore_wait(barrier, len(others))


def remote(src, dst, send, recv, device):
    return pltpu.make_async_remote_copy(
        src_ref=src, dst_ref=dst, send_sem=send, recv_sem=recv, device_id=device, device_id_type=MESH
    )


class Gather:
    def __init__(self, place, own, full, rows, side, sems):
        self.p = place
        self.own = own
        self.full = full
        self.rows = rows
        self.side = side
        self.main = rows - side
        self.z_send, self.z_recv, self.y_send, self.y_recv, self.x_send, self.x_recv, self.c_send, self.c_recv, self.local = sems

    def block(self, ref, start, size):
        return ref.at[:, pl.ds(pl.multiple_of(start, 16), size), :]

    def at(self, z, y, core, start, size):
        return self.block(self.full, self.p.shard(z, y, core) * self.rows + start, size)

    @property
    def main_start(self):
        return self.side * self.p.x

    def side_start(self, x):
        return self.main * x

    def copy_own(self):
        p = self.p
        return pltpu.make_async_copy(self.own, self.at(p.z, p.y, p.core, 0, self.rows), self.local.at[0])

    def z_copy(self, step, z):
        p = self.p
        return remote(
            self.block(self.own, self.main_start, self.main),
            self.at(z, p.y, p.core, self.main_start, self.main),
            self.z_send.at[step - 1],
            self.z_recv.at[step - 1],
            p.z_ahead(step),
        )

    def y_copy(self, step, y):
        p = self.p
        z = p.z_behind(step)
        src = (
            self.block(self.own, self.main_start, self.main)
            if step == 0
            else self.at(z, p.y, p.core, self.main_start, self.main)
        )
        return remote(
            src,
            self.at(z, y, p.core, self.main_start, self.main),
            self.y_send.at[step],
            self.y_recv.at[step],
            p.across_y,
        )

    def x_copy(self, index, x):
        p = self.p
        z, y = (p.z_behind(index + 1), p.y) if index < p.depth - 1 else (p.z_behind(index + 1 - p.depth), 1 - p.y)
        piece = self.at(z, y, p.core, self.side_start(x), self.side)
        return remote(piece, piece, self.x_send.at[index], self.x_recv.at[index], p.across_x)

    def c_copy(self, index, core):
        p = self.p
        depth = p.depth
        if index == 0:
            src, dst = self.own, self.at(p.z, p.y, core, 0, self.rows)
        else:
            if index < depth:
                z, y = p.z_behind(index), p.y
            elif index < 2 * depth:
                z, y = p.z_behind(index - depth), 1 - p.y
            elif index < 3 * depth - 1:
                z, y = p.z_behind(index - 2 * depth + 1), p.y
            else:
                z, y = p.z_behind(index - 3 * depth + 1), 1 - p.y
            if index < 2 * depth:
                start, size = self.main_start, self.main
            else:
                start, size = self.side_start(1 - p.x), self.side
            src = dst = self.at(z, y, core, start, size)
        return remote(src, dst, self.c_send.at[index], self.c_recv.at[index], p.across_core)

    def begin(self):
        p = self.p
        self.copy_own().start()
        self.y_copy(0, p.y).start()
        for step in range(1, p.depth):
            self.z_copy(step, p.z).start()
        self.c_copy(0, p.core).start()

    def pass_z(self):
        p = self.p
        for step in range(1, p.depth):
            self.z_copy(step, p.z_behind(step)).wait_recv()
            self.y_copy(step, p.y).start()
            if self.side:
                self.x_copy(step - 1, p.x).start()
            self.c_copy(step, p.core).start()

    def pass_y(self):
        p = self.p
        for step in range(p.depth):
            self.y_copy(step, 1 - p.y).wait_recv()
            if self.side:
                self.x_copy(p.depth - 1 + step, p.x).start()
            self.c_copy(p.depth + step, p.core).start()

    def pass_x(self):
        p = self.p
        if self.side:
            for index in range(2 * p.depth - 1):
                self.x_copy(index, 1 - p.x).wait_recv()
                self.c_copy(2 * p.depth + index, p.core).start()

    def arrive(self):
        p = self.p
        self.copy_own().wait()
        for index in range(2 * p.depth + (2 * p.depth - 1 if self.side else 0)):
            self.c_copy(index, 1 - p.core).wait_recv()

    def end(self):
        p = self.p
        for step in range(1, p.depth):
            self.z_copy(step, p.z).wait_send()
        for step in range(p.depth):
            self.y_copy(step, p.y).wait_send()
        if self.side:
            for index in range(2 * p.depth - 1):
                self.x_copy(index, p.x).wait_send()
        for index in range(2 * p.depth + (2 * p.depth - 1 if self.side else 0)):
            self.c_copy(index, p.core).wait_send()


def gather_sems(count, depth):
    sizes = (depth - 1, depth - 1, depth, depth, 2 * depth - 1, 2 * depth - 1, 4 * depth - 1, 4 * depth - 1, 1)
    return [pltpu.SemaphoreType.DMA((count, size)) for size in sizes]


def gather_kernel(depth, layout, own_refs, full_refs, sems):
    place = Place(depth)
    blocks = []
    for number, (array, first, last, side) in enumerate(layout):
        own, full = own_refs[array], full_refs[array]
        rows = own.shape[1]
        blocks.append(
            Gather(
                place, own.at[first:last], full.at[first:last], rows, side, [sem.at[number] for sem in sems]
            )
        )
    place.greet()
    count = len(blocks)
    ahead = 2
    for number in range(ahead):
        blocks[number].begin()
    for number in range(count):
        if number + ahead < count:
            blocks[number + ahead].begin()
        blocks[number].pass_z()
        blocks[number].pass_y()
        if number > 0:
            blocks[number - 1].pass_x()
    blocks[count - 1].pass_x()
    for block in blocks:
        block.arrive()
    for block in blocks:
        block.end()


def side_rows(rows):
    return rows // 48 * 16


def gather_all(self_weights, cross_weights, mlp_in, mlp_out, gains):
    wide = lax.axis_size("wide")
    depth = wide // 4
    gain_block = jnp.pad(gains, ((0, 16 - gains.shape[0]), (0, 128 - gains.shape[1])))
    arrays = (self_weights, cross_weights, mlp_in, mlp_out[None], gain_block[None])
    side = side_rows(self_weights.shape[1])
    layout = (
        (4, 0, 1, 0),
        (0, 0, 3, side),
        (0, 3, 4, side),
        (1, 0, 4, side),
        (2, 0, 1, side),
        (2, 1, 2, side),
        (3, 0, 1, side_rows(mlp_out.shape[0])),
    )

    def kernel(*refs):
        gather_kernel(depth, layout, refs[:5], refs[5:10], refs[10:])

    anywhere = pl.BlockSpec(memory_space=pl.ANY)
    gathered = pl.pallas_call(
        kernel,
        out_shape=[
            jax.ShapeDtypeStruct((a.shape[0], wide * a.shape[1], a.shape[2]), a.dtype) for a in arrays
        ],
        in_specs=[anywhere] * 5,
        out_specs=[anywhere] * 5,
        scratch_shapes=gather_sems(len(layout), depth),
        compiler_params=pltpu.CompilerParams(collective_id=0, has_side_effects=True),
        name="gather",
    )(*arrays)
    gain_rows = gathered[4].reshape(wide, 16, 128)[:, : gains.shape[0], : gains.shape[1]]
    gain_full = gain_rows.transpose(1, 0, 2).reshape(gains.shape[0], -1)
    return gathered[0], gathered[1], gathered[2], gathered[3][0], gain_full


class Scatter:
    def __init__(self, place, part, bufs, out, rows, side, sems):
        self.p = place
        self.part = part
        self.held, self.from_x, self.from_y, self.from_z, self.done, self.other = bufs
        self.out = out
        self.rows = rows
        self.side = side
        self.main = rows - side
        self.tile = 16 if part.dtype == jnp.bfloat16 else 8
        self.send, self.recv = sems

    def span(self, start, size):
        return pl.ds(pl.multiple_of(start, self.tile), size)

    @property
    def main_span(self):
        return self.span(self.side * self.p.x, self.main)

    def side_span(self, x):
        return self.span(self.main * x, self.side)

    def c_copy(self):
        p = self.p
        return remote(
            self.part.at[:, :, :, 1 - p.core], self.held, self.send.at[0], self.recv.at[0], p.across_core
        )

    def x_copy(self):
        p = self.p
        return remote(
            self.held.at[:, :, :, self.side_span(1 - p.x)],
            self.from_x,
            self.send.at[1],
            self.recv.at[1],
            p.across_x,
        )

    def y_copy(self):
        p = self.p
        return remote(
            self.held.at[:, :, 1 - p.y, self.main_span], self.from_y, self.send.at[2], self.recv.at[2], p.across_y
        )

    def z_copy(self, step):
        p = self.p
        return remote(
            self.held.at[:, (p.z + step) % p.depth, p.y, self.main_span],
            self.from_z.at[step - 1],
            self.send.at[2 + step],
            self.recv.at[2 + step],
            p.z_ahead(step),
        )

    def last_copy(self):
        p = self.p
        return remote(self.done, self.other, self.send.at[2 + p.depth], self.recv.at[2 + p.depth], p.across_x)

    def step(self, number):
        p = self.p
        mats = self.part.shape[0]
        held = self.held
        if number == 0:
            self.c_copy().start()
        elif number == 1:
            self.c_copy().wait_recv()

            @pl.loop(0, mats * p.depth * 2)
            def _(index):
                m, z, y = index // (2 * p.depth), (index // 2) % p.depth, index % 2
                total = held[m, z, y].astype(jnp.float32) + self.part[m, z, y, p.core].astype(jnp.float32)
                held[m, z, y] = total.astype(held.dtype)

            if self.side:
                self.x_copy().start()
        elif number == 2:
            if self.side:
                self.x_copy().wait_recv()

                @pl.loop(0, mats * p.depth * 2)
                def _(index):
                    m, z, y = index // (2 * p.depth), (index // 2) % p.depth, index % 2
                    total = held[m, z, y, self.side_span(p.x)].astype(jnp.float32) + self.from_x[m, z, y].astype(jnp.float32)
                    held[m, z, y, self.side_span(p.x)] = total.astype(held.dtype)

            self.y_copy().start()
        elif number == 3:
            self.y_copy().wait_recv()

            @pl.loop(0, mats * p.depth)
            def _(index):
                m, z = index // p.depth, index % p.depth
                total = held[m, z, p.y, self.main_span].astype(jnp.float32) + self.from_y[m, z].astype(jnp.float32)
                held[m, z, p.y, self.main_span] = total.astype(held.dtype)

            for step in range(1, p.depth):
                self.z_copy(step).start()
        elif number == 4:
            for step in range(1, p.depth):
                self.z_copy(step).wait_recv()

            @pl.loop(0, mats)
            def _(m):
                total = held[m, p.z, p.y, self.main_span].astype(jnp.float32)
                for step in range(1, p.depth):
                    total += self.from_z[step - 1, m].astype(jnp.float32)
                self.done[m] = total.astype(held.dtype)

            self.last_copy().start()
        elif number == 5:
            self.last_copy().wait_recv()
            both = self.main - self.side
            side = self.side

            @pl.loop(0, mats)
            def _(m):
                if side:
                    self.out[m, self.side_span(p.x)] = self.done[m, self.span(both * p.x, side)].astype(jnp.float32)
                    self.out[m, self.side_span(1 - p.x)] = self.other[m, self.span(both * (1 - p.x), side)].astype(
                        jnp.float32
                    )
                self.out[m, side : side + both] = self.done[m, self.span(side * (1 - p.x), both)].astype(
                    jnp.float32
                ) + self.other[m, self.span(side * p.x, both)].astype(jnp.float32)

    def end(self):
        p = self.p
        self.c_copy().wait_send()
        if self.side:
            self.x_copy().wait_send()
        self.y_copy().wait_send()
        for step in range(1, p.depth):
            self.z_copy(step).wait_send()
        self.last_copy().wait_send()


def scatter_buffers(mats, depth, rows, side, columns, dtype):
    main = rows - side
    return [
        pltpu.VMEM((mats, depth, 2, rows, columns), dtype),
        pltpu.VMEM((mats, depth, 2, max(side, 8), columns) if side else (8, 128), dtype),
        pltpu.VMEM((mats, depth, main, columns), dtype),
        pltpu.VMEM((depth - 1, mats, main, columns), dtype),
        pltpu.VMEM((mats, main, columns), dtype),
        pltpu.VMEM((mats, main, columns), dtype),
    ]


def scatter_all(self_grad, cross_grad, in_grad, out_grad, gain_grad):
    wide = lax.axis_size("wide")
    depth = wide // 4
    gain_rows = gain_grad.reshape(gain_grad.shape[0], wide, -1).transpose(1, 0, 2)
    gain_rows = jnp.pad(gain_rows, ((0, 0), (0, 8 - gain_rows.shape[1]), (0, 128 - gain_rows.shape[2])))
    low = jnp.bfloat16
    arrays = (self_grad.astype(low), cross_grad.astype(low), in_grad.astype(low), out_grad[None].astype(low), gain_rows[None])
    arrays = [a.reshape(a.shape[0], depth, 2, 2, -1, a.shape[-1]) for a in arrays]
    side = arrays[0].shape[4] // 3
    layout = (
        (3, 0, 1, arrays[3].shape[4] // 4),
        (2, 0, 1, side),
        (2, 1, 2, side),
        (1, 0, 3, side),
        (1, 3, 4, 0),
        (0, 0, 3, side),
        (0, 3, 4, 0),
        (4, 0, 1, 0),
    )
    buffers = []
    for array, first, last, side in layout:
        a = arrays[array]
        buffers += scatter_buffers(last - first, depth, a.shape[4], side, a.shape[5], a.dtype)

    def kernel(*refs):
        place = Place(depth)
        parts, outs, bufs, sems = refs[:5], refs[5:10], refs[10:-2], refs[-2:]
        blocks = []
        for number, (array, first, last, side) in enumerate(layout):
            blocks.append(
                Scatter(
                    place,
                    parts[array].at[first:last],
                    bufs[6 * number : 6 * number + 6],
                    outs[array].at[first:last],
                    parts[array].shape[4],
                    side,
                    [sem.at[number] for sem in sems],
                )
            )
        place.greet()
        count = len(blocks)
        for turn in range(count + 5):
            for number in range(count):
                if 0 <= turn - number < 6:
                    blocks[number].step(turn - number)
        for block in blocks:
            block.end()

    vmem = pl.BlockSpec(memory_space=pltpu.VMEM)
    outs = pl.pallas_call(
        kernel,
        out_shape=[jax.ShapeDtypeStruct((a.shape[0], a.shape[4], a.shape[5]), jnp.float32) for a in arrays],
        in_specs=[vmem] * 5,
        out_specs=[vmem] * 5,
        scratch_shapes=buffers + [pltpu.SemaphoreType.DMA((len(layout), 3 + depth))] * 2,
        compiler_params=pltpu.CompilerParams(
            collective_id=1, has_side_effects=True, vmem_limit_bytes=56 * 2**20
        ),
        name="scatter",
    )(*arrays)
    return outs[0], outs[1], outs[2], outs[3][0], outs[4][0, : gain_grad.shape[0], : gain_grad.shape[1] // wide]


def plain_gather(self_weights, cross_weights, mlp_in, mlp_out, gains):
    return (
        lax.all_gather(self_weights, "wide", axis=1, tiled=True),
        lax.all_gather(cross_weights, "wide", axis=1, tiled=True),
        lax.all_gather(mlp_in, "wide", axis=1, tiled=True),
        lax.all_gather(mlp_out, "wide", axis=0, tiled=True),
        lax.all_gather(gains, "wide", axis=1, tiled=True),
    )


def plain_scatter(*grads):
    outs = []
    for grad, axis in zip(grads, (1, 1, 1, 0, 1)):
        piece = lax.psum_scatter(grad, ("wide", "narrow"), scatter_dimension=axis, tiled=True)
        outs.append(lax.all_gather(piece.astype(jnp.bfloat16), "narrow", axis=axis, tiled=True).astype(jnp.float32))
    return tuple(outs)


def by_kernel(self_weights):
    return lax.axis_size("wide") == 16 and lax.axis_size("narrow") == 2 and self_weights.shape[1] % 48 == 0


def on_device(
    layer_input,
    memory,
    cotangent,
    segment_ids,
    padding,
    image_of_row,
    self_weights,
    cross_weights,
    mlp_in,
    mlp_out,
    gains,
):
    kernels = by_kernel(self_weights)
    self_full, cross_full, in_full, out_full, gain_full = (gather_all if kernels else plain_gather)(
        self_weights, cross_weights, mlp_in, mlp_out, gains
    )
    gain_float = gain_full.astype(jnp.float32)
    x_zero = layer_input[0].astype(jnp.float32)
    seg_row = segment_ids[0]
    pad_row = padding[0]
    seq_len = x_zero.shape[0]
    position = jnp.arange(seq_len)
    allowed = (
        (seg_row[:, None] == seg_row[None, :])
        & (position[None, :] <= position[:, None])
        & ((pad_row[None, :] == 1) | (position[:, None] == position[None, :]))
    )
    h_one = rms_norm(x_zero, gain_float[0]).astype(jnp.bfloat16)
    q_self = linear(h_one, self_full[0]).astype(jnp.bfloat16)
    k_self = linear(h_one, self_full[1]).astype(jnp.bfloat16)
    v_self = linear(h_one, self_full[2]).astype(jnp.bfloat16)
    self_mix, self_lse = forward_heads(q_self, k_self, v_self, allowed)
    x_one = x_zero + linear(self_mix, self_full[3])
    row_ids = jnp.arange(image_of_row.shape[0])
    starts = jnp.sum(image_of_row[None, :] < image_of_row[:, None], axis=1)
    offsets = row_ids - starts
    my_index = lax.axis_index(("wide", "narrow"))
    my_offset = jnp.sum(jnp.where(row_ids == my_index, offsets, 0))
    own_patches = memory[0]
    memory_use = own_patches
    for distance in (1, 2, 3):
        arrived = shifted(own_patches, ("wide", "narrow"), distance)
        memory_use = jnp.where(my_offset == distance, arrived, memory_use)
    h_two = rms_norm(x_one, gain_float[1]).astype(jnp.bfloat16)
    q_cross = linear(h_two, cross_full[0]).astype(jnp.bfloat16)
    k_cross = linear(memory_use, cross_full[1]).astype(jnp.bfloat16)
    v_cross = linear(memory_use, cross_full[2]).astype(jnp.bfloat16)
    cross_mix, cross_lse = forward_heads(q_cross, k_cross, v_cross, None)
    x_two = x_one + linear(cross_mix, cross_full[3])
    h_three = rms_norm(x_two, gain_float[2]).astype(jnp.bfloat16)
    gate_act = linear(h_three, in_full[0])
    up_act = linear(h_three, in_full[1])
    hidden = gated_product(gate_act, up_act).astype(jnp.bfloat16)
    result = x_two + linear(hidden, out_full)
    out_low = cotangent[0]
    out_grad_w = contract_rows(hidden, out_low)
    hidden_grad = times_transposed(out_low, out_full)
    _, pullback = jax.vjp(gated_product, gate_act, up_act)
    gate_grad, up_grad = pullback(hidden_grad)
    gate_low = gate_grad.astype(jnp.bfloat16)
    up_low = up_grad.astype(jnp.bfloat16)
    in_grad = jnp.stack([contract_rows(h_three, gate_low), contract_rows(h_three, up_low)])
    h_three_grad = times_transposed(gate_low, in_full[0]) + times_transposed(up_low, in_full[1])
    _, pullback = jax.vjp(rms_norm, x_two, gain_float[2])
    x_two_norm, gain_three = pullback(h_three_grad)
    x_two_grad = out_low.astype(jnp.float32) + x_two_norm
    cross_out_low = x_two_grad.astype(jnp.bfloat16)
    cross_o_grad = contract_rows(cross_mix, cross_out_low)
    cross_mix_grad = times_transposed(cross_out_low, cross_full[3]).astype(jnp.bfloat16)
    q_cross_grad, k_cross_grad, v_cross_grad = backward_heads(
        q_cross, k_cross, v_cross, cross_mix_grad, cross_lse, None
    )
    cross_grad = jnp.stack(
        [
            contract_rows(h_two, q_cross_grad),
            contract_rows(memory_use, k_cross_grad),
            contract_rows(memory_use, v_cross_grad),
            cross_o_grad,
        ]
    )
    mem_grad = times_transposed(k_cross_grad, cross_full[1]) + times_transposed(
        v_cross_grad, cross_full[2]
    )
    h_two_grad = times_transposed(q_cross_grad, cross_full[0])
    _, pullback = jax.vjp(rms_norm, x_one, gain_float[1])
    x_one_norm, gain_two = pullback(h_two_grad)
    x_one_grad = x_two_grad + x_one_norm
    self_out_low = x_one_grad.astype(jnp.bfloat16)
    self_o_grad = contract_rows(self_mix, self_out_low)
    self_mix_grad = times_transposed(self_out_low, self_full[3]).astype(jnp.bfloat16)
    q_self_grad, k_self_grad, v_self_grad = backward_heads(
        q_self, k_self, v_self, self_mix_grad, self_lse, allowed
    )
    self_grad = jnp.stack(
        [
            contract_rows(h_one, q_self_grad),
            contract_rows(h_one, k_self_grad),
            contract_rows(h_one, v_self_grad),
            self_o_grad,
        ]
    )
    h_one_grad = (
        times_transposed(q_self_grad, self_full[0])
        + times_transposed(k_self_grad, self_full[1])
        + times_transposed(v_self_grad, self_full[2])
    )
    _, pullback = jax.vjp(rms_norm, x_zero, gain_float[0])
    x_zero_norm, gain_one = pullback(h_one_grad)
    x_grad = x_one_grad + x_zero_norm
    mem_summed = jnp.where(my_offset == 0, mem_grad, 0.0)
    for distance in (1, 2, 3):
        arrived = shifted(mem_grad.astype(jnp.bfloat16), ("wide", "narrow"), -distance).astype(
            mem_grad.dtype
        )
        neighbour = jnp.sum(jnp.where(row_ids == my_index + distance, offsets, 0))
        mem_summed = mem_summed + jnp.where(neighbour == distance, arrived, 0.0)
    gain_grad = jnp.stack([gain_one, gain_two, gain_three])
    reduced = (scatter_all if kernels else plain_scatter)(self_grad, cross_grad, in_grad, out_grad_w, gain_grad)
    return (
        result.astype(jnp.bfloat16)[None],
        x_grad[None],
        mem_summed[None],
        reduced[0],
        reduced[1],
        reduced[2],
        reduced[3],
        reduced[4],
    )


def solution(mesh):
    in_specs = (
        P(("wide", "narrow"), None, None),
        P(("wide", "narrow"), None, None),
        P(("wide", "narrow"), None, None),
        P(("wide", "narrow"), None),
        P(("wide", "narrow"), None),
        P(),
        P(None, "wide", None),
        P(None, "wide", None),
        P(None, "wide", None),
        P("wide", None),
        P(None, "wide"),
    )
    out_specs = (
        P(("wide", "narrow"), None, None),
        P(("wide", "narrow"), None, None),
        P(("wide", "narrow"), None, None),
        P(None, "wide", None),
        P(None, "wide", None),
        P(None, "wide", None),
        P("wide", None),
        P(None, "wide"),
    )
    return jax.shard_map(
        on_device, mesh=mesh, in_specs=in_specs, out_specs=out_specs, check_vma=False
    )
```

```python
import functools

import jax
import jax.numpy as jnp
from jax import lax
from jax.experimental import pallas as pl
from jax.experimental.pallas import tpu as pltpu
from jax.sharding import PartitionSpec as P

HEAD_DIM = 64


EPSILON = 1e-06


def shifted(value, axis, steps):
    count = lax.axis_size(axis)
    first, last = (max(0, -steps), min(count, count - steps))
    return lax.ppermute(value, axis, [(source, source + steps) for source in range(first, last)])


def rms_norm(v, g):
    return v * lax.rsqrt(jnp.mean(v * v, axis=-1, keepdims=True) + EPSILON) * g


def contract_rows(a, b):
    return lax.dot_general(a, b, (((0,), (0,)), ((), ())), preferred_element_type=jnp.float32)


def times_transposed(a, w):
    return lax.dot_general(a, w, (((1,), (1,)), ((), ())), preferred_element_type=jnp.float32)


def linear(a, w):
    return jnp.dot(a, w, preferred_element_type=jnp.float32)


def head_scores(q_part, k_part, allowed):
    scores = jnp.einsum(
        "qhd,khd->hqk", q_part, k_part, preferred_element_type=jnp.float32
    ) * HEAD_DIM ** (-0.5)
    if allowed is not None:
        scores = jnp.where(allowed[None], scores, -1e30)
    return scores


def split_heads(a, head_start):
    return a[:, head_start * HEAD_DIM : (head_start + 4) * HEAD_DIM].reshape(
        a.shape[0], 4, HEAD_DIM
    )


def forward_heads(q, k, v, allowed):
    seq_len = q.shape[0]
    head_count = q.shape[1] // HEAD_DIM
    pieces = []
    log_sums = []
    for head_start in range(0, head_count, 4):
        q_part = split_heads(q, head_start)
        k_part = split_heads(k, head_start)
        v_part = split_heads(v, head_start)
        scores = head_scores(q_part, k_part, allowed)
        highest = jnp.max(scores, axis=-1, keepdims=True)
        powers = jnp.exp(scores - highest)
        summed = jnp.sum(powers, axis=-1, keepdims=True)
        shares = (powers / summed).astype(jnp.bfloat16)
        mixed = jnp.einsum("hqk,khd->qhd", shares, v_part, preferred_element_type=jnp.float32)
        pieces.append(mixed.reshape(seq_len, -1))
        log_sums.append(highest + jnp.log(summed))
    return (jnp.concatenate(pieces, axis=1).astype(jnp.bfloat16), jnp.concatenate(log_sums, axis=0))


def backward_heads(q, k, v, mix_grad, log_sum, allowed):
    seq_len = q.shape[0]
    head_count = q.shape[1] // HEAD_DIM
    q_pieces = []
    k_pieces = []
    v_pieces = []
    for head_start in range(0, head_count, 4):
        q_part = split_heads(q, head_start)
        k_part = split_heads(k, head_start)
        v_part = split_heads(v, head_start)
        o_part = split_heads(mix_grad, head_start)
        scores = head_scores(q_part, k_part, allowed)
        shares = jnp.exp(scores - log_sum[head_start : head_start + 4])
        v_grad = jnp.einsum(
            "hqk,qhd->khd", shares.astype(jnp.bfloat16), o_part, preferred_element_type=jnp.float32
        )
        p_grad = jnp.einsum("qhd,khd->hqk", o_part, v_part, preferred_element_type=jnp.float32)
        s_grad = shares * (p_grad - jnp.sum(shares * p_grad, axis=-1, keepdims=True))
        s_low = s_grad.astype(jnp.bfloat16)
        q_grad = jnp.einsum(
            "hqk,khd->qhd", s_low, k_part, preferred_element_type=jnp.float32
        ) * HEAD_DIM ** (-0.5)
        k_grad = jnp.einsum(
            "hqk,qhd->khd", s_low, q_part, preferred_element_type=jnp.float32
        ) * HEAD_DIM ** (-0.5)
        q_pieces.append(q_grad.reshape(seq_len, -1))
        k_pieces.append(k_grad.reshape(k.shape[0], -1))
        v_pieces.append(v_grad.reshape(k.shape[0], -1))
    return (
        jnp.concatenate(q_pieces, axis=1).astype(jnp.bfloat16),
        jnp.concatenate(k_pieces, axis=1).astype(jnp.bfloat16),
        jnp.concatenate(v_pieces, axis=1).astype(jnp.bfloat16),
    )


def gated_product(gate_act, up_act):
    return jax.nn.gelu(gate_act, approximate=True) * up_act


MESH = pl.DeviceIdType.MESH


class Place:
    def __init__(self, depth):
        self.depth = depth
        self.wide = lax.axis_index("wide")
        self.x = lax.axis_index("narrow")
        self.core = self.wide % 2
        self.y = (self.wide // 2) % 2
        self.z = self.wide // 4

    def shard(self, z, y, core):
        return z * 4 + y * 2 + core

    def z_ahead(self, step):
        return (self.shard((self.z + step) % self.depth, self.y, self.core), self.x)

    def z_behind(self, step):
        return (self.z + self.depth - step) % self.depth

    @property
    def across_x(self):
        return (self.wide, 1 - self.x)

    @property
    def across_y(self):
        return (self.shard(self.z, 1 - self.y, self.core), self.x)

    @property
    def across_core(self):
        return (self.shard(self.z, self.y, 1 - self.core), self.x)

    def greet(self):
        barrier = pltpu.get_barrier_semaphore()
        others = [self.across_x, self.across_y, self.across_core]
        others += [self.z_ahead(step) for step in range(1, self.depth)]
        for other in others:
            pl.semaphore_signal(barrier, inc=1, device_id=other, device_id_type=MESH)
        pl.semaphore_wait(barrier, len(others))


def remote(src, dst, send, recv, device):
    return pltpu.make_async_remote_copy(
        src_ref=src, dst_ref=dst, send_sem=send, recv_sem=recv, device_id=device, device_id_type=MESH
    )


class Gather:
    def __init__(self, place, own, full, rows, side, y_first, sems):
        self.p = place
        self.own = own
        self.full = full
        self.rows = rows
        self.side = side
        self.main = rows - side
        self.y_first = y_first
        self.main_send, self.main_recv, self.x_send, self.x_recv, self.c_send, self.c_recv = sems

    def block(self, ref, start, size):
        return ref.at[:, pl.ds(pl.multiple_of(start, 16), size), :]

    def at(self, z, y, core, start, size):
        return self.block(self.full, self.p.shard(z, y, core) * self.rows + start, size)

    def owner(self, n):
        step, other = n % self.p.depth, n // self.p.depth
        return self.p.z_behind(step), (1 - self.p.y if other else self.p.y)

    @property
    def main_start(self):
        return self.side * self.p.x

    def side_start(self, x):
        return self.main * x

    def main_piece(self, z, y, source=False):
        p = self.p
        return self.at(z, y, p.core, self.main_start, self.main)

    def arriving(self, n):
        p = self.p
        z, y = self.owner(n)
        piece = self.main_piece(z, y)
        return remote(piece, piece, self.main_send.at[0], self.main_recv.at[n], p.across_y)

    def y_copy(self, n):
        p = self.p
        z, y = self.owner(n)
        dst = self.main_piece(z, y)
        src = self.block(self.own, self.main_start, self.main) if n == 0 else dst
        return remote(src, dst, self.main_send.at[n], self.main_recv.at[n + p.depth], p.across_y)

    def z_copy(self, step, other):
        p = self.p
        y = 1 - p.y if other else p.y
        dst = self.main_piece(p.z, y)
        src = dst if other else self.block(self.own, self.main_start, self.main)
        slot = p.depth + (step - 1) + (p.depth - 1) * other
        return remote(
            src, dst, self.main_send.at[slot], self.main_recv.at[step + p.depth * other], p.z_ahead(step)
        )

    def relay_copy(self, other, up):
        p = self.p
        z, target = (0, 3) if up else (3, 0)
        y = 1 - p.y if other else p.y
        piece = self.main_piece(z, y)
        slot = p.depth + 2 * (p.depth - 1) + other
        step = 3 if up else 1
        device = (p.shard(target, p.y, p.core), p.x)
        return remote(piece, piece, self.main_send.at[slot], self.main_recv.at[step + p.depth * other], device)

    def x_copy(self, n, x):
        p = self.p
        z, y = self.owner(n)
        piece = self.at(z, y, p.core, self.side_start(x), self.side)
        return remote(piece, piece, self.x_send.at[n], self.x_recv.at[n], p.across_x)

    def c_copy(self, n, core, side):
        p = self.p
        slot = n + (2 * p.depth if side else 0)
        z, y = self.owner(n)
        if n == 0:
            src, dst = self.own, self.at(z, y, core, 0, self.rows)
        else:
            start, size = (self.side_start(1 - p.x), self.side) if side else (self.main_start, self.main)
            src = dst = self.at(z, y, core, start, size)
        return remote(src, dst, self.c_send.at[slot], self.c_recv.at[slot], p.across_core)

    def copy_own(self):
        p = self.p
        return pltpu.make_async_copy(self.own, self.at(p.z, p.y, p.core, 0, self.rows), self.main_send.at[4 * p.depth])

    def each_z(self, other, act):
        p = self.p
        for step in range(1, p.depth):
            if step == 2:
                act(self.z_copy(step, other))
            else:
                end = 0 if step == 3 else 3

                @pl.when(p.z != end)
                def _():
                    act(self.z_copy(step, other))

    def each_relay(self, other, act):
        p = self.p

        @pl.when(p.z == 2)
        def _():
            act(self.relay_copy(other, True))

        @pl.when(p.z == 1)
        def _():
            act(self.relay_copy(other, False))

    def begin(self):
        self.copy_own().start()
        self.y_copy(0).start()
        self.each_z(0, lambda copy: copy.start())
        self.c_copy(0, self.p.core, False).start()

    def order(self):
        depth = self.p.depth
        if self.y_first:
            return [depth, 2, 2 + depth, 1, 3, 1 + depth, 3 + depth]
        return [2, 1, 3, depth, depth + 2, depth + 1, depth + 3]

    def take(self, n):
        p = self.p
        depth = p.depth
        self.arriving(n).wait_recv()
        other = n // depth
        if n % depth == 2 and (self.y_first or other == 0):
            self.each_relay(other, lambda copy: copy.start())
        if self.y_first:
            if n == depth:
                self.each_z(1, lambda copy: copy.start())
        elif other == 0:
            self.y_copy(n).start()
        if self.side:
            self.x_copy(n, p.x).start()
        self.c_copy(n, p.core, False).start()

    def take_x(self, n):
        p = self.p
        if self.side:
            self.x_copy(n, 1 - p.x).wait_recv()
            self.c_copy(n, p.core, True).start()

    def complete(self):
        p = self.p
        self.copy_own().wait()
        for n in range(2 * p.depth):
            self.c_copy(n, 1 - p.core, False).wait_recv()
            if self.side and n:
                self.c_copy(n, 1 - p.core, True).wait_recv()

    def end(self):
        p = self.p

        def wait(copy):
            copy.wait_send()

        for n in range(1 if self.y_first else p.depth):
            self.y_copy(n).wait_send()
        for other in range(2 if self.y_first else 1):
            self.each_z(other, wait)
            self.each_relay(other, wait)
        for n in range(2 * p.depth):
            self.c_copy(n, p.core, False).wait_send()
            if self.side and n:
                self.x_copy(n, p.x).wait_send()
                self.c_copy(n, p.core, True).wait_send()


def gather_sems(count, depth):
    sizes = (4 * depth + 1, 2 * depth, 2 * depth, 2 * depth, 4 * depth, 4 * depth)
    return [pltpu.SemaphoreType.DMA((count, size)) for size in sizes]


LOW = jnp.bfloat16


def dot(a, b, ca=1, cb=0):
    return lax.dot_general(a, b, (((ca,), (cb,)), ((), ())), preferred_element_type=jnp.float32)


def norm_rows(source, gain, target):
    rows = source.shape[0]
    chunk = 64

    @pl.loop(0, rows // chunk)
    def _(i):
        span = pl.ds(pl.multiple_of(i * chunk, chunk), chunk)
        v = source[span].astype(jnp.float32)
        scale = lax.rsqrt(jnp.mean(v * v, axis=-1, keepdims=True) + EPSILON)
        target[span] = (v * scale * gain).astype(LOW)


def norm_back_rows(source, gain, grad, dout, target, gain_grad):
    rows, width = source.shape
    chunk = 64
    gain_grad[...] = jnp.zeros_like(gain_grad)

    @pl.loop(0, rows // chunk)
    def _(i):
        span = pl.ds(pl.multiple_of(i * chunk, chunk), chunk)
        v = source[span].astype(jnp.float32)
        dh = grad[span]
        scale = lax.rsqrt(jnp.mean(v * v, axis=-1, keepdims=True) + EPSILON)
        unit = v * scale
        gain_grad[...] += jnp.sum(dh * unit, axis=0, keepdims=True)
        scaled = dh * gain
        along = jnp.mean(scaled * unit, axis=-1, keepdims=True)
        target[span] = (dout[span].astype(jnp.float32) + scale * (scaled - unit * along)).astype(target.dtype)


def pair_span(pair):
    return pl.ds(pl.multiple_of(pair * 2 * HEAD_DIM, 2 * HEAD_DIM), 2 * HEAD_DIM)


def attend_pair(pair, q, k, v, bias, mixed, lse):
    span = pair_span(pair)
    q_two, k_two, v_two = q[:, span], k[:, span], v[:, span]
    rows = q_two.shape[0]
    low_half = lax.broadcasted_iota(jnp.int32, q_two.shape, 1) < HEAD_DIM
    lane = lax.broadcasted_iota(jnp.int32, (rows, 128), 1)
    outs = []
    sums = lse[...]
    for half in range(2):
        mine = low_half if half == 0 else ~low_half
        scores = dot(jnp.where(mine, q_two, jnp.zeros_like(q_two)), k_two, 1, 1) * HEAD_DIM ** (-0.5)
        if bias is not None:
            scores = scores + bias[...]
        highest = jnp.max(scores, axis=-1, keepdims=True)
        powers = jnp.exp(scores - highest)
        summed = jnp.sum(powers, axis=-1, keepdims=True)
        shares = (powers / summed).astype(LOW)
        outs.append(dot(shares, v_two))
        sums = jnp.where(lane == 2 * pair + half, highest + jnp.log(summed), sums)
    mixed[:, span] = jnp.where(low_half, outs[0], outs[1]).astype(LOW)
    lse[...] = sums


def gelu_parts(gate):
    inner = (2.0 / 3.141592653589793) ** 0.5
    square = gate * gate
    bent = jnp.tanh(inner * gate * (1.0 + 0.044715 * square))
    half = 0.5 * (1.0 + bent)
    slope = half + 0.5 * gate * (1.0 - bent * bent) * inner * (1.0 + 3 * 0.044715 * square)
    return gate * half, slope


class Rows:
    def __init__(self, place, count):
        self.p = place
        self.count = count
        self.row = place.wide * 2 + place.x

    def device(self, row):
        return (row // 2, row % 2)

    def when(self, distance, act):
        @pl.when((self.row + distance >= 0) & (self.row + distance < self.count))
        def _():
            act(self.device(self.row + distance))

    def near(self):
        return (-2, -1, 1, 2)

    def present(self):
        below = jnp.minimum(self.row, 2)
        above = jnp.minimum(self.count - 1 - self.row, 2)
        return below + above


def greet_all(place, rows):
    barrier = pltpu.get_barrier_semaphore()
    others = [place.across_x, place.across_y, place.across_core]
    others += [place.z_ahead(step) for step in range(1, place.depth)]

    def hello(device):
        pl.semaphore_signal(barrier, inc=1, device_id=device, device_id_type=MESH)

    for other in others:
        hello(other)
    for distance in rows.near():
        rows.when(distance, hello)
    pl.semaphore_wait(barrier, len(others) + rows.present())


def pass_rows(rows, source, target, distance, sems):
    send, recv = sems

    def copy(device):
        return remote(source, target, send, recv, device)

    def start():
        rows.when(distance, lambda device: copy(device).start())

    def arrive():
        rows.when(-distance, lambda device: copy(device).wait_recv())

    def end():
        rows.when(distance, lambda device: copy(device).wait_send())

    return start, arrive, end


GATHER_LAYOUT = (
    (4, 0, 1, 0, 128, 0),
    (0, 0, 3, 0, 768, 16),
    (0, 3, 4, 0, 768, 16),
    (1, 0, 2, 0, 768, 16),
    (1, 2, 4, 0, 768, 16),
    (3, 0, 1, 0, 768, 48),
    (2, 0, 2, 0, 512, 16),
    (2, 0, 2, 512, 1024, 16),
    (2, 0, 2, 1024, 1536, 16),
    (2, 0, 2, 1536, 2048, 16),
)
SELF_IN, SELF_OUT, CROSS_IN, CROSS_OUT, MLP_OUT, MLP_IN = 1, 2, 3, 4, 5, 6
WIDTH, HIDDEN, TOKENS, PATCHES = 768, 2048, 384, 256

KEPT = (
    ("gain", (8, WIDTH), jnp.float32),
    ("h1t", (WIDTH, TOKENS), LOW),
    ("q1", (TOKENS, WIDTH), LOW),
    ("k1", (TOKENS, WIDTH), LOW),
    ("v1", (TOKENS, WIDTH), LOW),
    ("o1t", (WIDTH, TOKENS), LOW),
    ("lse1", (128, TOKENS), jnp.float32),
    ("x1", (TOKENS, WIDTH), jnp.float32),
    ("h2t", (WIDTH, TOKENS), LOW),
    ("memt", (WIDTH, PATCHES), LOW),
    ("q2", (TOKENS, WIDTH), LOW),
    ("k2", (PATCHES, WIDTH), LOW),
    ("v2", (PATCHES, WIDTH), LOW),
    ("o2t", (WIDTH, TOKENS), LOW),
    ("lse2", (128, TOKENS), jnp.float32),
    ("h3t", (WIDTH, TOKENS), LOW),
    ("hiddent", (HIDDEN, TOKENS), LOW),
    ("dgate", (TOKENS, HIDDEN), LOW),
    ("dup", (TOKENS, HIDDEN), LOW),
    ("dx2", (TOKENS, WIDTH), jnp.float32),
    ("gain3", (1, WIDTH), jnp.float32),
)
WEIGHTS = (
    ("w_self", (4, WIDTH, WIDTH)),
    ("w_cross", (4, WIDTH, WIDTH)),
    ("w_in", (2, WIDTH, HIDDEN)),
    ("w_out", (1, HIDDEN, WIDTH)),
    ("w_gain", (1, 256, 128)),
)
FORWARD_LOCAL = (
    ("bias", (TOKENS, TOKENS), jnp.float32),
    ("h", (TOKENS, WIDTH), LOW),
    ("mix", (TOKENS, WIDTH), LOW),
    ("lse", (TOKENS, 128), jnp.float32),
    ("mem_one", (PATCHES, WIDTH), LOW),
    ("mem", (PATCHES, WIDTH), LOW),
    ("mem_got", (2, PATCHES, WIDTH), LOW),
    ("x2", (TOKENS, WIDTH), jnp.float32),
    ("gate", (TOKENS, 512), jnp.float32),
    ("up", (TOKENS, 512), jnp.float32),
    ("dhid", (TOKENS, 512), jnp.float32),
    ("hidden", (TOKENS, HIDDEN), LOW),
    ("dh", (TOKENS, WIDTH), jnp.float32),
)


def forward_kernel(depth, row_count, refs):
    (x0, dy, memory, seg_row, seg_col, flags) = refs[:6]
    owns = refs[6:11]
    out = refs[11]
    kept_out = dict(zip([k[0] for k in KEPT] + ["w_self", "w_cross"], refs[12 : 12 + len(KEPT) + 2]))
    rest = refs[12 + len(KEPT) + 2 :]
    kept = dict(zip([k[0] for k in KEPT], rest))
    rest = rest[len(KEPT) :]
    weights = dict(zip([w[0] for w in WEIGHTS], rest))
    rest = rest[len(WEIGHTS) :]
    local = dict(zip([k[0] for k in FORWARD_LOCAL], rest))
    rest = rest[len(FORWARD_LOCAL) :]
    gather_sem, row_sem, keep_sem = rest[:6], rest[6], rest[7]
    kept_numbers = {name: number for number, name in enumerate(kept_out)}

    def keep_copy(name):
        source = weights[name] if name in weights else kept[name]
        return pltpu.make_async_copy(source, kept_out[name], keep_sem.at[kept_numbers[name]])

    def keep(*names):
        for name in names:
            keep_copy(name).start()

    place = Place(depth)
    rows = Rows(place, row_count)
    fulls = [weights[w[0]] for w in WEIGHTS]
    blocks = []
    for number, (array, first, last, c0, c1, side) in enumerate(GATHER_LAYOUT):
        own, full = owns[array], fulls[array]
        blocks.append(
            Gather(
                place,
                own.at[first:last, :, c0:c1],
                full.at[first:last, :, c0:c1],
                own.shape[1],
                side,
                False,
                [sem.at[number] for sem in gather_sem],
            )
        )
    near_start, near_arrive, near_end = pass_rows(
        rows, memory, local["mem_got"].at[0], 1, (row_sem.at[0], row_sem.at[1])
    )
    far_start, far_arrive, far_end = pass_rows(
        rows, local["mem_one"], local["mem_got"].at[1], 2, (row_sem.at[2], row_sem.at[3])
    )
    gain = kept["gain"]

    def make_bias():
        seg_q, seg_k = seg_col[:, 0:1], seg_row[0:1, :]
        query = lax.broadcasted_iota(jnp.int32, (TOKENS, TOKENS), 0)
        key = lax.broadcasted_iota(jnp.int32, (TOKENS, TOKENS), 1)
        allowed = (seg_q == seg_k) & (key <= query) & ((seg_row[1:2, :] == 1) | (key == query))
        local["bias"][...] = jnp.where(allowed, 0.0, -1e30)

    def make_gain():
        total = jnp.zeros((16, WIDTH), jnp.float32)
        count = row_count // 2
        share = WIDTH // count
        for number in range(count):
            row = lax.broadcasted_iota(jnp.int32, (128, WIDTH), 0)
            column = lax.broadcasted_iota(jnp.int32, (128, WIDTH), 1)
            pick = ((column - number * share) == row) & (row < share)
            total += dot(weights["w_gain"][0, number * 16 : number * 16 + 16, :], pick.astype(LOW))
        gain[...] = total[:8]

    def first_norm():
        norm_rows(x0, gain[0:1], local["h"])
        kept["h1t"][...] = local["h"][...].T
        keep("gain", "h1t")

    def project(name, w, index):
        def run():
            kept[name][...] = dot(local["h"][...], weights[w][index]).astype(LOW)
            keep(name)

        return run

    def self_pair(pair):
        return lambda: attend_pair(pair, kept["q1"], kept["k1"], kept["v1"], local["bias"], local["mix"], local["lse"])

    def clear_lse():
        local["lse"][...] = jnp.zeros_like(local["lse"])

    def self_out():
        kept["lse1"][...] = local["lse"][...].T
        kept["o1t"][...] = local["mix"][...].T
        kept["x1"][...] = x0[...].astype(jnp.float32) + dot(local["mix"][...], weights["w_self"][3])
        keep("lse1", "o1t", "x1")

    def second_norm():
        norm_rows(kept["x1"], gain[1:2], local["h"])
        kept["h2t"][...] = local["h"][...].T
        keep("h2t")

    def memory_near():
        near_arrive()
        local["mem_one"][...] = jnp.where(flags[0] >= 1, local["mem_got"][0], memory[...])
        far_start()

    def memory_far():
        far_arrive()
        local["mem"][...] = jnp.where(flags[0] >= 2, local["mem_got"][1], local["mem_one"][...])
        kept["memt"][...] = local["mem"][...].T
        keep("memt")

    def project_memory(name, index):
        def run():
            kept[name][...] = dot(local["mem"][...], weights["w_cross"][index]).astype(LOW)
            keep(name)

        return run

    def cross_pair(pair):
        return lambda: attend_pair(pair, kept["q2"], kept["k2"], kept["v2"], None, local["mix"], local["lse"])

    def cross_out():
        kept["lse2"][...] = local["lse"][...].T
        kept["o2t"][...] = local["mix"][...].T
        local["x2"][...] = kept["x1"][...] + dot(local["mix"][...], weights["w_cross"][3])
        keep("lse2", "o2t")

    def third_norm():
        norm_rows(local["x2"], gain[2:3], local["h"])
        kept["h3t"][...] = local["h"][...].T
        keep("h3t")

    def mlp_dots(number):
        def run():
            c0 = number * 512
            h = local["h"][...]
            local["dhid"][...] = dot(dy[...], weights["w_out"][0, c0 : c0 + 512, :], 1, 1)
            local["gate"][...] = dot(h, weights["w_in"][0, :, c0 : c0 + 512])
            local["up"][...] = dot(h, weights["w_in"][1, :, c0 : c0 + 512])

        return run

    def mlp_point(number):
        def run():
            c0 = number * 512

            @pl.loop(0, TOKENS // 16)
            def _(i):
                span = pl.ds(pl.multiple_of(i * 16, 16), 16)
                act, slope = gelu_parts(local["gate"][span])
                up, dhid = local["up"][span], local["dhid"][span]
                local["hidden"][span, c0 : c0 + 512] = (act * up).astype(LOW)
                kept["dgate"][span, c0 : c0 + 512] = (dhid * up * slope).astype(LOW)
                kept["dup"][span, c0 : c0 + 512] = (dhid * act).astype(LOW)

            kept["hiddent"][c0 : c0 + 512, :] = local["hidden"][:, c0 : c0 + 512].T

        return run

    def mlp_keep():
        keep("hiddent", "dgate", "dup")

    def mlp_back_first():
        local["dh"][...] = dot(kept["dgate"][...], weights["w_in"][0], 1, 1)

    def mlp_back_second():
        local["dh"][...] += dot(kept["dup"][...], weights["w_in"][1], 1, 1)

    def mlp_norm():
        norm_back_rows(local["x2"], gain[2:3], local["dh"], dy, kept["dx2"], kept["gain3"])
        keep("dx2", "gain3")

    def mlp_out():
        out[...] = (local["x2"][...] + dot(local["hidden"][...], weights["w_out"][0])).astype(LOW)

    work = [
        (None, make_bias),
        (None, clear_lse),
        (0, make_gain),
        (0, first_norm),
        (1, project("q1", "w_self", 0)),
        (1, project("k1", "w_self", 1)),
        (1, project("v1", "w_self", 2)),
    ]
    work += [(1, self_pair(pair)) for pair in range(6)]
    work += [
        (2, lambda: keep("w_self")),
        (2, self_out),
        (2, second_norm),
        (2, memory_near),
        (3, project("q2", "w_cross", 0)),
        (3, memory_far),
        (3, project_memory("k2", 1)),
        (4, project_memory("v2", 2)),
        (4, lambda: keep("w_cross")),
    ]
    work += [(4, cross_pair(pair)) for pair in range(6)]
    work += [(4, cross_out), (4, third_norm)]
    for number in range(4):
        work += [(6 + number, mlp_dots(number)), (6 + number, mlp_point(number))]
    work += [
        (9, mlp_keep),
        (9, mlp_back_first),
        (9, mlp_back_second),
        (9, mlp_norm),
        (9, mlp_out),
    ]

    count = len(blocks)
    events = []
    for turn in range(count + 3):
        if turn + 2 < count:
            events.append((blocks[turn + 2].begin, None))
        if turn < count:
            for n in blocks[turn].order()[:3]:
                events.append((functools.partial(blocks[turn].take, n), None))
        if 0 <= turn - 1 < count:
            for n in blocks[turn - 1].order()[3:]:
                events.append((functools.partial(blocks[turn - 1].take, n), None))
        if 0 <= turn - 2 < count and blocks[turn - 2].side:
            for n in blocks[turn - 2].order():
                events.append((functools.partial(blocks[turn - 2].take_x, n), None))
        if 0 <= turn - 3 < count:
            events.append((blocks[turn - 3].complete, turn - 3))

    greet_all(place, rows)
    blocks[0].begin()
    blocks[1].begin()
    near_start()
    ready = -1
    done = 0

    def can():
        return done < len(work) and (work[done][0] is None or work[done][0] <= ready)

    for act, completes in events:
        act()
        if completes is not None:
            ready = completes
        if can():
            work[done][1]()
            done += 1
    while can():
        work[done][1]()
        done += 1
    for block in blocks:
        block.end()
    near_end()
    far_end()
    for name in kept_out:
        keep_copy(name).wait()


def forward(layer_input, cotangent, memory, seg_row, seg_col, flags, self_weights, cross_weights, mlp_in, mlp_out, gains):
    wide = lax.axis_size("wide")
    depth = wide // 4
    gain_block = jnp.pad(gains, ((0, 16 - gains.shape[0]), (0, 128 - gains.shape[1])))
    owns = (self_weights, cross_weights, mlp_in, mlp_out[None], gain_block[None])
    vmem, anywhere, smem = (pl.BlockSpec(memory_space=space) for space in (pltpu.VMEM, pl.ANY, pltpu.SMEM))
    kept = [jax.ShapeDtypeStruct(shape, dtype) for _, shape, dtype in KEPT]
    kept += [jax.ShapeDtypeStruct(shape, LOW) for _, shape in WEIGHTS[:2]]
    outs = pl.pallas_call(
        lambda *refs: forward_kernel(depth, 2 * wide, refs),
        out_shape=[jax.ShapeDtypeStruct(layer_input.shape, LOW)] + kept,
        in_specs=[vmem] * 5 + [smem] + [anywhere] * 5,
        out_specs=[vmem] + [anywhere] * len(kept),
        scratch_shapes=[pltpu.VMEM(shape, dtype) for _, shape, dtype in KEPT]
        + [pltpu.VMEM(shape, LOW) for _, shape in WEIGHTS]
        + [pltpu.VMEM(shape, dtype) for _, shape, dtype in FORWARD_LOCAL]
        + gather_sems(len(GATHER_LAYOUT), depth)
        + [pltpu.SemaphoreType.DMA((4,)), pltpu.SemaphoreType.DMA((len(kept),))],
        compiler_params=pltpu.CompilerParams(
            collective_id=0, has_side_effects=True, vmem_limit_bytes=60 * 2**20
        ),
        name="forward",
    )(layer_input, cotangent, memory, seg_row, seg_col, flags, *owns)
    return outs[0], dict(zip([k[0] for k in KEPT] + ["w_self", "w_cross"], outs[1:]))


class Scatter:
    def __init__(self, place, part, bufs, out, rows, side, sems):
        self.p = place
        self.part = part
        self.held, self.from_x, self.from_y, self.from_z, self.done, self.other = bufs
        self.out = out
        self.rows = rows
        self.side = side
        self.main = rows - side
        self.tile = 16 if part.dtype == jnp.bfloat16 else 8
        self.send, self.recv = sems

    def span(self, start, size):
        return pl.ds(pl.multiple_of(start, self.tile), size)

    @property
    def main_span(self):
        return self.span(self.side * self.p.x, self.main)

    def side_span(self, x):
        return self.span(self.main * x, self.side)

    def c_copy(self):
        p = self.p
        return remote(
            self.part.at[:, :, :, 1 - p.core], self.held, self.send.at[0], self.recv.at[0], p.across_core
        )

    def x_copy(self):
        p = self.p
        return remote(
            self.held.at[:, :, :, self.side_span(1 - p.x)],
            self.from_x,
            self.send.at[1],
            self.recv.at[1],
            p.across_x,
        )

    def y_copy(self):
        p = self.p
        return remote(
            self.held.at[:, :, 1 - p.y, self.main_span], self.from_y, self.send.at[2], self.recv.at[2], p.across_y
        )

    def z_copy(self, step):
        p = self.p
        return remote(
            self.held.at[:, (p.z + step) % p.depth, p.y, self.main_span],
            self.from_z.at[step - 1],
            self.send.at[2 + step],
            self.recv.at[2 + step],
            p.z_ahead(step),
        )

    def last_copy(self):
        p = self.p
        return remote(self.done, self.other, self.send.at[2 + p.depth], self.recv.at[2 + p.depth], p.across_x)

    def step(self, number):
        p = self.p
        mats = self.part.shape[0]
        held = self.held
        if number == 0:
            self.c_copy().start()
        elif number == 1:
            self.c_copy().wait_recv()

            @pl.loop(0, mats * p.depth * 2)
            def _(index):
                m, z, y = index // (2 * p.depth), (index // 2) % p.depth, index % 2
                total = held[m, z, y].astype(jnp.float32) + self.part[m, z, y, p.core].astype(jnp.float32)
                held[m, z, y] = total.astype(held.dtype)

            if self.side:
                self.x_copy().start()
        elif number == 2:
            if self.side:
                self.x_copy().wait_recv()

                @pl.loop(0, mats * p.depth * 2)
                def _(index):
                    m, z, y = index // (2 * p.depth), (index // 2) % p.depth, index % 2
                    total = held[m, z, y, self.side_span(p.x)].astype(jnp.float32) + self.from_x[m, z, y].astype(jnp.float32)
                    held[m, z, y, self.side_span(p.x)] = total.astype(held.dtype)

            self.y_copy().start()
        elif number == 3:
            self.y_copy().wait_recv()

            @pl.loop(0, mats * p.depth)
            def _(index):
                m, z = index // p.depth, index % p.depth
                total = held[m, z, p.y, self.main_span].astype(jnp.float32) + self.from_y[m, z].astype(jnp.float32)
                held[m, z, p.y, self.main_span] = total.astype(held.dtype)

            for step in range(1, p.depth):
                self.z_copy(step).start()
        elif number == 4:
            for step in range(1, p.depth):
                self.z_copy(step).wait_recv()

            @pl.loop(0, mats)
            def _(m):
                total = held[m, p.z, p.y, self.main_span].astype(jnp.float32)
                for step in range(1, p.depth):
                    total += self.from_z[step - 1, m].astype(jnp.float32)
                self.done[m] = total.astype(held.dtype)

            self.last_copy().start()
        elif number == 5:
            self.last_copy().wait_recv()
            both = self.main - self.side
            side = self.side

            @pl.loop(0, mats)
            def _(m):
                if side:
                    self.out[m, self.side_span(p.x)] = self.done[m, self.span(both * p.x, side)].astype(jnp.float32)
                    self.out[m, self.side_span(1 - p.x)] = self.other[m, self.span(both * (1 - p.x), side)].astype(
                        jnp.float32
                    )
                self.out[m, side : side + both] = self.done[m, self.span(side * (1 - p.x), both)].astype(
                    jnp.float32
                ) + self.other[m, self.span(side * p.x, both)].astype(jnp.float32)

    def end(self):
        p = self.p
        self.c_copy().wait_send()
        if self.side:
            self.x_copy().wait_send()
        self.y_copy().wait_send()
        for step in range(1, p.depth):
            self.z_copy(step).wait_send()
        self.last_copy().wait_send()


def scatter_buffers(mats, depth, rows, side, columns, dtype):
    main = rows - side
    return [
        pltpu.VMEM((mats, depth, 2, rows, columns), dtype),
        pltpu.VMEM((mats, depth, 2, max(side, 8), columns) if side else (8, 128), dtype),
        pltpu.VMEM((mats, depth, main, columns), dtype),
        pltpu.VMEM((depth - 1, mats, main, columns), dtype),
        pltpu.VMEM((mats, main, columns), dtype),
        pltpu.VMEM((mats, main, columns), dtype),
    ]


def scatter_all(self_grad, cross_grad, in_grad, out_grad, gain_grad):
    wide = lax.axis_size("wide")
    depth = wide // 4
    gain_rows = gain_grad.reshape(gain_grad.shape[0], wide, -1).transpose(1, 0, 2)
    gain_rows = jnp.pad(gain_rows, ((0, 0), (0, 8 - gain_rows.shape[1]), (0, 128 - gain_rows.shape[2])))
    low = jnp.bfloat16
    arrays = (self_grad.astype(low), cross_grad.astype(low), in_grad.astype(low), out_grad[None].astype(low), gain_rows[None])
    arrays = [a.reshape(a.shape[0], depth, 2, 2, -1, a.shape[-1]) for a in arrays]
    side = arrays[0].shape[4] // 3
    layout = (
        (3, 0, 1, arrays[3].shape[4] // 4),
        (2, 0, 1, side),
        (2, 1, 2, side),
        (1, 0, 3, side),
        (1, 3, 4, 0),
        (0, 0, 3, side),
        (0, 3, 4, 0),
        (4, 0, 1, 0),
    )
    buffers = []
    for array, first, last, side in layout:
        a = arrays[array]
        buffers += scatter_buffers(last - first, depth, a.shape[4], side, a.shape[5], a.dtype)

    def kernel(*refs):
        place = Place(depth)
        parts, outs, bufs, sems = refs[:5], refs[5:10], refs[10:-2], refs[-2:]
        blocks = []
        for number, (array, first, last, side) in enumerate(layout):
            blocks.append(
                Scatter(
                    place,
                    parts[array].at[first:last],
                    bufs[6 * number : 6 * number + 6],
                    outs[array].at[first:last],
                    parts[array].shape[4],
                    side,
                    [sem.at[number] for sem in sems],
                )
            )
        place.greet()
        count = len(blocks)
        for turn in range(count + 5):
            for number in range(count):
                if 0 <= turn - number < 6:
                    blocks[number].step(turn - number)
        for block in blocks:
            block.end()

    vmem = pl.BlockSpec(memory_space=pltpu.VMEM)
    outs = pl.pallas_call(
        kernel,
        out_shape=[jax.ShapeDtypeStruct((a.shape[0], a.shape[4], a.shape[5]), jnp.float32) for a in arrays],
        in_specs=[vmem] * 5,
        out_specs=[vmem] * 5,
        scratch_shapes=buffers + [pltpu.SemaphoreType.DMA((len(layout), 3 + depth))] * 2,
        compiler_params=pltpu.CompilerParams(
            collective_id=1, has_side_effects=True, vmem_limit_bytes=56 * 2**20
        ),
        name="scatter",
    )(*arrays)
    return outs[0], outs[1], outs[2], outs[3][0], outs[4][0, : gain_grad.shape[0], : gain_grad.shape[1] // wide]


def plain_gather(self_weights, cross_weights, mlp_in, mlp_out, gains):
    return (
        lax.all_gather(self_weights, "wide", axis=1, tiled=True),
        lax.all_gather(cross_weights, "wide", axis=1, tiled=True),
        lax.all_gather(mlp_in, "wide", axis=1, tiled=True),
        lax.all_gather(mlp_out, "wide", axis=0, tiled=True),
        lax.all_gather(gains, "wide", axis=1, tiled=True),
    )


def plain_scatter(*grads):
    outs = []
    for grad, axis in zip(grads, (1, 1, 1, 0, 1)):
        piece = lax.psum_scatter(grad, ("wide", "narrow"), scatter_dimension=axis, tiled=True)
        outs.append(lax.all_gather(piece.astype(jnp.bfloat16), "narrow", axis=axis, tiled=True).astype(jnp.float32))
    return tuple(outs)


def by_kernel(self_weights):
    return lax.axis_size("wide") == 16 and lax.axis_size("narrow") == 2 and self_weights.shape[1] % 48 == 0


def plain_device(
    layer_input,
    memory,
    cotangent,
    segment_ids,
    padding,
    image_of_row,
    self_weights,
    cross_weights,
    mlp_in,
    mlp_out,
    gains,
):
    self_full, cross_full, in_full, out_full, gain_full = plain_gather(
        self_weights, cross_weights, mlp_in, mlp_out, gains
    )
    gain_float = gain_full.astype(jnp.float32)
    x_zero = layer_input[0].astype(jnp.float32)
    seg_row = segment_ids[0]
    pad_row = padding[0]
    seq_len = x_zero.shape[0]
    position = jnp.arange(seq_len)
    allowed = (
        (seg_row[:, None] == seg_row[None, :])
        & (position[None, :] <= position[:, None])
        & ((pad_row[None, :] == 1) | (position[:, None] == position[None, :]))
    )
    h_one = rms_norm(x_zero, gain_float[0]).astype(jnp.bfloat16)
    q_self = linear(h_one, self_full[0]).astype(jnp.bfloat16)
    k_self = linear(h_one, self_full[1]).astype(jnp.bfloat16)
    v_self = linear(h_one, self_full[2]).astype(jnp.bfloat16)
    self_mix, self_lse = forward_heads(q_self, k_self, v_self, allowed)
    x_one = x_zero + linear(self_mix, self_full[3])
    row_ids = jnp.arange(image_of_row.shape[0])
    starts = jnp.sum(image_of_row[None, :] < image_of_row[:, None], axis=1)
    offsets = row_ids - starts
    my_index = lax.axis_index(("wide", "narrow"))
    my_offset = jnp.sum(jnp.where(row_ids == my_index, offsets, 0))
    own_patches = memory[0]
    memory_use = own_patches
    for distance in (1, 2, 3):
        arrived = shifted(own_patches, ("wide", "narrow"), distance)
        memory_use = jnp.where(my_offset == distance, arrived, memory_use)
    h_two = rms_norm(x_one, gain_float[1]).astype(jnp.bfloat16)
    q_cross = linear(h_two, cross_full[0]).astype(jnp.bfloat16)
    k_cross = linear(memory_use, cross_full[1]).astype(jnp.bfloat16)
    v_cross = linear(memory_use, cross_full[2]).astype(jnp.bfloat16)
    cross_mix, cross_lse = forward_heads(q_cross, k_cross, v_cross, None)
    x_two = x_one + linear(cross_mix, cross_full[3])
    h_three = rms_norm(x_two, gain_float[2]).astype(jnp.bfloat16)
    gate_act = linear(h_three, in_full[0])
    up_act = linear(h_three, in_full[1])
    hidden = gated_product(gate_act, up_act).astype(jnp.bfloat16)
    result = x_two + linear(hidden, out_full)
    out_low = cotangent[0]
    out_grad_w = contract_rows(hidden, out_low)
    hidden_grad = times_transposed(out_low, out_full)
    _, pullback = jax.vjp(gated_product, gate_act, up_act)
    gate_grad, up_grad = pullback(hidden_grad)
    gate_low = gate_grad.astype(jnp.bfloat16)
    up_low = up_grad.astype(jnp.bfloat16)
    in_grad = jnp.stack([contract_rows(h_three, gate_low), contract_rows(h_three, up_low)])
    h_three_grad = times_transposed(gate_low, in_full[0]) + times_transposed(up_low, in_full[1])
    _, pullback = jax.vjp(rms_norm, x_two, gain_float[2])
    x_two_norm, gain_three = pullback(h_three_grad)
    x_two_grad = out_low.astype(jnp.float32) + x_two_norm
    cross_out_low = x_two_grad.astype(jnp.bfloat16)
    cross_o_grad = contract_rows(cross_mix, cross_out_low)
    cross_mix_grad = times_transposed(cross_out_low, cross_full[3]).astype(jnp.bfloat16)
    q_cross_grad, k_cross_grad, v_cross_grad = backward_heads(
        q_cross, k_cross, v_cross, cross_mix_grad, cross_lse, None
    )
    cross_grad = jnp.stack(
        [
            contract_rows(h_two, q_cross_grad),
            contract_rows(memory_use, k_cross_grad),
            contract_rows(memory_use, v_cross_grad),
            cross_o_grad,
        ]
    )
    mem_grad = times_transposed(k_cross_grad, cross_full[1]) + times_transposed(
        v_cross_grad, cross_full[2]
    )
    h_two_grad = times_transposed(q_cross_grad, cross_full[0])
    _, pullback = jax.vjp(rms_norm, x_one, gain_float[1])
    x_one_norm, gain_two = pullback(h_two_grad)
    x_one_grad = x_two_grad + x_one_norm
    self_out_low = x_one_grad.astype(jnp.bfloat16)
    self_o_grad = contract_rows(self_mix, self_out_low)
    self_mix_grad = times_transposed(self_out_low, self_full[3]).astype(jnp.bfloat16)
    q_self_grad, k_self_grad, v_self_grad = backward_heads(
        q_self, k_self, v_self, self_mix_grad, self_lse, allowed
    )
    self_grad = jnp.stack(
        [
            contract_rows(h_one, q_self_grad),
            contract_rows(h_one, k_self_grad),
            contract_rows(h_one, v_self_grad),
            self_o_grad,
        ]
    )
    h_one_grad = (
        times_transposed(q_self_grad, self_full[0])
        + times_transposed(k_self_grad, self_full[1])
        + times_transposed(v_self_grad, self_full[2])
    )
    _, pullback = jax.vjp(rms_norm, x_zero, gain_float[0])
    x_zero_norm, gain_one = pullback(h_one_grad)
    x_grad = x_one_grad + x_zero_norm
    mem_summed = jnp.where(my_offset == 0, mem_grad, 0.0)
    for distance in (1, 2, 3):
        arrived = shifted(mem_grad.astype(jnp.bfloat16), ("wide", "narrow"), -distance).astype(
            mem_grad.dtype
        )
        neighbour = jnp.sum(jnp.where(row_ids == my_index + distance, offsets, 0))
        mem_summed = mem_summed + jnp.where(neighbour == distance, arrived, 0.0)
    gain_grad = jnp.stack([gain_one, gain_two, gain_three])
    reduced = plain_scatter(self_grad, cross_grad, in_grad, out_grad_w, gain_grad)
    return (
        result.astype(jnp.bfloat16)[None],
        x_grad[None],
        mem_summed[None],
        reduced[0],
        reduced[1],
        reduced[2],
        reduced[3],
        reduced[4],
    )


def kernel_device(
    layer_input,
    memory,
    cotangent,
    segment_ids,
    padding,
    image_of_row,
    self_weights,
    cross_weights,
    mlp_in,
    mlp_out,
    gains,
):
    seg_rows = jnp.pad(jnp.concatenate([segment_ids, padding]), ((0, 6), (0, 0)))
    seg_cols = jnp.pad(seg_rows[:2].T, ((0, 0), (0, 126)))
    row_ids = jnp.arange(image_of_row.shape[0])
    starts = jnp.sum(image_of_row[None, :] < image_of_row[:, None], axis=1)
    offsets = row_ids - starts
    my_index = lax.axis_index(("wide", "narrow"))
    flags = jnp.stack([jnp.sum(jnp.where(row_ids == my_index + ahead, offsets, 0)) for ahead in range(4)]).astype(jnp.int32)
    my_offset = flags[0]
    result, kept = forward(
        layer_input[0], cotangent[0], memory[0], seg_rows, seg_cols, flags, self_weights, cross_weights, mlp_in, mlp_out, gains
    )
    x_zero = layer_input[0].astype(jnp.float32)
    seg_row, pad_row = segment_ids[0], padding[0]
    position = jnp.arange(x_zero.shape[0])
    allowed = (
        (seg_row[:, None] == seg_row[None, :])
        & (position[None, :] <= position[:, None])
        & ((pad_row[None, :] == 1) | (position[:, None] == position[None, :]))
    )
    gain_float = kept["gain"]
    gain_three = kept["gain3"][0]
    x_one, x_two_grad = kept["x1"], kept["dx2"]
    hidden, h_three = kept["hiddent"].T, kept["h3t"].T
    h_one, h_two, memory_use = kept["h1t"].T, kept["h2t"].T, kept["memt"].T
    self_mix, cross_mix = kept["o1t"].T, kept["o2t"].T
    q_self, k_self, v_self = kept["q1"], kept["k1"], kept["v1"]
    q_cross, k_cross, v_cross = kept["q2"], kept["k2"], kept["v2"]
    self_lse, cross_lse = kept["lse1"][:12, :, None], kept["lse2"][:12, :, None]
    self_full, cross_full = kept["w_self"], kept["w_cross"]
    out_grad_w = contract_rows(hidden, cotangent[0])
    in_grad = jnp.stack([contract_rows(h_three, kept["dgate"]), contract_rows(h_three, kept["dup"])])
    cross_out_low = x_two_grad.astype(jnp.bfloat16)
    cross_o_grad = contract_rows(cross_mix, cross_out_low)
    cross_mix_grad = times_transposed(cross_out_low, cross_full[3]).astype(jnp.bfloat16)
    q_cross_grad, k_cross_grad, v_cross_grad = backward_heads(
        q_cross, k_cross, v_cross, cross_mix_grad, cross_lse, None
    )
    cross_grad = jnp.stack(
        [
            contract_rows(h_two, q_cross_grad),
            contract_rows(memory_use, k_cross_grad),
            contract_rows(memory_use, v_cross_grad),
            cross_o_grad,
        ]
    )
    mem_grad = times_transposed(k_cross_grad, cross_full[1]) + times_transposed(
        v_cross_grad, cross_full[2]
    )
    h_two_grad = times_transposed(q_cross_grad, cross_full[0])
    _, pullback = jax.vjp(rms_norm, x_one, gain_float[1])
    x_one_norm, gain_two = pullback(h_two_grad)
    x_one_grad = x_two_grad + x_one_norm
    self_out_low = x_one_grad.astype(jnp.bfloat16)
    self_o_grad = contract_rows(self_mix, self_out_low)
    self_mix_grad = times_transposed(self_out_low, self_full[3]).astype(jnp.bfloat16)
    q_self_grad, k_self_grad, v_self_grad = backward_heads(
        q_self, k_self, v_self, self_mix_grad, self_lse, allowed
    )
    self_grad = jnp.stack(
        [
            contract_rows(h_one, q_self_grad),
            contract_rows(h_one, k_self_grad),
            contract_rows(h_one, v_self_grad),
            self_o_grad,
        ]
    )
    h_one_grad = (
        times_transposed(q_self_grad, self_full[0])
        + times_transposed(k_self_grad, self_full[1])
        + times_transposed(v_self_grad, self_full[2])
    )
    _, pullback = jax.vjp(rms_norm, x_zero, gain_float[0])
    x_zero_norm, gain_one = pullback(h_one_grad)
    x_grad = x_one_grad + x_zero_norm
    mem_summed = jnp.where(my_offset == 0, mem_grad, 0.0)
    for distance in (1, 2, 3):
        arrived = shifted(mem_grad.astype(jnp.bfloat16), ("wide", "narrow"), -distance).astype(
            mem_grad.dtype
        )
        neighbour = jnp.sum(jnp.where(row_ids == my_index + distance, offsets, 0))
        mem_summed = mem_summed + jnp.where(neighbour == distance, arrived, 0.0)
    gain_grad = jnp.stack([gain_one, gain_two, gain_three])
    reduced = scatter_all(self_grad, cross_grad, in_grad, out_grad_w, gain_grad)
    return (
        result.astype(jnp.bfloat16)[None],
        x_grad[None],
        mem_summed[None],
        reduced[0],
        reduced[1],
        reduced[2],
        reduced[3],
        reduced[4],
    )


def on_device(
    layer_input,
    memory,
    cotangent,
    segment_ids,
    padding,
    image_of_row,
    self_weights,
    cross_weights,
    mlp_in,
    mlp_out,
    gains,
):
    run = kernel_device if by_kernel(self_weights) else plain_device
    return run(
        layer_input,
        memory,
        cotangent,
        segment_ids,
        padding,
        image_of_row,
        self_weights,
        cross_weights,
        mlp_in,
        mlp_out,
        gains,
    )


def solution(mesh):
    in_specs = (
        P(("wide", "narrow"), None, None),
        P(("wide", "narrow"), None, None),
        P(("wide", "narrow"), None, None),
        P(("wide", "narrow"), None),
        P(("wide", "narrow"), None),
        P(),
        P(None, "wide", None),
        P(None, "wide", None),
        P(None, "wide", None),
        P("wide", None),
        P(None, "wide"),
    )
    out_specs = (
        P(("wide", "narrow"), None, None),
        P(("wide", "narrow"), None, None),
        P(("wide", "narrow"), None, None),
        P(None, "wide", None),
        P(None, "wide", None),
        P(None, "wide", None),
        P("wide", None),
        P(None, "wide"),
    )
    return jax.shard_map(
        on_device, mesh=mesh, in_specs=in_specs, out_specs=out_specs, check_vma=False
    )
```

```python
import functools

import jax
import jax.numpy as jnp
from jax import lax
from jax.experimental import pallas as pl
from jax.experimental.pallas import tpu as pltpu
from jax.sharding import PartitionSpec as P

HEAD_DIM = 64


EPSILON = 1e-06


def shifted(value, axis, steps):
    count = lax.axis_size(axis)
    first, last = (max(0, -steps), min(count, count - steps))
    return lax.ppermute(value, axis, [(source, source + steps) for source in range(first, last)])


def rms_norm(v, g):
    return v * lax.rsqrt(jnp.mean(v * v, axis=-1, keepdims=True) + EPSILON) * g


def contract_rows(a, b):
    return lax.dot_general(a, b, (((0,), (0,)), ((), ())), preferred_element_type=jnp.float32)


def times_transposed(a, w):
    return lax.dot_general(a, w, (((1,), (1,)), ((), ())), preferred_element_type=jnp.float32)


def linear(a, w):
    return jnp.dot(a, w, preferred_element_type=jnp.float32)


def head_scores(q_part, k_part, allowed):
    scores = jnp.einsum(
        "qhd,khd->hqk", q_part, k_part, preferred_element_type=jnp.float32
    ) * HEAD_DIM ** (-0.5)
    if allowed is not None:
        scores = jnp.where(allowed[None], scores, -1e30)
    return scores


def split_heads(a, head_start):
    return a[:, head_start * HEAD_DIM : (head_start + 4) * HEAD_DIM].reshape(
        a.shape[0], 4, HEAD_DIM
    )


def forward_heads(q, k, v, allowed):
    seq_len = q.shape[0]
    head_count = q.shape[1] // HEAD_DIM
    pieces = []
    log_sums = []
    for head_start in range(0, head_count, 4):
        q_part = split_heads(q, head_start)
        k_part = split_heads(k, head_start)
        v_part = split_heads(v, head_start)
        scores = head_scores(q_part, k_part, allowed)
        highest = jnp.max(scores, axis=-1, keepdims=True)
        powers = jnp.exp(scores - highest)
        summed = jnp.sum(powers, axis=-1, keepdims=True)
        shares = (powers / summed).astype(jnp.bfloat16)
        mixed = jnp.einsum("hqk,khd->qhd", shares, v_part, preferred_element_type=jnp.float32)
        pieces.append(mixed.reshape(seq_len, -1))
        log_sums.append(highest + jnp.log(summed))
    return (jnp.concatenate(pieces, axis=1).astype(jnp.bfloat16), jnp.concatenate(log_sums, axis=0))


def backward_heads(q, k, v, mix_grad, log_sum, allowed):
    seq_len = q.shape[0]
    head_count = q.shape[1] // HEAD_DIM
    q_pieces = []
    k_pieces = []
    v_pieces = []
    for head_start in range(0, head_count, 4):
        q_part = split_heads(q, head_start)
        k_part = split_heads(k, head_start)
        v_part = split_heads(v, head_start)
        o_part = split_heads(mix_grad, head_start)
        scores = head_scores(q_part, k_part, allowed)
        shares = jnp.exp(scores - log_sum[head_start : head_start + 4])
        v_grad = jnp.einsum(
            "hqk,qhd->khd", shares.astype(jnp.bfloat16), o_part, preferred_element_type=jnp.float32
        )
        p_grad = jnp.einsum("qhd,khd->hqk", o_part, v_part, preferred_element_type=jnp.float32)
        s_grad = shares * (p_grad - jnp.sum(shares * p_grad, axis=-1, keepdims=True))
        s_low = s_grad.astype(jnp.bfloat16)
        q_grad = jnp.einsum(
            "hqk,khd->qhd", s_low, k_part, preferred_element_type=jnp.float32
        ) * HEAD_DIM ** (-0.5)
        k_grad = jnp.einsum(
            "hqk,qhd->khd", s_low, q_part, preferred_element_type=jnp.float32
        ) * HEAD_DIM ** (-0.5)
        q_pieces.append(q_grad.reshape(seq_len, -1))
        k_pieces.append(k_grad.reshape(k.shape[0], -1))
        v_pieces.append(v_grad.reshape(k.shape[0], -1))
    return (
        jnp.concatenate(q_pieces, axis=1).astype(jnp.bfloat16),
        jnp.concatenate(k_pieces, axis=1).astype(jnp.bfloat16),
        jnp.concatenate(v_pieces, axis=1).astype(jnp.bfloat16),
    )


def gated_product(gate_act, up_act):
    return jax.nn.gelu(gate_act, approximate=True) * up_act


MESH = pl.DeviceIdType.MESH


class Place:
    def __init__(self, depth):
        self.depth = depth
        self.wide = lax.axis_index("wide")
        self.x = lax.axis_index("narrow")
        self.core = self.wide % 2
        self.y = (self.wide // 2) % 2
        self.z = self.wide // 4

    def shard(self, z, y, core):
        return z * 4 + y * 2 + core

    def z_ahead(self, step):
        return (self.shard((self.z + step) % self.depth, self.y, self.core), self.x)

    def z_behind(self, step):
        return (self.z + self.depth - step) % self.depth

    @property
    def across_x(self):
        return (self.wide, 1 - self.x)

    @property
    def across_y(self):
        return (self.shard(self.z, 1 - self.y, self.core), self.x)

    @property
    def across_core(self):
        return (self.shard(self.z, self.y, 1 - self.core), self.x)

    def greet(self):
        barrier = pltpu.get_barrier_semaphore()
        others = [self.across_x, self.across_y, self.across_core]
        others += [self.z_ahead(step) for step in range(1, self.depth)]
        for other in others:
            pl.semaphore_signal(barrier, inc=1, device_id=other, device_id_type=MESH)
        pl.semaphore_wait(barrier, len(others))


def remote(src, dst, send, recv, device):
    return pltpu.make_async_remote_copy(
        src_ref=src, dst_ref=dst, send_sem=send, recv_sem=recv, device_id=device, device_id_type=MESH
    )


class Gather:
    def __init__(self, place, own, full, rows, side, y_first, sems):
        self.p = place
        self.own = own
        self.full = full
        self.rows = rows
        self.side = side
        self.main = rows - side
        self.y_first = y_first
        self.main_send, self.main_recv, self.x_send, self.x_recv, self.c_send, self.c_recv = sems

    def block(self, ref, start, size):
        return ref.at[:, pl.ds(pl.multiple_of(start, 16), size), :]

    def at(self, z, y, core, start, size):
        return self.block(self.full, self.p.shard(z, y, core) * self.rows + start, size)

    def owner(self, n):
        step, other = n % self.p.depth, n // self.p.depth
        return self.p.z_behind(step), (1 - self.p.y if other else self.p.y)

    @property
    def main_start(self):
        return self.side * self.p.x

    def side_start(self, x):
        return self.main * x

    def main_piece(self, z, y, source=False):
        p = self.p
        return self.at(z, y, p.core, self.main_start, self.main)

    def arriving(self, n):
        p = self.p
        z, y = self.owner(n)
        piece = self.main_piece(z, y)
        return remote(piece, piece, self.main_send.at[0], self.main_recv.at[n], p.across_y)

    def y_copy(self, n):
        p = self.p
        z, y = self.owner(n)
        dst = self.main_piece(z, y)
        src = self.block(self.own, self.main_start, self.main) if n == 0 else dst
        return remote(src, dst, self.main_send.at[n], self.main_recv.at[n + p.depth], p.across_y)

    def z_copy(self, step, other):
        p = self.p
        y = 1 - p.y if other else p.y
        dst = self.main_piece(p.z, y)
        src = dst if other else self.block(self.own, self.main_start, self.main)
        slot = p.depth + (step - 1) + (p.depth - 1) * other
        return remote(
            src, dst, self.main_send.at[slot], self.main_recv.at[step + p.depth * other], p.z_ahead(step)
        )

    def relay_copy(self, other, up):
        p = self.p
        z, target = (0, 3) if up else (3, 0)
        y = 1 - p.y if other else p.y
        piece = self.main_piece(z, y)
        slot = p.depth + 2 * (p.depth - 1) + other
        step = 3 if up else 1
        device = (p.shard(target, p.y, p.core), p.x)
        return remote(piece, piece, self.main_send.at[slot], self.main_recv.at[step + p.depth * other], device)

    def x_copy(self, n, x):
        p = self.p
        z, y = self.owner(n)
        piece = self.at(z, y, p.core, self.side_start(x), self.side)
        return remote(piece, piece, self.x_send.at[n], self.x_recv.at[n], p.across_x)

    def c_copy(self, n, core, side):
        p = self.p
        slot = n + (2 * p.depth if side else 0)
        z, y = self.owner(n)
        if n == 0:
            src, dst = self.own, self.at(z, y, core, 0, self.rows)
        else:
            start, size = (self.side_start(1 - p.x), self.side) if side else (self.main_start, self.main)
            src = dst = self.at(z, y, core, start, size)
        return remote(src, dst, self.c_send.at[slot], self.c_recv.at[slot], p.across_core)

    def copy_own(self):
        p = self.p
        return pltpu.make_async_copy(self.own, self.at(p.z, p.y, p.core, 0, self.rows), self.main_send.at[4 * p.depth])

    def each_z(self, other, act):
        p = self.p
        for step in range(1, p.depth):
            if step == 2:
                act(self.z_copy(step, other))
            else:
                end = 0 if step == 3 else 3

                @pl.when(p.z != end)
                def _():
                    act(self.z_copy(step, other))

    def each_relay(self, other, act):
        p = self.p

        @pl.when(p.z == 2)
        def _():
            act(self.relay_copy(other, True))

        @pl.when(p.z == 1)
        def _():
            act(self.relay_copy(other, False))

    def begin(self):
        self.copy_own().start()
        self.y_copy(0).start()
        self.each_z(0, lambda copy: copy.start())
        self.c_copy(0, self.p.core, False).start()

    def order(self):
        depth = self.p.depth
        if self.y_first:
            return [depth, 2, 2 + depth, 1, 3, 1 + depth, 3 + depth]
        return [2, 1, 3, depth, depth + 2, depth + 1, depth + 3]

    def take(self, n):
        p = self.p
        depth = p.depth
        self.arriving(n).wait_recv()
        other = n // depth
        if n % depth == 2 and (self.y_first or other == 0):
            self.each_relay(other, lambda copy: copy.start())
        if self.y_first:
            if n == depth:
                self.each_z(1, lambda copy: copy.start())
        elif other == 0:
            self.y_copy(n).start()
        if self.side:
            self.x_copy(n, p.x).start()
        self.c_copy(n, p.core, False).start()

    def take_x(self, n):
        p = self.p
        if self.side:
            self.x_copy(n, 1 - p.x).wait_recv()
            self.c_copy(n, p.core, True).start()

    def complete(self):
        p = self.p
        self.copy_own().wait()
        for n in range(2 * p.depth):
            self.c_copy(n, 1 - p.core, False).wait_recv()
            if self.side and n:
                self.c_copy(n, 1 - p.core, True).wait_recv()

    def end(self):
        p = self.p

        def wait(copy):
            copy.wait_send()

        for n in range(1 if self.y_first else p.depth):
            self.y_copy(n).wait_send()
        for other in range(2 if self.y_first else 1):
            self.each_z(other, wait)
            self.each_relay(other, wait)
        for n in range(2 * p.depth):
            self.c_copy(n, p.core, False).wait_send()
            if self.side and n:
                self.x_copy(n, p.x).wait_send()
                self.c_copy(n, p.core, True).wait_send()


def gather_sems(count, depth):
    sizes = (4 * depth + 1, 2 * depth, 2 * depth, 2 * depth, 4 * depth, 4 * depth)
    return [pltpu.SemaphoreType.DMA((count, size)) for size in sizes]


LOW = jnp.bfloat16


def dot(a, b, ca=1, cb=0):
    return lax.dot_general(a, b, (((ca,), (cb,)), ((), ())), preferred_element_type=jnp.float32)


def norm_rows(source, gain, target):
    rows = source.shape[0]
    chunk = 64

    @pl.loop(0, rows // chunk)
    def _(i):
        span = pl.ds(pl.multiple_of(i * chunk, chunk), chunk)
        v = source[span].astype(jnp.float32)
        scale = lax.rsqrt(jnp.mean(v * v, axis=-1, keepdims=True) + EPSILON)
        target[span] = (v * scale * gain).astype(LOW)


def norm_back_rows(source, gain, grad, dout, target, gain_grad):
    rows, width = source.shape
    chunk = 64
    gain_grad[...] = jnp.zeros_like(gain_grad)

    @pl.loop(0, rows // chunk)
    def _(i):
        span = pl.ds(pl.multiple_of(i * chunk, chunk), chunk)
        v = source[span].astype(jnp.float32)
        dh = grad[span]
        scale = lax.rsqrt(jnp.mean(v * v, axis=-1, keepdims=True) + EPSILON)
        unit = v * scale
        gain_grad[...] += jnp.sum(dh * unit, axis=0, keepdims=True)
        scaled = dh * gain
        along = jnp.mean(scaled * unit, axis=-1, keepdims=True)
        target[span] = (dout[span].astype(jnp.float32) + scale * (scaled - unit * along)).astype(target.dtype)


def pair_span(pair):
    return pl.ds(pl.multiple_of(pair * 2 * HEAD_DIM, 2 * HEAD_DIM), 2 * HEAD_DIM)


def attend_pair(pair, q, k, v, bias, mixed, lse):
    span = pair_span(pair)
    q_two, k_two, v_two = q[:, span], k[:, span], v[:, span]
    rows = q_two.shape[0]
    low_half = lax.broadcasted_iota(jnp.int32, q_two.shape, 1) < HEAD_DIM
    lane = lax.broadcasted_iota(jnp.int32, (rows, 128), 1)
    outs = []
    sums = lse[...]
    for half in range(2):
        mine = low_half if half == 0 else ~low_half
        scores = dot(jnp.where(mine, q_two, jnp.zeros_like(q_two)), k_two, 1, 1) * HEAD_DIM ** (-0.5)
        if bias is not None:
            scores = scores + bias[...]
        highest = jnp.max(scores, axis=-1, keepdims=True)
        powers = jnp.exp(scores - highest)
        summed = jnp.sum(powers, axis=-1, keepdims=True)
        shares = (powers / summed).astype(LOW)
        outs.append(dot(shares, v_two))
        sums = jnp.where(lane == 2 * pair + half, highest + jnp.log(summed), sums)
    mixed[:, span] = jnp.where(low_half, outs[0], outs[1]).astype(LOW)
    lse[...] = sums


def gelu_parts(gate):
    inner = (2.0 / 3.141592653589793) ** 0.5
    square = gate * gate
    bent = jnp.tanh(inner * gate * (1.0 + 0.044715 * square))
    half = 0.5 * (1.0 + bent)
    slope = half + 0.5 * gate * (1.0 - bent * bent) * inner * (1.0 + 3 * 0.044715 * square)
    return gate * half, slope


class Rows:
    def __init__(self, place, count):
        self.p = place
        self.count = count
        self.row = place.wide * 2 + place.x

    def device(self, row):
        return (row // 2, row % 2)

    def when(self, distance, act):
        @pl.when((self.row + distance >= 0) & (self.row + distance < self.count))
        def _():
            act(self.device(self.row + distance))

    def near(self):
        return (-2, -1, 1, 2)

    def present(self):
        below = jnp.minimum(self.row, 2)
        above = jnp.minimum(self.count - 1 - self.row, 2)
        return below + above


def greet_all(place, rows):
    barrier = pltpu.get_barrier_semaphore()
    others = [place.across_x, place.across_y, place.across_core]
    others += [place.z_ahead(step) for step in range(1, place.depth)]

    def hello(device):
        pl.semaphore_signal(barrier, inc=1, device_id=device, device_id_type=MESH)

    for other in others:
        hello(other)
    for distance in rows.near():
        rows.when(distance, hello)
    pl.semaphore_wait(barrier, len(others) + rows.present())


def pass_rows(rows, source, target, distance, sems):
    send, recv = sems

    def copy(device):
        return remote(source, target, send, recv, device)

    def start():
        rows.when(distance, lambda device: copy(device).start())

    def arrive():
        rows.when(-distance, lambda device: copy(device).wait_recv())

    def end():
        rows.when(distance, lambda device: copy(device).wait_send())

    return start, arrive, end


GATHER_LAYOUT = (
    (4, 0, 1, 0, 128, 0),
    (0, 0, 3, 0, 768, 16),
    (0, 3, 4, 0, 768, 16),
    (1, 0, 2, 0, 768, 16),
    (1, 2, 4, 0, 768, 16),
    (3, 0, 1, 0, 768, 48),
    (2, 0, 2, 0, 512, 16),
    (2, 0, 2, 512, 1024, 16),
    (2, 0, 2, 1024, 1536, 16),
    (2, 0, 2, 1536, 2048, 16),
)
WIDTH, HIDDEN, TOKENS, PATCHES = 768, 2048, 384, 256

class Spec:
    def __init__(self, *shape, dtype=LOW):
        self.shape = shape
        self.dtype = dtype

    def array(self):
        return jax.ShapeDtypeStruct(self.shape, self.dtype)

    def scratch(self):
        return pltpu.VMEM(self.shape, self.dtype)


def specs(table):
    return [spec for spec in vars(table).values() if isinstance(spec, Spec)]


class K:
    gain = Spec(8, WIDTH, dtype=jnp.float32)
    h1t = Spec(WIDTH, TOKENS)
    q1 = Spec(TOKENS, WIDTH)
    k1 = Spec(TOKENS, WIDTH)
    v1 = Spec(TOKENS, WIDTH)
    o1t = Spec(WIDTH, TOKENS)
    lse1 = Spec(128, TOKENS, dtype=jnp.float32)
    x1 = Spec(TOKENS, WIDTH, dtype=jnp.float32)
    h2t = Spec(WIDTH, TOKENS)
    memt = Spec(WIDTH, PATCHES)
    q2 = Spec(TOKENS, WIDTH)
    k2 = Spec(PATCHES, WIDTH)
    v2 = Spec(PATCHES, WIDTH)
    o2t = Spec(WIDTH, TOKENS)
    lse2 = Spec(128, TOKENS, dtype=jnp.float32)
    h3t = Spec(WIDTH, TOKENS)
    hiddent = Spec(HIDDEN, TOKENS)
    dgate = Spec(TOKENS, HIDDEN)
    dup = Spec(TOKENS, HIDDEN)
    dx2 = Spec(TOKENS, WIDTH, dtype=jnp.float32)
    gain3 = Spec(1, WIDTH, dtype=jnp.float32)


class W:
    w_self = Spec(4, WIDTH, WIDTH)
    w_cross = Spec(4, WIDTH, WIDTH)
    w_in = Spec(2, WIDTH, HIDDEN)
    w_out = Spec(1, HIDDEN, WIDTH)
    w_gain = Spec(1, 256, 128)


class F:
    bias = Spec(TOKENS, TOKENS, dtype=jnp.float32)
    h = Spec(TOKENS, WIDTH)
    mix = Spec(TOKENS, WIDTH)
    lse = Spec(TOKENS, 128, dtype=jnp.float32)
    mem_one = Spec(PATCHES, WIDTH)
    mem = Spec(PATCHES, WIDTH)
    mem_got = Spec(2, PATCHES, WIDTH)
    x2 = Spec(TOKENS, WIDTH, dtype=jnp.float32)
    gate = Spec(TOKENS, 512, dtype=jnp.float32)
    up = Spec(TOKENS, 512, dtype=jnp.float32)
    dhid = Spec(TOKENS, 512, dtype=jnp.float32)
    hidden = Spec(TOKENS, HIDDEN)
    dh = Spec(TOKENS, WIDTH, dtype=jnp.float32)


PASSED = specs(K) + [W.w_self, W.w_cross]


def forward_kernel(depth, row_count, refs):
    (x0, dy, memory, seg_row, seg_col, flags) = refs[:6]
    owns = refs[6:11]
    out = refs[11]
    rest = refs[12:]
    kept_out, rest = dict(zip(PASSED, rest)), rest[len(PASSED) :]
    kept, rest = dict(zip(specs(K), rest)), rest[len(specs(K)) :]
    weights, rest = dict(zip(specs(W), rest)), rest[len(specs(W)) :]
    local, rest = dict(zip(specs(F), rest)), rest[len(specs(F)) :]
    gather_sem, row_sem, keep_sem = rest[:6], rest[6], rest[7]
    kept_numbers = {name: number for number, name in enumerate(kept_out)}

    def keep_copy(name):
        source = weights[name] if name in weights else kept[name]
        return pltpu.make_async_copy(source, kept_out[name], keep_sem.at[kept_numbers[name]])

    def keep(*names):
        for name in names:
            keep_copy(name).start()

    place = Place(depth)
    rows = Rows(place, row_count)
    fulls = [weights[spec] for spec in specs(W)]
    blocks = []
    for number, (array, first, last, c0, c1, side) in enumerate(GATHER_LAYOUT):
        own, full = owns[array], fulls[array]
        blocks.append(
            Gather(
                place,
                own.at[first:last, :, c0:c1],
                full.at[first:last, :, c0:c1],
                own.shape[1],
                side,
                False,
                [sem.at[number] for sem in gather_sem],
            )
        )
    near_start, near_arrive, near_end = pass_rows(
        rows, memory, local[F.mem_got].at[0], 1, (row_sem.at[0], row_sem.at[1])
    )
    far_start, far_arrive, far_end = pass_rows(
        rows, local[F.mem_one], local[F.mem_got].at[1], 2, (row_sem.at[2], row_sem.at[3])
    )
    gain = kept[K.gain]

    def make_bias():
        seg_q, seg_k = seg_col[:, 0:1], seg_row[0:1, :]
        query = lax.broadcasted_iota(jnp.int32, (TOKENS, TOKENS), 0)
        key = lax.broadcasted_iota(jnp.int32, (TOKENS, TOKENS), 1)
        allowed = (seg_q == seg_k) & (key <= query) & ((seg_row[1:2, :] == 1) | (key == query))
        local[F.bias][...] = jnp.where(allowed, 0.0, -1e30)

    def make_gain():
        total = jnp.zeros((16, WIDTH), jnp.float32)
        count = row_count // 2
        share = WIDTH // count
        for number in range(count):
            row = lax.broadcasted_iota(jnp.int32, (128, WIDTH), 0)
            column = lax.broadcasted_iota(jnp.int32, (128, WIDTH), 1)
            pick = ((column - number * share) == row) & (row < share)
            total += dot(weights[W.w_gain][0, number * 16 : number * 16 + 16, :], pick.astype(LOW))
        gain[...] = total[:8]

    def first_norm():
        norm_rows(x0, gain[0:1], local[F.h])
        kept[K.h1t][...] = local[F.h][...].T
        keep(K.gain, K.h1t)

    def project(name, w, index):
        def run():
            kept[name][...] = dot(local[F.h][...], weights[w][index]).astype(LOW)
            keep(name)

        return run

    def self_pair(pair):
        return lambda: attend_pair(pair, kept[K.q1], kept[K.k1], kept[K.v1], local[F.bias], local[F.mix], local[F.lse])

    def clear_lse():
        local[F.lse][...] = jnp.zeros_like(local[F.lse])

    def self_out():
        kept[K.lse1][...] = local[F.lse][...].T
        kept[K.o1t][...] = local[F.mix][...].T
        kept[K.x1][...] = x0[...].astype(jnp.float32) + dot(local[F.mix][...], weights[W.w_self][3])
        keep(K.lse1, K.o1t, K.x1)

    def second_norm():
        norm_rows(kept[K.x1], gain[1:2], local[F.h])
        kept[K.h2t][...] = local[F.h][...].T
        keep(K.h2t)

    def memory_near():
        near_arrive()
        local[F.mem_one][...] = jnp.where(flags[0] >= 1, local[F.mem_got][0], memory[...])
        far_start()

    def memory_far():
        far_arrive()
        local[F.mem][...] = jnp.where(flags[0] >= 2, local[F.mem_got][1], local[F.mem_one][...])
        kept[K.memt][...] = local[F.mem][...].T
        keep(K.memt)

    def project_memory(name, index):
        def run():
            kept[name][...] = dot(local[F.mem][...], weights[W.w_cross][index]).astype(LOW)
            keep(name)

        return run

    def cross_pair(pair):
        return lambda: attend_pair(pair, kept[K.q2], kept[K.k2], kept[K.v2], None, local[F.mix], local[F.lse])

    def cross_out():
        kept[K.lse2][...] = local[F.lse][...].T
        kept[K.o2t][...] = local[F.mix][...].T
        local[F.x2][...] = kept[K.x1][...] + dot(local[F.mix][...], weights[W.w_cross][3])
        keep(K.lse2, K.o2t)

    def third_norm():
        norm_rows(local[F.x2], gain[2:3], local[F.h])
        kept[K.h3t][...] = local[F.h][...].T
        keep(K.h3t)

    def mlp_dots(number):
        def run():
            c0 = number * 512
            h = local[F.h][...]
            local[F.dhid][...] = dot(dy[...], weights[W.w_out][0, c0 : c0 + 512, :], 1, 1)
            local[F.gate][...] = dot(h, weights[W.w_in][0, :, c0 : c0 + 512])
            local[F.up][...] = dot(h, weights[W.w_in][1, :, c0 : c0 + 512])

        return run

    def mlp_point(number):
        def run():
            c0 = number * 512

            @pl.loop(0, TOKENS // 16)
            def _(i):
                span = pl.ds(pl.multiple_of(i * 16, 16), 16)
                act, slope = gelu_parts(local[F.gate][span])
                up, dhid = local[F.up][span], local[F.dhid][span]
                local[F.hidden][span, c0 : c0 + 512] = (act * up).astype(LOW)
                kept[K.dgate][span, c0 : c0 + 512] = (dhid * up * slope).astype(LOW)
                kept[K.dup][span, c0 : c0 + 512] = (dhid * act).astype(LOW)

            kept[K.hiddent][c0 : c0 + 512, :] = local[F.hidden][:, c0 : c0 + 512].T

        return run

    def mlp_keep():
        keep(K.hiddent, K.dgate, K.dup)

    def mlp_back_first():
        local[F.dh][...] = dot(kept[K.dgate][...], weights[W.w_in][0], 1, 1)

    def mlp_back_second():
        local[F.dh][...] += dot(kept[K.dup][...], weights[W.w_in][1], 1, 1)

    def mlp_norm():
        norm_back_rows(local[F.x2], gain[2:3], local[F.dh], dy, kept[K.dx2], kept[K.gain3])
        keep(K.dx2, K.gain3)

    def mlp_out():
        out[...] = (local[F.x2][...] + dot(local[F.hidden][...], weights[W.w_out][0])).astype(LOW)

    work = [
        (None, make_bias),
        (None, clear_lse),
        (0, make_gain),
        (0, first_norm),
        (1, project(K.q1, W.w_self, 0)),
        (1, project(K.k1, W.w_self, 1)),
        (1, project(K.v1, W.w_self, 2)),
    ]
    work += [(1, self_pair(pair)) for pair in range(6)]
    work += [
        (2, lambda: keep(W.w_self)),
        (2, self_out),
        (2, second_norm),
        (2, memory_near),
        (3, project(K.q2, W.w_cross, 0)),
        (3, memory_far),
        (3, project_memory(K.k2, 1)),
        (4, project_memory(K.v2, 2)),
        (4, lambda: keep(W.w_cross)),
    ]
    work += [(4, cross_pair(pair)) for pair in range(6)]
    work += [(4, cross_out), (4, third_norm)]
    for number in range(4):
        work += [(6 + number, mlp_dots(number)), (6 + number, mlp_point(number))]
    work += [
        (9, mlp_keep),
        (9, mlp_back_first),
        (9, mlp_back_second),
        (9, mlp_norm),
        (9, mlp_out),
    ]

    count = len(blocks)
    events = []
    for turn in range(count + 3):
        if turn + 2 < count:
            events.append((blocks[turn + 2].begin, None))
        if turn < count:
            for n in blocks[turn].order()[:3]:
                events.append((functools.partial(blocks[turn].take, n), None))
        if 0 <= turn - 1 < count:
            for n in blocks[turn - 1].order()[3:]:
                events.append((functools.partial(blocks[turn - 1].take, n), None))
        if 0 <= turn - 2 < count and blocks[turn - 2].side:
            for n in blocks[turn - 2].order():
                events.append((functools.partial(blocks[turn - 2].take_x, n), None))
        if 0 <= turn - 3 < count:
            events.append((blocks[turn - 3].complete, turn - 3))

    greet_all(place, rows)
    blocks[0].begin()
    blocks[1].begin()
    near_start()
    ready = -1
    done = 0

    def can():
        return done < len(work) and (work[done][0] is None or work[done][0] <= ready)

    for act, completes in events:
        act()
        if completes is not None:
            ready = completes
        if can():
            work[done][1]()
            done += 1
    while can():
        work[done][1]()
        done += 1
    for block in blocks:
        block.end()
    near_end()
    far_end()
    for name in kept_out:
        keep_copy(name).wait()


def forward(layer_input, cotangent, memory, seg_row, seg_col, flags, self_weights, cross_weights, mlp_in, mlp_out, gains):
    wide = lax.axis_size("wide")
    depth = wide // 4
    gain_block = jnp.pad(gains, ((0, 16 - gains.shape[0]), (0, 128 - gains.shape[1])))
    owns = (self_weights, cross_weights, mlp_in, mlp_out[None], gain_block[None])
    vmem, anywhere, smem = (pl.BlockSpec(memory_space=space) for space in (pltpu.VMEM, pl.ANY, pltpu.SMEM))
    kept = [spec.array() for spec in PASSED]
    outs = pl.pallas_call(
        lambda *refs: forward_kernel(depth, 2 * wide, refs),
        out_shape=[jax.ShapeDtypeStruct(layer_input.shape, LOW)] + kept,
        in_specs=[vmem] * 5 + [smem] + [anywhere] * 5,
        out_specs=[vmem] + [anywhere] * len(kept),
        scratch_shapes=[spec.scratch() for table in (K, W, F) for spec in specs(table)]
        + gather_sems(len(GATHER_LAYOUT), depth)
        + [pltpu.SemaphoreType.DMA((4,)), pltpu.SemaphoreType.DMA((len(kept),))],
        compiler_params=pltpu.CompilerParams(
            collective_id=0, has_side_effects=True, vmem_limit_bytes=60 * 2**20
        ),
        name="forward",
    )(layer_input, cotangent, memory, seg_row, seg_col, flags, *owns)
    return outs[0], dict(zip(PASSED, outs[1:]))


class Scatter:
    def __init__(self, place, bufs, outs, rows, side, sems):
        self.p = place
        self.staged, self.held, self.from_x, self.from_y, self.from_z, self.relayed, self.done, self.other = bufs
        self.outs = outs
        self.rows = rows
        self.side = side
        self.main = rows - side
        self.send, self.recv = sems

    def span(self, start, size):
        return pl.ds(pl.multiple_of(start, 16), size)

    @property
    def main_span(self):
        return self.span(self.side * self.p.x, self.main)

    def side_span(self, x):
        return self.span(self.main * x, self.side)

    def c_copy(self):
        return remote(self.staged, self.held, self.send.at[0], self.recv.at[0], self.p.across_core)

    def x_copy(self):
        p = self.p
        return remote(
            self.held.at[:, :, :, self.side_span(1 - p.x)],
            self.from_x,
            self.send.at[1],
            self.recv.at[1],
            p.across_x,
        )

    def y_copy(self):
        p = self.p
        return remote(
            self.held.at[:, :, 1 - p.y, self.main_span], self.from_y, self.send.at[2], self.recv.at[2], p.across_y
        )

    def z_piece(self, z):
        return self.held.at[:, z, self.p.y, self.main_span]

    def z_copy(self, step):
        p = self.p
        return remote(
            self.z_piece((p.z + step) % p.depth),
            self.from_z.at[step - 1],
            self.send.at[2 + step],
            self.recv.at[2 + step],
            p.z_ahead(step),
        )

    def relay_copy(self, up):
        p = self.p
        target, between = (3, 2) if up else (0, 1)
        device = (p.shard(between, p.y, p.core), p.x)
        return remote(self.z_piece(target), self.relayed, self.send.at[6], self.recv.at[6], device)

    def last_copy(self):
        return remote(self.done, self.other, self.send.at[7], self.recv.at[7], self.p.across_x)

    def blank(self):
        p = self.p

        @pl.when(p.z == 0)
        def _():
            self.from_z[0] = jnp.zeros_like(self.from_z[0])

        @pl.when(p.z == 3)
        def _():
            self.from_z[2] = jnp.zeros_like(self.from_z[2])

    def each_z(self, act_direct, act_late, act_relay):
        p = self.p
        if act_direct is not None:
            act_direct(self.z_copy(2))

            @pl.when(p.z != 0)
            def _():
                @pl.when(p.z != 1)
                def _():
                    act_direct(self.z_copy(3))

            @pl.when(p.z != 3)
            def _():
                @pl.when(p.z != 2)
                def _():
                    act_direct(self.z_copy(1))

        if act_late is not None:

            @pl.when(p.z == 1)
            def _():
                act_late(self.z_copy(3), 0)

            @pl.when(p.z == 2)
            def _():
                act_late(self.z_copy(1), 3)

        if act_relay is not None:

            @pl.when(p.z == 0)
            def _():
                act_relay(self.relay_copy(True))

            @pl.when(p.z == 3)
            def _():
                act_relay(self.relay_copy(False))

    def start_c(self):
        self.c_copy().start()

    def start_x(self):
        if self.side:
            self.x_copy().start()
        else:
            self.y_copy().start()

    def take_x(self):
        if self.side:
            self.x_copy().wait_recv()
            span = self.side_span(self.p.x)
            self.held[:, :, :, span] = self.held[:, :, :, span] + self.from_x[...]
            self.y_copy().start()

    def take_y(self):
        p = self.p
        self.y_copy().wait_recv()
        span = self.main_span
        self.held[:, :, p.y, span] = self.held[:, :, p.y, span] + self.from_y[...]
        self.each_z(lambda copy: copy.start(), None, lambda copy: copy.start())

    def take_relay(self):
        def late(copy, target):
            self.relay_copy(True).wait_recv()
            p = self.p
            span = self.main_span
            self.held[:, target, p.y, span] = self.held[:, target, p.y, span] + self.relayed[...]
            copy.start()

        self.each_z(None, late, None)

    def take_z(self):
        p = self.p
        self.z_copy(2).wait_recv()

        @pl.when(p.z != 0)
        def _():
            self.z_copy(1).wait_recv()

        @pl.when(p.z != 3)
        def _():
            self.z_copy(3).wait_recv()

        total = self.held[:, p.z, p.y, self.main_span].astype(jnp.float32)
        for step in range(1, p.depth):
            total += self.from_z[step - 1].astype(jnp.float32)
        self.done[...] = total.astype(LOW)
        self.last_copy().start()

    def take_last(self):
        p = self.p
        self.last_copy().wait_recv()
        side, both = self.side, self.main - self.side
        for number, (out, mat, column) in enumerate(self.outs):
            columns = slice(column, column + 256)
            if side:
                out[mat, self.side_span(p.x), columns] = self.done[number, self.span(both * p.x, side)].astype(
                    jnp.float32
                )
                out[mat, self.side_span(1 - p.x), columns] = self.other[
                    number, self.span(both * (1 - p.x), side)
                ].astype(jnp.float32)
            out[mat, side : side + both, columns] = self.done[number, self.span(side * (1 - p.x), both)].astype(
                jnp.float32
            ) + self.other[number, self.span(side * p.x, both)].astype(jnp.float32)

    def end(self):
        def wait(copy, target=None):
            copy.wait_send()

        if self.side:
            self.x_copy().wait_send()
        self.y_copy().wait_send()
        self.each_z(wait, wait, wait)
        self.last_copy().wait_send()


SCATTER_LAYOUT = (
    (3, ((0, 0),), 128, 32),
    (3, ((0, 256),), 128, 32),
    (3, ((0, 512),), 128, 32),
    (2, tuple((0, c) for c in range(0, 1024, 256)), 48, 16),
    (2, tuple((0, c) for c in range(1024, 2048, 256)), 48, 16),
    (2, tuple((1, c) for c in range(0, 1024, 256)), 48, 16),
    (2, tuple((1, c) for c in range(1024, 2048, 256)), 48, 16),
    (1, tuple((3, c) for c in range(0, 768, 256)), 48, 0),
    (1, tuple((m, 0) for m in range(3)), 48, 16),
    (1, tuple((m, 256) for m in range(3)), 48, 16),
    (1, tuple((m, 512) for m in range(3)), 48, 16),
    (0, tuple((3, c) for c in range(0, 768, 256)), 48, 0),
    (0, tuple((m, 0) for m in range(3)), 48, 16),
    (0, tuple((m, 256) for m in range(3)), 48, 16),
    (0, tuple((m, 512) for m in range(3)), 48, 16),
)
RINGS = {128: 2, 48: 3}


def scatter_buffers(depth):
    bufs = []
    for _, pieces, rows, side in SCATTER_LAYOUT:
        subs, main = len(pieces), rows - side
        bufs += [
            pltpu.VMEM((subs, depth, 2, rows, 256), LOW),
            pltpu.VMEM((subs, depth, 2, side, 256) if side else (16, 128), LOW),
            pltpu.VMEM((subs, depth, main, 256), LOW),
            pltpu.VMEM((depth - 1, subs, main, 256), LOW),
            pltpu.VMEM((subs, main, 256), LOW),
            pltpu.VMEM((subs, main, 256), LOW),
            pltpu.VMEM((subs, main, 256), LOW),
        ]
    return bufs


def staging_buffers(depth):
    return [
        pltpu.VMEM((RINGS[128], 1, depth, 2, 128, 256), LOW),
        pltpu.VMEM((RINGS[48], 4, depth, 2, 48, 256), LOW),
    ]


class K0:
    x0 = Spec(TOKENS, WIDTH)


class B:
    biast = Spec(TOKENS, TOKENS, dtype=jnp.float32)
    dlow = Spec(TOKENS, WIDTH)
    do = Spec(TOKENS, WIDTH)
    dq = Spec(TOKENS, WIDTH)
    dk = Spec(TOKENS, WIDTH)
    dv = Spec(TOKENS, WIDTH)
    dh = Spec(TOKENS, WIDTH, dtype=jnp.float32)
    mem_sum = Spec(PATCHES, WIDTH, dtype=jnp.float32)
    mem_low = Spec(2, PATCHES, WIDTH)
    mem_got = Spec(2, PATCHES, WIDTH)
    gains = Spec(8, WIDTH, dtype=jnp.float32)
    gain_got = Spec(6, 8, WIDTH, dtype=jnp.float32)
    gain_row = Spec(1, WIDTH, dtype=jnp.float32)


def attend_back_pair(pair, q, k, v, do, lse, bias, dq, dk, dv):
    span = pair_span(pair)
    q_two, k_two, v_two, do_two = q[:, span], k[:, span], v[:, span], do[:, span]
    low_q = lax.broadcasted_iota(jnp.int32, q_two.shape, 1) < HEAD_DIM
    low_k = lax.broadcasted_iota(jnp.int32, k_two.shape, 1) < HEAD_DIM
    scale = HEAD_DIM ** (-0.5)
    grads = []
    for half in range(2):
        mine = low_q if half == 0 else ~low_q
        scores = dot(k_two, jnp.where(mine, q_two, jnp.zeros_like(q_two)), 1, 1) * scale
        if bias is not None:
            scores = scores + bias[...]
        head = 2 * pair + half
        shares = jnp.exp(scores - lse[head : head + 1, :])
        p_grad = dot(v_two, jnp.where(mine, do_two, jnp.zeros_like(do_two)), 1, 1)
        along = jnp.sum(shares * p_grad, axis=0, keepdims=True)
        s_low = (shares * (p_grad - along)).astype(LOW)
        v_grad = dot(shares.astype(LOW), do_two)
        k_grad = dot(s_low, q_two) * scale
        q_grad = dot(s_low, k_two, 0, 0) * scale
        grads.append((q_grad, k_grad, v_grad))
    dq[:, span] = jnp.where(low_q, grads[0][0], grads[1][0]).astype(LOW)
    count = k_two.shape[0]
    dk[:count, span] = jnp.where(low_k, grads[0][1], grads[1][1]).astype(LOW)
    dv[:count, span] = jnp.where(low_k, grads[0][2], grads[1][2]).astype(LOW)


class Total:
    def __init__(self, place, value, got, send, recv):
        self.p, self.value, self.got, self.send, self.recv = place, value, got, send, recv

    def copy(self, slot):
        p = self.p
        device = (p.across_core, p.across_x, p.across_y, *(p.z_ahead(step) for step in (1, 2, 3)))[slot]
        return remote(self.value, self.got.at[slot], self.send.at[slot], self.recv.at[slot], device)

    def start(self, slots):
        for slot in slots:
            self.copy(slot).start()

    def take(self, slots):
        for slot in slots:
            self.copy(slot).wait()
        total = self.value[...]
        for slot in slots:
            total = total + self.got[slot]
        self.value[...] = total


class Plan:
    def __init__(self):
        self.now = 0.0
        self.free = {"c": 0.0, "x": 0.0, "y": 0.0, "z": 0.0}
        self.rate = {"c": 400e3, "x": 42e3, "y": 42e3, "z": 42e3}
        self.waiting = []

    def sent(self, link, size, then, cost=0.3):
        begin = max(self.now, self.free[link])
        end = begin + size / self.rate[link]
        self.free[link] = end
        self.waiting.append((end + 1.5, len(self.waiting), cost, then))

    def due(self):
        ready = [w for w in self.waiting if w[0] <= self.now]
        return min(ready)[:2] if ready else None

    def take(self):
        first = min(self.waiting, key=lambda w: w[:2])
        self.waiting.remove(first)
        self.now = max(self.now, first[0]) + first[2]
        first[3]()

    def drain(self):
        while self.waiting and min(self.waiting, key=lambda w: w[:2])[0] <= self.now:
            self.take()

    def work(self, cost, run):
        self.drain()
        run()
        self.now += cost


def backward_kernel(depth, row_count, refs):
    (dy, seg_row, seg_col, flags) = refs[:4]
    names = PASSED + [K0.x0]
    given = dict(zip(names, refs[4:]))
    rest = refs[4 + len(names) :]
    outs, (x_grad, mem_grad, gain_grad) = rest[:4], rest[4:7]
    rest = rest[7:]
    kept = dict(zip(names, rest))
    rest = rest[len(names) :]
    local, rest = dict(zip(specs(B), rest)), rest[len(specs(B)) :]
    staging = {128: rest[0], 48: rest[1]}
    rest = rest[2:]
    count = len(SCATTER_LAYOUT)
    bufs, (load_sem, send_sem, recv_sem, row_sem, total_send, total_recv) = rest[: 7 * count], rest[7 * count :]
    place = Place(depth)
    rows = Rows(place, row_count)
    core = place.core
    plan = Plan()

    def load(*chosen):
        for name in chosen:
            number = names.index(name)
            pltpu.make_async_copy(given[name], kept[name], load_sem.at[number]).start()

    def loaded(*chosen):
        for name in chosen:
            number = names.index(name)
            pltpu.make_async_copy(given[name], kept[name], load_sem.at[number]).wait()

    blocks, rings = [], {128: [], 48: []}
    for number, (out, pieces, share_rows, side) in enumerate(SCATTER_LAYOUT):
        ring = rings[share_rows]
        slot = len(ring) % RINGS[share_rows]
        staged = staging[share_rows].at[slot, 0 : len(pieces)]
        block = Scatter(
            place,
            (staged,) + tuple(bufs[7 * number : 7 * number + 7]),
            [(outs[out], mat, column) for mat, column in pieces],
            share_rows,
            side,
            [send_sem.at[number], recv_sem.at[number]],
        )
        block.before = ring[-RINGS[share_rows]] if len(ring) >= RINGS[share_rows] else None
        ring.append(block)
        blocks.append(block)

    near_start, near_arrive, near_end = pass_rows(
        rows, local[B.mem_low].at[1], local[B.mem_got].at[1], -1, (row_sem.at[0], row_sem.at[1])
    )
    far_start, far_arrive, far_end = pass_rows(
        rows, local[B.mem_low].at[0], local[B.mem_got].at[0], -2, (row_sem.at[2], row_sem.at[3])
    )
    total = Total(place, local[B.gains], local[B.gain_got], total_send, total_recv)

    def half(left, which):
        part = kept[left][:, :, which]
        return part.reshape(-1, part.shape[-1])

    def products(terms, which):
        found = []
        for left, right, first, width in terms:
            value = dot(half(left, which), right[: kept[left].shape[-1], first : first + width])
            value = value.reshape(depth, 2, -1, width)
            found += [value[..., c : c + 256] for c in range(0, width, 256)]
        return found

    def size(block, what):
        subs = len(block.outs)
        return subs * 256 * 2 * {"c": 8 * block.rows, "x": 8 * block.side, "y": 4 * block.main, "z": 2 * block.main, "r": block.main, "l": block.main}[what]

    def give(number, terms):
        block = blocks[number]

        def run():
            if block.before is not None:
                block.before.c_copy().wait_send()
                block.before.sent = True
            for sub, value in enumerate(products(terms, 1 - core)):
                block.staged[sub] = value.astype(LOW)
            block.start_c()
            plan.free["c"] = max(plan.now, plan.free["c"]) + size(block, "c") / plan.rate["c"]

        return run

    def hold(number, terms):
        block = blocks[number]

        def run():
            block.c_copy().wait_recv()
            for sub, value in enumerate(products(terms, core)):
                block.held[sub] = (value + block.held[sub].astype(jnp.float32)).astype(LOW)
            block.start_x()

            def to_y():
                block.take_x()
                plan.sent("y", size(block, "y"), to_z, 0.2)

            def to_z():
                block.take_y()
                plan.sent("z", size(block, "z"), to_relay, 0.2)

            def to_relay():
                block.take_relay()
                plan.sent("z", size(block, "r"), to_last, 0.2)

            def to_last():
                block.take_z()
                plan.sent("x", size(block, "l"), block.take_last, 0.2)

            if block.side:
                plan.sent("x", size(block, "x"), to_y, 0.2)
            else:
                plan.sent("y", size(block, "y"), to_z, 0.2)

        return run

    def make_bias():
        seg_k, seg_q = seg_col[:, 0:1], seg_row[0:1, :]
        key = lax.broadcasted_iota(jnp.int32, (TOKENS, TOKENS), 0)
        query = lax.broadcasted_iota(jnp.int32, (TOKENS, TOKENS), 1)
        allowed = (seg_q == seg_k) & (key <= query) & ((seg_col[:, 1:2] == 1) | (key == query))
        local[B.biast][...] = jnp.where(allowed, 0.0, -1e30)

    def cross_begin():
        local[B.dlow][...] = kept[K.dx2][...].astype(LOW)

    def cross_do():
        local[B.do][...] = dot(local[B.dlow][...], kept[W.w_cross][3], 1, 1).astype(LOW)

    def cross_pair(pair):
        def run():
            attend_back_pair(
                pair,
                kept[K.q2],
                kept[K.k2],
                kept[K.v2],
                local[B.do],
                kept[K.lse2],
                None,
                local[B.dq],
                local[B.dk],
                local[B.dv],
            )

        return run

    def self_pair(pair):
        def run():
            attend_back_pair(
                pair,
                kept[K.q1],
                kept[K.k1],
                kept[K.v1],
                local[B.do],
                kept[K.lse1],
                local[B.biast],
                local[B.dq],
                local[B.dk],
                local[B.dv],
            )

        return run

    def mem_back():
        value = dot(local[B.dk][:PATCHES], kept[W.w_cross][1], 1, 1)
        value += dot(local[B.dv][:PATCHES], kept[W.w_cross][2], 1, 1)
        local[B.mem_sum][...] = value
        local[B.mem_low][0] = value.astype(LOW)
        far_start()

    def mem_far():
        far_arrive()
        got = jnp.where(flags[2] >= 2, local[B.mem_got][0].astype(jnp.float32), 0.0)
        value = local[B.mem_sum][...] + got
        local[B.mem_sum][...] = value
        local[B.mem_low][1] = value.astype(LOW)
        near_start()

    def mem_near():
        near_arrive()
        got = jnp.where(flags[1] == 1, local[B.mem_got][1].astype(jnp.float32), 0.0)
        mem_grad[...] = jnp.where(flags[0] == 0, local[B.mem_sum][...] + got, 0.0)

    def cross_dh():
        local[B.dh][...] = dot(local[B.dq][...], kept[W.w_cross][0], 1, 1)

    def cross_norm():
        norm_back_rows(kept[K.x1], kept[K.gain][1:2], local[B.dh], kept[K.dx2], kept[K.dx2], local[B.gain_row])
        local[B.gains][1:2, :] = local[B.gain_row][...]
        local[B.dlow][...] = kept[K.dx2][...].astype(LOW)

    def self_do():
        local[B.do][...] = dot(local[B.dlow][...], kept[W.w_self][3], 1, 1).astype(LOW)

    def self_dh_first():
        local[B.dh][...] = dot(local[B.dq][...], kept[W.w_self][0], 1, 1)

    def self_dh_second():
        local[B.dh][...] += dot(local[B.dk][...], kept[W.w_self][1], 1, 1)

    def self_dh_third():
        local[B.dh][...] += dot(local[B.dv][...], kept[W.w_self][2], 1, 1)

    def self_norm():
        norm_back_rows(kept[K0.x0], kept[K.gain][0:1], local[B.dh], kept[K.dx2], x_grad, local[B.gain_row])
        local[B.gains][0:1, :] = local[B.gain_row][...]
        local[B.gains][2:3, :] = kept[K.gain3][...]
        total.start((0,))

    def load_cross():
        load(K.dx2, W.w_cross, K.o2t, K.q2, K.k2, K.v2, K.lse2, K.h2t, K.memt, K.x1, K.gain, K.gain3)

    def load_self():
        load(W.w_self, K.o1t, K.q1, K.k1, K.v1, K.lse1, K.h1t, K0.x0)

    do_low, dq, dk, dv = local[B.dlow], local[B.dq], local[B.dk], local[B.dv]
    out_terms = [[(K.hiddent, dy, 256 * j, 256)] for j in range(3)]
    in_terms = [[(K.h3t, kept[name], first, 1024)] for name in (K.dgate, K.dup) for first in (0, 1024)]

    load(K.hiddent, K.h3t, K.dgate, K.dup)
    local[B.gains][...] = jnp.zeros_like(local[B.gains])
    for block in blocks:
        block.sent = False
        block.blank()
    greet_all(place, rows)
    load_cross()
    loaded(K.hiddent)
    plan.work(0.8, give(0, out_terms[0]))
    plan.work(0.8, give(1, out_terms[1]))
    plan.work(0.9, hold(0, out_terms[0]))
    plan.work(0.8, give(2, out_terms[2]))
    plan.work(0.9, hold(1, out_terms[1]))
    loaded(K.h3t, K.dgate, K.dup)
    load_self()
    plan.work(1.0, give(3, in_terms[0]))
    plan.work(0.9, hold(2, out_terms[2]))
    for j in range(1, 4):
        plan.work(1.0, give(3 + j, in_terms[j]))
        plan.work(1.1, hold(2 + j, in_terms[j - 1]))
    loaded(K.dx2, W.w_cross, K.o2t, K.q2, K.k2, K.v2, K.lse2, K.h2t, K.memt, K.x1, K.gain, K.gain3)
    plan.work(0.3, cross_begin)
    o_terms = [(K.o2t, do_low, 0, 768)]
    plan.work(0.8, give(7, o_terms))
    plan.work(1.1, hold(6, in_terms[3]))
    plan.work(0.8, cross_do)
    plan.work(0.9, hold(7, o_terms))

    def attention(pair_work, first, lefts):
        previous = None
        for group in range(3):
            for pair in (2 * group, 2 * group + 1):
                plan.work(1.4, pair_work(pair))
            terms = [(left, right, 256 * group, 256) for left, right in zip(lefts, (dq, dk, dv))]
            plan.work(1.0, give(first + group, terms))
            if previous is not None:
                plan.work(1.0, hold(*previous))
            previous = (first + group, terms)
        return previous

    previous = attention(cross_pair, 8, (K.h2t, K.memt, K.memt))
    plan.work(1.5, mem_back)
    plan.work(1.0, hold(*previous))
    plan.work(0.8, cross_dh)
    plan.work(1.2, cross_norm)
    loaded(W.w_self, K.o1t, K.q1, K.k1, K.v1, K.lse1, K.h1t, K0.x0)
    o_terms = [(K.o1t, do_low, 0, 768)]
    plan.work(0.8, give(11, o_terms))
    plan.work(0.3, mem_far)
    plan.work(0.8, self_do)
    plan.work(0.5, make_bias)
    plan.work(0.9, hold(11, o_terms))
    previous = attention(self_pair, 12, (K.h1t, K.h1t, K.h1t))
    plan.work(0.8, self_dh_first)
    plan.work(1.0, hold(*previous))
    plan.work(0.8, self_dh_second)
    plan.work(0.8, self_dh_third)
    plan.work(0.5, mem_near)
    plan.work(1.5, self_norm)

    def total_step(slots, after):
        def run():
            total.take(slots)
            if after:
                total.start(after[0])
                plan.waiting.append((plan.now + 2.5, -1, 0.2, total_step(after[0], after[1:])))
            else:
                gain_grad[...] = local[B.gains][...]

        return run

    plan.waiting.append((plan.now + 2.5, -1, 0.2, total_step((0,), ((1,), (2,), (3, 4, 5)))))
    while plan.waiting:
        plan.take()
    for block in blocks:
        if not block.sent:
            block.c_copy().wait_send()
        block.end()
    near_end()
    far_end()


def backward(kept, layer_input, cotangent, seg_row, seg_col, flags):
    wide = lax.axis_size("wide")
    depth = wide // 4

    def owners(array):
        return array.reshape(depth, 2, 2, -1, array.shape[-1])

    names = PASSED + [K0.x0]
    given = {**kept, K0.x0: layer_input}
    for name in (K.h1t, K.o1t, K.h2t, K.o2t, K.memt, K.h3t, K.hiddent):
        given[name] = owners(given[name])
    arrays = [given[name] for name in names]
    vmem, anywhere, smem = (pl.BlockSpec(memory_space=space) for space in (pltpu.VMEM, pl.ANY, pltpu.SMEM))
    outs = [
        ((4, WIDTH // wide, WIDTH), jnp.float32),
        ((4, WIDTH // wide, WIDTH), jnp.float32),
        ((2, WIDTH // wide, HIDDEN), jnp.float32),
        ((1, HIDDEN // wide, WIDTH), jnp.float32),
        ((TOKENS, WIDTH), jnp.float32),
        ((PATCHES, WIDTH), jnp.float32),
        ((8, WIDTH), jnp.float32),
    ]
    count = len(SCATTER_LAYOUT)
    return pl.pallas_call(
        lambda *refs: backward_kernel(depth, 2 * wide, refs),
        out_shape=[jax.ShapeDtypeStruct(*o) for o in outs],
        in_specs=[vmem] * 3 + [smem] + [anywhere] * len(arrays),
        out_specs=[vmem] * len(outs),
        scratch_shapes=[pltpu.VMEM(a.shape, a.dtype) for a in arrays]
        + [spec.scratch() for spec in specs(B)]
        + staging_buffers(depth)
        + scatter_buffers(depth)
        + [
            pltpu.SemaphoreType.DMA((len(arrays),)),
            pltpu.SemaphoreType.DMA((count, 8)),
            pltpu.SemaphoreType.DMA((count, 8)),
            pltpu.SemaphoreType.DMA((4,)),
            pltpu.SemaphoreType.DMA((6,)),
            pltpu.SemaphoreType.DMA((6,)),
        ],
        compiler_params=pltpu.CompilerParams(
            collective_id=1, has_side_effects=True, vmem_limit_bytes=63 * 2**20
        ),
        name="backward",
    )(cotangent, seg_row, seg_col, flags, *arrays)


def plain_gather(self_weights, cross_weights, mlp_in, mlp_out, gains):
    return (
        lax.all_gather(self_weights, "wide", axis=1, tiled=True),
        lax.all_gather(cross_weights, "wide", axis=1, tiled=True),
        lax.all_gather(mlp_in, "wide", axis=1, tiled=True),
        lax.all_gather(mlp_out, "wide", axis=0, tiled=True),
        lax.all_gather(gains, "wide", axis=1, tiled=True),
    )


def plain_scatter(*grads):
    outs = []
    for grad, axis in zip(grads, (1, 1, 1, 0, 1)):
        piece = lax.psum_scatter(grad, ("wide", "narrow"), scatter_dimension=axis, tiled=True)
        outs.append(lax.all_gather(piece.astype(jnp.bfloat16), "narrow", axis=axis, tiled=True).astype(jnp.float32))
    return tuple(outs)


def by_kernel(self_weights):
    return lax.axis_size("wide") == 16 and lax.axis_size("narrow") == 2 and self_weights.shape[1] % 48 == 0


def plain_device(
    layer_input,
    memory,
    cotangent,
    segment_ids,
    padding,
    image_of_row,
    self_weights,
    cross_weights,
    mlp_in,
    mlp_out,
    gains,
):
    self_full, cross_full, in_full, out_full, gain_full = plain_gather(
        self_weights, cross_weights, mlp_in, mlp_out, gains
    )
    gain_float = gain_full.astype(jnp.float32)
    x_zero = layer_input[0].astype(jnp.float32)
    seg_row = segment_ids[0]
    pad_row = padding[0]
    seq_len = x_zero.shape[0]
    position = jnp.arange(seq_len)
    allowed = (
        (seg_row[:, None] == seg_row[None, :])
        & (position[None, :] <= position[:, None])
        & ((pad_row[None, :] == 1) | (position[:, None] == position[None, :]))
    )
    h_one = rms_norm(x_zero, gain_float[0]).astype(jnp.bfloat16)
    q_self = linear(h_one, self_full[0]).astype(jnp.bfloat16)
    k_self = linear(h_one, self_full[1]).astype(jnp.bfloat16)
    v_self = linear(h_one, self_full[2]).astype(jnp.bfloat16)
    self_mix, self_lse = forward_heads(q_self, k_self, v_self, allowed)
    x_one = x_zero + linear(self_mix, self_full[3])
    row_ids = jnp.arange(image_of_row.shape[0])
    starts = jnp.sum(image_of_row[None, :] < image_of_row[:, None], axis=1)
    offsets = row_ids - starts
    my_index = lax.axis_index(("wide", "narrow"))
    my_offset = jnp.sum(jnp.where(row_ids == my_index, offsets, 0))
    own_patches = memory[0]
    memory_use = own_patches
    for distance in (1, 2, 3):
        arrived = shifted(own_patches, ("wide", "narrow"), distance)
        memory_use = jnp.where(my_offset == distance, arrived, memory_use)
    h_two = rms_norm(x_one, gain_float[1]).astype(jnp.bfloat16)
    q_cross = linear(h_two, cross_full[0]).astype(jnp.bfloat16)
    k_cross = linear(memory_use, cross_full[1]).astype(jnp.bfloat16)
    v_cross = linear(memory_use, cross_full[2]).astype(jnp.bfloat16)
    cross_mix, cross_lse = forward_heads(q_cross, k_cross, v_cross, None)
    x_two = x_one + linear(cross_mix, cross_full[3])
    h_three = rms_norm(x_two, gain_float[2]).astype(jnp.bfloat16)
    gate_act = linear(h_three, in_full[0])
    up_act = linear(h_three, in_full[1])
    hidden = gated_product(gate_act, up_act).astype(jnp.bfloat16)
    result = x_two + linear(hidden, out_full)
    out_low = cotangent[0]
    out_grad_w = contract_rows(hidden, out_low)
    hidden_grad = times_transposed(out_low, out_full)
    _, pullback = jax.vjp(gated_product, gate_act, up_act)
    gate_grad, up_grad = pullback(hidden_grad)
    gate_low = gate_grad.astype(jnp.bfloat16)
    up_low = up_grad.astype(jnp.bfloat16)
    in_grad = jnp.stack([contract_rows(h_three, gate_low), contract_rows(h_three, up_low)])
    h_three_grad = times_transposed(gate_low, in_full[0]) + times_transposed(up_low, in_full[1])
    _, pullback = jax.vjp(rms_norm, x_two, gain_float[2])
    x_two_norm, gain_three = pullback(h_three_grad)
    x_two_grad = out_low.astype(jnp.float32) + x_two_norm
    cross_out_low = x_two_grad.astype(jnp.bfloat16)
    cross_o_grad = contract_rows(cross_mix, cross_out_low)
    cross_mix_grad = times_transposed(cross_out_low, cross_full[3]).astype(jnp.bfloat16)
    q_cross_grad, k_cross_grad, v_cross_grad = backward_heads(
        q_cross, k_cross, v_cross, cross_mix_grad, cross_lse, None
    )
    cross_grad = jnp.stack(
        [
            contract_rows(h_two, q_cross_grad),
            contract_rows(memory_use, k_cross_grad),
            contract_rows(memory_use, v_cross_grad),
            cross_o_grad,
        ]
    )
    mem_grad = times_transposed(k_cross_grad, cross_full[1]) + times_transposed(
        v_cross_grad, cross_full[2]
    )
    h_two_grad = times_transposed(q_cross_grad, cross_full[0])
    _, pullback = jax.vjp(rms_norm, x_one, gain_float[1])
    x_one_norm, gain_two = pullback(h_two_grad)
    x_one_grad = x_two_grad + x_one_norm
    self_out_low = x_one_grad.astype(jnp.bfloat16)
    self_o_grad = contract_rows(self_mix, self_out_low)
    self_mix_grad = times_transposed(self_out_low, self_full[3]).astype(jnp.bfloat16)
    q_self_grad, k_self_grad, v_self_grad = backward_heads(
        q_self, k_self, v_self, self_mix_grad, self_lse, allowed
    )
    self_grad = jnp.stack(
        [
            contract_rows(h_one, q_self_grad),
            contract_rows(h_one, k_self_grad),
            contract_rows(h_one, v_self_grad),
            self_o_grad,
        ]
    )
    h_one_grad = (
        times_transposed(q_self_grad, self_full[0])
        + times_transposed(k_self_grad, self_full[1])
        + times_transposed(v_self_grad, self_full[2])
    )
    _, pullback = jax.vjp(rms_norm, x_zero, gain_float[0])
    x_zero_norm, gain_one = pullback(h_one_grad)
    x_grad = x_one_grad + x_zero_norm
    mem_summed = jnp.where(my_offset == 0, mem_grad, 0.0)
    for distance in (1, 2, 3):
        arrived = shifted(mem_grad.astype(jnp.bfloat16), ("wide", "narrow"), -distance).astype(
            mem_grad.dtype
        )
        neighbour = jnp.sum(jnp.where(row_ids == my_index + distance, offsets, 0))
        mem_summed = mem_summed + jnp.where(neighbour == distance, arrived, 0.0)
    gain_grad = jnp.stack([gain_one, gain_two, gain_three])
    reduced = plain_scatter(self_grad, cross_grad, in_grad, out_grad_w, gain_grad)
    return (
        result.astype(jnp.bfloat16)[None],
        x_grad[None],
        mem_summed[None],
        reduced[0],
        reduced[1],
        reduced[2],
        reduced[3],
        reduced[4],
    )


def kernel_device(
    layer_input,
    memory,
    cotangent,
    segment_ids,
    padding,
    image_of_row,
    self_weights,
    cross_weights,
    mlp_in,
    mlp_out,
    gains,
):
    seg_rows = jnp.pad(jnp.concatenate([segment_ids, padding]), ((0, 6), (0, 0)))
    seg_cols = jnp.pad(seg_rows[:2].T, ((0, 0), (0, 126)))
    row_ids = jnp.arange(image_of_row.shape[0])
    starts = jnp.sum(image_of_row[None, :] < image_of_row[:, None], axis=1)
    offsets = row_ids - starts
    my_index = lax.axis_index(("wide", "narrow"))
    flags = jnp.stack([jnp.sum(jnp.where(row_ids == my_index + ahead, offsets, 0)) for ahead in range(4)]).astype(jnp.int32)
    result, kept = forward(
        layer_input[0], cotangent[0], memory[0], seg_rows, seg_cols, flags, self_weights, cross_weights, mlp_in, mlp_out, gains
    )
    self_grad, cross_grad, in_grad, out_grad, x_grad, mem_grad, gain_total = backward(
        kept, layer_input[0], cotangent[0], seg_rows, seg_cols, flags
    )
    share = gains.shape[1]
    gain_grad = lax.dynamic_slice(
        gain_total, (0, lax.axis_index("wide") * share), (gains.shape[0], share)
    )
    return (result[None], x_grad[None], mem_grad[None], self_grad, cross_grad, in_grad, out_grad[0], gain_grad)


def on_device(
    layer_input,
    memory,
    cotangent,
    segment_ids,
    padding,
    image_of_row,
    self_weights,
    cross_weights,
    mlp_in,
    mlp_out,
    gains,
):
    run = kernel_device if by_kernel(self_weights) else plain_device
    return run(
        layer_input,
        memory,
        cotangent,
        segment_ids,
        padding,
        image_of_row,
        self_weights,
        cross_weights,
        mlp_in,
        mlp_out,
        gains,
    )


def solution(mesh):
    in_specs = (
        P(("wide", "narrow"), None, None),
        P(("wide", "narrow"), None, None),
        P(("wide", "narrow"), None, None),
        P(("wide", "narrow"), None),
        P(("wide", "narrow"), None),
        P(),
        P(None, "wide", None),
        P(None, "wide", None),
        P(None, "wide", None),
        P("wide", None),
        P(None, "wide"),
    )
    out_specs = (
        P(("wide", "narrow"), None, None),
        P(("wide", "narrow"), None, None),
        P(("wide", "narrow"), None, None),
        P(None, "wide", None),
        P(None, "wide", None),
        P(None, "wide", None),
        P("wide", None),
        P(None, "wide"),
    )
    return jax.shard_map(
        on_device, mesh=mesh, in_specs=in_specs, out_specs=out_specs, check_vma=False
    )
```

```python
import functools

import jax
import jax.numpy as jnp
from jax import lax
from jax.experimental import pallas as pl
from jax.experimental.pallas import tpu as pltpu
from jax.sharding import PartitionSpec as P

HEAD_DIM = 64


EPSILON = 1e-06


def shifted(value, axis, steps):
    count = lax.axis_size(axis)
    first, last = (max(0, -steps), min(count, count - steps))
    return lax.ppermute(value, axis, [(source, source + steps) for source in range(first, last)])


def rms_norm(v, g):
    return v * lax.rsqrt(jnp.mean(v * v, axis=-1, keepdims=True) + EPSILON) * g


def contract_rows(a, b):
    return lax.dot_general(a, b, (((0,), (0,)), ((), ())), preferred_element_type=jnp.float32)


def times_transposed(a, w):
    return lax.dot_general(a, w, (((1,), (1,)), ((), ())), preferred_element_type=jnp.float32)


def linear(a, w):
    return jnp.dot(a, w, preferred_element_type=jnp.float32)


def head_scores(q_part, k_part, allowed):
    scores = jnp.einsum(
        "qhd,khd->hqk", q_part, k_part, preferred_element_type=jnp.float32
    ) * HEAD_DIM ** (-0.5)
    if allowed is not None:
        scores = jnp.where(allowed[None], scores, -1e30)
    return scores


def split_heads(a, head_start):
    return a[:, head_start * HEAD_DIM : (head_start + 4) * HEAD_DIM].reshape(
        a.shape[0], 4, HEAD_DIM
    )


def forward_heads(q, k, v, allowed):
    seq_len = q.shape[0]
    head_count = q.shape[1] // HEAD_DIM
    pieces = []
    log_sums = []
    for head_start in range(0, head_count, 4):
        q_part = split_heads(q, head_start)
        k_part = split_heads(k, head_start)
        v_part = split_heads(v, head_start)
        scores = head_scores(q_part, k_part, allowed)
        highest = jnp.max(scores, axis=-1, keepdims=True)
        powers = jnp.exp(scores - highest)
        summed = jnp.sum(powers, axis=-1, keepdims=True)
        shares = (powers / summed).astype(jnp.bfloat16)
        mixed = jnp.einsum("hqk,khd->qhd", shares, v_part, preferred_element_type=jnp.float32)
        pieces.append(mixed.reshape(seq_len, -1))
        log_sums.append(highest + jnp.log(summed))
    return (jnp.concatenate(pieces, axis=1).astype(jnp.bfloat16), jnp.concatenate(log_sums, axis=0))


def backward_heads(q, k, v, mix_grad, log_sum, allowed):
    seq_len = q.shape[0]
    head_count = q.shape[1] // HEAD_DIM
    q_pieces = []
    k_pieces = []
    v_pieces = []
    for head_start in range(0, head_count, 4):
        q_part = split_heads(q, head_start)
        k_part = split_heads(k, head_start)
        v_part = split_heads(v, head_start)
        o_part = split_heads(mix_grad, head_start)
        scores = head_scores(q_part, k_part, allowed)
        shares = jnp.exp(scores - log_sum[head_start : head_start + 4])
        v_grad = jnp.einsum(
            "hqk,qhd->khd", shares.astype(jnp.bfloat16), o_part, preferred_element_type=jnp.float32
        )
        p_grad = jnp.einsum("qhd,khd->hqk", o_part, v_part, preferred_element_type=jnp.float32)
        s_grad = shares * (p_grad - jnp.sum(shares * p_grad, axis=-1, keepdims=True))
        s_low = s_grad.astype(jnp.bfloat16)
        q_grad = jnp.einsum(
            "hqk,khd->qhd", s_low, k_part, preferred_element_type=jnp.float32
        ) * HEAD_DIM ** (-0.5)
        k_grad = jnp.einsum(
            "hqk,qhd->khd", s_low, q_part, preferred_element_type=jnp.float32
        ) * HEAD_DIM ** (-0.5)
        q_pieces.append(q_grad.reshape(seq_len, -1))
        k_pieces.append(k_grad.reshape(k.shape[0], -1))
        v_pieces.append(v_grad.reshape(k.shape[0], -1))
    return (
        jnp.concatenate(q_pieces, axis=1).astype(jnp.bfloat16),
        jnp.concatenate(k_pieces, axis=1).astype(jnp.bfloat16),
        jnp.concatenate(v_pieces, axis=1).astype(jnp.bfloat16),
    )


def gated_product(gate_act, up_act):
    return jax.nn.gelu(gate_act, approximate=True) * up_act


MESH = pl.DeviceIdType.MESH


class Place:
    def __init__(self, depth):
        self.depth = depth
        self.wide = lax.axis_index("wide")
        self.x = lax.axis_index("narrow")
        self.core = self.wide % 2
        self.y = (self.wide // 2) % 2
        self.z = self.wide // 4

    def shard(self, z, y, core):
        return z * 4 + y * 2 + core

    def z_ahead(self, step):
        return (self.shard((self.z + step) % self.depth, self.y, self.core), self.x)

    def z_behind(self, step):
        return (self.z + self.depth - step) % self.depth

    @property
    def across_x(self):
        return (self.wide, 1 - self.x)

    @property
    def across_y(self):
        return (self.shard(self.z, 1 - self.y, self.core), self.x)

    @property
    def across_core(self):
        return (self.shard(self.z, self.y, 1 - self.core), self.x)

    def greet(self):
        barrier = pltpu.get_barrier_semaphore()
        others = [self.across_x, self.across_y, self.across_core]
        others += [self.z_ahead(step) for step in range(1, self.depth)]
        for other in others:
            pl.semaphore_signal(barrier, inc=1, device_id=other, device_id_type=MESH)
        pl.semaphore_wait(barrier, len(others))


def remote(src, dst, send, recv, device):
    return pltpu.make_async_remote_copy(
        src_ref=src, dst_ref=dst, send_sem=send, recv_sem=recv, device_id=device, device_id_type=MESH
    )


class Plan:
    def __init__(self, slack=2.5, latency=1.5):
        self.now = 0.0
        self.slack = slack
        self.latency = latency
        self.rate = {"c": 400e3, "x": 50e3, "y": 50e3, "z": 50e3}
        self.free = dict.fromkeys(self.rate, 0.0)
        self.queues = {link: [] for link in self.rate}
        self.flying = []
        self.serial = 0

    def send(self, link, rank, size, start, arrive, cost=0.2):
        self.serial += 1
        self.queues[link].append((rank, self.serial, size, start, arrive, cost))

    def later(self, delay, arrive, cost=0.2):
        self.serial += 1
        self.flying.append((self.now + delay, self.serial, cost, arrive))

    def issue(self):
        for link, queue in self.queues.items():
            while queue and self.free[link] <= self.now + self.slack:
                first = min(queue, key=lambda q: q[:2])
                queue.remove(first)
                _, serial, size, start, arrive, cost = first
                start()
                self.now += 0.03
                self.free[link] = max(self.free[link], self.now) + size / self.rate[link]
                if arrive is not None:
                    self.flying.append((self.free[link] + self.latency, serial, cost, arrive))

    def drain(self):
        self.issue()
        while self.flying:
            first = min(self.flying, key=lambda f: f[:2])
            if first[0] > self.now:
                break
            self.flying.remove(first)
            first[3]()
            self.now += first[2]
            self.issue()

    def busy(self):
        return bool(self.flying) or any(self.queues.values())

    def step(self):
        self.issue()
        times = [f[0] for f in self.flying]
        times += [self.free[link] - self.slack for link, queue in self.queues.items() if queue]
        self.now = max(self.now, min(times))
        self.drain()

    def work(self, cost, run):
        self.drain()
        run()
        self.now += cost


class Gather:
    def __init__(self, place, own, full, rows, side, y_first, sems):
        self.p = place
        self.own = own
        self.full = full
        self.rows = rows
        self.side = side
        self.main = rows - side
        self.y_first = y_first
        self.main_send, self.main_recv, self.x_send, self.x_recv, self.c_send, self.c_recv = sems

    def block(self, ref, start, size):
        return ref.at[:, pl.ds(pl.multiple_of(start, 16), size), :]

    def at(self, z, y, core, start, size):
        return self.block(self.full, self.p.shard(z, y, core) * self.rows + start, size)

    def owner(self, n):
        step, other = n % self.p.depth, n // self.p.depth
        return self.p.z_behind(step), (1 - self.p.y if other else self.p.y)

    @property
    def main_start(self):
        return self.side * self.p.x

    def side_start(self, x):
        return self.main * x

    def main_piece(self, z, y, source=False):
        p = self.p
        return self.at(z, y, p.core, self.main_start, self.main)

    def arriving(self, n):
        p = self.p
        z, y = self.owner(n)
        piece = self.main_piece(z, y)
        return remote(piece, piece, self.main_send.at[0], self.main_recv.at[n], p.across_y)

    def y_copy(self, n):
        p = self.p
        z, y = self.owner(n)
        dst = self.main_piece(z, y)
        src = self.block(self.own, self.main_start, self.main) if n == 0 else dst
        return remote(src, dst, self.main_send.at[n], self.main_recv.at[n + p.depth], p.across_y)

    def z_copy(self, step, other):
        p = self.p
        y = 1 - p.y if other else p.y
        dst = self.main_piece(p.z, y)
        src = dst if other else self.block(self.own, self.main_start, self.main)
        slot = p.depth + (step - 1) + (p.depth - 1) * other
        return remote(
            src, dst, self.main_send.at[slot], self.main_recv.at[step + p.depth * other], p.z_ahead(step)
        )

    def relay_copy(self, other, up):
        p = self.p
        z, target = (0, 3) if up else (3, 0)
        y = 1 - p.y if other else p.y
        piece = self.main_piece(z, y)
        slot = p.depth + 2 * (p.depth - 1) + other
        step = 3 if up else 1
        device = (p.shard(target, p.y, p.core), p.x)
        return remote(piece, piece, self.main_send.at[slot], self.main_recv.at[step + p.depth * other], device)

    def x_copy(self, n, x):
        p = self.p
        z, y = self.owner(n)
        piece = self.at(z, y, p.core, self.side_start(x), self.side)
        return remote(piece, piece, self.x_send.at[n], self.x_recv.at[n], p.across_x)

    def c_copy(self, n, core, side):
        p = self.p
        slot = n + (2 * p.depth if side else 0)
        z, y = self.owner(n)
        if n == 0:
            src, dst = self.own, self.at(z, y, core, 0, self.rows)
        else:
            start, size = (self.side_start(1 - p.x), self.side) if side else (self.main_start, self.main)
            src = dst = self.at(z, y, core, start, size)
        return remote(src, dst, self.c_send.at[slot], self.c_recv.at[slot], p.across_core)

    def copy_own(self):
        p = self.p
        return pltpu.make_async_copy(self.own, self.at(p.z, p.y, p.core, 0, self.rows), self.main_send.at[4 * p.depth])

    def each_z(self, other, act):
        p = self.p
        for step in range(1, p.depth):
            if step == 2:
                act(self.z_copy(step, other))
            else:
                end = 0 if step == 3 else 3

                @pl.when(p.z != end)
                def _():
                    act(self.z_copy(step, other))

    def each_relay(self, other, act):
        p = self.p

        @pl.when(p.z == 2)
        def _():
            act(self.relay_copy(other, True))

        @pl.when(p.z == 1)
        def _():
            act(self.relay_copy(other, False))

    def begin(self):
        self.copy_own().start()
        self.y_copy(0).start()
        self.each_z(0, lambda copy: copy.start())
        self.c_copy(0, self.p.core, False).start()

    def order(self):
        depth = self.p.depth
        if self.y_first:
            return [depth, 2, 2 + depth, 1, 3, 1 + depth, 3 + depth]
        return [2, 1, 3, depth, depth + 2, depth + 1, depth + 3]

    def take(self, n):
        p = self.p
        depth = p.depth
        self.arriving(n).wait_recv()
        other = n // depth
        if n % depth == 2 and (self.y_first or other == 0):
            self.each_relay(other, lambda copy: copy.start())
        if self.y_first:
            if n == depth:
                self.each_z(1, lambda copy: copy.start())
        elif other == 0:
            self.y_copy(n).start()
        if self.side:
            self.x_copy(n, p.x).start()
        self.c_copy(n, p.core, False).start()

    def take_x(self, n):
        p = self.p
        if self.side:
            self.x_copy(n, 1 - p.x).wait_recv()
            self.c_copy(n, p.core, True).start()

    def complete(self):
        p = self.p
        self.copy_own().wait()
        for n in range(2 * p.depth):
            self.c_copy(n, 1 - p.core, False).wait_recv()
            if self.side and n:
                self.c_copy(n, 1 - p.core, True).wait_recv()

    def end(self):
        p = self.p

        def wait(copy):
            copy.wait_send()

        for n in range(1 if self.y_first else p.depth):
            self.y_copy(n).wait_send()
        for other in range(2 if self.y_first else 1):
            self.each_z(other, wait)
            self.each_relay(other, wait)
        for n in range(2 * p.depth):
            self.c_copy(n, p.core, False).wait_send()
            if self.side and n:
                self.x_copy(n, p.x).wait_send()
                self.c_copy(n, p.core, True).wait_send()


def gather_sems(count, depth):
    sizes = (4 * depth + 1, 2 * depth, 2 * depth, 2 * depth, 4 * depth, 4 * depth)
    return [pltpu.SemaphoreType.DMA((count, size)) for size in sizes]


LOW = jnp.bfloat16


def dot(a, b, ca=1, cb=0):
    return lax.dot_general(a, b, (((ca,), (cb,)), ((), ())), preferred_element_type=jnp.float32)


def norm_rows(source, gain, target):
    rows = source.shape[0]
    chunk = 64

    @pl.loop(0, rows // chunk)
    def _(i):
        span = pl.ds(pl.multiple_of(i * chunk, chunk), chunk)
        v = source[span].astype(jnp.float32)
        scale = lax.rsqrt(jnp.mean(v * v, axis=-1, keepdims=True) + EPSILON)
        target[span] = (v * scale * gain).astype(LOW)


def norm_back_rows(source, gain, grad, dout, target, gain_grad):
    rows, width = source.shape
    chunk = 64
    gain_grad[...] = jnp.zeros_like(gain_grad)

    @pl.loop(0, rows // chunk)
    def _(i):
        span = pl.ds(pl.multiple_of(i * chunk, chunk), chunk)
        v = source[span].astype(jnp.float32)
        dh = grad[span]
        scale = lax.rsqrt(jnp.mean(v * v, axis=-1, keepdims=True) + EPSILON)
        unit = v * scale
        gain_grad[...] += jnp.sum(dh * unit, axis=0, keepdims=True)
        scaled = dh * gain
        along = jnp.mean(scaled * unit, axis=-1, keepdims=True)
        target[span] = (dout[span].astype(jnp.float32) + scale * (scaled - unit * along)).astype(target.dtype)


def pair_span(pair):
    return pl.ds(pl.multiple_of(pair * 2 * HEAD_DIM, 2 * HEAD_DIM), 2 * HEAD_DIM)


def attend_pair(pair, q, k, v, bias, mixed, lse):
    span = pair_span(pair)
    q_two, k_two, v_two = q[:, span], k[:, span], v[:, span]
    rows = q_two.shape[0]
    low_half = lax.broadcasted_iota(jnp.int32, q_two.shape, 1) < HEAD_DIM
    lane = lax.broadcasted_iota(jnp.int32, (rows, 128), 1)
    outs = []
    sums = lse[...]
    for half in range(2):
        mine = low_half if half == 0 else ~low_half
        scores = dot(jnp.where(mine, q_two, jnp.zeros_like(q_two)), k_two, 1, 1) * HEAD_DIM ** (-0.5)
        if bias is not None:
            scores = scores + bias[...]
        highest = jnp.max(scores, axis=-1, keepdims=True)
        powers = jnp.exp(scores - highest)
        summed = jnp.sum(powers, axis=-1, keepdims=True)
        shares = (powers / summed).astype(LOW)
        outs.append(dot(shares, v_two))
        sums = jnp.where(lane == 2 * pair + half, highest + jnp.log(summed), sums)
    mixed[:, span] = jnp.where(low_half, outs[0], outs[1]).astype(LOW)
    lse[...] = sums


def gelu_parts(gate):
    inner = (2.0 / 3.141592653589793) ** 0.5
    square = gate * gate
    bent = jnp.tanh(inner * gate * (1.0 + 0.044715 * square))
    half = 0.5 * (1.0 + bent)
    slope = half + 0.5 * gate * (1.0 - bent * bent) * inner * (1.0 + 3 * 0.044715 * square)
    return gate * half, slope


class Rows:
    def __init__(self, place, count):
        self.p = place
        self.count = count
        self.row = place.wide * 2 + place.x

    def device(self, row):
        return (row // 2, row % 2)

    def when(self, distance, act):
        @pl.when((self.row + distance >= 0) & (self.row + distance < self.count))
        def _():
            act(self.device(self.row + distance))

    def near(self):
        return (-2, -1, 1, 2)

    def present(self):
        below = jnp.minimum(self.row, 2)
        above = jnp.minimum(self.count - 1 - self.row, 2)
        return below + above


def greet_all(place, rows):
    barrier = pltpu.get_barrier_semaphore()
    others = [place.across_x, place.across_y, place.across_core]
    others += [place.z_ahead(step) for step in range(1, place.depth)]

    def hello(device):
        pl.semaphore_signal(barrier, inc=1, device_id=device, device_id_type=MESH)

    for other in others:
        hello(other)
    for distance in rows.near():
        rows.when(distance, hello)
    pl.semaphore_wait(barrier, len(others) + rows.present())


def pass_rows(rows, source, target, distance, sems):
    send, recv = sems

    def copy(device):
        return remote(source, target, send, recv, device)

    def start():
        rows.when(distance, lambda device: copy(device).start())

    def arrive():
        rows.when(-distance, lambda device: copy(device).wait_recv())

    def end():
        rows.when(distance, lambda device: copy(device).wait_send())

    return start, arrive, end


GATHER_LAYOUT = (
    (4, 0, 1, 0, 128, 0),
    (0, 0, 3, 0, 768, 16),
    (0, 3, 4, 0, 768, 16),
    (1, 0, 2, 0, 768, 16),
    (1, 2, 4, 0, 768, 16),
    (3, 0, 1, 0, 768, 48),
    (2, 0, 2, 0, 512, 16),
    (2, 0, 2, 512, 1024, 16),
    (2, 0, 2, 1024, 1536, 16),
    (2, 0, 2, 1536, 2048, 16),
)
WIDTH, HIDDEN, TOKENS, PATCHES = 768, 2048, 384, 256

class Spec:
    def __init__(self, *shape, dtype=LOW):
        self.shape = shape
        self.dtype = dtype

    def array(self):
        return jax.ShapeDtypeStruct(self.shape, self.dtype)

    def scratch(self):
        return pltpu.VMEM(self.shape, self.dtype)


def specs(table):
    return [spec for spec in vars(table).values() if isinstance(spec, Spec)]


class K:
    gain = Spec(8, WIDTH, dtype=jnp.float32)
    h1t = Spec(WIDTH, TOKENS)
    q1 = Spec(TOKENS, WIDTH)
    k1 = Spec(TOKENS, WIDTH)
    v1 = Spec(TOKENS, WIDTH)
    o1t = Spec(WIDTH, TOKENS)
    lse1 = Spec(128, TOKENS, dtype=jnp.float32)
    x1 = Spec(TOKENS, WIDTH, dtype=jnp.float32)
    h2t = Spec(WIDTH, TOKENS)
    memt = Spec(WIDTH, PATCHES)
    q2 = Spec(TOKENS, WIDTH)
    k2 = Spec(PATCHES, WIDTH)
    v2 = Spec(PATCHES, WIDTH)
    o2t = Spec(WIDTH, TOKENS)
    lse2 = Spec(128, TOKENS, dtype=jnp.float32)
    h3t = Spec(WIDTH, TOKENS)
    hiddent = Spec(HIDDEN, TOKENS)
    dgate = Spec(TOKENS, HIDDEN)
    dup = Spec(TOKENS, HIDDEN)
    dx2 = Spec(TOKENS, WIDTH, dtype=jnp.float32)
    gain3 = Spec(1, WIDTH, dtype=jnp.float32)


class W:
    w_self = Spec(4, WIDTH, WIDTH)
    w_cross = Spec(4, WIDTH, WIDTH)
    w_in = Spec(2, WIDTH, HIDDEN)
    w_out = Spec(1, HIDDEN, WIDTH)
    w_gain = Spec(1, 256, 128)


class F:
    bias = Spec(TOKENS, TOKENS, dtype=jnp.float32)
    h = Spec(TOKENS, WIDTH)
    mix = Spec(TOKENS, WIDTH)
    lse = Spec(TOKENS, 128, dtype=jnp.float32)
    mem_one = Spec(PATCHES, WIDTH)
    mem = Spec(PATCHES, WIDTH)
    mem_got = Spec(2, PATCHES, WIDTH)
    x2 = Spec(TOKENS, WIDTH, dtype=jnp.float32)
    gate = Spec(TOKENS, 512, dtype=jnp.float32)
    up = Spec(TOKENS, 512, dtype=jnp.float32)
    dhid = Spec(TOKENS, 512, dtype=jnp.float32)
    hidden = Spec(TOKENS, HIDDEN)
    gain_own = Spec(1, 16, 128)
    dh = Spec(TOKENS, WIDTH, dtype=jnp.float32)


PASSED = specs(K) + [W.w_self, W.w_cross]


def as_column(row):
    return jnp.broadcast_to(row.astype(jnp.float32), (128, row.shape[1])).T


def row_offset(images, row, count):
    image = images[jnp.minimum(row, count - 1)]
    start = sum((images[other] < image).astype(jnp.int32) for other in range(count))
    return jnp.where(row < count, row - start, 0)


def forward_kernel(depth, row_count, refs):
    (x0, dy, memory, segments, padding, images, gains) = refs[:7]
    owns = refs[7:11]
    out = refs[11]
    rest = refs[12:]
    kept_out, rest = dict(zip(PASSED, rest)), rest[len(PASSED) :]
    kept, rest = dict(zip(specs(K), rest)), rest[len(specs(K)) :]
    weights, rest = dict(zip(specs(W), rest)), rest[len(specs(W)) :]
    local, rest = dict(zip(specs(F), rest)), rest[len(specs(F)) :]
    gather_sem, row_sem, keep_sem = rest[:6], rest[6], rest[7]
    owns = (*owns, local[F.gain_own])
    kept_numbers = {name: number for number, name in enumerate(kept_out)}

    def keep_copy(name):
        source = weights[name] if name in weights else kept[name]
        return pltpu.make_async_copy(source, kept_out[name], keep_sem.at[kept_numbers[name]])

    def keep(*names):
        for name in names:
            keep_copy(name).start()

    place = Place(depth)
    rows = Rows(place, row_count)
    fulls = [weights[spec] for spec in specs(W)]
    blocks = []
    for number, (array, first, last, c0, c1, side) in enumerate(GATHER_LAYOUT):
        own, full = owns[array], fulls[array]
        blocks.append(
            Gather(
                place,
                own.at[first:last, :, c0:c1],
                full.at[first:last, :, c0:c1],
                own.shape[1],
                side,
                False,
                [sem.at[number] for sem in gather_sem],
            )
        )
    near_start, near_arrive, near_end = pass_rows(
        rows, memory, local[F.mem_got].at[0], 1, (row_sem.at[0], row_sem.at[1])
    )
    far_start, far_arrive, far_end = pass_rows(
        rows, local[F.mem_one], local[F.mem_got].at[1], 2, (row_sem.at[2], row_sem.at[3])
    )
    gain = kept[K.gain]
    offset = row_offset(images, rows.row, row_count)
    local[F.gain_own][...] = jnp.zeros_like(local[F.gain_own])
    local[F.gain_own][0, 0 : gains.shape[0], 0 : gains.shape[1]] = gains[...]

    def make_bias():
        seg_q, seg_k = as_column(segments[...])[:, 0:1], segments[...].astype(jnp.float32)
        query = lax.broadcasted_iota(jnp.int32, (TOKENS, TOKENS), 0)
        key = lax.broadcasted_iota(jnp.int32, (TOKENS, TOKENS), 1)
        allowed = (seg_q == seg_k) & (key <= query) & ((padding[...] == 1) | (key == query))
        local[F.bias][...] = jnp.where(allowed, 0.0, -1e30)

    def make_gain():
        total = jnp.zeros((16, WIDTH), jnp.float32)
        count = row_count // 2
        share = WIDTH // count
        for number in range(count):
            row = lax.broadcasted_iota(jnp.int32, (128, WIDTH), 0)
            column = lax.broadcasted_iota(jnp.int32, (128, WIDTH), 1)
            pick = ((column - number * share) == row) & (row < share)
            total += dot(weights[W.w_gain][0, number * 16 : number * 16 + 16, :], pick.astype(LOW))
        gain[...] = total[:8]

    def first_norm():
        norm_rows(x0, gain[0:1], local[F.h])
        kept[K.h1t][...] = local[F.h][...].T
        keep(K.gain, K.h1t)

    def project(name, w, index):
        def run():
            kept[name][...] = dot(local[F.h][...], weights[w][index]).astype(LOW)
            keep(name)

        return run

    def self_pair(pair):
        return lambda: attend_pair(pair, kept[K.q1], kept[K.k1], kept[K.v1], local[F.bias], local[F.mix], local[F.lse])

    def clear_lse():
        local[F.lse][...] = jnp.zeros_like(local[F.lse])

    def self_out():
        kept[K.lse1][...] = local[F.lse][...].T
        kept[K.o1t][...] = local[F.mix][...].T
        kept[K.x1][...] = x0[...].astype(jnp.float32) + dot(local[F.mix][...], weights[W.w_self][3])
        keep(K.lse1, K.o1t, K.x1)

    def second_norm():
        norm_rows(kept[K.x1], gain[1:2], local[F.h])
        kept[K.h2t][...] = local[F.h][...].T
        keep(K.h2t)

    def memory_near():
        near_arrive()
        local[F.mem_one][...] = jnp.where(offset >= 1, local[F.mem_got][0], memory[...])
        far_start()

    def memory_far():
        far_arrive()
        local[F.mem][...] = jnp.where(offset >= 2, local[F.mem_got][1], local[F.mem_one][...])
        kept[K.memt][...] = local[F.mem][...].T
        keep(K.memt)

    def project_memory(name, index):
        def run():
            kept[name][...] = dot(local[F.mem][...], weights[W.w_cross][index]).astype(LOW)
            keep(name)

        return run

    def cross_pair(pair):
        return lambda: attend_pair(pair, kept[K.q2], kept[K.k2], kept[K.v2], None, local[F.mix], local[F.lse])

    def cross_out():
        kept[K.lse2][...] = local[F.lse][...].T
        kept[K.o2t][...] = local[F.mix][...].T
        local[F.x2][...] = kept[K.x1][...] + dot(local[F.mix][...], weights[W.w_cross][3])
        keep(K.lse2, K.o2t)

    def third_norm():
        norm_rows(local[F.x2], gain[2:3], local[F.h])
        kept[K.h3t][...] = local[F.h][...].T
        keep(K.h3t)

    def mlp_dots(number):
        def run():
            c0 = number * 512
            h = local[F.h][...]
            local[F.dhid][...] = dot(dy[...], weights[W.w_out][0, c0 : c0 + 512, :], 1, 1)
            local[F.gate][...] = dot(h, weights[W.w_in][0, :, c0 : c0 + 512])
            local[F.up][...] = dot(h, weights[W.w_in][1, :, c0 : c0 + 512])

        return run

    def mlp_point(number):
        def run():
            c0 = number * 512

            @pl.loop(0, TOKENS // 16)
            def _(i):
                span = pl.ds(pl.multiple_of(i * 16, 16), 16)
                act, slope = gelu_parts(local[F.gate][span])
                up, dhid = local[F.up][span], local[F.dhid][span]
                local[F.hidden][span, c0 : c0 + 512] = (act * up).astype(LOW)
                kept[K.dgate][span, c0 : c0 + 512] = (dhid * up * slope).astype(LOW)
                kept[K.dup][span, c0 : c0 + 512] = (dhid * act).astype(LOW)

            kept[K.hiddent][c0 : c0 + 512, :] = local[F.hidden][:, c0 : c0 + 512].T

        return run

    def mlp_keep():
        keep(K.hiddent, K.dgate, K.dup)

    def mlp_back_first():
        local[F.dh][...] = dot(kept[K.dgate][...], weights[W.w_in][0], 1, 1)

    def mlp_back_second():
        local[F.dh][...] += dot(kept[K.dup][...], weights[W.w_in][1], 1, 1)

    def mlp_norm():
        norm_back_rows(local[F.x2], gain[2:3], local[F.dh], dy, kept[K.dx2], kept[K.gain3])
        keep(K.dx2, K.gain3)

    def mlp_out():
        out[...] = (local[F.x2][...] + dot(local[F.hidden][...], weights[W.w_out][0])).astype(LOW)

    work = [
        (None, make_bias),
        (None, clear_lse),
        (0, make_gain),
        (0, first_norm),
        (1, project(K.q1, W.w_self, 0)),
        (1, project(K.k1, W.w_self, 1)),
        (1, project(K.v1, W.w_self, 2)),
    ]
    work += [(1, self_pair(pair)) for pair in range(6)]
    work += [
        (2, lambda: keep(W.w_self)),
        (2, self_out),
        (2, second_norm),
        (2, memory_near),
        (3, project(K.q2, W.w_cross, 0)),
        (3, memory_far),
        (3, project_memory(K.k2, 1)),
        (4, project_memory(K.v2, 2)),
        (4, lambda: keep(W.w_cross)),
    ]
    work += [(4, cross_pair(pair)) for pair in range(6)]
    work += [(4, cross_out), (4, third_norm)]
    for number in range(4):
        work += [(6 + number, mlp_dots(number)), (6 + number, mlp_point(number))]
    work += [
        (9, mlp_keep),
        (9, mlp_back_first),
        (9, mlp_back_second),
        (9, mlp_norm),
        (9, mlp_out),
    ]

    count = len(blocks)
    events = []
    for turn in range(count + 3):
        if turn + 2 < count:
            events.append((blocks[turn + 2].begin, None))
        if turn < count:
            for n in blocks[turn].order()[:3]:
                events.append((functools.partial(blocks[turn].take, n), None))
        if 0 <= turn - 1 < count:
            for n in blocks[turn - 1].order()[3:]:
                events.append((functools.partial(blocks[turn - 1].take, n), None))
        if 0 <= turn - 2 < count and blocks[turn - 2].side:
            for n in blocks[turn - 2].order():
                events.append((functools.partial(blocks[turn - 2].take_x, n), None))
        if 0 <= turn - 3 < count:
            events.append((blocks[turn - 3].complete, turn - 3))

    greet_all(place, rows)
    blocks[0].begin()
    blocks[1].begin()
    near_start()
    ready = -1
    done = 0

    def can():
        return done < len(work) and (work[done][0] is None or work[done][0] <= ready)

    for act, completes in events:
        act()
        if completes is not None:
            ready = completes
        if can():
            work[done][1]()
            done += 1
    while can():
        work[done][1]()
        done += 1
    for block in blocks:
        block.end()
    near_end()
    far_end()
    for name in kept_out:
        keep_copy(name).wait()


def forward(
    layer_input,
    cotangent,
    memory,
    segments,
    padding,
    image_of_row,
    gains,
    self_weights,
    cross_weights,
    mlp_in,
    mlp_out,
):
    wide = lax.axis_size("wide")
    depth = wide // 4
    owns = (self_weights, cross_weights, mlp_in, mlp_out[None])
    vmem, anywhere, smem = (pl.BlockSpec(memory_space=space) for space in (pltpu.VMEM, pl.ANY, pltpu.SMEM))
    kept = [spec.array() for spec in PASSED]
    outs = pl.pallas_call(
        lambda *refs: forward_kernel(depth, 2 * wide, refs),
        out_shape=[jax.ShapeDtypeStruct(layer_input.shape, LOW)] + kept,
        in_specs=[vmem] * 5 + [smem, vmem] + [anywhere] * 4,
        out_specs=[vmem] + [anywhere] * len(kept),
        scratch_shapes=[spec.scratch() for table in (K, W, F) for spec in specs(table)]
        + gather_sems(len(GATHER_LAYOUT), depth)
        + [pltpu.SemaphoreType.DMA((4,)), pltpu.SemaphoreType.DMA((len(kept),))],
        compiler_params=pltpu.CompilerParams(
            collective_id=0, has_side_effects=True, vmem_limit_bytes=60 * 2**20
        ),
        name="forward",
    )(layer_input, cotangent, memory, segments, padding, image_of_row, gains, *owns)
    return outs[0], dict(zip(PASSED, outs[1:]))


class Scatter:
    def __init__(self, place, bufs, outs, block, sems):
        self.p = place
        rows, side = block.rows, block.side
        self.width = block.width
        self.relay = block.relay
        self.staged, self.held, self.from_x, self.from_y, self.from_z, self.relayed, self.done, self.other = bufs
        self.outs = outs
        self.rows = rows
        self.side = side
        self.main = rows - side
        self.send, self.recv = sems

    def span(self, start, size):
        return pl.ds(pl.multiple_of(start, 16), size)

    @property
    def main_span(self):
        return self.span(self.side * self.p.x, self.main)

    def side_span(self, x):
        return self.span(self.main * x, self.side)

    def c_copy(self):
        return remote(self.staged, self.held, self.send.at[0], self.recv.at[0], self.p.across_core)

    def x_copy(self):
        p = self.p
        return remote(
            self.held.at[:, :, :, self.side_span(1 - p.x)],
            self.from_x,
            self.send.at[1],
            self.recv.at[1],
            p.across_x,
        )

    def y_copy(self):
        p = self.p
        return remote(
            self.held.at[:, :, 1 - p.y, self.main_span], self.from_y, self.send.at[2], self.recv.at[2], p.across_y
        )

    def z_piece(self, z):
        return self.held.at[:, z, self.p.y, self.main_span]

    def z_copy(self, step):
        p = self.p
        return remote(
            self.z_piece((p.z + step) % p.depth),
            self.from_z.at[step - 1],
            self.send.at[2 + step],
            self.recv.at[2 + step],
            p.z_ahead(step),
        )

    def relay_copy(self, up):
        p = self.p
        target, between = (3, 1) if up else (0, 2)
        device = (p.shard(between, p.y, p.core), p.x)
        return remote(self.z_piece(target), self.relayed, self.send.at[6], self.recv.at[6], device)

    def last_copy(self):
        return remote(self.done, self.other, self.send.at[7], self.recv.at[7], self.p.across_x)

    def blank(self):
        p = self.p
        if not self.relay:
            return

        @pl.when(p.z == 0)
        def _():
            self.from_z[0] = jnp.zeros_like(self.from_z[0])

        @pl.when(p.z == 3)
        def _():
            self.from_z[2] = jnp.zeros_like(self.from_z[2])

    def each_z(self, act_direct, act_late, act_relay):
        p = self.p
        if not self.relay:
            if act_direct is not None:
                for step in range(1, p.depth):
                    act_direct(self.z_copy(step))
            return
        if act_direct is not None:

            @pl.when(p.z != 0)
            def _():
                act_direct(self.z_copy(3))

            @pl.when(p.z != 3)
            def _():
                act_direct(self.z_copy(1))

            @pl.when((p.z == 0) | (p.z == 3))
            def _():
                act_direct(self.z_copy(2))

        if act_late is not None:

            @pl.when(p.z == 1)
            def _():
                act_late(self.z_copy(2), 3)

            @pl.when(p.z == 2)
            def _():
                act_late(self.z_copy(2), 0)

        if act_relay is not None:

            @pl.when(p.z == 0)
            def _():
                act_relay(self.relay_copy(True))

            @pl.when(p.z == 3)
            def _():
                act_relay(self.relay_copy(False))

    def start_c(self):
        self.c_copy().start()

    def take_x(self):
        self.x_copy().wait_recv()
        span = self.side_span(self.p.x)
        self.held[:, :, :, span] = self.held[:, :, :, span] + self.from_x[...]

    def take_y(self):
        p = self.p
        self.y_copy().wait_recv()
        span = self.main_span
        self.held[:, :, p.y, span] = self.held[:, :, p.y, span] + self.from_y[...]

    def start_z(self):
        self.each_z(lambda copy: copy.start(), None, lambda copy: copy.start())

    def take_relay(self):
        def late(copy, target):
            self.relay_copy(True).wait_recv()
            p = self.p
            span = self.main_span
            self.held[:, target, p.y, span] = self.held[:, target, p.y, span] + self.relayed[...]
            copy.start()

        self.each_z(None, late, None)

    def take_z(self):
        p = self.p
        self.z_copy(2).wait_recv()
        if self.relay:

            @pl.when(p.z != 0)
            def _():
                self.z_copy(1).wait_recv()

            @pl.when(p.z != 3)
            def _():
                self.z_copy(3).wait_recv()

        else:
            self.z_copy(1).wait_recv()
            self.z_copy(3).wait_recv()

        total = self.held[:, p.z, p.y, self.main_span].astype(jnp.float32)
        for step in range(1, p.depth):
            total += self.from_z[step - 1].astype(jnp.float32)
        self.done[...] = total.astype(LOW)

    def take_last(self):
        p = self.p
        self.last_copy().wait_recv()
        side, both = self.side, self.main - self.side
        for number, (out, mat, column) in enumerate(self.outs):
            columns = slice(column, column + self.width)
            if side:
                out[mat, self.side_span(p.x), columns] = self.done[number, self.span(both * p.x, side)].astype(
                    jnp.float32
                )
                out[mat, self.side_span(1 - p.x), columns] = self.other[
                    number, self.span(both * (1 - p.x), side)
                ].astype(jnp.float32)
            out[mat, side : side + both, columns] = self.done[number, self.span(side * (1 - p.x), both)].astype(
                jnp.float32
            ) + self.other[number, self.span(side * p.x, both)].astype(jnp.float32)

    def end(self):
        def wait(copy, target=None):
            copy.wait_send()

        if self.side:
            self.x_copy().wait_send()
        self.y_copy().wait_send()
        self.each_z(wait, wait, wait)
        self.last_copy().wait_send()


class Block:
    def __init__(self, out, pieces, rows, side, width=256, relay=True):
        self.out, self.pieces, self.rows, self.side = out, tuple(pieces), rows, side
        self.width, self.relay = width, relay

    @property
    def ring(self):
        return self.rows, self.width


def block_list():
    found = [Block(3, [(0, c)], 128, 32) for c in (0, 256, 512)]
    found += [Block(2, [(m, first + c) for c in range(0, 1024, 256)], 48, 16) for m in (0, 1) for first in (0, 1024)]
    found += [Block(1, [(3, c) for c in range(0, 768, 256)], 48, 0)]
    found += [Block(1, [(m, c) for m in range(3)], 48, 16) for c in (0, 256, 512)]
    found += [Block(0, [(3, c) for c in range(0, 768, 256)], 48, 0)]
    found += [Block(0, [(m, c) for m in range(3)], 48, 16, 128, False) for c in range(0, 768, 128)]
    return found


SCATTER_LAYOUT = block_list()
RINGS = {(128, 256): (2, 1), (48, 256): (3, 4), (48, 128): (2, 3)}


def scatter_buffers(depth):
    bufs = []
    for block in SCATTER_LAYOUT:
        subs, rows, side, width = len(block.pieces), block.rows, block.side, block.width
        main = rows - side
        bufs += [
            pltpu.VMEM((subs, depth, 2, rows, width), LOW),
            pltpu.VMEM((subs, depth, 2, side, width) if side else (16, 128), LOW),
            pltpu.VMEM((subs, depth, main, width), LOW),
            pltpu.VMEM((depth - 1, subs, main, width), LOW),
            pltpu.VMEM((subs, main, width), LOW),
            pltpu.VMEM((subs, main, width), LOW),
            pltpu.VMEM((subs, main, width), LOW),
        ]
    return bufs


def staging_buffers(depth):
    return [
        pltpu.VMEM((slots, subs, depth, 2, rows, width), LOW) for (rows, width), (slots, subs) in RINGS.items()
    ]


class K0:
    x0 = Spec(TOKENS, WIDTH)


class B:
    biast = Spec(TOKENS, TOKENS, dtype=jnp.float32)
    dlow = Spec(TOKENS, WIDTH)
    do = Spec(TOKENS, WIDTH)
    dq = Spec(TOKENS, WIDTH)
    dk = Spec(TOKENS, WIDTH)
    dv = Spec(TOKENS, WIDTH)
    dh = Spec(TOKENS, WIDTH, dtype=jnp.float32)
    mem_sum = Spec(PATCHES, WIDTH, dtype=jnp.float32)
    mem_low = Spec(2, PATCHES, WIDTH)
    mem_got = Spec(2, PATCHES, WIDTH)
    gains = Spec(8, WIDTH, dtype=jnp.float32)
    gain_got = Spec(6, 8, WIDTH, dtype=jnp.float32)
    gain_row = Spec(1, WIDTH, dtype=jnp.float32)


def attend_back_pair(pair, q, k, v, do, lse, bias, dq, dk, dv):
    span = pair_span(pair)
    q_two, k_two, v_two, do_two = q[:, span], k[:, span], v[:, span], do[:, span]
    low_q = lax.broadcasted_iota(jnp.int32, q_two.shape, 1) < HEAD_DIM
    low_k = lax.broadcasted_iota(jnp.int32, k_two.shape, 1) < HEAD_DIM
    scale = HEAD_DIM ** (-0.5)
    grads = []
    for half in range(2):
        mine = low_q if half == 0 else ~low_q
        scores = dot(k_two, jnp.where(mine, q_two, jnp.zeros_like(q_two)), 1, 1) * scale
        if bias is not None:
            scores = scores + bias[...]
        head = 2 * pair + half
        shares = jnp.exp(scores - lse[head : head + 1, :])
        p_grad = dot(v_two, jnp.where(mine, do_two, jnp.zeros_like(do_two)), 1, 1)
        along = jnp.sum(shares * p_grad, axis=0, keepdims=True)
        s_low = (shares * (p_grad - along)).astype(LOW)
        v_grad = dot(shares.astype(LOW), do_two)
        k_grad = dot(s_low, q_two) * scale
        q_grad = dot(s_low, k_two, 0, 0) * scale
        grads.append((q_grad, k_grad, v_grad))
    dq[:, span] = jnp.where(low_q, grads[0][0], grads[1][0]).astype(LOW)
    count = k_two.shape[0]
    dk[:count, span] = jnp.where(low_k, grads[0][1], grads[1][1]).astype(LOW)
    dv[:count, span] = jnp.where(low_k, grads[0][2], grads[1][2]).astype(LOW)


class Total:
    def __init__(self, place, value, got, send, recv):
        self.p, self.value, self.got, self.send, self.recv = place, value, got, send, recv

    def copy(self, slot):
        p = self.p
        device = (p.across_core, p.across_x, p.across_y, *(p.z_ahead(step) for step in (1, 2, 3)))[slot]
        return remote(self.value, self.got.at[slot], self.send.at[slot], self.recv.at[slot], device)

    def start(self, slots):
        for slot in slots:
            self.copy(slot).start()

    def take(self, slots):
        for slot in slots:
            self.copy(slot).wait()
        total = self.value[...]
        for slot in slots:
            total = total + self.got[slot]
        self.value[...] = total


def backward_kernel(depth, row_count, refs):
    (dy, segments, padding, images) = refs[:4]
    names = PASSED + [K0.x0]
    given = dict(zip(names, refs[4:]))
    rest = refs[4 + len(names) :]
    outs, (x_grad, mem_grad, gain_grad) = rest[:4], rest[4:7]
    rest = rest[7:]
    kept = dict(zip(names, rest))
    rest = rest[len(names) :]
    local, rest = dict(zip(specs(B), rest)), rest[len(specs(B)) :]
    staging, rest = dict(zip(RINGS, rest)), rest[len(RINGS) :]
    count = len(SCATTER_LAYOUT)
    bufs, (load_sem, send_sem, recv_sem, row_sem, total_send, total_recv) = rest[: 7 * count], rest[7 * count :]
    place = Place(depth)
    rows = Rows(place, row_count)
    core = place.core
    plan = Plan(6, 1.5)

    def load(*chosen):
        for name in chosen:
            number = names.index(name)
            pltpu.make_async_copy(given[name], kept[name], load_sem.at[number]).start()

    def loaded(*chosen):
        for name in chosen:
            number = names.index(name)
            pltpu.make_async_copy(given[name], kept[name], load_sem.at[number]).wait()

    blocks, rings = [], {key: [] for key in RINGS}
    for number, spec in enumerate(SCATTER_LAYOUT):
        ring, slots = rings[spec.ring], RINGS[spec.ring][0]
        staged = staging[spec.ring].at[len(ring) % slots, 0 : len(spec.pieces)]
        block = Scatter(
            place,
            (staged,) + tuple(bufs[7 * number : 7 * number + 7]),
            [(outs[spec.out], mat, column) for mat, column in spec.pieces],
            spec,
            [send_sem.at[number], recv_sem.at[number]],
        )
        block.before = ring[-slots] if len(ring) >= slots else None
        ring.append(block)
        blocks.append(block)

    near_start, near_arrive, near_end = pass_rows(
        rows, local[B.mem_low].at[1], local[B.mem_got].at[1], -1, (row_sem.at[0], row_sem.at[1])
    )
    far_start, far_arrive, far_end = pass_rows(
        rows, local[B.mem_low].at[0], local[B.mem_got].at[0], -2, (row_sem.at[2], row_sem.at[3])
    )
    total = Total(place, local[B.gains], local[B.gain_got], total_send, total_recv)

    def half(left, which):
        part = kept[left][:, :, which]
        return part.reshape(-1, part.shape[-1])

    def products(block, terms, which):
        found = []
        for left, right, first, width in terms:
            value = dot(half(left, which), right[: kept[left].shape[-1], first : first + width])
            value = value.reshape(depth, 2, -1, width)
            found += [value[..., c : c + block.width] for c in range(0, width, block.width)]
        return found

    def size(block, what):
        each = {
            "c": 8 * block.rows,
            "x": 8 * block.side,
            "y": 4 * block.main,
            "z": (2.5 if block.relay else 4) * block.main,
            "r": block.main,
            "l": block.main,
        }
        return len(block.outs) * block.width * 2 * each[what]

    def give(number, terms):
        block = blocks[number]

        def run():
            if block.before is not None:
                block.before.c_copy().wait_send()
                block.before.sent = True
            for sub, value in enumerate(products(block, terms, 1 - core)):
                block.staged[sub] = value.astype(LOW)
            block.start_c()

        return run

    def hold(number, terms):
        block = blocks[number]

        def run():
            block.c_copy().wait_recv()
            for sub, value in enumerate(products(block, terms, core)):
                block.held[sub] = (value + block.held[sub].astype(jnp.float32)).astype(LOW)

            def to_y():
                if block.side:
                    block.take_x()
                plan.send("y", number, size(block, "y"), lambda: block.y_copy().start(), to_z)

            def to_z():
                block.take_y()
                plan.send("z", number, size(block, "z"), block.start_z, to_relay)

            def to_relay():
                if not block.relay:
                    to_last()
                    return
                block.take_relay()
                plan.later(size(block, "r") / plan.rate["z"] + plan.latency, to_last)

            def to_last():
                block.take_z()
                plan.send("x", number, size(block, "l"), lambda: block.last_copy().start(), block.take_last)

            if block.side:
                plan.send("x", number, size(block, "x"), lambda: block.x_copy().start(), to_y)
            else:
                to_y()

        return run

    def make_bias():
        seg_k, seg_q = as_column(segments[...])[:, 0:1], segments[...].astype(jnp.float32)
        real = as_column(padding[...])[:, 0:1] == 1.0
        key = lax.broadcasted_iota(jnp.int32, (TOKENS, TOKENS), 0)
        query = lax.broadcasted_iota(jnp.int32, (TOKENS, TOKENS), 1)
        allowed = (seg_q == seg_k) & (key <= query) & (real | (key == query))
        local[B.biast][...] = jnp.where(allowed, 0.0, -1e30)

    def cross_begin():
        local[B.dlow][...] = kept[K.dx2][...].astype(LOW)

    def cross_do():
        local[B.do][...] = dot(local[B.dlow][...], kept[W.w_cross][3], 1, 1).astype(LOW)

    def cross_pair(pair):
        def run():
            attend_back_pair(
                pair,
                kept[K.q2],
                kept[K.k2],
                kept[K.v2],
                local[B.do],
                kept[K.lse2],
                None,
                local[B.dq],
                local[B.dk],
                local[B.dv],
            )

        return run

    def self_pair(pair):
        def run():
            attend_back_pair(
                pair,
                kept[K.q1],
                kept[K.k1],
                kept[K.v1],
                local[B.do],
                kept[K.lse1],
                local[B.biast],
                local[B.dq],
                local[B.dk],
                local[B.dv],
            )

        return run

    def mem_back():
        value = dot(local[B.dk][:PATCHES], kept[W.w_cross][1], 1, 1)
        value += dot(local[B.dv][:PATCHES], kept[W.w_cross][2], 1, 1)
        local[B.mem_sum][...] = value
        local[B.mem_low][0] = value.astype(LOW)
        far_start()

    def mem_far():
        far_arrive()
        got = jnp.where(row_offset(images, rows.row + 2, row_count) >= 2, local[B.mem_got][0].astype(jnp.float32), 0.0)
        value = local[B.mem_sum][...] + got
        local[B.mem_sum][...] = value
        local[B.mem_low][1] = value.astype(LOW)
        near_start()

    def mem_near():
        near_arrive()
        got = jnp.where(row_offset(images, rows.row + 1, row_count) == 1, local[B.mem_got][1].astype(jnp.float32), 0.0)
        mem_grad[...] = jnp.where(row_offset(images, rows.row, row_count) == 0, local[B.mem_sum][...] + got, 0.0)

    def cross_dh():
        local[B.dh][...] = dot(local[B.dq][...], kept[W.w_cross][0], 1, 1)

    def cross_norm():
        norm_back_rows(kept[K.x1], kept[K.gain][1:2], local[B.dh], kept[K.dx2], kept[K.dx2], local[B.gain_row])
        local[B.gains][1:2, :] = local[B.gain_row][...]
        local[B.dlow][...] = kept[K.dx2][...].astype(LOW)

    def self_do():
        local[B.do][...] = dot(local[B.dlow][...], kept[W.w_self][3], 1, 1).astype(LOW)

    def self_dh_first():
        local[B.dh][...] = dot(local[B.dq][...], kept[W.w_self][0], 1, 1)

    def self_dh_second():
        local[B.dh][...] += dot(local[B.dk][...], kept[W.w_self][1], 1, 1)

    def self_dh_third():
        local[B.dh][...] += dot(local[B.dv][...], kept[W.w_self][2], 1, 1)

    def self_norm():
        norm_back_rows(kept[K0.x0], kept[K.gain][0:1], local[B.dh], kept[K.dx2], x_grad, local[B.gain_row])
        local[B.gains][0:1, :] = local[B.gain_row][...]
        local[B.gains][2:3, :] = kept[K.gain3][...]
        total.start((0,))

    def load_cross():
        load(K.dx2, W.w_cross, K.o2t, K.q2, K.k2, K.v2, K.lse2, K.h2t, K.memt, K.x1, K.gain, K.gain3)

    def load_self():
        load(W.w_self, K.o1t, K.q1, K.k1, K.v1, K.lse1, K.h1t, K0.x0)

    do_low, dq, dk, dv = local[B.dlow], local[B.dq], local[B.dk], local[B.dv]
    out_terms = [[(K.hiddent, dy, 256 * j, 256)] for j in range(3)]
    in_terms = [[(K.h3t, kept[name], first, 1024)] for name in (K.dgate, K.dup) for first in (0, 1024)]

    load(K.hiddent, K.h3t, K.dgate, K.dup)
    local[B.gains][...] = jnp.zeros_like(local[B.gains])
    for block in blocks:
        block.sent = False
        block.blank()
    greet_all(place, rows)
    load_cross()
    loaded(K.hiddent)
    plan.work(0.8, give(0, out_terms[0]))
    plan.work(0.8, give(1, out_terms[1]))
    plan.work(0.9, hold(0, out_terms[0]))
    plan.work(0.8, give(2, out_terms[2]))
    plan.work(0.9, hold(1, out_terms[1]))
    loaded(K.h3t, K.dgate, K.dup)
    load_self()
    plan.work(1.0, give(3, in_terms[0]))
    plan.work(0.9, hold(2, out_terms[2]))
    for j in range(1, 4):
        plan.work(1.0, give(3 + j, in_terms[j]))
        plan.work(1.1, hold(2 + j, in_terms[j - 1]))
    loaded(K.dx2, W.w_cross, K.o2t, K.q2, K.k2, K.v2, K.lse2, K.h2t, K.memt, K.x1, K.gain, K.gain3)
    plan.work(0.3, cross_begin)
    o_terms = [(K.o2t, do_low, 0, 768)]
    plan.work(0.8, give(7, o_terms))
    plan.work(1.1, hold(6, in_terms[3]))
    plan.work(0.8, cross_do)
    plan.work(0.9, hold(7, o_terms))

    def attention(pair_work, first, lefts, pairs):
        previous = None
        width = 128 * pairs
        for group in range(6 // pairs):
            for pair in range(pairs * group, pairs * group + pairs):
                plan.work(1.4, pair_work(pair))
            terms = [(left, right, width * group, width) for left, right in zip(lefts, (dq, dk, dv))]
            plan.work(0.5 * pairs, give(first + group, terms))
            if previous is not None:
                plan.work(0.5 * pairs, hold(*previous))
            previous = (first + group, terms)
        return previous

    previous = attention(cross_pair, 8, (K.h2t, K.memt, K.memt), 2)
    plan.work(1.5, mem_back)
    plan.work(1.0, hold(*previous))
    plan.work(0.8, cross_dh)
    plan.work(1.2, cross_norm)
    loaded(W.w_self, K.o1t, K.q1, K.k1, K.v1, K.lse1, K.h1t, K0.x0)
    o_terms = [(K.o1t, do_low, 0, 768)]
    plan.work(0.8, give(11, o_terms))
    plan.work(0.3, mem_far)
    plan.work(0.8, self_do)
    plan.work(0.5, make_bias)
    plan.work(0.9, hold(11, o_terms))
    previous = attention(self_pair, 12, (K.h1t, K.h1t, K.h1t), 1)
    plan.work(0.8, self_dh_first)
    plan.work(1.0, hold(*previous))
    plan.work(0.8, self_dh_second)
    plan.work(0.8, self_dh_third)
    plan.work(0.5, mem_near)
    plan.work(1.5, self_norm)

    def total_step(slots, after):
        def run():
            total.take(slots)
            if after:
                total.start(after[0])
                plan.later(2.5, total_step(after[0], after[1:]))
            else:
                share = gain_grad.shape[1]
                turned = pltpu.roll(local[B.gains][...], (row_count // 2 - place.wide) * share, 1)
                gain_grad[...] = turned[0 : gain_grad.shape[0], 0:share]

        return run

    plan.later(2.5, total_step((0,), ((1,), (2,), (3, 4, 5))))
    while plan.busy():
        plan.step()
    for block in blocks:
        if not block.sent:
            block.c_copy().wait_send()
        block.end()
    near_end()
    far_end()


def backward(kept, layer_input, cotangent, segments, padding, image_of_row, share):
    wide = lax.axis_size("wide")
    depth = wide // 4

    def owners(array):
        return array.reshape(depth, 2, 2, -1, array.shape[-1])

    names = PASSED + [K0.x0]
    given = {**kept, K0.x0: layer_input}
    for name in (K.h1t, K.o1t, K.h2t, K.o2t, K.memt, K.h3t, K.hiddent):
        given[name] = owners(given[name])
    arrays = [given[name] for name in names]
    vmem, anywhere, smem = (pl.BlockSpec(memory_space=space) for space in (pltpu.VMEM, pl.ANY, pltpu.SMEM))
    outs = [
        ((4, WIDTH // wide, WIDTH), jnp.float32),
        ((4, WIDTH // wide, WIDTH), jnp.float32),
        ((2, WIDTH // wide, HIDDEN), jnp.float32),
        ((1, HIDDEN // wide, WIDTH), jnp.float32),
        ((TOKENS, WIDTH), jnp.float32),
        ((PATCHES, WIDTH), jnp.float32),
        ((3, share), jnp.float32),
    ]
    count = len(SCATTER_LAYOUT)
    return pl.pallas_call(
        lambda *refs: backward_kernel(depth, 2 * wide, refs),
        out_shape=[jax.ShapeDtypeStruct(*o) for o in outs],
        in_specs=[vmem] * 3 + [smem] + [anywhere] * len(arrays),
        out_specs=[vmem] * len(outs),
        scratch_shapes=[pltpu.VMEM(a.shape, a.dtype) for a in arrays]
        + [spec.scratch() for spec in specs(B)]
        + staging_buffers(depth)
        + scatter_buffers(depth)
        + [
            pltpu.SemaphoreType.DMA((len(arrays),)),
            pltpu.SemaphoreType.DMA((count, 8)),
            pltpu.SemaphoreType.DMA((count, 8)),
            pltpu.SemaphoreType.DMA((4,)),
            pltpu.SemaphoreType.DMA((6,)),
            pltpu.SemaphoreType.DMA((6,)),
        ],
        compiler_params=pltpu.CompilerParams(
            collective_id=1, has_side_effects=True, vmem_limit_bytes=63 * 2**20
        ),
        name="backward",
    )(cotangent, segments, padding, image_of_row, *arrays)


def finish(*arrays):
    count = len(arrays)

    def kernel(*refs):
        sems = refs[-1]
        loads = [pltpu.make_async_copy(refs[n], refs[2 * count + n], sems.at[0, n]) for n in range(count)]
        stores = [pltpu.make_async_copy(refs[2 * count + n], refs[count + n], sems.at[1, n]) for n in range(count)]
        for load in loads:
            load.start()
        for load, store in zip(loads, stores):
            load.wait()
            store.start()
        for store in stores:
            store.wait()

    anywhere = pl.BlockSpec(memory_space=pl.ANY)
    return pl.pallas_call(
        kernel,
        out_shape=[jax.ShapeDtypeStruct(a.shape, a.dtype) for a in arrays],
        in_specs=[anywhere] * count,
        out_specs=[anywhere] * count,
        scratch_shapes=[pltpu.VMEM(a.shape, a.dtype) for a in arrays] + [pltpu.SemaphoreType.DMA((2, count))],
        compiler_params=pltpu.CompilerParams(vmem_limit_bytes=60 * 2**20),
        name="finish",
    )(*arrays)


def plain_gather(self_weights, cross_weights, mlp_in, mlp_out, gains):
    return (
        lax.all_gather(self_weights, "wide", axis=1, tiled=True),
        lax.all_gather(cross_weights, "wide", axis=1, tiled=True),
        lax.all_gather(mlp_in, "wide", axis=1, tiled=True),
        lax.all_gather(mlp_out, "wide", axis=0, tiled=True),
        lax.all_gather(gains, "wide", axis=1, tiled=True),
    )


def plain_scatter(*grads):
    outs = []
    for grad, axis in zip(grads, (1, 1, 1, 0, 1)):
        piece = lax.psum_scatter(grad, ("wide", "narrow"), scatter_dimension=axis, tiled=True)
        outs.append(lax.all_gather(piece.astype(jnp.bfloat16), "narrow", axis=axis, tiled=True).astype(jnp.float32))
    return tuple(outs)


def by_kernel(self_weights):
    return lax.axis_size("wide") == 16 and lax.axis_size("narrow") == 2 and self_weights.shape[1] % 48 == 0


def plain_device(
    layer_input,
    memory,
    cotangent,
    segment_ids,
    padding,
    image_of_row,
    self_weights,
    cross_weights,
    mlp_in,
    mlp_out,
    gains,
):
    self_full, cross_full, in_full, out_full, gain_full = plain_gather(
        self_weights, cross_weights, mlp_in, mlp_out, gains
    )
    gain_float = gain_full.astype(jnp.float32)
    x_zero = layer_input[0].astype(jnp.float32)
    seg_row = segment_ids[0]
    pad_row = padding[0]
    seq_len = x_zero.shape[0]
    position = jnp.arange(seq_len)
    allowed = (
        (seg_row[:, None] == seg_row[None, :])
        & (position[None, :] <= position[:, None])
        & ((pad_row[None, :] == 1) | (position[:, None] == position[None, :]))
    )
    h_one = rms_norm(x_zero, gain_float[0]).astype(jnp.bfloat16)
    q_self = linear(h_one, self_full[0]).astype(jnp.bfloat16)
    k_self = linear(h_one, self_full[1]).astype(jnp.bfloat16)
    v_self = linear(h_one, self_full[2]).astype(jnp.bfloat16)
    self_mix, self_lse = forward_heads(q_self, k_self, v_self, allowed)
    x_one = x_zero + linear(self_mix, self_full[3])
    row_ids = jnp.arange(image_of_row.shape[0])
    starts = jnp.sum(image_of_row[None, :] < image_of_row[:, None], axis=1)
    offsets = row_ids - starts
    my_index = lax.axis_index(("wide", "narrow"))
    my_offset = jnp.sum(jnp.where(row_ids == my_index, offsets, 0))
    own_patches = memory[0]
    memory_use = own_patches
    for distance in (1, 2, 3):
        arrived = shifted(own_patches, ("wide", "narrow"), distance)
        memory_use = jnp.where(my_offset == distance, arrived, memory_use)
    h_two = rms_norm(x_one, gain_float[1]).astype(jnp.bfloat16)
    q_cross = linear(h_two, cross_full[0]).astype(jnp.bfloat16)
    k_cross = linear(memory_use, cross_full[1]).astype(jnp.bfloat16)
    v_cross = linear(memory_use, cross_full[2]).astype(jnp.bfloat16)
    cross_mix, cross_lse = forward_heads(q_cross, k_cross, v_cross, None)
    x_two = x_one + linear(cross_mix, cross_full[3])
    h_three = rms_norm(x_two, gain_float[2]).astype(jnp.bfloat16)
    gate_act = linear(h_three, in_full[0])
    up_act = linear(h_three, in_full[1])
    hidden = gated_product(gate_act, up_act).astype(jnp.bfloat16)
    result = x_two + linear(hidden, out_full)
    out_low = cotangent[0]
    out_grad_w = contract_rows(hidden, out_low)
    hidden_grad = times_transposed(out_low, out_full)
    _, pullback = jax.vjp(gated_product, gate_act, up_act)
    gate_grad, up_grad = pullback(hidden_grad)
    gate_low = gate_grad.astype(jnp.bfloat16)
    up_low = up_grad.astype(jnp.bfloat16)
    in_grad = jnp.stack([contract_rows(h_three, gate_low), contract_rows(h_three, up_low)])
    h_three_grad = times_transposed(gate_low, in_full[0]) + times_transposed(up_low, in_full[1])
    _, pullback = jax.vjp(rms_norm, x_two, gain_float[2])
    x_two_norm, gain_three = pullback(h_three_grad)
    x_two_grad = out_low.astype(jnp.float32) + x_two_norm
    cross_out_low = x_two_grad.astype(jnp.bfloat16)
    cross_o_grad = contract_rows(cross_mix, cross_out_low)
    cross_mix_grad = times_transposed(cross_out_low, cross_full[3]).astype(jnp.bfloat16)
    q_cross_grad, k_cross_grad, v_cross_grad = backward_heads(
        q_cross, k_cross, v_cross, cross_mix_grad, cross_lse, None
    )
    cross_grad = jnp.stack(
        [
            contract_rows(h_two, q_cross_grad),
            contract_rows(memory_use, k_cross_grad),
            contract_rows(memory_use, v_cross_grad),
            cross_o_grad,
        ]
    )
    mem_grad = times_transposed(k_cross_grad, cross_full[1]) + times_transposed(
        v_cross_grad, cross_full[2]
    )
    h_two_grad = times_transposed(q_cross_grad, cross_full[0])
    _, pullback = jax.vjp(rms_norm, x_one, gain_float[1])
    x_one_norm, gain_two = pullback(h_two_grad)
    x_one_grad = x_two_grad + x_one_norm
    self_out_low = x_one_grad.astype(jnp.bfloat16)
    self_o_grad = contract_rows(self_mix, self_out_low)
    self_mix_grad = times_transposed(self_out_low, self_full[3]).astype(jnp.bfloat16)
    q_self_grad, k_self_grad, v_self_grad = backward_heads(
        q_self, k_self, v_self, self_mix_grad, self_lse, allowed
    )
    self_grad = jnp.stack(
        [
            contract_rows(h_one, q_self_grad),
            contract_rows(h_one, k_self_grad),
            contract_rows(h_one, v_self_grad),
            self_o_grad,
        ]
    )
    h_one_grad = (
        times_transposed(q_self_grad, self_full[0])
        + times_transposed(k_self_grad, self_full[1])
        + times_transposed(v_self_grad, self_full[2])
    )
    _, pullback = jax.vjp(rms_norm, x_zero, gain_float[0])
    x_zero_norm, gain_one = pullback(h_one_grad)
    x_grad = x_one_grad + x_zero_norm
    mem_summed = jnp.where(my_offset == 0, mem_grad, 0.0)
    for distance in (1, 2, 3):
        arrived = shifted(mem_grad.astype(jnp.bfloat16), ("wide", "narrow"), -distance).astype(
            mem_grad.dtype
        )
        neighbour = jnp.sum(jnp.where(row_ids == my_index + distance, offsets, 0))
        mem_summed = mem_summed + jnp.where(neighbour == distance, arrived, 0.0)
    gain_grad = jnp.stack([gain_one, gain_two, gain_three])
    reduced = plain_scatter(self_grad, cross_grad, in_grad, out_grad_w, gain_grad)
    return (
        result.astype(jnp.bfloat16)[None],
        x_grad[None],
        mem_summed[None],
        reduced[0],
        reduced[1],
        reduced[2],
        reduced[3],
        reduced[4],
    )


def kernel_device(
    layer_input,
    memory,
    cotangent,
    segment_ids,
    padding,
    image_of_row,
    self_weights,
    cross_weights,
    mlp_in,
    mlp_out,
    gains,
):
    result, kept = forward(
        layer_input[0],
        cotangent[0],
        memory[0],
        segment_ids,
        padding,
        image_of_row,
        gains,
        self_weights,
        cross_weights,
        mlp_in,
        mlp_out,
    )
    self_grad, cross_grad, in_grad, out_grad, x_grad, mem_grad, gain_grad, result = finish(
        *backward(kept, layer_input[0], cotangent[0], segment_ids, padding, image_of_row, gains.shape[1]),
        result,
    )
    return (result[None], x_grad[None], mem_grad[None], self_grad, cross_grad, in_grad, out_grad[0], gain_grad)


def on_device(
    layer_input,
    memory,
    cotangent,
    segment_ids,
    padding,
    image_of_row,
    self_weights,
    cross_weights,
    mlp_in,
    mlp_out,
    gains,
):
    run = kernel_device if by_kernel(self_weights) else plain_device
    return run(
        layer_input,
        memory,
        cotangent,
        segment_ids,
        padding,
        image_of_row,
        self_weights,
        cross_weights,
        mlp_in,
        mlp_out,
        gains,
    )


def solution(mesh):
    in_specs = (
        P(("wide", "narrow"), None, None),
        P(("wide", "narrow"), None, None),
        P(("wide", "narrow"), None, None),
        P(("wide", "narrow"), None),
        P(("wide", "narrow"), None),
        P(),
        P(None, "wide", None),
        P(None, "wide", None),
        P(None, "wide", None),
        P("wide", None),
        P(None, "wide"),
    )
    out_specs = (
        P(("wide", "narrow"), None, None),
        P(("wide", "narrow"), None, None),
        P(("wide", "narrow"), None, None),
        P(None, "wide", None),
        P(None, "wide", None),
        P(None, "wide", None),
        P("wide", None),
        P(None, "wide"),
    )
    return jax.shard_map(
        on_device, mesh=mesh, in_specs=in_specs, out_specs=out_specs, check_vma=False
    )
```

```python
import functools

import jax
import jax.numpy as jnp
from jax import lax
from jax.experimental import pallas as pl
from jax.experimental.pallas import tpu as pltpu
from jax.sharding import PartitionSpec as P

HEAD_DIM = 64


EPSILON = 1e-06


def shifted(value, axis, steps):
    count = lax.axis_size(axis)
    first, last = (max(0, -steps), min(count, count - steps))
    return lax.ppermute(value, axis, [(source, source + steps) for source in range(first, last)])


def rms_norm(v, g):
    return v * lax.rsqrt(jnp.mean(v * v, axis=-1, keepdims=True) + EPSILON) * g


def contract_rows(a, b):
    return lax.dot_general(a, b, (((0,), (0,)), ((), ())), preferred_element_type=jnp.float32)


def times_transposed(a, w):
    return lax.dot_general(a, w, (((1,), (1,)), ((), ())), preferred_element_type=jnp.float32)


def linear(a, w):
    return jnp.dot(a, w, preferred_element_type=jnp.float32)


def head_scores(q_part, k_part, allowed):
    scores = jnp.einsum(
        "qhd,khd->hqk", q_part, k_part, preferred_element_type=jnp.float32
    ) * HEAD_DIM ** (-0.5)
    if allowed is not None:
        scores = jnp.where(allowed[None], scores, -1e30)
    return scores


def split_heads(a, head_start):
    return a[:, head_start * HEAD_DIM : (head_start + 4) * HEAD_DIM].reshape(
        a.shape[0], 4, HEAD_DIM
    )


def forward_heads(q, k, v, allowed):
    seq_len = q.shape[0]
    head_count = q.shape[1] // HEAD_DIM
    pieces = []
    log_sums = []
    for head_start in range(0, head_count, 4):
        q_part = split_heads(q, head_start)
        k_part = split_heads(k, head_start)
        v_part = split_heads(v, head_start)
        scores = head_scores(q_part, k_part, allowed)
        highest = jnp.max(scores, axis=-1, keepdims=True)
        powers = jnp.exp(scores - highest)
        summed = jnp.sum(powers, axis=-1, keepdims=True)
        shares = (powers / summed).astype(jnp.bfloat16)
        mixed = jnp.einsum("hqk,khd->qhd", shares, v_part, preferred_element_type=jnp.float32)
        pieces.append(mixed.reshape(seq_len, -1))
        log_sums.append(highest + jnp.log(summed))
    return (jnp.concatenate(pieces, axis=1).astype(jnp.bfloat16), jnp.concatenate(log_sums, axis=0))


def backward_heads(q, k, v, mix_grad, log_sum, allowed):
    seq_len = q.shape[0]
    head_count = q.shape[1] // HEAD_DIM
    q_pieces = []
    k_pieces = []
    v_pieces = []
    for head_start in range(0, head_count, 4):
        q_part = split_heads(q, head_start)
        k_part = split_heads(k, head_start)
        v_part = split_heads(v, head_start)
        o_part = split_heads(mix_grad, head_start)
        scores = head_scores(q_part, k_part, allowed)
        shares = jnp.exp(scores - log_sum[head_start : head_start + 4])
        v_grad = jnp.einsum(
            "hqk,qhd->khd", shares.astype(jnp.bfloat16), o_part, preferred_element_type=jnp.float32
        )
        p_grad = jnp.einsum("qhd,khd->hqk", o_part, v_part, preferred_element_type=jnp.float32)
        s_grad = shares * (p_grad - jnp.sum(shares * p_grad, axis=-1, keepdims=True))
        s_low = s_grad.astype(jnp.bfloat16)
        q_grad = jnp.einsum(
            "hqk,khd->qhd", s_low, k_part, preferred_element_type=jnp.float32
        ) * HEAD_DIM ** (-0.5)
        k_grad = jnp.einsum(
            "hqk,qhd->khd", s_low, q_part, preferred_element_type=jnp.float32
        ) * HEAD_DIM ** (-0.5)
        q_pieces.append(q_grad.reshape(seq_len, -1))
        k_pieces.append(k_grad.reshape(k.shape[0], -1))
        v_pieces.append(v_grad.reshape(k.shape[0], -1))
    return (
        jnp.concatenate(q_pieces, axis=1).astype(jnp.bfloat16),
        jnp.concatenate(k_pieces, axis=1).astype(jnp.bfloat16),
        jnp.concatenate(v_pieces, axis=1).astype(jnp.bfloat16),
    )


def gated_product(gate_act, up_act):
    return jax.nn.gelu(gate_act, approximate=True) * up_act


MESH = pl.DeviceIdType.MESH


class Place:
    def __init__(self, depth):
        self.depth = depth
        self.wide = lax.axis_index("wide")
        self.x = lax.axis_index("narrow")
        self.core = self.wide % 2
        self.y = (self.wide // 2) % 2
        self.z = self.wide // 4

    def shard(self, z, y, core):
        return z * 4 + y * 2 + core

    def z_ahead(self, step):
        return (self.shard((self.z + step) % self.depth, self.y, self.core), self.x)

    def z_behind(self, step):
        return (self.z + self.depth - step) % self.depth

    @property
    def across_x(self):
        return (self.wide, 1 - self.x)

    @property
    def across_y(self):
        return (self.shard(self.z, 1 - self.y, self.core), self.x)

    @property
    def across_core(self):
        return (self.shard(self.z, self.y, 1 - self.core), self.x)

    def greet(self):
        barrier = pltpu.get_barrier_semaphore()
        others = [self.across_x, self.across_y, self.across_core]
        others += [self.z_ahead(step) for step in range(1, self.depth)]
        for other in others:
            pl.semaphore_signal(barrier, inc=1, device_id=other, device_id_type=MESH)
        pl.semaphore_wait(barrier, len(others))


def remote(src, dst, send, recv, device):
    return pltpu.make_async_remote_copy(
        src_ref=src, dst_ref=dst, send_sem=send, recv_sem=recv, device_id=device, device_id_type=MESH
    )


class Plan:
    def __init__(self, slack=2.5, latency=1.5):
        self.now = 0.0
        self.slack = slack
        self.latency = latency
        self.rate = {"c": 400e3, "x": 50e3, "y": 50e3, "z": 50e3}
        self.free = dict.fromkeys(self.rate, 0.0)
        self.queues = {link: [] for link in self.rate}
        self.flying = []
        self.serial = 0

    def send(self, link, rank, size, start, arrive, cost=0.2):
        self.serial += 1
        self.queues[link].append((rank, self.serial, size, start, arrive, cost))

    def later(self, delay, arrive, cost=0.2):
        self.serial += 1
        self.flying.append((self.now + delay, self.serial, cost, arrive))

    def issue(self):
        for link, queue in self.queues.items():
            while queue and self.free[link] <= self.now + self.slack:
                first = min(queue, key=lambda q: q[:2])
                queue.remove(first)
                _, serial, size, start, arrive, cost = first
                start()
                self.now += 0.03
                self.free[link] = max(self.free[link], self.now) + size / self.rate[link]
                if arrive is not None:
                    self.flying.append((self.free[link] + self.latency, serial, cost, arrive))

    def drain(self):
        self.issue()
        while self.flying:
            first = min(self.flying, key=lambda f: f[:2])
            if first[0] > self.now:
                break
            self.flying.remove(first)
            first[3]()
            self.now += first[2]
            self.issue()

    def busy(self):
        return bool(self.flying) or any(self.queues.values())

    def step(self):
        self.issue()
        times = [f[0] for f in self.flying]
        times += [self.free[link] - self.slack for link, queue in self.queues.items() if queue]
        self.now = max(self.now, min(times))
        self.drain()

    def work(self, cost, run):
        self.drain()
        run()
        self.now += cost


class Gather:
    def __init__(self, place, own, full, rows, side, y_first, sems):
        self.p = place
        self.own = own
        self.full = full
        self.rows = rows
        self.side = side
        self.main = rows - side
        self.y_first = y_first
        self.main_send, self.main_recv, self.x_send, self.x_recv, self.c_send, self.c_recv = sems

    def block(self, ref, start, size):
        return ref.at[:, pl.ds(pl.multiple_of(start, 16), size), :]

    def at(self, z, y, core, start, size):
        return self.block(self.full, self.p.shard(z, y, core) * self.rows + start, size)

    def owner(self, n):
        step, other = n % self.p.depth, n // self.p.depth
        return self.p.z_behind(step), (1 - self.p.y if other else self.p.y)

    @property
    def main_start(self):
        return self.side * self.p.x

    def side_start(self, x):
        return self.main * x

    def main_piece(self, z, y, source=False):
        p = self.p
        return self.at(z, y, p.core, self.main_start, self.main)

    def arriving(self, n):
        p = self.p
        z, y = self.owner(n)
        piece = self.main_piece(z, y)
        return remote(piece, piece, self.main_send.at[0], self.main_recv.at[n], p.across_y)

    def y_copy(self, n):
        p = self.p
        z, y = self.owner(n)
        dst = self.main_piece(z, y)
        src = self.block(self.own, self.main_start, self.main) if n == 0 else dst
        return remote(src, dst, self.main_send.at[n], self.main_recv.at[n + p.depth], p.across_y)

    def z_copy(self, step, other):
        p = self.p
        y = 1 - p.y if other else p.y
        dst = self.main_piece(p.z, y)
        src = dst if other else self.block(self.own, self.main_start, self.main)
        slot = p.depth + (step - 1) + (p.depth - 1) * other
        return remote(
            src, dst, self.main_send.at[slot], self.main_recv.at[step + p.depth * other], p.z_ahead(step)
        )

    def relay_copy(self, other, up):
        p = self.p
        z, target = (0, 3) if up else (3, 0)
        y = 1 - p.y if other else p.y
        piece = self.main_piece(z, y)
        slot = p.depth + 2 * (p.depth - 1) + other
        step = 3 if up else 1
        device = (p.shard(target, p.y, p.core), p.x)
        return remote(piece, piece, self.main_send.at[slot], self.main_recv.at[step + p.depth * other], device)

    def x_copy(self, n, x):
        p = self.p
        z, y = self.owner(n)
        piece = self.at(z, y, p.core, self.side_start(x), self.side)
        return remote(piece, piece, self.x_send.at[n], self.x_recv.at[n], p.across_x)

    def c_copy(self, n, core, side):
        p = self.p
        slot = n + (2 * p.depth if side else 0)
        z, y = self.owner(n)
        if n == 0:
            src, dst = self.own, self.at(z, y, core, 0, self.rows)
        else:
            start, size = (self.side_start(1 - p.x), self.side) if side else (self.main_start, self.main)
            src = dst = self.at(z, y, core, start, size)
        return remote(src, dst, self.c_send.at[slot], self.c_recv.at[slot], p.across_core)

    def copy_own(self):
        p = self.p
        return pltpu.make_async_copy(self.own, self.at(p.z, p.y, p.core, 0, self.rows), self.main_send.at[4 * p.depth])

    def each_z(self, other, act):
        p = self.p
        for step in range(1, p.depth):
            if step == 2:
                act(self.z_copy(step, other))
            else:
                end = 0 if step == 3 else 3

                @pl.when(p.z != end)
                def _():
                    act(self.z_copy(step, other))

    def each_relay(self, other, act):
        p = self.p

        @pl.when(p.z == 2)
        def _():
            act(self.relay_copy(other, True))

        @pl.when(p.z == 1)
        def _():
            act(self.relay_copy(other, False))

    def begin(self):
        self.copy_own().start()
        self.y_copy(0).start()
        self.each_z(0, lambda copy: copy.start())
        self.c_copy(0, self.p.core, False).start()

    def order(self):
        depth = self.p.depth
        if self.y_first:
            return [depth, 2, 2 + depth, 1, 3, 1 + depth, 3 + depth]
        return [2, 1, 3, depth, depth + 2, depth + 1, depth + 3]

    def take(self, n):
        p = self.p
        depth = p.depth
        self.arriving(n).wait_recv()
        other = n // depth
        if n % depth == 2 and (self.y_first or other == 0):
            self.each_relay(other, lambda copy: copy.start())
        if self.y_first:
            if n == depth:
                self.each_z(1, lambda copy: copy.start())
        elif other == 0:
            self.y_copy(n).start()
        if self.side:
            self.x_copy(n, p.x).start()
        self.c_copy(n, p.core, False).start()

    def take_x(self, n):
        p = self.p
        if self.side:
            self.x_copy(n, 1 - p.x).wait_recv()
            self.c_copy(n, p.core, True).start()

    def complete(self):
        p = self.p
        self.copy_own().wait()
        for n in range(2 * p.depth):
            self.c_copy(n, 1 - p.core, False).wait_recv()
            if self.side and n:
                self.c_copy(n, 1 - p.core, True).wait_recv()

    def end(self):
        p = self.p

        def wait(copy):
            copy.wait_send()

        for n in range(1 if self.y_first else p.depth):
            self.y_copy(n).wait_send()
        for other in range(2 if self.y_first else 1):
            self.each_z(other, wait)
            self.each_relay(other, wait)
        for n in range(2 * p.depth):
            self.c_copy(n, p.core, False).wait_send()
            if self.side and n:
                self.x_copy(n, p.x).wait_send()
                self.c_copy(n, p.core, True).wait_send()


def gather_sems(count, depth):
    sizes = (4 * depth + 1, 2 * depth, 2 * depth, 2 * depth, 4 * depth, 4 * depth)
    return [pltpu.SemaphoreType.DMA((count, size)) for size in sizes]


LOW = jnp.bfloat16


def dot(a, b, ca=1, cb=0):
    return lax.dot_general(a, b, (((ca,), (cb,)), ((), ())), preferred_element_type=jnp.float32)


def norm_rows(source, gain, target):
    rows = source.shape[0]
    chunk = 64

    @pl.loop(0, rows // chunk)
    def _(i):
        span = pl.ds(pl.multiple_of(i * chunk, chunk), chunk)
        v = source[span].astype(jnp.float32)
        scale = lax.rsqrt(jnp.mean(v * v, axis=-1, keepdims=True) + EPSILON)
        target[span] = (v * scale * gain).astype(LOW)


def norm_back_rows(source, gain, grad, dout, target, gain_grad):
    rows, width = source.shape
    chunk = 64
    gain_grad[...] = jnp.zeros_like(gain_grad)

    @pl.loop(0, rows // chunk)
    def _(i):
        span = pl.ds(pl.multiple_of(i * chunk, chunk), chunk)
        v = source[span].astype(jnp.float32)
        dh = grad[span]
        scale = lax.rsqrt(jnp.mean(v * v, axis=-1, keepdims=True) + EPSILON)
        unit = v * scale
        gain_grad[...] += jnp.sum(dh * unit, axis=0, keepdims=True)
        scaled = dh * gain
        along = jnp.mean(scaled * unit, axis=-1, keepdims=True)
        target[span] = (dout[span].astype(jnp.float32) + scale * (scaled - unit * along)).astype(target.dtype)


def pair_span(pair):
    return pl.ds(pl.multiple_of(pair * 2 * HEAD_DIM, 2 * HEAD_DIM), 2 * HEAD_DIM)


def attend_pair(pair, q, k, v, bias, mixed, lse):
    span = pair_span(pair)
    q_two, k_two, v_two = q[:, span], k[:, span], v[:, span]
    rows = q_two.shape[0]
    low_half = lax.broadcasted_iota(jnp.int32, q_two.shape, 1) < HEAD_DIM
    lane = lax.broadcasted_iota(jnp.int32, (rows, 128), 1)
    outs = []
    sums = lse[...]
    for half in range(2):
        mine = low_half if half == 0 else ~low_half
        scores = dot(jnp.where(mine, q_two, jnp.zeros_like(q_two)), k_two, 1, 1) * HEAD_DIM ** (-0.5)
        if bias is not None:
            scores = scores + bias[...]
        highest = jnp.max(scores, axis=-1, keepdims=True)
        powers = jnp.exp(scores - highest)
        summed = jnp.sum(powers, axis=-1, keepdims=True)
        shares = (powers / summed).astype(LOW)
        outs.append(dot(shares, v_two))
        sums = jnp.where(lane == 2 * pair + half, highest + jnp.log(summed), sums)
    mixed[:, span] = jnp.where(low_half, outs[0], outs[1]).astype(LOW)
    lse[...] = sums


def gelu_parts(gate):
    inner = (2.0 / 3.141592653589793) ** 0.5
    square = gate * gate
    bent = jnp.tanh(inner * gate * (1.0 + 0.044715 * square))
    half = 0.5 * (1.0 + bent)
    slope = half + 0.5 * gate * (1.0 - bent * bent) * inner * (1.0 + 3 * 0.044715 * square)
    return gate * half, slope


class Rows:
    def __init__(self, place, count):
        self.p = place
        self.count = count
        self.row = place.wide * 2 + place.x

    def device(self, row):
        return (row // 2, row % 2)

    def when(self, distance, act):
        @pl.when((self.row + distance >= 0) & (self.row + distance < self.count))
        def _():
            act(self.device(self.row + distance))

    def near(self):
        return (-2, -1, 1, 2)

    def present(self):
        below = jnp.minimum(self.row, 2)
        above = jnp.minimum(self.count - 1 - self.row, 2)
        return below + above


def greet_all(place, rows):
    barrier = pltpu.get_barrier_semaphore()
    others = [place.across_x, place.across_y, place.across_core]
    others += [place.z_ahead(step) for step in range(1, place.depth)]

    def hello(device):
        pl.semaphore_signal(barrier, inc=1, device_id=device, device_id_type=MESH)

    for other in others:
        hello(other)
    for distance in rows.near():
        rows.when(distance, hello)
    pl.semaphore_wait(barrier, len(others) + rows.present())


def pass_rows(rows, source, target, distance, sems):
    send, recv = sems

    def copy(device):
        return remote(source, target, send, recv, device)

    def start():
        rows.when(distance, lambda device: copy(device).start())

    def arrive():
        rows.when(-distance, lambda device: copy(device).wait_recv())

    def end():
        rows.when(distance, lambda device: copy(device).wait_send())

    return start, arrive, end


MLP_CUTS = (0, 512, 1024, 1536, 1792, 2048)
GATHER_LAYOUT = (
    (4, 0, 1, 0, 128, 0),
    (0, 0, 3, 0, 768, 16),
    (0, 3, 4, 0, 768, 16),
    (1, 0, 2, 0, 768, 16),
    (1, 2, 4, 0, 768, 16),
    (3, 0, 1, 0, 768, 48),
    *((2, 0, 2, first, last, 16) for first, last in zip(MLP_CUTS, MLP_CUTS[1:])),
)
WIDTH, HIDDEN, TOKENS, PATCHES = 768, 2048, 384, 256

class Spec:
    def __init__(self, *shape, dtype=LOW):
        self.shape = shape
        self.dtype = dtype

    def array(self):
        return jax.ShapeDtypeStruct(self.shape, self.dtype)

    def scratch(self):
        return pltpu.VMEM(self.shape, self.dtype)


def specs(table):
    return [spec for spec in vars(table).values() if isinstance(spec, Spec)]


class K:
    gain = Spec(8, WIDTH, dtype=jnp.float32)
    h1t = Spec(WIDTH, TOKENS)
    q1 = Spec(TOKENS, WIDTH)
    k1 = Spec(TOKENS, WIDTH)
    v1 = Spec(TOKENS, WIDTH)
    o1t = Spec(WIDTH, TOKENS)
    lse1 = Spec(128, TOKENS, dtype=jnp.float32)
    x1 = Spec(TOKENS, WIDTH, dtype=jnp.float32)
    h2t = Spec(WIDTH, TOKENS)
    memt = Spec(WIDTH, PATCHES)
    q2 = Spec(TOKENS, WIDTH)
    k2 = Spec(PATCHES, WIDTH)
    v2 = Spec(PATCHES, WIDTH)
    o2t = Spec(WIDTH, TOKENS)
    lse2 = Spec(128, TOKENS, dtype=jnp.float32)
    h3t = Spec(WIDTH, TOKENS)
    hiddent = Spec(HIDDEN, TOKENS)
    dgate = Spec(TOKENS, HIDDEN)
    dup = Spec(TOKENS, HIDDEN)
    dx2 = Spec(TOKENS, WIDTH, dtype=jnp.float32)
    gain3 = Spec(1, WIDTH, dtype=jnp.float32)


class W:
    w_self = Spec(4, WIDTH, WIDTH)
    w_cross = Spec(4, WIDTH, WIDTH)
    w_in = Spec(2, WIDTH, HIDDEN)
    w_out = Spec(1, HIDDEN, WIDTH)
    w_gain = Spec(1, 256, 128)


class F:
    bias = Spec(TOKENS, TOKENS, dtype=jnp.float32)
    h = Spec(TOKENS, WIDTH)
    mix = Spec(TOKENS, WIDTH)
    lse = Spec(TOKENS, 128, dtype=jnp.float32)
    mem_one = Spec(PATCHES, WIDTH)
    mem = Spec(PATCHES, WIDTH)
    mem_got = Spec(2, PATCHES, WIDTH)
    x2 = Spec(TOKENS, WIDTH, dtype=jnp.float32)
    gate = Spec(TOKENS, 512, dtype=jnp.float32)
    up = Spec(TOKENS, 512, dtype=jnp.float32)
    dhid = Spec(TOKENS, 512, dtype=jnp.float32)
    hidden = Spec(TOKENS, HIDDEN)
    gain_own = Spec(1, 16, 128)
    total = Spec(TOKENS, WIDTH, dtype=jnp.float32)
    dh = Spec(TOKENS, WIDTH, dtype=jnp.float32)


PASSED = specs(K) + [W.w_self, W.w_cross]


def as_column(row):
    return jnp.broadcast_to(row.astype(jnp.float32), (128, row.shape[1])).T


def row_offset(images, row, count):
    image = images[jnp.minimum(row, count - 1)]
    start = sum((images[other] < image).astype(jnp.int32) for other in range(count))
    return jnp.where(row < count, row - start, 0)


def forward_kernel(depth, row_count, refs):
    (x0, dy, memory, segments, padding, images, gains) = refs[:7]
    owns = refs[7:11]
    out = refs[11]
    rest = refs[12:]
    kept_out, rest = dict(zip(PASSED, rest)), rest[len(PASSED) :]
    kept, rest = dict(zip(specs(K), rest)), rest[len(specs(K)) :]
    weights, rest = dict(zip(specs(W), rest)), rest[len(specs(W)) :]
    local, rest = dict(zip(specs(F), rest)), rest[len(specs(F)) :]
    gather_sem, row_sem, keep_sem, mlp_sem = rest[:6], rest[6], rest[7], rest[8]
    owns = (*owns, local[F.gain_own])
    kept_numbers = {name: number for number, name in enumerate(kept_out)}

    def keep_copy(name):
        source = weights[name] if name in weights else kept[name]
        return pltpu.make_async_copy(source, kept_out[name], keep_sem.at[kept_numbers[name]])

    def keep(*names):
        for name in names:
            keep_copy(name).start()

    place = Place(depth)
    rows = Rows(place, row_count)
    fulls = [weights[spec] for spec in specs(W)]
    blocks = []
    for number, (array, first, last, c0, c1, side) in enumerate(GATHER_LAYOUT):
        own, full = owns[array], fulls[array]
        blocks.append(
            Gather(
                place,
                own.at[first:last, :, c0:c1],
                full.at[first:last, :, c0:c1],
                own.shape[1],
                side,
                False,
                [sem.at[number] for sem in gather_sem],
            )
        )
    near_start, near_arrive, near_end = pass_rows(
        rows, memory, local[F.mem_got].at[0], 1, (row_sem.at[0], row_sem.at[1])
    )
    far_start, far_arrive, far_end = pass_rows(
        rows, local[F.mem_one], local[F.mem_got].at[1], 2, (row_sem.at[2], row_sem.at[3])
    )
    gain = kept[K.gain]
    offset = row_offset(images, rows.row, row_count)
    local[F.gain_own][...] = jnp.zeros_like(local[F.gain_own])
    local[F.gain_own][0, 0 : gains.shape[0], 0 : gains.shape[1]] = gains[...]

    def make_bias():
        seg_q, seg_k = as_column(segments[...])[:, 0:1], segments[...].astype(jnp.float32)
        query = lax.broadcasted_iota(jnp.int32, (TOKENS, TOKENS), 0)
        key = lax.broadcasted_iota(jnp.int32, (TOKENS, TOKENS), 1)
        allowed = (seg_q == seg_k) & (key <= query) & ((padding[...] == 1) | (key == query))
        local[F.bias][...] = jnp.where(allowed, 0.0, -1e30)

    def make_gain():
        total = jnp.zeros((16, WIDTH), jnp.float32)
        count = row_count // 2
        share = WIDTH // count
        for number in range(count):
            row = lax.broadcasted_iota(jnp.int32, (128, WIDTH), 0)
            column = lax.broadcasted_iota(jnp.int32, (128, WIDTH), 1)
            pick = ((column - number * share) == row) & (row < share)
            total += dot(weights[W.w_gain][0, number * 16 : number * 16 + 16, :], pick.astype(LOW))
        gain[...] = total[:8]

    def first_norm():
        norm_rows(x0, gain[0:1], local[F.h])
        kept[K.h1t][...] = local[F.h][...].T
        keep(K.gain, K.h1t)

    def project(name, w, index):
        def run():
            kept[name][...] = dot(local[F.h][...], weights[w][index]).astype(LOW)
            keep(name)

        return run

    def self_pair(pair):
        return lambda: attend_pair(pair, kept[K.q1], kept[K.k1], kept[K.v1], local[F.bias], local[F.mix], local[F.lse])

    def clear_lse():
        local[F.lse][...] = jnp.zeros_like(local[F.lse])

    def self_out():
        kept[K.lse1][...] = local[F.lse][...].T
        kept[K.o1t][...] = local[F.mix][...].T
        kept[K.x1][...] = x0[...].astype(jnp.float32) + dot(local[F.mix][...], weights[W.w_self][3])
        keep(K.lse1, K.o1t, K.x1)

    def second_norm():
        norm_rows(kept[K.x1], gain[1:2], local[F.h])
        kept[K.h2t][...] = local[F.h][...].T
        keep(K.h2t)

    def memory_near():
        near_arrive()
        local[F.mem_one][...] = jnp.where(offset >= 1, local[F.mem_got][0], memory[...])
        far_start()

    def memory_far():
        far_arrive()
        local[F.mem][...] = jnp.where(offset >= 2, local[F.mem_got][1], local[F.mem_one][...])
        kept[K.memt][...] = local[F.mem][...].T
        keep(K.memt)

    def project_memory(name, index):
        def run():
            kept[name][...] = dot(local[F.mem][...], weights[W.w_cross][index]).astype(LOW)
            keep(name)

        return run

    def cross_pair(pair):
        return lambda: attend_pair(pair, kept[K.q2], kept[K.k2], kept[K.v2], None, local[F.mix], local[F.lse])

    def cross_out():
        kept[K.lse2][...] = local[F.lse][...].T
        kept[K.o2t][...] = local[F.mix][...].T
        local[F.x2][...] = kept[K.x1][...] + dot(local[F.mix][...], weights[W.w_cross][3])
        keep(K.lse2, K.o2t)

    def third_norm():
        norm_rows(local[F.x2], gain[2:3], local[F.h])
        kept[K.h3t][...] = local[F.h][...].T
        keep(K.h3t)

    def mlp_dots(number):
        c0, c1 = MLP_CUTS[number], MLP_CUTS[number + 1]

        def run():
            h = local[F.h][...]
            local[F.dhid][:, : c1 - c0] = dot(dy[...], weights[W.w_out][0, c0:c1, :], 1, 1)
            local[F.gate][:, : c1 - c0] = dot(h, weights[W.w_in][0, :, c0:c1])
            local[F.up][:, : c1 - c0] = dot(h, weights[W.w_in][1, :, c0:c1])

        return run

    def mlp_copies(number):
        c0, c1 = MLP_CUTS[number], MLP_CUTS[number + 1]
        cuts = ((K.hiddent, (slice(c0, c1), slice(None))), (K.dgate, (slice(None), slice(c0, c1))))
        cuts += ((K.dup, (slice(None), slice(c0, c1))),)
        return [
            pltpu.make_async_copy(kept[name].at[cut], kept_out[name].at[cut], mlp_sem.at[number, place_of])
            for place_of, (name, cut) in enumerate(cuts)
        ]

    def mlp_point(number):
        c0, c1 = MLP_CUTS[number], MLP_CUTS[number + 1]
        width = c1 - c0

        def run():
            @pl.loop(0, TOKENS // 16)
            def _(i):
                span = pl.ds(pl.multiple_of(i * 16, 16), 16)
                act, slope = gelu_parts(local[F.gate][span, :width])
                up, dhid = local[F.up][span, :width], local[F.dhid][span, :width]
                local[F.hidden][span, c0:c1] = (act * up).astype(LOW)
                kept[K.dgate][span, c0:c1] = (dhid * up * slope).astype(LOW)
                kept[K.dup][span, c0:c1] = (dhid * act).astype(LOW)

            kept[K.hiddent][c0:c1, :] = local[F.hidden][:, c0:c1].T
            for copy in mlp_copies(number):
                copy.start()

        return run

    def mlp_back(number):
        c0, c1 = MLP_CUTS[number], MLP_CUTS[number + 1]

        def run():
            value = dot(kept[K.dgate][:, c0:c1], weights[W.w_in][0, :, c0:c1], 1, 1)
            value += dot(kept[K.dup][:, c0:c1], weights[W.w_in][1, :, c0:c1], 1, 1)
            local[F.dh][...] = value if number == 0 else local[F.dh][...] + value

        return run

    def mlp_sum(number):
        c0, c1 = MLP_CUTS[number], MLP_CUTS[number + 1]

        def run():
            before = local[F.x2] if number == 0 else local[F.total]
            value = before[...] + dot(local[F.hidden][:, c0:c1], weights[W.w_out][0, c0:c1, :])
            if c1 == HIDDEN:
                out[...] = value.astype(LOW)
            else:
                local[F.total][...] = value

        return run

    def mlp_norm():
        norm_back_rows(local[F.x2], gain[2:3], local[F.dh], dy, kept[K.dx2], kept[K.gain3])
        keep(K.dx2, K.gain3)

    work = [
        (None, 0.5, make_bias),
        (None, 0.1, clear_lse),
        (0, 2.0, make_gain),
        (0, 1.5, first_norm),
        (1, 0.7, project(K.q1, W.w_self, 0)),
        (1, 0.7, project(K.k1, W.w_self, 1)),
        (1, 0.7, project(K.v1, W.w_self, 2)),
    ]
    work += [(1, 1.2, self_pair(pair)) for pair in range(6)]
    work += [
        (2, 0.1, lambda: keep(W.w_self)),
        (2, 1.5, self_out),
        (2, 1.2, second_norm),
        (2, 0.5, memory_near),
        (3, 0.7, project(K.q2, W.w_cross, 0)),
        (3, 0.6, memory_far),
        (3, 0.6, project_memory(K.k2, 1)),
        (4, 0.6, project_memory(K.v2, 2)),
        (4, 0.1, lambda: keep(W.w_cross)),
    ]
    work += [(4, 0.9, cross_pair(pair)) for pair in range(6)]
    work += [(4, 1.5, cross_out), (4, 1.2, third_norm)]
    for number in range(len(MLP_CUTS) - 1):
        share = (MLP_CUTS[number + 1] - MLP_CUTS[number]) / 512
        need = 6 + number
        work += [(need, 1.7 * share, mlp_dots(number)), (need, 1.8 * share, mlp_point(number))]
        work += [(need, 1.2 * share, mlp_back(number)), (need, 0.7 * share, mlp_sum(number))]
    work += [(None, 1.2, mlp_norm)]

    count = len(blocks)
    events = []
    for turn in range(count + 3):
        if turn + 2 < count:
            events.append((blocks[turn + 2].begin, None))
        if turn < count:
            for n in blocks[turn].order()[:3]:
                events.append((functools.partial(blocks[turn].take, n), None))
        if 0 <= turn - 1 < count:
            for n in blocks[turn - 1].order()[3:]:
                events.append((functools.partial(blocks[turn - 1].take, n), None))
        if 0 <= turn - 2 < count and blocks[turn - 2].side:
            for n in blocks[turn - 2].order():
                events.append((functools.partial(blocks[turn - 2].take_x, n), None))
        if 0 <= turn - 3 < count:
            events.append((blocks[turn - 3].complete, turn - 3))

    greet_all(place, rows)
    blocks[0].begin()
    blocks[1].begin()
    near_start()
    ready = -1
    done = 0

    def can():
        return done < len(work) and (work[done][0] is None or work[done][0] <= ready)

    for act, completes in events:
        act()
        if completes is not None:
            ready = completes
        if can():
            work[done][2]()
            done += 1
    while can():
        work[done][2]()
        done += 1
    for block in blocks:
        block.end()
    near_end()
    far_end()
    for number in range(len(MLP_CUTS) - 1):
        for copy in mlp_copies(number):
            copy.wait()
    for name in kept_out:
        if name not in (K.hiddent, K.dgate, K.dup):
            keep_copy(name).wait()


def forward(
    layer_input,
    cotangent,
    memory,
    segments,
    padding,
    image_of_row,
    gains,
    self_weights,
    cross_weights,
    mlp_in,
    mlp_out,
):
    wide = lax.axis_size("wide")
    depth = wide // 4
    owns = (self_weights, cross_weights, mlp_in, mlp_out[None])
    vmem, anywhere, smem = (pl.BlockSpec(memory_space=space) for space in (pltpu.VMEM, pl.ANY, pltpu.SMEM))
    kept = [spec.array() for spec in PASSED]
    outs = pl.pallas_call(
        lambda *refs: forward_kernel(depth, 2 * wide, refs),
        out_shape=[jax.ShapeDtypeStruct(layer_input.shape, LOW)] + kept,
        in_specs=[vmem] * 5 + [smem, vmem] + [anywhere] * 4,
        out_specs=[vmem] + [anywhere] * len(kept),
        scratch_shapes=[spec.scratch() for table in (K, W, F) for spec in specs(table)]
        + gather_sems(len(GATHER_LAYOUT), depth)
        + [
            pltpu.SemaphoreType.DMA((4,)),
            pltpu.SemaphoreType.DMA((len(kept),)),
            pltpu.SemaphoreType.DMA((len(MLP_CUTS) - 1, 3)),
        ],
        compiler_params=pltpu.CompilerParams(
            collective_id=0, has_side_effects=True, vmem_limit_bytes=60 * 2**20
        ),
        name="forward",
    )(layer_input, cotangent, memory, segments, padding, image_of_row, gains, *owns)
    return outs[0], dict(zip(PASSED, outs[1:]))


class Scatter:
    def __init__(self, place, bufs, outs, block, sems):
        self.p = place
        rows, side = block.rows, block.side
        self.width = block.width
        self.relay = block.relay
        self.staged, self.held, self.from_x, self.from_y, self.from_z, self.relayed, self.done, self.other = bufs
        self.outs = outs
        self.rows = rows
        self.side = side
        self.main = rows - side
        self.send, self.recv = sems

    def span(self, start, size):
        return pl.ds(pl.multiple_of(start, 16), size)

    @property
    def main_span(self):
        return self.span(self.side * self.p.x, self.main)

    def side_span(self, x):
        return self.span(self.main * x, self.side)

    def c_copy(self):
        return remote(self.staged, self.held, self.send.at[0], self.recv.at[0], self.p.across_core)

    def x_copy(self):
        p = self.p
        return remote(
            self.held.at[:, :, :, self.side_span(1 - p.x)],
            self.from_x,
            self.send.at[1],
            self.recv.at[1],
            p.across_x,
        )

    def y_copy(self):
        p = self.p
        return remote(
            self.held.at[:, :, 1 - p.y, self.main_span], self.from_y, self.send.at[2], self.recv.at[2], p.across_y
        )

    def z_piece(self, z):
        return self.held.at[:, z, self.p.y, self.main_span]

    def z_copy(self, step):
        p = self.p
        return remote(
            self.z_piece((p.z + step) % p.depth),
            self.from_z.at[step - 1],
            self.send.at[2 + step],
            self.recv.at[2 + step],
            p.z_ahead(step),
        )

    def relay_copy(self, up):
        p = self.p
        target, between = (3, 1) if up else (0, 2)
        device = (p.shard(between, p.y, p.core), p.x)
        return remote(self.z_piece(target), self.relayed, self.send.at[6], self.recv.at[6], device)

    def last_copy(self):
        return remote(self.done, self.other, self.send.at[7], self.recv.at[7], self.p.across_x)

    def blank(self):
        p = self.p
        if not self.relay:
            return

        @pl.when(p.z == 0)
        def _():
            self.from_z[0] = jnp.zeros_like(self.from_z[0])

        @pl.when(p.z == 3)
        def _():
            self.from_z[2] = jnp.zeros_like(self.from_z[2])

    def each_z(self, act_direct, act_late, act_relay):
        p = self.p
        if not self.relay:
            if act_direct is not None:
                for step in range(1, p.depth):
                    act_direct(self.z_copy(step))
            return
        if act_direct is not None:

            @pl.when(p.z != 0)
            def _():
                act_direct(self.z_copy(3))

            @pl.when(p.z != 3)
            def _():
                act_direct(self.z_copy(1))

            @pl.when((p.z == 0) | (p.z == 3))
            def _():
                act_direct(self.z_copy(2))

        if act_late is not None:

            @pl.when(p.z == 1)
            def _():
                act_late(self.z_copy(2), 3)

            @pl.when(p.z == 2)
            def _():
                act_late(self.z_copy(2), 0)

        if act_relay is not None:

            @pl.when(p.z == 0)
            def _():
                act_relay(self.relay_copy(True))

            @pl.when(p.z == 3)
            def _():
                act_relay(self.relay_copy(False))

    def start_c(self):
        self.c_copy().start()

    def take_x(self):
        self.x_copy().wait_recv()
        span = self.side_span(self.p.x)
        self.held[:, :, :, span] = self.held[:, :, :, span] + self.from_x[...]

    def take_y(self):
        p = self.p
        self.y_copy().wait_recv()
        span = self.main_span
        self.held[:, :, p.y, span] = self.held[:, :, p.y, span] + self.from_y[...]

    def start_z(self):
        self.each_z(lambda copy: copy.start(), None, lambda copy: copy.start())

    def take_relay(self):
        def late(copy, target):
            self.relay_copy(True).wait_recv()
            p = self.p
            span = self.main_span
            self.held[:, target, p.y, span] = self.held[:, target, p.y, span] + self.relayed[...]
            copy.start()

        self.each_z(None, late, None)

    def take_z(self):
        p = self.p
        self.z_copy(2).wait_recv()
        if self.relay:

            @pl.when(p.z != 0)
            def _():
                self.z_copy(1).wait_recv()

            @pl.when(p.z != 3)
            def _():
                self.z_copy(3).wait_recv()

        else:
            self.z_copy(1).wait_recv()
            self.z_copy(3).wait_recv()

        total = self.held[:, p.z, p.y, self.main_span].astype(jnp.float32)
        for step in range(1, p.depth):
            total += self.from_z[step - 1].astype(jnp.float32)
        self.done[...] = total.astype(LOW)

    def take_last(self):
        p = self.p
        self.last_copy().wait_recv()
        side, both = self.side, self.main - self.side
        for number, (out, mat, column) in enumerate(self.outs):
            columns = slice(column, column + self.width)
            if side:
                out[mat, self.side_span(p.x), columns] = self.done[number, self.span(both * p.x, side)].astype(
                    jnp.float32
                )
                out[mat, self.side_span(1 - p.x), columns] = self.other[
                    number, self.span(both * (1 - p.x), side)
                ].astype(jnp.float32)
            out[mat, side : side + both, columns] = self.done[number, self.span(side * (1 - p.x), both)].astype(
                jnp.float32
            ) + self.other[number, self.span(side * p.x, both)].astype(jnp.float32)

    def end(self):
        def wait(copy, target=None):
            copy.wait_send()

        if self.side:
            self.x_copy().wait_send()
        self.y_copy().wait_send()
        self.each_z(wait, wait, wait)
        self.last_copy().wait_send()


class Block:
    def __init__(self, out, pieces, rows, side, width=256, relay=True):
        self.out, self.pieces, self.rows, self.side = out, tuple(pieces), rows, side
        self.width, self.relay = width, relay

    @property
    def ring(self):
        return self.rows, self.width


def block_list():
    found = [Block(3, [(0, 0)], 128, 0, 256, False)] + [Block(3, [(0, c)], 128, 32) for c in (256, 512)]
    found += [Block(2, [(m, first + c) for c in range(0, 1024, 256)], 48, 16) for m in (0, 1) for first in (0, 1024)]
    found += [Block(1, [(3, c) for c in range(0, 768, 256)], 48, 0)]
    found += [Block(1, [(m, c) for m in range(3)], 48, 16) for c in (0, 256, 512)]
    found += [Block(0, [(3, c) for c in range(0, 768, 256)], 48, 0)]
    found += [Block(0, [(m, c) for m in range(3)], 48, 16, 128, False) for c in range(0, 768, 128)]
    return found


SCATTER_LAYOUT = block_list()
RINGS = {(128, 256): (2, 1), (48, 256): (3, 4), (48, 128): (2, 3)}


def scatter_buffers(depth):
    bufs = []
    for block in SCATTER_LAYOUT:
        subs, rows, side, width = len(block.pieces), block.rows, block.side, block.width
        main = rows - side
        bufs += [
            pltpu.VMEM((subs, depth, 2, rows, width), LOW),
            pltpu.VMEM((subs, depth, 2, side, width) if side else (16, 128), LOW),
            pltpu.VMEM((subs, depth, main, width), LOW),
            pltpu.VMEM((depth - 1, subs, main, width), LOW),
            pltpu.VMEM((subs, main, width), LOW),
            pltpu.VMEM((subs, main, width), LOW),
            pltpu.VMEM((subs, main, width), LOW),
        ]
    return bufs


def staging_buffers(depth):
    return [
        pltpu.VMEM((slots, subs, depth, 2, rows, width), LOW) for (rows, width), (slots, subs) in RINGS.items()
    ]


class K0:
    x0 = Spec(TOKENS, WIDTH)


class B:
    biast = Spec(TOKENS, TOKENS, dtype=jnp.float32)
    dlow = Spec(TOKENS, WIDTH)
    do = Spec(TOKENS, WIDTH)
    dq = Spec(TOKENS, WIDTH)
    dk = Spec(TOKENS, WIDTH)
    dv = Spec(TOKENS, WIDTH)
    dh = Spec(TOKENS, WIDTH, dtype=jnp.float32)
    mem_sum = Spec(PATCHES, WIDTH, dtype=jnp.float32)
    mem_low = Spec(2, PATCHES, WIDTH)
    mem_got = Spec(2, PATCHES, WIDTH)
    gains = Spec(8, WIDTH, dtype=jnp.float32)
    gain_got = Spec(6, 8, WIDTH, dtype=jnp.float32)
    gain_row = Spec(1, WIDTH, dtype=jnp.float32)


def attend_back_pair(pair, q, k, v, do, lse, bias, dq, dk, dv):
    span = pair_span(pair)
    q_two, k_two, v_two, do_two = q[:, span], k[:, span], v[:, span], do[:, span]
    low_q = lax.broadcasted_iota(jnp.int32, q_two.shape, 1) < HEAD_DIM
    low_k = lax.broadcasted_iota(jnp.int32, k_two.shape, 1) < HEAD_DIM
    scale = HEAD_DIM ** (-0.5)
    grads = []
    for half in range(2):
        mine = low_q if half == 0 else ~low_q
        scores = dot(k_two, jnp.where(mine, q_two, jnp.zeros_like(q_two)), 1, 1) * scale
        if bias is not None:
            scores = scores + bias[...]
        head = 2 * pair + half
        shares = jnp.exp(scores - lse[head : head + 1, :])
        p_grad = dot(v_two, jnp.where(mine, do_two, jnp.zeros_like(do_two)), 1, 1)
        along = jnp.sum(shares * p_grad, axis=0, keepdims=True)
        s_low = (shares * (p_grad - along)).astype(LOW)
        v_grad = dot(shares.astype(LOW), do_two)
        k_grad = dot(s_low, q_two) * scale
        q_grad = dot(s_low, k_two, 0, 0) * scale
        grads.append((q_grad, k_grad, v_grad))
    dq[:, span] = jnp.where(low_q, grads[0][0], grads[1][0]).astype(LOW)
    count = k_two.shape[0]
    dk[:count, span] = jnp.where(low_k, grads[0][1], grads[1][1]).astype(LOW)
    dv[:count, span] = jnp.where(low_k, grads[0][2], grads[1][2]).astype(LOW)


class Total:
    def __init__(self, place, value, got, send, recv):
        self.p, self.value, self.got, self.send, self.recv = place, value, got, send, recv

    def copy(self, slot):
        p = self.p
        device = (p.across_core, p.across_x, p.across_y, *(p.z_ahead(step) for step in (1, 2, 3)))[slot]
        return remote(self.value, self.got.at[slot], self.send.at[slot], self.recv.at[slot], device)

    def start(self, slots):
        for slot in slots:
            self.copy(slot).start()

    def take(self, slots):
        for slot in slots:
            self.copy(slot).wait()
        total = self.value[...]
        for slot in slots:
            total = total + self.got[slot]
        self.value[...] = total


def backward_kernel(depth, row_count, refs):
    (dy, segments, padding, images) = refs[:4]
    names = PASSED + [K0.x0]
    given = dict(zip(names, refs[4:]))
    rest = refs[4 + len(names) :]
    outs, (x_grad, mem_grad, gain_grad) = rest[:4], rest[4:7]
    rest = rest[7:]
    kept = dict(zip(names, rest))
    rest = rest[len(names) :]
    local, rest = dict(zip(specs(B), rest)), rest[len(specs(B)) :]
    staging, rest = dict(zip(RINGS, rest)), rest[len(RINGS) :]
    count = len(SCATTER_LAYOUT)
    bufs, (load_sem, send_sem, recv_sem, row_sem, total_send, total_recv) = rest[: 7 * count], rest[7 * count :]
    place = Place(depth)
    rows = Rows(place, row_count)
    core = place.core
    plan = Plan(6, 1.5)

    def load(*chosen):
        for name in chosen:
            number = names.index(name)
            pltpu.make_async_copy(given[name], kept[name], load_sem.at[number]).start()

    def loaded(*chosen):
        for name in chosen:
            number = names.index(name)
            pltpu.make_async_copy(given[name], kept[name], load_sem.at[number]).wait()

    blocks, rings = [], {key: [] for key in RINGS}
    for number, spec in enumerate(SCATTER_LAYOUT):
        ring, slots = rings[spec.ring], RINGS[spec.ring][0]
        staged = staging[spec.ring].at[len(ring) % slots, 0 : len(spec.pieces)]
        block = Scatter(
            place,
            (staged,) + tuple(bufs[7 * number : 7 * number + 7]),
            [(outs[spec.out], mat, column) for mat, column in spec.pieces],
            spec,
            [send_sem.at[number], recv_sem.at[number]],
        )
        block.before = ring[-slots] if len(ring) >= slots else None
        ring.append(block)
        blocks.append(block)

    near_start, near_arrive, near_end = pass_rows(
        rows, local[B.mem_low].at[1], local[B.mem_got].at[1], -1, (row_sem.at[0], row_sem.at[1])
    )
    far_start, far_arrive, far_end = pass_rows(
        rows, local[B.mem_low].at[0], local[B.mem_got].at[0], -2, (row_sem.at[2], row_sem.at[3])
    )
    total = Total(place, local[B.gains], local[B.gain_got], total_send, total_recv)

    def half(left, which):
        part = kept[left][:, :, which]
        return part.reshape(-1, part.shape[-1])

    def products(block, terms, which):
        found = []
        for left, right, first, width in terms:
            value = dot(half(left, which), right[: kept[left].shape[-1], first : first + width])
            value = value.reshape(depth, 2, -1, width)
            found += [value[..., c : c + block.width] for c in range(0, width, block.width)]
        return found

    def size(block, what):
        each = {
            "c": 8 * block.rows,
            "x": 8 * block.side,
            "y": 4 * block.main,
            "z": (2.5 if block.relay else 4) * block.main,
            "r": block.main,
            "l": block.main,
        }
        return len(block.outs) * block.width * 2 * each[what]

    def give(number, terms):
        block = blocks[number]

        def run():
            if block.before is not None:
                block.before.c_copy().wait_send()
                block.before.sent = True
            for sub, value in enumerate(products(block, terms, 1 - core)):
                block.staged[sub] = value.astype(LOW)
            block.start_c()

        return run

    def hold(number, terms):
        block = blocks[number]

        def run():
            block.c_copy().wait_recv()
            for sub, value in enumerate(products(block, terms, core)):
                block.held[sub] = (value + block.held[sub].astype(jnp.float32)).astype(LOW)

            def to_y():
                if block.side:
                    block.take_x()
                plan.send("y", number, size(block, "y"), lambda: block.y_copy().start(), to_z)

            def to_z():
                block.take_y()
                plan.send("z", number, size(block, "z"), block.start_z, to_relay)

            def to_relay():
                if not block.relay:
                    to_last()
                    return
                block.take_relay()
                plan.later(size(block, "r") / plan.rate["z"] + plan.latency, to_last)

            def to_last():
                block.take_z()
                plan.send("x", number, size(block, "l"), lambda: block.last_copy().start(), block.take_last)

            if block.side:
                plan.send("x", number, size(block, "x"), lambda: block.x_copy().start(), to_y)
            else:
                to_y()

        return run

    def make_bias():
        seg_k, seg_q = as_column(segments[...])[:, 0:1], segments[...].astype(jnp.float32)
        real = as_column(padding[...])[:, 0:1] == 1.0
        key = lax.broadcasted_iota(jnp.int32, (TOKENS, TOKENS), 0)
        query = lax.broadcasted_iota(jnp.int32, (TOKENS, TOKENS), 1)
        allowed = (seg_q == seg_k) & (key <= query) & (real | (key == query))
        local[B.biast][...] = jnp.where(allowed, 0.0, -1e30)

    def cross_begin():
        local[B.dlow][...] = kept[K.dx2][...].astype(LOW)

    def cross_do():
        local[B.do][...] = dot(local[B.dlow][...], kept[W.w_cross][3], 1, 1).astype(LOW)

    def cross_pair(pair):
        def run():
            attend_back_pair(
                pair,
                kept[K.q2],
                kept[K.k2],
                kept[K.v2],
                local[B.do],
                kept[K.lse2],
                None,
                local[B.dq],
                local[B.dk],
                local[B.dv],
            )

        return run

    def self_pair(pair):
        def run():
            attend_back_pair(
                pair,
                kept[K.q1],
                kept[K.k1],
                kept[K.v1],
                local[B.do],
                kept[K.lse1],
                local[B.biast],
                local[B.dq],
                local[B.dk],
                local[B.dv],
            )

        return run

    def mem_back():
        value = dot(local[B.dk][:PATCHES], kept[W.w_cross][1], 1, 1)
        value += dot(local[B.dv][:PATCHES], kept[W.w_cross][2], 1, 1)
        local[B.mem_sum][...] = value
        local[B.mem_low][0] = value.astype(LOW)
        far_start()

    def mem_far():
        far_arrive()
        got = jnp.where(row_offset(images, rows.row + 2, row_count) >= 2, local[B.mem_got][0].astype(jnp.float32), 0.0)
        value = local[B.mem_sum][...] + got
        local[B.mem_sum][...] = value
        local[B.mem_low][1] = value.astype(LOW)
        near_start()

    def mem_near():
        near_arrive()
        got = jnp.where(row_offset(images, rows.row + 1, row_count) == 1, local[B.mem_got][1].astype(jnp.float32), 0.0)
        mem_grad[...] = jnp.where(row_offset(images, rows.row, row_count) == 0, local[B.mem_sum][...] + got, 0.0)

    def cross_dh():
        local[B.dh][...] = dot(local[B.dq][...], kept[W.w_cross][0], 1, 1)

    def cross_norm():
        norm_back_rows(kept[K.x1], kept[K.gain][1:2], local[B.dh], kept[K.dx2], kept[K.dx2], local[B.gain_row])
        local[B.gains][1:2, :] = local[B.gain_row][...]
        local[B.dlow][...] = kept[K.dx2][...].astype(LOW)

    def self_do():
        local[B.do][...] = dot(local[B.dlow][...], kept[W.w_self][3], 1, 1).astype(LOW)

    def self_dh_first():
        local[B.dh][...] = dot(local[B.dq][...], kept[W.w_self][0], 1, 1)

    def self_dh_second():
        local[B.dh][...] += dot(local[B.dk][...], kept[W.w_self][1], 1, 1)

    def self_dh_third():
        local[B.dh][...] += dot(local[B.dv][...], kept[W.w_self][2], 1, 1)

    def self_norm():
        norm_back_rows(kept[K0.x0], kept[K.gain][0:1], local[B.dh], kept[K.dx2], x_grad, local[B.gain_row])
        local[B.gains][0:1, :] = local[B.gain_row][...]
        local[B.gains][2:3, :] = kept[K.gain3][...]
        total.start((0,))

    def load_cross():
        load(K.dx2, W.w_cross, K.o2t, K.q2, K.k2, K.v2, K.lse2, K.h2t, K.memt, K.x1, K.gain, K.gain3)

    def load_self():
        load(W.w_self, K.o1t, K.q1, K.k1, K.v1, K.lse1, K.h1t, K0.x0)

    do_low, dq, dk, dv = local[B.dlow], local[B.dq], local[B.dk], local[B.dv]
    out_terms = [[(K.hiddent, dy, 256 * j, 256)] for j in range(3)]
    in_terms = [[(K.h3t, kept[name], first, 1024)] for name in (K.dgate, K.dup) for first in (0, 1024)]

    load(K.hiddent, K.h3t, K.dgate, K.dup)
    local[B.gains][...] = jnp.zeros_like(local[B.gains])
    for block in blocks:
        block.sent = False
        block.blank()
    greet_all(place, rows)
    load_cross()
    loaded(K.hiddent)
    plan.work(0.8, give(0, out_terms[0]))
    plan.work(0.8, give(1, out_terms[1]))
    plan.work(0.9, hold(0, out_terms[0]))
    plan.work(0.8, give(2, out_terms[2]))
    plan.work(0.9, hold(1, out_terms[1]))
    loaded(K.h3t, K.dgate, K.dup)
    load_self()
    plan.work(1.0, give(3, in_terms[0]))
    plan.work(0.9, hold(2, out_terms[2]))
    for j in range(1, 4):
        plan.work(1.0, give(3 + j, in_terms[j]))
        plan.work(1.1, hold(2 + j, in_terms[j - 1]))
    loaded(K.dx2, W.w_cross, K.o2t, K.q2, K.k2, K.v2, K.lse2, K.h2t, K.memt, K.x1, K.gain, K.gain3)
    plan.work(0.3, cross_begin)
    o_terms = [(K.o2t, do_low, 0, 768)]
    plan.work(0.8, give(7, o_terms))
    plan.work(1.1, hold(6, in_terms[3]))
    plan.work(0.8, cross_do)
    plan.work(0.9, hold(7, o_terms))

    def attention(pair_work, first, lefts, pairs):
        previous = None
        width = 128 * pairs
        for group in range(6 // pairs):
            for pair in range(pairs * group, pairs * group + pairs):
                plan.work(1.4, pair_work(pair))
            terms = [(left, right, width * group, width) for left, right in zip(lefts, (dq, dk, dv))]
            plan.work(0.5 * pairs, give(first + group, terms))
            if previous is not None:
                plan.work(0.5 * pairs, hold(*previous))
            previous = (first + group, terms)
        return previous

    previous = attention(cross_pair, 8, (K.h2t, K.memt, K.memt), 2)
    plan.work(1.5, mem_back)
    plan.work(1.0, hold(*previous))
    plan.work(0.8, cross_dh)
    plan.work(1.2, cross_norm)
    loaded(W.w_self, K.o1t, K.q1, K.k1, K.v1, K.lse1, K.h1t, K0.x0)
    o_terms = [(K.o1t, do_low, 0, 768)]
    plan.work(0.8, give(11, o_terms))
    plan.work(0.3, mem_far)
    plan.work(0.8, self_do)
    plan.work(0.5, make_bias)
    plan.work(0.9, hold(11, o_terms))
    previous = attention(self_pair, 12, (K.h1t, K.h1t, K.h1t), 1)
    plan.work(0.8, self_dh_first)
    plan.work(1.0, hold(*previous))
    plan.work(0.8, self_dh_second)
    plan.work(0.8, self_dh_third)
    plan.work(0.5, mem_near)
    plan.work(1.5, self_norm)

    def total_step(slots, after):
        def run():
            total.take(slots)
            if after:
                total.start(after[0])
                plan.later(2.5, total_step(after[0], after[1:]))
            else:
                share = gain_grad.shape[1]
                turned = pltpu.roll(local[B.gains][...], (row_count // 2 - place.wide) * share, 1)
                gain_grad[...] = turned[0 : gain_grad.shape[0], 0:share]

        return run

    plan.later(2.5, total_step((0,), ((1,), (2,), (3, 4, 5))))
    while plan.busy():
        plan.step()
    for block in blocks:
        if not block.sent:
            block.c_copy().wait_send()
        block.end()
    near_end()
    far_end()


def backward(kept, layer_input, cotangent, segments, padding, image_of_row, share):
    wide = lax.axis_size("wide")
    depth = wide // 4

    def owners(array):
        return array.reshape(depth, 2, 2, -1, array.shape[-1])

    names = PASSED + [K0.x0]
    given = {**kept, K0.x0: layer_input}
    for name in (K.h1t, K.o1t, K.h2t, K.o2t, K.memt, K.h3t, K.hiddent):
        given[name] = owners(given[name])
    arrays = [given[name] for name in names]
    vmem, anywhere, smem = (pl.BlockSpec(memory_space=space) for space in (pltpu.VMEM, pl.ANY, pltpu.SMEM))
    outs = [
        ((4, WIDTH // wide, WIDTH), jnp.float32),
        ((4, WIDTH // wide, WIDTH), jnp.float32),
        ((2, WIDTH // wide, HIDDEN), jnp.float32),
        ((1, HIDDEN // wide, WIDTH), jnp.float32),
        ((TOKENS, WIDTH), jnp.float32),
        ((PATCHES, WIDTH), jnp.float32),
        ((3, share), jnp.float32),
    ]
    count = len(SCATTER_LAYOUT)
    return pl.pallas_call(
        lambda *refs: backward_kernel(depth, 2 * wide, refs),
        out_shape=[jax.ShapeDtypeStruct(*o) for o in outs],
        in_specs=[vmem] * 3 + [smem] + [anywhere] * len(arrays),
        out_specs=[vmem] * len(outs),
        scratch_shapes=[pltpu.VMEM(a.shape, a.dtype) for a in arrays]
        + [spec.scratch() for spec in specs(B)]
        + staging_buffers(depth)
        + scatter_buffers(depth)
        + [
            pltpu.SemaphoreType.DMA((len(arrays),)),
            pltpu.SemaphoreType.DMA((count, 8)),
            pltpu.SemaphoreType.DMA((count, 8)),
            pltpu.SemaphoreType.DMA((4,)),
            pltpu.SemaphoreType.DMA((6,)),
            pltpu.SemaphoreType.DMA((6,)),
        ],
        compiler_params=pltpu.CompilerParams(
            collective_id=1, has_side_effects=True, vmem_limit_bytes=63 * 2**20
        ),
        name="backward",
    )(cotangent, segments, padding, image_of_row, *arrays)


def finish(*arrays):
    count = len(arrays)

    def kernel(*refs):
        sems = refs[-1]
        loads = [pltpu.make_async_copy(refs[n], refs[2 * count + n], sems.at[0, n]) for n in range(count)]
        stores = [pltpu.make_async_copy(refs[2 * count + n], refs[count + n], sems.at[1, n]) for n in range(count)]
        for load in loads:
            load.start()
        for load, store in zip(loads, stores):
            load.wait()
            store.start()
        for store in stores:
            store.wait()

    anywhere = pl.BlockSpec(memory_space=pl.ANY)
    return pl.pallas_call(
        kernel,
        out_shape=[jax.ShapeDtypeStruct(a.shape, a.dtype) for a in arrays],
        in_specs=[anywhere] * count,
        out_specs=[anywhere] * count,
        scratch_shapes=[pltpu.VMEM(a.shape, a.dtype) for a in arrays] + [pltpu.SemaphoreType.DMA((2, count))],
        compiler_params=pltpu.CompilerParams(vmem_limit_bytes=60 * 2**20),
        name="finish",
    )(*arrays)


def plain_gather(self_weights, cross_weights, mlp_in, mlp_out, gains):
    return (
        lax.all_gather(self_weights, "wide", axis=1, tiled=True),
        lax.all_gather(cross_weights, "wide", axis=1, tiled=True),
        lax.all_gather(mlp_in, "wide", axis=1, tiled=True),
        lax.all_gather(mlp_out, "wide", axis=0, tiled=True),
        lax.all_gather(gains, "wide", axis=1, tiled=True),
    )


def plain_scatter(*grads):
    outs = []
    for grad, axis in zip(grads, (1, 1, 1, 0, 1)):
        piece = lax.psum_scatter(grad, ("wide", "narrow"), scatter_dimension=axis, tiled=True)
        outs.append(lax.all_gather(piece.astype(jnp.bfloat16), "narrow", axis=axis, tiled=True).astype(jnp.float32))
    return tuple(outs)


def by_kernel(self_weights):
    return lax.axis_size("wide") == 16 and lax.axis_size("narrow") == 2 and self_weights.shape[1] % 48 == 0


def plain_device(
    layer_input,
    memory,
    cotangent,
    segment_ids,
    padding,
    image_of_row,
    self_weights,
    cross_weights,
    mlp_in,
    mlp_out,
    gains,
):
    self_full, cross_full, in_full, out_full, gain_full = plain_gather(
        self_weights, cross_weights, mlp_in, mlp_out, gains
    )
    gain_float = gain_full.astype(jnp.float32)
    x_zero = layer_input[0].astype(jnp.float32)
    seg_row = segment_ids[0]
    pad_row = padding[0]
    seq_len = x_zero.shape[0]
    position = jnp.arange(seq_len)
    allowed = (
        (seg_row[:, None] == seg_row[None, :])
        & (position[None, :] <= position[:, None])
        & ((pad_row[None, :] == 1) | (position[:, None] == position[None, :]))
    )
    h_one = rms_norm(x_zero, gain_float[0]).astype(jnp.bfloat16)
    q_self = linear(h_one, self_full[0]).astype(jnp.bfloat16)
    k_self = linear(h_one, self_full[1]).astype(jnp.bfloat16)
    v_self = linear(h_one, self_full[2]).astype(jnp.bfloat16)
    self_mix, self_lse = forward_heads(q_self, k_self, v_self, allowed)
    x_one = x_zero + linear(self_mix, self_full[3])
    row_ids = jnp.arange(image_of_row.shape[0])
    starts = jnp.sum(image_of_row[None, :] < image_of_row[:, None], axis=1)
    offsets = row_ids - starts
    my_index = lax.axis_index(("wide", "narrow"))
    my_offset = jnp.sum(jnp.where(row_ids == my_index, offsets, 0))
    own_patches = memory[0]
    memory_use = own_patches
    for distance in (1, 2, 3):
        arrived = shifted(own_patches, ("wide", "narrow"), distance)
        memory_use = jnp.where(my_offset == distance, arrived, memory_use)
    h_two = rms_norm(x_one, gain_float[1]).astype(jnp.bfloat16)
    q_cross = linear(h_two, cross_full[0]).astype(jnp.bfloat16)
    k_cross = linear(memory_use, cross_full[1]).astype(jnp.bfloat16)
    v_cross = linear(memory_use, cross_full[2]).astype(jnp.bfloat16)
    cross_mix, cross_lse = forward_heads(q_cross, k_cross, v_cross, None)
    x_two = x_one + linear(cross_mix, cross_full[3])
    h_three = rms_norm(x_two, gain_float[2]).astype(jnp.bfloat16)
    gate_act = linear(h_three, in_full[0])
    up_act = linear(h_three, in_full[1])
    hidden = gated_product(gate_act, up_act).astype(jnp.bfloat16)
    result = x_two + linear(hidden, out_full)
    out_low = cotangent[0]
    out_grad_w = contract_rows(hidden, out_low)
    hidden_grad = times_transposed(out_low, out_full)
    _, pullback = jax.vjp(gated_product, gate_act, up_act)
    gate_grad, up_grad = pullback(hidden_grad)
    gate_low = gate_grad.astype(jnp.bfloat16)
    up_low = up_grad.astype(jnp.bfloat16)
    in_grad = jnp.stack([contract_rows(h_three, gate_low), contract_rows(h_three, up_low)])
    h_three_grad = times_transposed(gate_low, in_full[0]) + times_transposed(up_low, in_full[1])
    _, pullback = jax.vjp(rms_norm, x_two, gain_float[2])
    x_two_norm, gain_three = pullback(h_three_grad)
    x_two_grad = out_low.astype(jnp.float32) + x_two_norm
    cross_out_low = x_two_grad.astype(jnp.bfloat16)
    cross_o_grad = contract_rows(cross_mix, cross_out_low)
    cross_mix_grad = times_transposed(cross_out_low, cross_full[3]).astype(jnp.bfloat16)
    q_cross_grad, k_cross_grad, v_cross_grad = backward_heads(
        q_cross, k_cross, v_cross, cross_mix_grad, cross_lse, None
    )
    cross_grad = jnp.stack(
        [
            contract_rows(h_two, q_cross_grad),
            contract_rows(memory_use, k_cross_grad),
            contract_rows(memory_use, v_cross_grad),
            cross_o_grad,
        ]
    )
    mem_grad = times_transposed(k_cross_grad, cross_full[1]) + times_transposed(
        v_cross_grad, cross_full[2]
    )
    h_two_grad = times_transposed(q_cross_grad, cross_full[0])
    _, pullback = jax.vjp(rms_norm, x_one, gain_float[1])
    x_one_norm, gain_two = pullback(h_two_grad)
    x_one_grad = x_two_grad + x_one_norm
    self_out_low = x_one_grad.astype(jnp.bfloat16)
    self_o_grad = contract_rows(self_mix, self_out_low)
    self_mix_grad = times_transposed(self_out_low, self_full[3]).astype(jnp.bfloat16)
    q_self_grad, k_self_grad, v_self_grad = backward_heads(
        q_self, k_self, v_self, self_mix_grad, self_lse, allowed
    )
    self_grad = jnp.stack(
        [
            contract_rows(h_one, q_self_grad),
            contract_rows(h_one, k_self_grad),
            contract_rows(h_one, v_self_grad),
            self_o_grad,
        ]
    )
    h_one_grad = (
        times_transposed(q_self_grad, self_full[0])
        + times_transposed(k_self_grad, self_full[1])
        + times_transposed(v_self_grad, self_full[2])
    )
    _, pullback = jax.vjp(rms_norm, x_zero, gain_float[0])
    x_zero_norm, gain_one = pullback(h_one_grad)
    x_grad = x_one_grad + x_zero_norm
    mem_summed = jnp.where(my_offset == 0, mem_grad, 0.0)
    for distance in (1, 2, 3):
        arrived = shifted(mem_grad.astype(jnp.bfloat16), ("wide", "narrow"), -distance).astype(
            mem_grad.dtype
        )
        neighbour = jnp.sum(jnp.where(row_ids == my_index + distance, offsets, 0))
        mem_summed = mem_summed + jnp.where(neighbour == distance, arrived, 0.0)
    gain_grad = jnp.stack([gain_one, gain_two, gain_three])
    reduced = plain_scatter(self_grad, cross_grad, in_grad, out_grad_w, gain_grad)
    return (
        result.astype(jnp.bfloat16)[None],
        x_grad[None],
        mem_summed[None],
        reduced[0],
        reduced[1],
        reduced[2],
        reduced[3],
        reduced[4],
    )


def kernel_device(
    layer_input,
    memory,
    cotangent,
    segment_ids,
    padding,
    image_of_row,
    self_weights,
    cross_weights,
    mlp_in,
    mlp_out,
    gains,
):
    result, kept = forward(
        layer_input[0],
        cotangent[0],
        memory[0],
        segment_ids,
        padding,
        image_of_row,
        gains,
        self_weights,
        cross_weights,
        mlp_in,
        mlp_out,
    )
    self_grad, cross_grad, in_grad, out_grad, x_grad, mem_grad, gain_grad, result = finish(
        *backward(kept, layer_input[0], cotangent[0], segment_ids, padding, image_of_row, gains.shape[1]),
        result,
    )
    return (result[None], x_grad[None], mem_grad[None], self_grad, cross_grad, in_grad, out_grad[0], gain_grad)


def on_device(
    layer_input,
    memory,
    cotangent,
    segment_ids,
    padding,
    image_of_row,
    self_weights,
    cross_weights,
    mlp_in,
    mlp_out,
    gains,
):
    run = kernel_device if by_kernel(self_weights) else plain_device
    return run(
        layer_input,
        memory,
        cotangent,
        segment_ids,
        padding,
        image_of_row,
        self_weights,
        cross_weights,
        mlp_in,
        mlp_out,
        gains,
    )


def solution(mesh):
    in_specs = (
        P(("wide", "narrow"), None, None),
        P(("wide", "narrow"), None, None),
        P(("wide", "narrow"), None, None),
        P(("wide", "narrow"), None),
        P(("wide", "narrow"), None),
        P(),
        P(None, "wide", None),
        P(None, "wide", None),
        P(None, "wide", None),
        P("wide", None),
        P(None, "wide"),
    )
    out_specs = (
        P(("wide", "narrow"), None, None),
        P(("wide", "narrow"), None, None),
        P(("wide", "narrow"), None, None),
        P(None, "wide", None),
        P(None, "wide", None),
        P(None, "wide", None),
        P("wide", None),
        P(None, "wide"),
    )
    return jax.shard_map(
        on_device, mesh=mesh, in_specs=in_specs, out_specs=out_specs, check_vma=False
    )
```

```python
import functools

import jax
import jax.numpy as jnp
from jax import lax
from jax.experimental import pallas as pl
from jax.experimental.pallas import tpu as pltpu
from jax.sharding import PartitionSpec as P

HEAD_DIM = 64


EPSILON = 1e-06


def shifted(value, axis, steps):
    count = lax.axis_size(axis)
    first, last = (max(0, -steps), min(count, count - steps))
    return lax.ppermute(value, axis, [(source, source + steps) for source in range(first, last)])


def rms_norm(v, g):
    return v * lax.rsqrt(jnp.mean(v * v, axis=-1, keepdims=True) + EPSILON) * g


def contract_rows(a, b):
    return lax.dot_general(a, b, (((0,), (0,)), ((), ())), preferred_element_type=jnp.float32)


def times_transposed(a, w):
    return lax.dot_general(a, w, (((1,), (1,)), ((), ())), preferred_element_type=jnp.float32)


def linear(a, w):
    return jnp.dot(a, w, preferred_element_type=jnp.float32)


def head_scores(q_part, k_part, allowed):
    scores = jnp.einsum(
        "qhd,khd->hqk", q_part, k_part, preferred_element_type=jnp.float32
    ) * HEAD_DIM ** (-0.5)
    if allowed is not None:
        scores = jnp.where(allowed[None], scores, -1e30)
    return scores


def split_heads(a, head_start):
    return a[:, head_start * HEAD_DIM : (head_start + 4) * HEAD_DIM].reshape(
        a.shape[0], 4, HEAD_DIM
    )


def forward_heads(q, k, v, allowed):
    seq_len = q.shape[0]
    head_count = q.shape[1] // HEAD_DIM
    pieces = []
    log_sums = []
    for head_start in range(0, head_count, 4):
        q_part = split_heads(q, head_start)
        k_part = split_heads(k, head_start)
        v_part = split_heads(v, head_start)
        scores = head_scores(q_part, k_part, allowed)
        highest = jnp.max(scores, axis=-1, keepdims=True)
        powers = jnp.exp(scores - highest)
        summed = jnp.sum(powers, axis=-1, keepdims=True)
        shares = (powers / summed).astype(jnp.bfloat16)
        mixed = jnp.einsum("hqk,khd->qhd", shares, v_part, preferred_element_type=jnp.float32)
        pieces.append(mixed.reshape(seq_len, -1))
        log_sums.append(highest + jnp.log(summed))
    return (jnp.concatenate(pieces, axis=1).astype(jnp.bfloat16), jnp.concatenate(log_sums, axis=0))


def backward_heads(q, k, v, mix_grad, log_sum, allowed):
    seq_len = q.shape[0]
    head_count = q.shape[1] // HEAD_DIM
    q_pieces = []
    k_pieces = []
    v_pieces = []
    for head_start in range(0, head_count, 4):
        q_part = split_heads(q, head_start)
        k_part = split_heads(k, head_start)
        v_part = split_heads(v, head_start)
        o_part = split_heads(mix_grad, head_start)
        scores = head_scores(q_part, k_part, allowed)
        shares = jnp.exp(scores - log_sum[head_start : head_start + 4])
        v_grad = jnp.einsum(
            "hqk,qhd->khd", shares.astype(jnp.bfloat16), o_part, preferred_element_type=jnp.float32
        )
        p_grad = jnp.einsum("qhd,khd->hqk", o_part, v_part, preferred_element_type=jnp.float32)
        s_grad = shares * (p_grad - jnp.sum(shares * p_grad, axis=-1, keepdims=True))
        s_low = s_grad.astype(jnp.bfloat16)
        q_grad = jnp.einsum(
            "hqk,khd->qhd", s_low, k_part, preferred_element_type=jnp.float32
        ) * HEAD_DIM ** (-0.5)
        k_grad = jnp.einsum(
            "hqk,qhd->khd", s_low, q_part, preferred_element_type=jnp.float32
        ) * HEAD_DIM ** (-0.5)
        q_pieces.append(q_grad.reshape(seq_len, -1))
        k_pieces.append(k_grad.reshape(k.shape[0], -1))
        v_pieces.append(v_grad.reshape(k.shape[0], -1))
    return (
        jnp.concatenate(q_pieces, axis=1).astype(jnp.bfloat16),
        jnp.concatenate(k_pieces, axis=1).astype(jnp.bfloat16),
        jnp.concatenate(v_pieces, axis=1).astype(jnp.bfloat16),
    )


def gated_product(gate_act, up_act):
    return jax.nn.gelu(gate_act, approximate=True) * up_act


MESH = pl.DeviceIdType.MESH


class Place:
    def __init__(self, depth):
        self.depth = depth
        self.wide = lax.axis_index("wide")
        self.x = lax.axis_index("narrow")
        self.core = self.wide % 2
        self.y = (self.wide // 2) % 2
        self.z = self.wide // 4

    def shard(self, z, y, core):
        return z * 4 + y * 2 + core

    def z_ahead(self, step):
        return (self.shard((self.z + step) % self.depth, self.y, self.core), self.x)

    def z_behind(self, step):
        return (self.z + self.depth - step) % self.depth

    @property
    def across_x(self):
        return (self.wide, 1 - self.x)

    @property
    def across_y(self):
        return (self.shard(self.z, 1 - self.y, self.core), self.x)

    @property
    def across_core(self):
        return (self.shard(self.z, self.y, 1 - self.core), self.x)

    def greet(self):
        barrier = pltpu.get_barrier_semaphore()
        others = [self.across_x, self.across_y, self.across_core]
        others += [self.z_ahead(step) for step in range(1, self.depth)]
        for other in others:
            pl.semaphore_signal(barrier, inc=1, device_id=other, device_id_type=MESH)
        pl.semaphore_wait(barrier, len(others))


def remote(src, dst, send, recv, device):
    return pltpu.make_async_remote_copy(
        src_ref=src, dst_ref=dst, send_sem=send, recv_sem=recv, device_id=device, device_id_type=MESH
    )


class Plan:
    def __init__(self, slack=2.5, latency=1.5):
        self.now = 0.0
        self.slack = slack
        self.latency = latency
        self.rate = {"c": 400e3, "x": 50e3, "y": 50e3, "z": 50e3}
        self.free = dict.fromkeys(self.rate, 0.0)
        self.queues = {link: [] for link in self.rate}
        self.flying = []
        self.serial = 0

    def send(self, link, rank, size, start, arrive, cost=0.2):
        self.serial += 1
        self.queues[link].append((rank, self.serial, size, start, arrive, cost))

    def later(self, delay, arrive, cost=0.2):
        self.serial += 1
        self.flying.append((self.now + delay, self.serial, cost, arrive))

    def issue(self):
        for link, queue in self.queues.items():
            while queue and self.free[link] <= self.now + self.slack:
                first = min(queue, key=lambda q: q[:2])
                queue.remove(first)
                _, serial, size, start, arrive, cost = first
                start()
                self.now += 0.03
                self.free[link] = max(self.free[link], self.now) + size / self.rate[link]
                if arrive is not None:
                    self.flying.append((self.free[link] + self.latency, serial, cost, arrive))

    def drain(self):
        self.issue()
        while self.flying:
            first = min(self.flying, key=lambda f: f[:2])
            if first[0] > self.now:
                break
            self.flying.remove(first)
            first[3]()
            self.now += first[2]
            self.issue()

    def busy(self):
        return bool(self.flying) or any(self.queues.values())

    def step(self):
        self.issue()
        times = [f[0] for f in self.flying]
        times += [self.free[link] - self.slack for link, queue in self.queues.items() if queue]
        self.now = max(self.now, min(times))
        self.drain()

    def work(self, cost, run):
        self.drain()
        run()
        self.now += cost


class Gather:
    def __init__(self, place, own, full, rows, side, y_first, sems):
        self.p = place
        self.own = own
        self.full = full
        self.rows = rows
        self.side = side
        self.main = rows - side
        self.y_first = y_first
        self.main_send, self.main_recv, self.x_send, self.x_recv, self.c_send, self.c_recv = sems

    def block(self, ref, start, size):
        return ref.at[:, pl.ds(pl.multiple_of(start, 16), size), :]

    def at(self, z, y, core, start, size):
        return self.block(self.full, self.p.shard(z, y, core) * self.rows + start, size)

    def owner(self, n):
        step, other = n % self.p.depth, n // self.p.depth
        return self.p.z_behind(step), (1 - self.p.y if other else self.p.y)

    @property
    def main_start(self):
        return self.side * self.p.x

    def side_start(self, x):
        return self.main * x

    def main_piece(self, z, y, source=False):
        p = self.p
        return self.at(z, y, p.core, self.main_start, self.main)

    def arriving(self, n):
        p = self.p
        z, y = self.owner(n)
        piece = self.main_piece(z, y)
        return remote(piece, piece, self.main_send.at[0], self.main_recv.at[n], p.across_y)

    def y_copy(self, n):
        p = self.p
        z, y = self.owner(n)
        dst = self.main_piece(z, y)
        src = self.block(self.own, self.main_start, self.main) if n == 0 else dst
        return remote(src, dst, self.main_send.at[n], self.main_recv.at[n + p.depth], p.across_y)

    def z_copy(self, step, other):
        p = self.p
        y = 1 - p.y if other else p.y
        dst = self.main_piece(p.z, y)
        src = dst if other else self.block(self.own, self.main_start, self.main)
        slot = p.depth + (step - 1) + (p.depth - 1) * other
        return remote(
            src, dst, self.main_send.at[slot], self.main_recv.at[step + p.depth * other], p.z_ahead(step)
        )

    def relay_copy(self, other, up):
        p = self.p
        z, target = (0, 3) if up else (3, 0)
        y = 1 - p.y if other else p.y
        piece = self.main_piece(z, y)
        slot = p.depth + 2 * (p.depth - 1) + other
        step = 3 if up else 1
        device = (p.shard(target, p.y, p.core), p.x)
        return remote(piece, piece, self.main_send.at[slot], self.main_recv.at[step + p.depth * other], device)

    def x_copy(self, n, x):
        p = self.p
        z, y = self.owner(n)
        piece = self.at(z, y, p.core, self.side_start(x), self.side)
        return remote(piece, piece, self.x_send.at[n], self.x_recv.at[n], p.across_x)

    def c_copy(self, n, core, side):
        p = self.p
        slot = n + (2 * p.depth if side else 0)
        z, y = self.owner(n)
        if n == 0:
            src, dst = self.own, self.at(z, y, core, 0, self.rows)
        else:
            start, size = (self.side_start(1 - p.x), self.side) if side else (self.main_start, self.main)
            src = dst = self.at(z, y, core, start, size)
        return remote(src, dst, self.c_send.at[slot], self.c_recv.at[slot], p.across_core)

    def copy_own(self):
        p = self.p
        return pltpu.make_async_copy(self.own, self.at(p.z, p.y, p.core, 0, self.rows), self.main_send.at[4 * p.depth])

    def each_z(self, other, act):
        p = self.p
        for step in range(1, p.depth):
            if step == 2:
                act(self.z_copy(step, other))
            else:
                end = 0 if step == 3 else 3

                @pl.when(p.z != end)
                def _():
                    act(self.z_copy(step, other))

    def each_relay(self, other, act):
        p = self.p

        @pl.when(p.z == 2)
        def _():
            act(self.relay_copy(other, True))

        @pl.when(p.z == 1)
        def _():
            act(self.relay_copy(other, False))

    def begin(self):
        self.copy_own().start()
        self.y_copy(0).start()
        self.each_z(0, lambda copy: copy.start())
        self.c_copy(0, self.p.core, False).start()

    def order(self):
        depth = self.p.depth
        if self.y_first:
            return [depth, 2, 2 + depth, 1, 3, 1 + depth, 3 + depth]
        return [2, 1, 3, depth, depth + 2, depth + 1, depth + 3]

    def take(self, n):
        p = self.p
        depth = p.depth
        self.arriving(n).wait_recv()
        other = n // depth
        if n % depth == 2 and (self.y_first or other == 0):
            self.each_relay(other, lambda copy: copy.start())
        if self.y_first:
            if n == depth:
                self.each_z(1, lambda copy: copy.start())
        elif other == 0:
            self.y_copy(n).start()
        if self.side:
            self.x_copy(n, p.x).start()
        self.c_copy(n, p.core, False).start()

    def take_x(self, n):
        p = self.p
        if self.side:
            self.x_copy(n, 1 - p.x).wait_recv()
            self.c_copy(n, p.core, True).start()

    def complete(self):
        p = self.p
        self.copy_own().wait()
        for n in range(2 * p.depth):
            self.c_copy(n, 1 - p.core, False).wait_recv()
            if self.side and n:
                self.c_copy(n, 1 - p.core, True).wait_recv()

    def end(self):
        p = self.p

        def wait(copy):
            copy.wait_send()

        for n in range(1 if self.y_first else p.depth):
            self.y_copy(n).wait_send()
        for other in range(2 if self.y_first else 1):
            self.each_z(other, wait)
            self.each_relay(other, wait)
        for n in range(2 * p.depth):
            self.c_copy(n, p.core, False).wait_send()
            if self.side and n:
                self.x_copy(n, p.x).wait_send()
                self.c_copy(n, p.core, True).wait_send()


def gather_sems(count, depth):
    sizes = (4 * depth + 1, 2 * depth, 2 * depth, 2 * depth, 4 * depth, 4 * depth)
    return [pltpu.SemaphoreType.DMA((count, size)) for size in sizes]


LOW = jnp.bfloat16


def dot(a, b, ca=1, cb=0):
    return lax.dot_general(a, b, (((ca,), (cb,)), ((), ())), preferred_element_type=jnp.float32)


def norm_rows(source, gain, target):
    rows = source.shape[0]
    chunk = 64

    @pl.loop(0, rows // chunk)
    def _(i):
        span = pl.ds(pl.multiple_of(i * chunk, chunk), chunk)
        v = source[span].astype(jnp.float32)
        scale = lax.rsqrt(jnp.mean(v * v, axis=-1, keepdims=True) + EPSILON)
        target[span] = (v * scale * gain).astype(LOW)


def norm_back_rows(source, gain, grad, dout, target, gain_grad):
    rows, width = source.shape
    chunk = 64
    gain_grad[...] = jnp.zeros_like(gain_grad)

    @pl.loop(0, rows // chunk)
    def _(i):
        span = pl.ds(pl.multiple_of(i * chunk, chunk), chunk)
        v = source[span].astype(jnp.float32)
        dh = grad[span]
        scale = lax.rsqrt(jnp.mean(v * v, axis=-1, keepdims=True) + EPSILON)
        unit = v * scale
        gain_grad[...] += jnp.sum(dh * unit, axis=0, keepdims=True)
        scaled = dh * gain
        along = jnp.mean(scaled * unit, axis=-1, keepdims=True)
        target[span] = (dout[span].astype(jnp.float32) + scale * (scaled - unit * along)).astype(target.dtype)


def pair_span(pair):
    return pl.ds(pl.multiple_of(pair * 2 * HEAD_DIM, 2 * HEAD_DIM), 2 * HEAD_DIM)


def attend_pair(pair, q, k, v, bias, mixed, lse):
    span = pair_span(pair)
    q_two, k_two, v_two = q[:, span], k[:, span], v[:, span]
    rows = q_two.shape[0]
    low_half = lax.broadcasted_iota(jnp.int32, q_two.shape, 1) < HEAD_DIM
    lane = lax.broadcasted_iota(jnp.int32, (rows, 128), 1)
    outs = []
    sums = lse[...]
    for half in range(2):
        mine = low_half if half == 0 else ~low_half
        scores = dot(jnp.where(mine, q_two, jnp.zeros_like(q_two)), k_two, 1, 1) * HEAD_DIM ** (-0.5)
        if bias is not None:
            scores = scores + bias[...]
        highest = jnp.max(scores, axis=-1, keepdims=True)
        powers = jnp.exp(scores - highest)
        summed = jnp.sum(powers, axis=-1, keepdims=True)
        shares = (powers / summed).astype(LOW)
        outs.append(dot(shares, v_two))
        sums = jnp.where(lane == 2 * pair + half, highest + jnp.log(summed), sums)
    mixed[:, span] = jnp.where(low_half, outs[0], outs[1]).astype(LOW)
    lse[...] = sums


def gelu_parts(gate):
    inner = (2.0 / 3.141592653589793) ** 0.5
    square = gate * gate
    bent = jnp.tanh(inner * gate * (1.0 + 0.044715 * square))
    half = 0.5 * (1.0 + bent)
    slope = half + 0.5 * gate * (1.0 - bent * bent) * inner * (1.0 + 3 * 0.044715 * square)
    return gate * half, slope


class Rows:
    def __init__(self, place, count):
        self.p = place
        self.count = count
        self.row = place.wide * 2 + place.x

    def device(self, row):
        return (row // 2, row % 2)

    def when(self, distance, act):
        @pl.when((self.row + distance >= 0) & (self.row + distance < self.count))
        def _():
            act(self.device(self.row + distance))

    def near(self):
        return (-2, -1, 1, 2)

    def present(self):
        below = jnp.minimum(self.row, 2)
        above = jnp.minimum(self.count - 1 - self.row, 2)
        return below + above


def greet_all(place, rows):
    barrier = pltpu.get_barrier_semaphore()
    others = [place.across_x, place.across_y, place.across_core]
    others += [place.z_ahead(step) for step in range(1, place.depth)]

    def hello(device):
        pl.semaphore_signal(barrier, inc=1, device_id=device, device_id_type=MESH)

    for other in others:
        hello(other)
    for distance in rows.near():
        rows.when(distance, hello)
    pl.semaphore_wait(barrier, len(others) + rows.present())


def pass_rows(rows, source, target, distance, sems):
    send, recv = sems

    def copy(device):
        return remote(source, target, send, recv, device)

    def start():
        rows.when(distance, lambda device: copy(device).start())

    def arrive():
        rows.when(-distance, lambda device: copy(device).wait_recv())

    def end():
        rows.when(distance, lambda device: copy(device).wait_send())

    return start, arrive, end


MLP_CUTS = (0, 512, 1024, 1536, 1792, 2048)
GATHER_LAYOUT = (
    (4, 0, 1, 0, 128, 0),
    (0, 0, 3, 0, 768, 16),
    (0, 3, 4, 0, 768, 16),
    (1, 0, 2, 0, 768, 16),
    (1, 2, 4, 0, 768, 16),
    (3, 0, 1, 0, 768, 48),
    *((2, 0, 2, first, last, 16) for first, last in zip(MLP_CUTS, MLP_CUTS[1:])),
)
WIDTH, HIDDEN, TOKENS, PATCHES = 768, 2048, 384, 256

class Spec:
    def __init__(self, *shape, dtype=LOW):
        self.shape = shape
        self.dtype = dtype

    def array(self):
        return jax.ShapeDtypeStruct(self.shape, self.dtype)

    def scratch(self):
        return pltpu.VMEM(self.shape, self.dtype)


def specs(table):
    return [spec for spec in vars(table).values() if isinstance(spec, Spec)]


class K:
    gain = Spec(8, WIDTH, dtype=jnp.float32)
    h1t = Spec(WIDTH, TOKENS)
    q1 = Spec(TOKENS, WIDTH)
    k1 = Spec(TOKENS, WIDTH)
    v1 = Spec(TOKENS, WIDTH)
    o1t = Spec(WIDTH, TOKENS)
    lse1 = Spec(128, TOKENS, dtype=jnp.float32)
    x1 = Spec(TOKENS, WIDTH, dtype=jnp.float32)
    h2t = Spec(WIDTH, TOKENS)
    memt = Spec(WIDTH, PATCHES)
    q2 = Spec(TOKENS, WIDTH)
    k2 = Spec(PATCHES, WIDTH)
    v2 = Spec(PATCHES, WIDTH)
    o2t = Spec(WIDTH, TOKENS)
    lse2 = Spec(128, TOKENS, dtype=jnp.float32)
    h3t = Spec(WIDTH, TOKENS)
    hiddent = Spec(HIDDEN, TOKENS)
    dgate = Spec(TOKENS, HIDDEN)
    dup = Spec(TOKENS, HIDDEN)
    dx2 = Spec(TOKENS, WIDTH, dtype=jnp.float32)
    gain3 = Spec(1, WIDTH, dtype=jnp.float32)


class W:
    w_self = Spec(4, WIDTH, WIDTH)
    w_cross = Spec(4, WIDTH, WIDTH)
    w_in = Spec(2, WIDTH, HIDDEN)
    w_out = Spec(1, HIDDEN, WIDTH)
    w_gain = Spec(1, 256, 128)


class F:
    bias = Spec(TOKENS, TOKENS, dtype=jnp.float32)
    h = Spec(TOKENS, WIDTH)
    mix = Spec(TOKENS, WIDTH)
    lse = Spec(TOKENS, 128, dtype=jnp.float32)
    mem_one = Spec(PATCHES, WIDTH)
    mem = Spec(PATCHES, WIDTH)
    mem_got = Spec(2, PATCHES, WIDTH)
    x2 = Spec(TOKENS, WIDTH, dtype=jnp.float32)
    gate = Spec(TOKENS, 512, dtype=jnp.float32)
    up = Spec(TOKENS, 512, dtype=jnp.float32)
    dhid = Spec(TOKENS, 512, dtype=jnp.float32)
    hidden = Spec(TOKENS, HIDDEN)
    gain_own = Spec(1, 16, 128)
    total = Spec(TOKENS, WIDTH, dtype=jnp.float32)
    dh = Spec(TOKENS, WIDTH, dtype=jnp.float32)


PASSED = specs(K) + [W.w_self, W.w_cross]


def as_column(row):
    return jnp.broadcast_to(row.astype(jnp.float32), (128, row.shape[1])).T


def row_offset(images, row, count):
    image = images[jnp.minimum(row, count - 1)]
    start = sum((images[other] < image).astype(jnp.int32) for other in range(count))
    return jnp.where(row < count, row - start, 0)


def forward_kernel(depth, row_count, refs):
    (x0, dy, memory, segments, padding, images, gains) = refs[:7]
    owns = refs[7:11]
    out = refs[11]
    rest = refs[12:]
    kept_out, rest = dict(zip(PASSED, rest)), rest[len(PASSED) :]
    kept, rest = dict(zip(specs(K), rest)), rest[len(specs(K)) :]
    weights, rest = dict(zip(specs(W), rest)), rest[len(specs(W)) :]
    local, rest = dict(zip(specs(F), rest)), rest[len(specs(F)) :]
    gather_sem, row_sem, keep_sem, mlp_sem = rest[:6], rest[6], rest[7], rest[8]
    owns = (*owns, local[F.gain_own])
    kept_numbers = {name: number for number, name in enumerate(kept_out)}

    def keep_copy(name):
        source = weights[name] if name in weights else kept[name]
        return pltpu.make_async_copy(source, kept_out[name], keep_sem.at[kept_numbers[name]])

    def keep(*names):
        for name in names:
            keep_copy(name).start()

    place = Place(depth)
    rows = Rows(place, row_count)
    fulls = [weights[spec] for spec in specs(W)]
    blocks = []
    for number, (array, first, last, c0, c1, side) in enumerate(GATHER_LAYOUT):
        own, full = owns[array], fulls[array]
        blocks.append(
            Gather(
                place,
                own.at[first:last, :, c0:c1],
                full.at[first:last, :, c0:c1],
                own.shape[1],
                side,
                False,
                [sem.at[number] for sem in gather_sem],
            )
        )
    near_start, near_arrive, near_end = pass_rows(
        rows, memory, local[F.mem_got].at[0], 1, (row_sem.at[0], row_sem.at[1])
    )
    far_start, far_arrive, far_end = pass_rows(
        rows, local[F.mem_one], local[F.mem_got].at[1], 2, (row_sem.at[2], row_sem.at[3])
    )
    gain = kept[K.gain]
    offset = row_offset(images, rows.row, row_count)
    local[F.gain_own][...] = jnp.zeros_like(local[F.gain_own])
    local[F.gain_own][0, 0 : gains.shape[0], 0 : gains.shape[1]] = gains[...]

    def make_bias():
        seg_q, seg_k = as_column(segments[...])[:, 0:1], segments[...].astype(jnp.float32)
        query = lax.broadcasted_iota(jnp.int32, (TOKENS, TOKENS), 0)
        key = lax.broadcasted_iota(jnp.int32, (TOKENS, TOKENS), 1)
        allowed = (seg_q == seg_k) & (key <= query) & ((padding[...] == 1) | (key == query))
        local[F.bias][...] = jnp.where(allowed, 0.0, -1e30)

    def make_gain():
        total = jnp.zeros((16, WIDTH), jnp.float32)
        count = row_count // 2
        share = WIDTH // count
        for number in range(count):
            row = lax.broadcasted_iota(jnp.int32, (128, WIDTH), 0)
            column = lax.broadcasted_iota(jnp.int32, (128, WIDTH), 1)
            pick = ((column - number * share) == row) & (row < share)
            total += dot(weights[W.w_gain][0, number * 16 : number * 16 + 16, :], pick.astype(LOW))
        gain[...] = total[:8]

    def first_norm():
        norm_rows(x0, gain[0:1], local[F.h])
        kept[K.h1t][...] = local[F.h][...].T
        keep(K.gain, K.h1t)

    def project(name, w, index):
        def run():
            kept[name][...] = dot(local[F.h][...], weights[w][index]).astype(LOW)
            keep(name)

        return run

    def self_pair(pair):
        return lambda: attend_pair(pair, kept[K.q1], kept[K.k1], kept[K.v1], local[F.bias], local[F.mix], local[F.lse])

    def clear_lse():
        local[F.lse][...] = jnp.zeros_like(local[F.lse])

    def self_out():
        kept[K.lse1][...] = local[F.lse][...].T
        kept[K.o1t][...] = local[F.mix][...].T
        kept[K.x1][...] = x0[...].astype(jnp.float32) + dot(local[F.mix][...], weights[W.w_self][3])
        keep(K.lse1, K.o1t, K.x1)

    def second_norm():
        norm_rows(kept[K.x1], gain[1:2], local[F.h])
        kept[K.h2t][...] = local[F.h][...].T
        keep(K.h2t)

    def memory_near():
        near_arrive()
        local[F.mem_one][...] = jnp.where(offset >= 1, local[F.mem_got][0], memory[...])
        far_start()

    def memory_far():
        far_arrive()
        local[F.mem][...] = jnp.where(offset >= 2, local[F.mem_got][1], local[F.mem_one][...])
        kept[K.memt][...] = local[F.mem][...].T
        keep(K.memt)

    def project_memory(name, index):
        def run():
            kept[name][...] = dot(local[F.mem][...], weights[W.w_cross][index]).astype(LOW)
            keep(name)

        return run

    def cross_pair(pair):
        return lambda: attend_pair(pair, kept[K.q2], kept[K.k2], kept[K.v2], None, local[F.mix], local[F.lse])

    def cross_out():
        kept[K.lse2][...] = local[F.lse][...].T
        kept[K.o2t][...] = local[F.mix][...].T
        local[F.x2][...] = kept[K.x1][...] + dot(local[F.mix][...], weights[W.w_cross][3])
        keep(K.lse2, K.o2t)

    def third_norm():
        norm_rows(local[F.x2], gain[2:3], local[F.h])
        kept[K.h3t][...] = local[F.h][...].T
        keep(K.h3t)

    def mlp_dots(number):
        c0, c1 = MLP_CUTS[number], MLP_CUTS[number + 1]

        def run():
            h = local[F.h][...]
            local[F.dhid][:, : c1 - c0] = dot(dy[...], weights[W.w_out][0, c0:c1, :], 1, 1)
            local[F.gate][:, : c1 - c0] = dot(h, weights[W.w_in][0, :, c0:c1])
            local[F.up][:, : c1 - c0] = dot(h, weights[W.w_in][1, :, c0:c1])

        return run

    def mlp_copies(number):
        c0, c1 = MLP_CUTS[number], MLP_CUTS[number + 1]
        cuts = ((K.hiddent, (slice(c0, c1), slice(None))), (K.dgate, (slice(None), slice(c0, c1))))
        cuts += ((K.dup, (slice(None), slice(c0, c1))),)
        return [
            pltpu.make_async_copy(kept[name].at[cut], kept_out[name].at[cut], mlp_sem.at[number, place_of])
            for place_of, (name, cut) in enumerate(cuts)
        ]

    def mlp_point(number):
        c0, c1 = MLP_CUTS[number], MLP_CUTS[number + 1]
        width = c1 - c0

        def run():
            @pl.loop(0, TOKENS // 16)
            def _(i):
                span = pl.ds(pl.multiple_of(i * 16, 16), 16)
                act, slope = gelu_parts(local[F.gate][span, :width])
                up, dhid = local[F.up][span, :width], local[F.dhid][span, :width]
                local[F.hidden][span, c0:c1] = (act * up).astype(LOW)
                kept[K.dgate][span, c0:c1] = (dhid * up * slope).astype(LOW)
                kept[K.dup][span, c0:c1] = (dhid * act).astype(LOW)

            kept[K.hiddent][c0:c1, :] = local[F.hidden][:, c0:c1].T
            for copy in mlp_copies(number):
                copy.start()

        return run

    def mlp_back(number):
        c0, c1 = MLP_CUTS[number], MLP_CUTS[number + 1]

        def run():
            value = dot(kept[K.dgate][:, c0:c1], weights[W.w_in][0, :, c0:c1], 1, 1)
            value += dot(kept[K.dup][:, c0:c1], weights[W.w_in][1, :, c0:c1], 1, 1)
            local[F.dh][...] = value if number == 0 else local[F.dh][...] + value

        return run

    def mlp_sum(number):
        c0, c1 = MLP_CUTS[number], MLP_CUTS[number + 1]

        def run():
            before = local[F.x2] if number == 0 else local[F.total]
            value = before[...] + dot(local[F.hidden][:, c0:c1], weights[W.w_out][0, c0:c1, :])
            if c1 == HIDDEN:
                out[...] = value.astype(LOW)
            else:
                local[F.total][...] = value

        return run

    def mlp_norm():
        norm_back_rows(local[F.x2], gain[2:3], local[F.dh], dy, kept[K.dx2], kept[K.gain3])
        keep(K.dx2, K.gain3)

    work = [
        (None, 0.5, make_bias),
        (None, 0.1, clear_lse),
        (0, 2.0, make_gain),
        (0, 1.5, first_norm),
        (1, 0.7, project(K.q1, W.w_self, 0)),
        (1, 0.7, project(K.k1, W.w_self, 1)),
        (1, 0.7, project(K.v1, W.w_self, 2)),
    ]
    work += [(1, 1.2, self_pair(pair)) for pair in range(6)]
    work += [
        (2, 0.1, lambda: keep(W.w_self)),
        (2, 1.5, self_out),
        (2, 1.2, second_norm),
        (2, 0.5, memory_near),
        (3, 0.7, project(K.q2, W.w_cross, 0)),
        (3, 0.6, memory_far),
        (3, 0.6, project_memory(K.k2, 1)),
        (4, 0.6, project_memory(K.v2, 2)),
        (4, 0.1, lambda: keep(W.w_cross)),
    ]
    work += [(4, 0.9, cross_pair(pair)) for pair in range(6)]
    work += [(4, 1.5, cross_out), (4, 1.2, third_norm)]
    for number in range(len(MLP_CUTS) - 1):
        share = (MLP_CUTS[number + 1] - MLP_CUTS[number]) / 512
        need = 6 + number
        work += [(need, 1.7 * share, mlp_dots(number)), (need, 1.8 * share, mlp_point(number))]
        work += [(need, 1.2 * share, mlp_back(number)), (need, 0.7 * share, mlp_sum(number))]
    work += [(None, 1.2, mlp_norm)]

    count = len(blocks)
    events = []
    for turn in range(count + 3):
        if turn + 2 < count:
            events.append((blocks[turn + 2].begin, None))
        if turn < count:
            for n in blocks[turn].order()[:3]:
                events.append((functools.partial(blocks[turn].take, n), None))
        if 0 <= turn - 1 < count:
            for n in blocks[turn - 1].order()[3:]:
                events.append((functools.partial(blocks[turn - 1].take, n), None))
        if 0 <= turn - 2 < count and blocks[turn - 2].side:
            for n in blocks[turn - 2].order():
                events.append((functools.partial(blocks[turn - 2].take_x, n), None))
        if 0 <= turn - 3 < count:
            events.append((blocks[turn - 3].complete, turn - 3))

    greet_all(place, rows)
    blocks[0].begin()
    blocks[1].begin()
    near_start()
    ready = -1
    done = 0

    def can():
        return done < len(work) and (work[done][0] is None or work[done][0] <= ready)

    for act, completes in events:
        act()
        if completes is not None:
            ready = completes
        if can():
            work[done][2]()
            done += 1
    while can():
        work[done][2]()
        done += 1
    for block in blocks:
        block.end()
    near_end()
    far_end()
    for number in range(len(MLP_CUTS) - 1):
        for copy in mlp_copies(number):
            copy.wait()
    for name in kept_out:
        if name not in (K.hiddent, K.dgate, K.dup):
            keep_copy(name).wait()


def forward(
    layer_input,
    cotangent,
    memory,
    segments,
    padding,
    image_of_row,
    gains,
    self_weights,
    cross_weights,
    mlp_in,
    mlp_out,
):
    wide = lax.axis_size("wide")
    depth = wide // 4
    owns = (self_weights, cross_weights, mlp_in, mlp_out[None])
    vmem, anywhere, smem = (pl.BlockSpec(memory_space=space) for space in (pltpu.VMEM, pl.ANY, pltpu.SMEM))
    kept = [spec.array() for spec in PASSED]
    outs = pl.pallas_call(
        lambda *refs: forward_kernel(depth, 2 * wide, refs),
        out_shape=[jax.ShapeDtypeStruct(layer_input.shape, LOW)] + kept,
        in_specs=[vmem] * 5 + [smem, vmem] + [anywhere] * 4,
        out_specs=[vmem] + [anywhere] * len(kept),
        scratch_shapes=[spec.scratch() for table in (K, W, F) for spec in specs(table)]
        + gather_sems(len(GATHER_LAYOUT), depth)
        + [
            pltpu.SemaphoreType.DMA((4,)),
            pltpu.SemaphoreType.DMA((len(kept),)),
            pltpu.SemaphoreType.DMA((len(MLP_CUTS) - 1, 3)),
        ],
        compiler_params=pltpu.CompilerParams(
            collective_id=0, has_side_effects=True, vmem_limit_bytes=60 * 2**20
        ),
        name="forward",
    )(layer_input, cotangent, memory, segments, padding, image_of_row, gains, *owns)
    return outs[0], dict(zip(PASSED, outs[1:]))


class Scatter:
    def __init__(self, place, bufs, outs, block, sems):
        self.p = place
        rows, side = block.rows, block.side
        self.width = block.width
        self.relay = block.relay
        self.staged, self.held, self.from_x, self.from_y, self.from_z, self.relayed, self.done, self.other = bufs
        self.outs = outs
        self.rows = rows
        self.side = side
        self.main = rows - side
        self.send, self.recv = sems

    def span(self, start, size):
        return pl.ds(pl.multiple_of(start, 16), size)

    @property
    def main_span(self):
        return self.span(self.side * self.p.x, self.main)

    def side_span(self, x):
        return self.span(self.main * x, self.side)

    def c_copy(self):
        return remote(self.staged, self.held, self.send.at[0], self.recv.at[0], self.p.across_core)

    def x_copy(self):
        p = self.p
        return remote(
            self.held.at[:, :, :, self.side_span(1 - p.x)],
            self.from_x,
            self.send.at[1],
            self.recv.at[1],
            p.across_x,
        )

    def y_copy(self):
        p = self.p
        return remote(
            self.held.at[:, :, 1 - p.y, self.main_span], self.from_y, self.send.at[2], self.recv.at[2], p.across_y
        )

    def z_piece(self, z):
        return self.held.at[:, z, self.p.y, self.main_span]

    def z_copy(self, step):
        p = self.p
        return remote(
            self.z_piece((p.z + step) % p.depth),
            self.from_z.at[step - 1],
            self.send.at[2 + step],
            self.recv.at[2 + step],
            p.z_ahead(step),
        )

    def relay_copy(self, up):
        p = self.p
        target, between = (3, 1) if up else (0, 2)
        device = (p.shard(between, p.y, p.core), p.x)
        return remote(self.z_piece(target), self.relayed, self.send.at[6], self.recv.at[6], device)

    def last_copy(self):
        return remote(self.done, self.other, self.send.at[7], self.recv.at[7], self.p.across_x)

    def blank(self):
        p = self.p
        if not self.relay:
            return

        @pl.when(p.z == 0)
        def _():
            self.from_z[0] = jnp.zeros_like(self.from_z[0])

        @pl.when(p.z == 3)
        def _():
            self.from_z[2] = jnp.zeros_like(self.from_z[2])

    def each_z(self, act_direct, act_late, act_relay):
        p = self.p
        if not self.relay:
            if act_direct is not None:
                for step in range(1, p.depth):
                    act_direct(self.z_copy(step))
            return
        if act_direct is not None:

            @pl.when(p.z != 0)
            def _():
                act_direct(self.z_copy(3))

            @pl.when(p.z != 3)
            def _():
                act_direct(self.z_copy(1))

            @pl.when((p.z == 0) | (p.z == 3))
            def _():
                act_direct(self.z_copy(2))

        if act_late is not None:

            @pl.when(p.z == 1)
            def _():
                act_late(self.z_copy(2), 3)

            @pl.when(p.z == 2)
            def _():
                act_late(self.z_copy(2), 0)

        if act_relay is not None:

            @pl.when(p.z == 0)
            def _():
                act_relay(self.relay_copy(True))

            @pl.when(p.z == 3)
            def _():
                act_relay(self.relay_copy(False))

    def start_c(self):
        self.c_copy().start()

    def take_x(self):
        self.x_copy().wait_recv()
        span = self.side_span(self.p.x)
        self.held[:, :, :, span] = self.held[:, :, :, span] + self.from_x[...]

    def take_y(self):
        p = self.p
        self.y_copy().wait_recv()
        span = self.main_span
        self.held[:, :, p.y, span] = self.held[:, :, p.y, span] + self.from_y[...]

    def start_z(self):
        self.each_z(lambda copy: copy.start(), None, lambda copy: copy.start())

    def take_relay(self):
        def late(copy, target):
            self.relay_copy(True).wait_recv()
            p = self.p
            span = self.main_span
            self.held[:, target, p.y, span] = self.held[:, target, p.y, span] + self.relayed[...]
            copy.start()

        self.each_z(None, late, None)

    def take_z(self):
        p = self.p
        self.z_copy(2).wait_recv()
        if self.relay:

            @pl.when(p.z != 0)
            def _():
                self.z_copy(1).wait_recv()

            @pl.when(p.z != 3)
            def _():
                self.z_copy(3).wait_recv()

        else:
            self.z_copy(1).wait_recv()
            self.z_copy(3).wait_recv()

        total = self.held[:, p.z, p.y, self.main_span].astype(jnp.float32)
        for step in range(1, p.depth):
            total += self.from_z[step - 1].astype(jnp.float32)
        self.done[...] = total.astype(LOW)

    def take_last(self):
        p = self.p
        self.last_copy().wait_recv()
        side, both = self.side, self.main - self.side
        for number, (out, mat, column) in enumerate(self.outs):
            columns = slice(column, column + self.width)
            if side:
                out[mat, self.side_span(p.x), columns] = self.done[number, self.span(both * p.x, side)].astype(
                    jnp.float32
                )
                out[mat, self.side_span(1 - p.x), columns] = self.other[
                    number, self.span(both * (1 - p.x), side)
                ].astype(jnp.float32)
            out[mat, side : side + both, columns] = self.done[number, self.span(side * (1 - p.x), both)].astype(
                jnp.float32
            ) + self.other[number, self.span(side * p.x, both)].astype(jnp.float32)

    def end(self):
        def wait(copy, target=None):
            copy.wait_send()

        if self.side:
            self.x_copy().wait_send()
        self.y_copy().wait_send()
        self.each_z(wait, wait, wait)
        self.last_copy().wait_send()


class Block:
    def __init__(self, out, pieces, rows, side, width=256, relay=True):
        self.out, self.pieces, self.rows, self.side = out, tuple(pieces), rows, side
        self.width, self.relay = width, relay

    @property
    def ring(self):
        return self.rows, self.width


def block_list():
    found = [Block(3, [(0, 0)], 128, 0, 256, False)] + [Block(3, [(0, c)], 128, 32) for c in (256, 512)]
    found += [Block(2, [(m, first + c) for c in range(0, 1024, 256)], 48, 16) for m in (0, 1) for first in (0, 1024)]
    found += [Block(1, [(3, c) for c in range(0, 768, 256)], 48, 0)]
    found += [Block(1, [(m, c) for m in range(3)], 48, 16) for c in (0, 256, 512)]
    found += [Block(0, [(3, c) for c in range(0, 768, 256)], 48, 0)]
    found += [Block(0, [(m, c) for m in range(3)], 48, 16, 128, False) for c in range(0, 768, 128)]
    return found


SCATTER_LAYOUT = block_list()
RINGS = {(128, 256): (2, 1), (48, 256): (3, 4), (48, 128): (2, 3)}


def scatter_buffers(depth):
    bufs = []
    for block in SCATTER_LAYOUT:
        subs, rows, side, width = len(block.pieces), block.rows, block.side, block.width
        main = rows - side
        bufs += [
            pltpu.VMEM((subs, depth, 2, rows, width), LOW),
            pltpu.VMEM((subs, depth, 2, side, width) if side else (16, 128), LOW),
            pltpu.VMEM((subs, depth, main, width), LOW),
            pltpu.VMEM((depth - 1, subs, main, width), LOW),
            pltpu.VMEM((subs, main, width), LOW),
            pltpu.VMEM((subs, main, width), LOW),
            pltpu.VMEM((subs, main, width), LOW),
        ]
    return bufs


def staging_buffers(depth):
    return [
        pltpu.VMEM((slots, subs, depth, 2, rows, width), LOW) for (rows, width), (slots, subs) in RINGS.items()
    ]


class K0:
    x0 = Spec(TOKENS, WIDTH)


class B:
    biast = Spec(TOKENS, TOKENS, dtype=jnp.float32)
    dlow = Spec(TOKENS, WIDTH)
    do = Spec(TOKENS, WIDTH)
    dq = Spec(TOKENS, WIDTH)
    dk = Spec(TOKENS, WIDTH)
    dv = Spec(TOKENS, WIDTH)
    dh = Spec(TOKENS, WIDTH, dtype=jnp.float32)
    mem_sum = Spec(PATCHES, WIDTH, dtype=jnp.float32)
    mem_low = Spec(2, PATCHES, WIDTH)
    mem_got = Spec(2, PATCHES, WIDTH)
    gains = Spec(8, WIDTH, dtype=jnp.float32)
    gain_got = Spec(6, 8, WIDTH, dtype=jnp.float32)
    gain_row = Spec(1, WIDTH, dtype=jnp.float32)


def attend_back_pair(pair, q, k, v, do, lse, bias, dq, dk, dv):
    span = pair_span(pair)
    q_two, k_two, v_two, do_two = q[:, span], k[:, span], v[:, span], do[:, span]
    low_q = lax.broadcasted_iota(jnp.int32, q_two.shape, 1) < HEAD_DIM
    low_k = lax.broadcasted_iota(jnp.int32, k_two.shape, 1) < HEAD_DIM
    scale = HEAD_DIM ** (-0.5)
    grads = []
    for half in range(2):
        mine = low_q if half == 0 else ~low_q
        scores = dot(k_two, jnp.where(mine, q_two, jnp.zeros_like(q_two)), 1, 1) * scale
        if bias is not None:
            scores = scores + bias[...]
        head = 2 * pair + half
        shares = jnp.exp(scores - lse[head : head + 1, :])
        p_grad = dot(v_two, jnp.where(mine, do_two, jnp.zeros_like(do_two)), 1, 1)
        along = jnp.sum(shares * p_grad, axis=0, keepdims=True)
        s_low = (shares * (p_grad - along)).astype(LOW)
        v_grad = dot(shares.astype(LOW), do_two)
        k_grad = dot(s_low, q_two) * scale
        q_grad = dot(s_low, k_two, 0, 0) * scale
        grads.append((q_grad, k_grad, v_grad))
    dq[:, span] = jnp.where(low_q, grads[0][0], grads[1][0]).astype(LOW)
    count = k_two.shape[0]
    dk[:count, span] = jnp.where(low_k, grads[0][1], grads[1][1]).astype(LOW)
    dv[:count, span] = jnp.where(low_k, grads[0][2], grads[1][2]).astype(LOW)


class Total:
    def __init__(self, place, value, got, send, recv):
        self.p, self.value, self.got, self.send, self.recv = place, value, got, send, recv

    def copy(self, slot):
        p = self.p
        device = (p.across_core, p.across_x, p.across_y, *(p.z_ahead(step) for step in (1, 2, 3)))[slot]
        return remote(self.value, self.got.at[slot], self.send.at[slot], self.recv.at[slot], device)

    def start(self, slots):
        for slot in slots:
            self.copy(slot).start()

    def take(self, slots):
        for slot in slots:
            self.copy(slot).wait()
        total = self.value[...]
        for slot in slots:
            total = total + self.got[slot]
        self.value[...] = total


def backward_kernel(depth, row_count, refs):
    (dy, segments, padding, images) = refs[:4]
    names = PASSED + [K0.x0]
    given = dict(zip(names, refs[4:]))
    rest = refs[4 + len(names) :]
    outs, (x_grad, mem_grad, gain_grad) = rest[:4], rest[4:7]
    rest = rest[7:]
    kept = dict(zip(names, rest))
    rest = rest[len(names) :]
    local, rest = dict(zip(specs(B), rest)), rest[len(specs(B)) :]
    staging, rest = dict(zip(RINGS, rest)), rest[len(RINGS) :]
    count = len(SCATTER_LAYOUT)
    bufs, sems = rest[: 7 * count], rest[7 * count :]
    load_sem, send_sem, recv_sem, row_sem, total_send, total_recv, out_sem = sems
    place = Place(depth)
    rows = Rows(place, row_count)
    core = place.core
    plan = Plan(6, 2.5)

    def load(*chosen):
        for name in chosen:
            number = names.index(name)
            pltpu.make_async_copy(given[name], kept[name], load_sem.at[number]).start()

    def loaded(*chosen):
        for name in chosen:
            number = names.index(name)
            pltpu.make_async_copy(given[name], kept[name], load_sem.at[number]).wait()

    blocks, rings = [], {key: [] for key in RINGS}
    for number, spec in enumerate(SCATTER_LAYOUT):
        ring, slots = rings[spec.ring], RINGS[spec.ring][0]
        staged = staging[spec.ring].at[len(ring) % slots, 0 : len(spec.pieces)]
        block = Scatter(
            place,
            (staged,) + tuple(bufs[7 * number : 7 * number + 7]),
            [(outs[spec.out], mat, column) for mat, column in spec.pieces],
            spec,
            [send_sem.at[number], recv_sem.at[number]],
        )
        block.before = ring[-slots] if len(ring) >= slots else None
        ring.append(block)
        blocks.append(block)

    near_start, near_arrive, near_end = pass_rows(
        rows, local[B.mem_low].at[1], local[B.mem_got].at[1], -1, (row_sem.at[0], row_sem.at[1])
    )
    far_start, far_arrive, far_end = pass_rows(
        rows, local[B.mem_low].at[0], local[B.mem_got].at[0], -2, (row_sem.at[2], row_sem.at[3])
    )
    total = Total(place, local[B.gains], local[B.gain_got], total_send, total_recv)

    def half(left, which):
        part = kept[left][:, :, which]
        return part.reshape(-1, part.shape[-1])

    def products(block, terms, which):
        found = []
        for left, right, first, width in terms:
            value = dot(half(left, which), right[: kept[left].shape[-1], first : first + width])
            value = value.reshape(depth, 2, -1, width)
            found += [value[..., c : c + block.width] for c in range(0, width, block.width)]
        return found

    def size(block, what):
        each = {
            "c": 8 * block.rows,
            "x": 8 * block.side,
            "y": 4 * block.main,
            "z": (2.5 if block.relay else 4) * block.main,
            "r": block.main,
            "l": block.main,
        }
        return len(block.outs) * block.width * 2 * each[what]

    def give(number, terms):
        block = blocks[number]

        def run():
            if block.before is not None:
                block.before.c_copy().wait_send()
                block.before.sent = True
            for sub, value in enumerate(products(block, terms, 1 - core)):
                block.staged[sub] = value.astype(LOW)
            block.start_c()

        return run

    def hold(number, terms):
        block = blocks[number]

        def run():
            block.c_copy().wait_recv()
            for sub, value in enumerate(products(block, terms, core)):
                block.held[sub] = (value + block.held[sub].astype(jnp.float32)).astype(LOW)

            def to_y():
                if block.side:
                    block.take_x()
                plan.send("y", number, size(block, "y"), lambda: block.y_copy().start(), to_z)

            def to_z():
                block.take_y()
                plan.send("z", number, size(block, "z"), block.start_z, to_relay)

            def to_relay():
                if not block.relay:
                    to_last()
                    return
                block.take_relay()
                plan.later(size(block, "r") / plan.rate["z"] + plan.latency, to_last)

            def to_last():
                block.take_z()
                plan.send("x", number, size(block, "l"), lambda: block.last_copy().start(), block.take_last)

            if block.side:
                plan.send("x", number, size(block, "x"), lambda: block.x_copy().start(), to_y)
            else:
                to_y()

        return run

    def make_bias():
        seg_k, seg_q = as_column(segments[...])[:, 0:1], segments[...].astype(jnp.float32)
        real = as_column(padding[...])[:, 0:1] == 1.0
        key = lax.broadcasted_iota(jnp.int32, (TOKENS, TOKENS), 0)
        query = lax.broadcasted_iota(jnp.int32, (TOKENS, TOKENS), 1)
        allowed = (seg_q == seg_k) & (key <= query) & (real | (key == query))
        local[B.biast][...] = jnp.where(allowed, 0.0, -1e30)

    def cross_begin():
        local[B.dlow][...] = kept[K.dx2][...].astype(LOW)

    def cross_do():
        local[B.do][...] = dot(local[B.dlow][...], kept[W.w_cross][3], 1, 1).astype(LOW)

    def cross_pair(pair):
        def run():
            attend_back_pair(
                pair,
                kept[K.q2],
                kept[K.k2],
                kept[K.v2],
                local[B.do],
                kept[K.lse2],
                None,
                local[B.dq],
                local[B.dk],
                local[B.dv],
            )

        return run

    def self_pair(pair):
        def run():
            attend_back_pair(
                pair,
                kept[K.q1],
                kept[K.k1],
                kept[K.v1],
                local[B.do],
                kept[K.lse1],
                local[B.biast],
                local[B.dq],
                local[B.dk],
                local[B.dv],
            )

        return run

    def mem_out():
        return pltpu.make_async_copy(local[B.mem_sum], mem_grad, out_sem.at[0])

    def x_out():
        return pltpu.make_async_copy(kept[K.dx2], x_grad, out_sem.at[1])

    def mem_back():
        value = dot(local[B.dk][:PATCHES], kept[W.w_cross][1], 1, 1)
        value += dot(local[B.dv][:PATCHES], kept[W.w_cross][2], 1, 1)
        local[B.mem_sum][...] = value
        local[B.mem_low][0] = value.astype(LOW)
        far_start()

    def mem_far():
        far_arrive()
        got = jnp.where(row_offset(images, rows.row + 2, row_count) >= 2, local[B.mem_got][0].astype(jnp.float32), 0.0)
        value = local[B.mem_sum][...] + got
        local[B.mem_sum][...] = value
        local[B.mem_low][1] = value.astype(LOW)
        near_start()

    def mem_near():
        near_arrive()
        got = jnp.where(row_offset(images, rows.row + 1, row_count) == 1, local[B.mem_got][1].astype(jnp.float32), 0.0)
        first = row_offset(images, rows.row, row_count) == 0
        local[B.mem_sum][...] = jnp.where(first, local[B.mem_sum][...] + got, 0.0)
        mem_out().start()

    def cross_dh():
        local[B.dh][...] = dot(local[B.dq][...], kept[W.w_cross][0], 1, 1)

    def cross_norm():
        norm_back_rows(kept[K.x1], kept[K.gain][1:2], local[B.dh], kept[K.dx2], kept[K.dx2], local[B.gain_row])
        local[B.gains][1:2, :] = local[B.gain_row][...]
        local[B.dlow][...] = kept[K.dx2][...].astype(LOW)

    def self_do():
        local[B.do][...] = dot(local[B.dlow][...], kept[W.w_self][3], 1, 1).astype(LOW)

    def self_dh_first():
        local[B.dh][...] = dot(local[B.dq][...], kept[W.w_self][0], 1, 1)

    def self_dh_second():
        local[B.dh][...] += dot(local[B.dk][...], kept[W.w_self][1], 1, 1)

    def self_dh_third():
        local[B.dh][...] += dot(local[B.dv][...], kept[W.w_self][2], 1, 1)

    def self_norm():
        norm_back_rows(kept[K0.x0], kept[K.gain][0:1], local[B.dh], kept[K.dx2], kept[K.dx2], local[B.gain_row])
        x_out().start()
        local[B.gains][0:1, :] = local[B.gain_row][...]
        local[B.gains][2:3, :] = kept[K.gain3][...]
        total.start((0,))

    def load_cross():
        load(K.dx2, W.w_cross, K.o2t, K.q2, K.k2, K.v2, K.lse2, K.h2t, K.memt, K.x1, K.gain, K.gain3)

    def load_self():
        load(W.w_self, K.o1t, K.q1, K.k1, K.v1, K.lse1, K.h1t, K0.x0)

    do_low, dq, dk, dv = local[B.dlow], local[B.dq], local[B.dk], local[B.dv]
    out_terms = [[(K.hiddent, dy, 256 * j, 256)] for j in range(3)]
    in_terms = [[(K.h3t, kept[name], first, 1024)] for name in (K.dgate, K.dup) for first in (0, 1024)]

    load(K.hiddent, K.h3t, K.dgate, K.dup)
    local[B.gains][...] = jnp.zeros_like(local[B.gains])
    for block in blocks:
        block.sent = False
        block.blank()
    greet_all(place, rows)
    load_cross()
    loaded(K.hiddent)
    plan.work(0.8, give(0, out_terms[0]))
    plan.work(0.8, give(1, out_terms[1]))
    plan.work(0.9, hold(0, out_terms[0]))
    plan.work(0.8, give(2, out_terms[2]))
    plan.work(0.9, hold(1, out_terms[1]))
    loaded(K.h3t, K.dgate, K.dup)
    load_self()
    plan.work(1.0, give(3, in_terms[0]))
    plan.work(0.9, hold(2, out_terms[2]))
    for j in range(1, 4):
        plan.work(1.0, give(3 + j, in_terms[j]))
        plan.work(1.1, hold(2 + j, in_terms[j - 1]))
    loaded(K.dx2, W.w_cross, K.o2t, K.q2, K.k2, K.v2, K.lse2, K.h2t, K.memt, K.x1, K.gain, K.gain3)
    plan.work(0.3, cross_begin)
    o_terms = [(K.o2t, do_low, 0, 768)]
    plan.work(0.8, give(7, o_terms))
    plan.work(1.1, hold(6, in_terms[3]))
    plan.work(0.8, cross_do)
    plan.work(0.9, hold(7, o_terms))

    def attention(pair_work, first, lefts, pairs):
        previous = None
        width = 128 * pairs
        for group in range(6 // pairs):
            for pair in range(pairs * group, pairs * group + pairs):
                plan.work(1.4, pair_work(pair))
            terms = [(left, right, width * group, width) for left, right in zip(lefts, (dq, dk, dv))]
            plan.work(0.5 * pairs, give(first + group, terms))
            if previous is not None:
                plan.work(0.5 * pairs, hold(*previous))
            previous = (first + group, terms)
        return previous

    previous = attention(cross_pair, 8, (K.h2t, K.memt, K.memt), 2)
    plan.work(1.5, mem_back)
    plan.work(1.0, hold(*previous))
    plan.work(0.8, cross_dh)
    plan.work(1.2, cross_norm)
    loaded(W.w_self, K.o1t, K.q1, K.k1, K.v1, K.lse1, K.h1t, K0.x0)
    o_terms = [(K.o1t, do_low, 0, 768)]
    plan.work(0.8, give(11, o_terms))
    plan.work(0.3, mem_far)
    plan.work(0.8, self_do)
    plan.work(0.5, make_bias)
    plan.work(0.9, hold(11, o_terms))
    previous = attention(self_pair, 12, (K.h1t, K.h1t, K.h1t), 1)
    plan.work(0.8, self_dh_first)
    plan.work(1.0, hold(*previous))
    plan.work(0.8, self_dh_second)
    plan.work(0.8, self_dh_third)
    plan.work(0.5, mem_near)
    plan.work(1.5, self_norm)

    def total_step(slots, after):
        def run():
            total.take(slots)
            if after:
                total.start(after[0])
                plan.later(2.5, total_step(after[0], after[1:]))
            else:
                share = gain_grad.shape[1]
                turned = pltpu.roll(local[B.gains][...], (row_count // 2 - place.wide) * share, 1)
                gain_grad[...] = turned[0 : gain_grad.shape[0], 0:share]

        return run

    plan.later(2.5, total_step((0,), ((1,), (2,), (3, 4, 5))))
    while plan.busy():
        plan.step()
    for block in blocks:
        if not block.sent:
            block.c_copy().wait_send()
        block.end()
    near_end()
    far_end()
    mem_out().wait()
    x_out().wait()


def backward(kept, layer_input, cotangent, segments, padding, image_of_row, share):
    wide = lax.axis_size("wide")
    depth = wide // 4

    def owners(array):
        return array.reshape(depth, 2, 2, -1, array.shape[-1])

    names = PASSED + [K0.x0]
    given = {**kept, K0.x0: layer_input}
    for name in (K.h1t, K.o1t, K.h2t, K.o2t, K.memt, K.h3t, K.hiddent):
        given[name] = owners(given[name])
    arrays = [given[name] for name in names]
    vmem, anywhere, smem = (pl.BlockSpec(memory_space=space) for space in (pltpu.VMEM, pl.ANY, pltpu.SMEM))
    outs = [
        ((4, WIDTH // wide, WIDTH), jnp.float32),
        ((4, WIDTH // wide, WIDTH), jnp.float32),
        ((2, WIDTH // wide, HIDDEN), jnp.float32),
        ((1, HIDDEN // wide, WIDTH), jnp.float32),
        ((TOKENS, WIDTH), jnp.float32),
        ((PATCHES, WIDTH), jnp.float32),
        ((3, share), jnp.float32),
    ]
    count = len(SCATTER_LAYOUT)
    return pl.pallas_call(
        lambda *refs: backward_kernel(depth, 2 * wide, refs),
        out_shape=[jax.ShapeDtypeStruct(*o) for o in outs],
        in_specs=[vmem] * 3 + [smem] + [anywhere] * len(arrays),
        out_specs=[vmem] * 4 + [anywhere] * 2 + [vmem],
        scratch_shapes=[pltpu.VMEM(a.shape, a.dtype) for a in arrays]
        + [spec.scratch() for spec in specs(B)]
        + staging_buffers(depth)
        + scatter_buffers(depth)
        + [
            pltpu.SemaphoreType.DMA((len(arrays),)),
            pltpu.SemaphoreType.DMA((count, 8)),
            pltpu.SemaphoreType.DMA((count, 8)),
            pltpu.SemaphoreType.DMA((4,)),
            pltpu.SemaphoreType.DMA((6,)),
            pltpu.SemaphoreType.DMA((6,)),
            pltpu.SemaphoreType.DMA((2,)),
        ],
        compiler_params=pltpu.CompilerParams(
            collective_id=1, has_side_effects=True, vmem_limit_bytes=63 * 2**20
        ),
        name="backward",
    )(cotangent, segments, padding, image_of_row, *arrays)


def finish(*arrays):
    count = len(arrays)

    def kernel(*refs):
        sems = refs[-1]
        loads = [pltpu.make_async_copy(refs[n], refs[2 * count + n], sems.at[0, n]) for n in range(count)]
        stores = [pltpu.make_async_copy(refs[2 * count + n], refs[count + n], sems.at[1, n]) for n in range(count)]
        for load in loads:
            load.start()
        for load, store in zip(loads, stores):
            load.wait()
            store.start()
        for store in stores:
            store.wait()

    anywhere = pl.BlockSpec(memory_space=pl.ANY)
    return pl.pallas_call(
        kernel,
        out_shape=[jax.ShapeDtypeStruct(a.shape, a.dtype) for a in arrays],
        in_specs=[anywhere] * count,
        out_specs=[anywhere] * count,
        scratch_shapes=[pltpu.VMEM(a.shape, a.dtype) for a in arrays] + [pltpu.SemaphoreType.DMA((2, count))],
        compiler_params=pltpu.CompilerParams(vmem_limit_bytes=60 * 2**20),
        name="finish",
    )(*arrays)


def plain_gather(self_weights, cross_weights, mlp_in, mlp_out, gains):
    return (
        lax.all_gather(self_weights, "wide", axis=1, tiled=True),
        lax.all_gather(cross_weights, "wide", axis=1, tiled=True),
        lax.all_gather(mlp_in, "wide", axis=1, tiled=True),
        lax.all_gather(mlp_out, "wide", axis=0, tiled=True),
        lax.all_gather(gains, "wide", axis=1, tiled=True),
    )


def plain_scatter(*grads):
    outs = []
    for grad, axis in zip(grads, (1, 1, 1, 0, 1)):
        piece = lax.psum_scatter(grad, ("wide", "narrow"), scatter_dimension=axis, tiled=True)
        outs.append(lax.all_gather(piece.astype(jnp.bfloat16), "narrow", axis=axis, tiled=True).astype(jnp.float32))
    return tuple(outs)


def by_kernel(self_weights):
    return lax.axis_size("wide") == 16 and lax.axis_size("narrow") == 2 and self_weights.shape[1] % 48 == 0


def plain_device(
    layer_input,
    memory,
    cotangent,
    segment_ids,
    padding,
    image_of_row,
    self_weights,
    cross_weights,
    mlp_in,
    mlp_out,
    gains,
):
    self_full, cross_full, in_full, out_full, gain_full = plain_gather(
        self_weights, cross_weights, mlp_in, mlp_out, gains
    )
    gain_float = gain_full.astype(jnp.float32)
    x_zero = layer_input[0].astype(jnp.float32)
    seg_row = segment_ids[0]
    pad_row = padding[0]
    seq_len = x_zero.shape[0]
    position = jnp.arange(seq_len)
    allowed = (
        (seg_row[:, None] == seg_row[None, :])
        & (position[None, :] <= position[:, None])
        & ((pad_row[None, :] == 1) | (position[:, None] == position[None, :]))
    )
    h_one = rms_norm(x_zero, gain_float[0]).astype(jnp.bfloat16)
    q_self = linear(h_one, self_full[0]).astype(jnp.bfloat16)
    k_self = linear(h_one, self_full[1]).astype(jnp.bfloat16)
    v_self = linear(h_one, self_full[2]).astype(jnp.bfloat16)
    self_mix, self_lse = forward_heads(q_self, k_self, v_self, allowed)
    x_one = x_zero + linear(self_mix, self_full[3])
    row_ids = jnp.arange(image_of_row.shape[0])
    starts = jnp.sum(image_of_row[None, :] < image_of_row[:, None], axis=1)
    offsets = row_ids - starts
    my_index = lax.axis_index(("wide", "narrow"))
    my_offset = jnp.sum(jnp.where(row_ids == my_index, offsets, 0))
    own_patches = memory[0]
    memory_use = own_patches
    for distance in (1, 2, 3):
        arrived = shifted(own_patches, ("wide", "narrow"), distance)
        memory_use = jnp.where(my_offset == distance, arrived, memory_use)
    h_two = rms_norm(x_one, gain_float[1]).astype(jnp.bfloat16)
    q_cross = linear(h_two, cross_full[0]).astype(jnp.bfloat16)
    k_cross = linear(memory_use, cross_full[1]).astype(jnp.bfloat16)
    v_cross = linear(memory_use, cross_full[2]).astype(jnp.bfloat16)
    cross_mix, cross_lse = forward_heads(q_cross, k_cross, v_cross, None)
    x_two = x_one + linear(cross_mix, cross_full[3])
    h_three = rms_norm(x_two, gain_float[2]).astype(jnp.bfloat16)
    gate_act = linear(h_three, in_full[0])
    up_act = linear(h_three, in_full[1])
    hidden = gated_product(gate_act, up_act).astype(jnp.bfloat16)
    result = x_two + linear(hidden, out_full)
    out_low = cotangent[0]
    out_grad_w = contract_rows(hidden, out_low)
    hidden_grad = times_transposed(out_low, out_full)
    _, pullback = jax.vjp(gated_product, gate_act, up_act)
    gate_grad, up_grad = pullback(hidden_grad)
    gate_low = gate_grad.astype(jnp.bfloat16)
    up_low = up_grad.astype(jnp.bfloat16)
    in_grad = jnp.stack([contract_rows(h_three, gate_low), contract_rows(h_three, up_low)])
    h_three_grad = times_transposed(gate_low, in_full[0]) + times_transposed(up_low, in_full[1])
    _, pullback = jax.vjp(rms_norm, x_two, gain_float[2])
    x_two_norm, gain_three = pullback(h_three_grad)
    x_two_grad = out_low.astype(jnp.float32) + x_two_norm
    cross_out_low = x_two_grad.astype(jnp.bfloat16)
    cross_o_grad = contract_rows(cross_mix, cross_out_low)
    cross_mix_grad = times_transposed(cross_out_low, cross_full[3]).astype(jnp.bfloat16)
    q_cross_grad, k_cross_grad, v_cross_grad = backward_heads(
        q_cross, k_cross, v_cross, cross_mix_grad, cross_lse, None
    )
    cross_grad = jnp.stack(
        [
            contract_rows(h_two, q_cross_grad),
            contract_rows(memory_use, k_cross_grad),
            contract_rows(memory_use, v_cross_grad),
            cross_o_grad,
        ]
    )
    mem_grad = times_transposed(k_cross_grad, cross_full[1]) + times_transposed(
        v_cross_grad, cross_full[2]
    )
    h_two_grad = times_transposed(q_cross_grad, cross_full[0])
    _, pullback = jax.vjp(rms_norm, x_one, gain_float[1])
    x_one_norm, gain_two = pullback(h_two_grad)
    x_one_grad = x_two_grad + x_one_norm
    self_out_low = x_one_grad.astype(jnp.bfloat16)
    self_o_grad = contract_rows(self_mix, self_out_low)
    self_mix_grad = times_transposed(self_out_low, self_full[3]).astype(jnp.bfloat16)
    q_self_grad, k_self_grad, v_self_grad = backward_heads(
        q_self, k_self, v_self, self_mix_grad, self_lse, allowed
    )
    self_grad = jnp.stack(
        [
            contract_rows(h_one, q_self_grad),
            contract_rows(h_one, k_self_grad),
            contract_rows(h_one, v_self_grad),
            self_o_grad,
        ]
    )
    h_one_grad = (
        times_transposed(q_self_grad, self_full[0])
        + times_transposed(k_self_grad, self_full[1])
        + times_transposed(v_self_grad, self_full[2])
    )
    _, pullback = jax.vjp(rms_norm, x_zero, gain_float[0])
    x_zero_norm, gain_one = pullback(h_one_grad)
    x_grad = x_one_grad + x_zero_norm
    mem_summed = jnp.where(my_offset == 0, mem_grad, 0.0)
    for distance in (1, 2, 3):
        arrived = shifted(mem_grad.astype(jnp.bfloat16), ("wide", "narrow"), -distance).astype(
            mem_grad.dtype
        )
        neighbour = jnp.sum(jnp.where(row_ids == my_index + distance, offsets, 0))
        mem_summed = mem_summed + jnp.where(neighbour == distance, arrived, 0.0)
    gain_grad = jnp.stack([gain_one, gain_two, gain_three])
    reduced = plain_scatter(self_grad, cross_grad, in_grad, out_grad_w, gain_grad)
    return (
        result.astype(jnp.bfloat16)[None],
        x_grad[None],
        mem_summed[None],
        reduced[0],
        reduced[1],
        reduced[2],
        reduced[3],
        reduced[4],
    )


def kernel_device(
    layer_input,
    memory,
    cotangent,
    segment_ids,
    padding,
    image_of_row,
    self_weights,
    cross_weights,
    mlp_in,
    mlp_out,
    gains,
):
    result, kept = forward(
        layer_input[0],
        cotangent[0],
        memory[0],
        segment_ids,
        padding,
        image_of_row,
        gains,
        self_weights,
        cross_weights,
        mlp_in,
        mlp_out,
    )
    self_grad, cross_grad, in_grad, out_grad, x_grad, mem_grad, gain_grad, result = finish(
        *backward(kept, layer_input[0], cotangent[0], segment_ids, padding, image_of_row, gains.shape[1]),
        result,
    )
    return (result[None], x_grad[None], mem_grad[None], self_grad, cross_grad, in_grad, out_grad[0], gain_grad)


def on_device(
    layer_input,
    memory,
    cotangent,
    segment_ids,
    padding,
    image_of_row,
    self_weights,
    cross_weights,
    mlp_in,
    mlp_out,
    gains,
):
    run = kernel_device if by_kernel(self_weights) else plain_device
    return run(
        layer_input,
        memory,
        cotangent,
        segment_ids,
        padding,
        image_of_row,
        self_weights,
        cross_weights,
        mlp_in,
        mlp_out,
        gains,
    )


def solution(mesh):
    in_specs = (
        P(("wide", "narrow"), None, None),
        P(("wide", "narrow"), None, None),
        P(("wide", "narrow"), None, None),
        P(("wide", "narrow"), None),
        P(("wide", "narrow"), None),
        P(),
        P(None, "wide", None),
        P(None, "wide", None),
        P(None, "wide", None),
        P("wide", None),
        P(None, "wide"),
    )
    out_specs = (
        P(("wide", "narrow"), None, None),
        P(("wide", "narrow"), None, None),
        P(("wide", "narrow"), None, None),
        P(None, "wide", None),
        P(None, "wide", None),
        P(None, "wide", None),
        P("wide", None),
        P(None, "wide"),
    )
    return jax.shard_map(
        on_device, mesh=mesh, in_specs=in_specs, out_specs=out_specs, check_vma=False
    )
```

```python
import functools

import jax
import jax.numpy as jnp
from jax import lax
from jax.experimental import pallas as pl
from jax.experimental.pallas import tpu as pltpu
from jax.sharding import PartitionSpec as P

HEAD_DIM = 64


EPSILON = 1e-06


def shifted(value, axis, steps):
    count = lax.axis_size(axis)
    first, last = (max(0, -steps), min(count, count - steps))
    return lax.ppermute(value, axis, [(source, source + steps) for source in range(first, last)])


def rms_norm(v, g):
    return v * lax.rsqrt(jnp.mean(v * v, axis=-1, keepdims=True) + EPSILON) * g


def contract_rows(a, b):
    return lax.dot_general(a, b, (((0,), (0,)), ((), ())), preferred_element_type=jnp.float32)


def times_transposed(a, w):
    return lax.dot_general(a, w, (((1,), (1,)), ((), ())), preferred_element_type=jnp.float32)


def linear(a, w):
    return jnp.dot(a, w, preferred_element_type=jnp.float32)


def head_scores(q_part, k_part, allowed):
    scores = jnp.einsum(
        "qhd,khd->hqk", q_part, k_part, preferred_element_type=jnp.float32
    ) * HEAD_DIM ** (-0.5)
    if allowed is not None:
        scores = jnp.where(allowed[None], scores, -1e30)
    return scores


def split_heads(a, head_start):
    return a[:, head_start * HEAD_DIM : (head_start + 4) * HEAD_DIM].reshape(
        a.shape[0], 4, HEAD_DIM
    )


def forward_heads(q, k, v, allowed):
    seq_len = q.shape[0]
    head_count = q.shape[1] // HEAD_DIM
    pieces = []
    log_sums = []
    for head_start in range(0, head_count, 4):
        q_part = split_heads(q, head_start)
        k_part = split_heads(k, head_start)
        v_part = split_heads(v, head_start)
        scores = head_scores(q_part, k_part, allowed)
        highest = jnp.max(scores, axis=-1, keepdims=True)
        powers = jnp.exp(scores - highest)
        summed = jnp.sum(powers, axis=-1, keepdims=True)
        shares = (powers / summed).astype(jnp.bfloat16)
        mixed = jnp.einsum("hqk,khd->qhd", shares, v_part, preferred_element_type=jnp.float32)
        pieces.append(mixed.reshape(seq_len, -1))
        log_sums.append(highest + jnp.log(summed))
    return (jnp.concatenate(pieces, axis=1).astype(jnp.bfloat16), jnp.concatenate(log_sums, axis=0))


def backward_heads(q, k, v, mix_grad, log_sum, allowed):
    seq_len = q.shape[0]
    head_count = q.shape[1] // HEAD_DIM
    q_pieces = []
    k_pieces = []
    v_pieces = []
    for head_start in range(0, head_count, 4):
        q_part = split_heads(q, head_start)
        k_part = split_heads(k, head_start)
        v_part = split_heads(v, head_start)
        o_part = split_heads(mix_grad, head_start)
        scores = head_scores(q_part, k_part, allowed)
        shares = jnp.exp(scores - log_sum[head_start : head_start + 4])
        v_grad = jnp.einsum(
            "hqk,qhd->khd", shares.astype(jnp.bfloat16), o_part, preferred_element_type=jnp.float32
        )
        p_grad = jnp.einsum("qhd,khd->hqk", o_part, v_part, preferred_element_type=jnp.float32)
        s_grad = shares * (p_grad - jnp.sum(shares * p_grad, axis=-1, keepdims=True))
        s_low = s_grad.astype(jnp.bfloat16)
        q_grad = jnp.einsum(
            "hqk,khd->qhd", s_low, k_part, preferred_element_type=jnp.float32
        ) * HEAD_DIM ** (-0.5)
        k_grad = jnp.einsum(
            "hqk,qhd->khd", s_low, q_part, preferred_element_type=jnp.float32
        ) * HEAD_DIM ** (-0.5)
        q_pieces.append(q_grad.reshape(seq_len, -1))
        k_pieces.append(k_grad.reshape(k.shape[0], -1))
        v_pieces.append(v_grad.reshape(k.shape[0], -1))
    return (
        jnp.concatenate(q_pieces, axis=1).astype(jnp.bfloat16),
        jnp.concatenate(k_pieces, axis=1).astype(jnp.bfloat16),
        jnp.concatenate(v_pieces, axis=1).astype(jnp.bfloat16),
    )


def gated_product(gate_act, up_act):
    return jax.nn.gelu(gate_act, approximate=True) * up_act


MESH = pl.DeviceIdType.MESH


class Place:
    def __init__(self, depth):
        self.depth = depth
        self.wide = lax.axis_index("wide")
        self.x = lax.axis_index("narrow")
        self.core = self.wide % 2
        self.y = (self.wide // 2) % 2
        self.z = self.wide // 4

    def shard(self, z, y, core):
        return z * 4 + y * 2 + core

    def z_ahead(self, step):
        return (self.shard((self.z + step) % self.depth, self.y, self.core), self.x)

    def z_behind(self, step):
        return (self.z + self.depth - step) % self.depth

    @property
    def across_x(self):
        return (self.wide, 1 - self.x)

    @property
    def across_y(self):
        return (self.shard(self.z, 1 - self.y, self.core), self.x)

    @property
    def across_core(self):
        return (self.shard(self.z, self.y, 1 - self.core), self.x)

    def greet(self):
        barrier = pltpu.get_barrier_semaphore()
        others = [self.across_x, self.across_y, self.across_core]
        others += [self.z_ahead(step) for step in range(1, self.depth)]
        for other in others:
            pl.semaphore_signal(barrier, inc=1, device_id=other, device_id_type=MESH)
        pl.semaphore_wait(barrier, len(others))


def remote(src, dst, send, recv, device):
    return pltpu.make_async_remote_copy(
        src_ref=src, dst_ref=dst, send_sem=send, recv_sem=recv, device_id=device, device_id_type=MESH
    )


class Plan:
    def __init__(self, slack=2.5, latency=1.5):
        self.now = 0.0
        self.slack = slack
        self.latency = latency
        self.rate = {"c": 400e3, "x": 50e3, "y": 50e3, "z": 50e3}
        self.free = dict.fromkeys(self.rate, 0.0)
        self.queues = {link: [] for link in self.rate}
        self.flying = []
        self.serial = 0

    def send(self, link, rank, size, start, arrive, cost=0.2):
        self.serial += 1
        self.queues[link].append((rank, self.serial, size, start, arrive, cost))

    def later(self, delay, arrive, cost=0.2):
        self.serial += 1
        self.flying.append((self.now + delay, self.serial, cost, arrive))

    def issue(self):
        for link, queue in self.queues.items():
            while queue and self.free[link] <= self.now + self.slack:
                first = min(queue, key=lambda q: q[:2])
                queue.remove(first)
                _, serial, size, start, arrive, cost = first
                start()
                self.now += 0.03
                self.free[link] = max(self.free[link], self.now) + size / self.rate[link]
                if arrive is not None:
                    self.flying.append((self.free[link] + self.latency, serial, cost, arrive))

    def drain(self):
        self.issue()
        while self.flying:
            first = min(self.flying, key=lambda f: f[:2])
            if first[0] > self.now:
                break
            self.flying.remove(first)
            first[3]()
            self.now += first[2]
            self.issue()

    def busy(self):
        return bool(self.flying) or any(self.queues.values())

    def step(self):
        self.issue()
        times = [f[0] for f in self.flying]
        times += [self.free[link] - self.slack for link, queue in self.queues.items() if queue]
        self.now = max(self.now, min(times))
        self.drain()

    def work(self, cost, run):
        self.drain()
        run()
        self.now += cost


class Gather:
    def __init__(self, place, own, full, rows, side, y_first, sems):
        self.p = place
        self.own = own
        self.full = full
        self.rows = rows
        self.side = side
        self.main = rows - side
        self.y_first = y_first
        self.main_send, self.main_recv, self.x_send, self.x_recv, self.c_send, self.c_recv = sems

    def block(self, ref, start, size):
        return ref.at[:, pl.ds(pl.multiple_of(start, 16), size), :]

    def at(self, z, y, core, start, size):
        return self.block(self.full, self.p.shard(z, y, core) * self.rows + start, size)

    def owner(self, n):
        step, other = n % self.p.depth, n // self.p.depth
        return self.p.z_behind(step), (1 - self.p.y if other else self.p.y)

    @property
    def main_start(self):
        return self.side * self.p.x

    def side_start(self, x):
        return self.main * x

    def main_piece(self, z, y, source=False):
        p = self.p
        return self.at(z, y, p.core, self.main_start, self.main)

    def arriving(self, n):
        p = self.p
        z, y = self.owner(n)
        piece = self.main_piece(z, y)
        return remote(piece, piece, self.main_send.at[0], self.main_recv.at[n], p.across_y)

    def y_copy(self, n):
        p = self.p
        z, y = self.owner(n)
        dst = self.main_piece(z, y)
        src = self.block(self.own, self.main_start, self.main) if n == 0 else dst
        return remote(src, dst, self.main_send.at[n], self.main_recv.at[n + p.depth], p.across_y)

    def z_copy(self, step, other):
        p = self.p
        y = 1 - p.y if other else p.y
        dst = self.main_piece(p.z, y)
        src = dst if other else self.block(self.own, self.main_start, self.main)
        slot = p.depth + (step - 1) + (p.depth - 1) * other
        return remote(
            src, dst, self.main_send.at[slot], self.main_recv.at[step + p.depth * other], p.z_ahead(step)
        )

    def relay_copy(self, other, up):
        p = self.p
        z, target = (0, 3) if up else (3, 0)
        y = 1 - p.y if other else p.y
        piece = self.main_piece(z, y)
        slot = p.depth + 2 * (p.depth - 1) + other
        step = 3 if up else 1
        device = (p.shard(target, p.y, p.core), p.x)
        return remote(piece, piece, self.main_send.at[slot], self.main_recv.at[step + p.depth * other], device)

    def x_copy(self, n, x):
        p = self.p
        z, y = self.owner(n)
        piece = self.at(z, y, p.core, self.side_start(x), self.side)
        return remote(piece, piece, self.x_send.at[n], self.x_recv.at[n], p.across_x)

    def c_copy(self, n, core, side):
        p = self.p
        slot = n + (2 * p.depth if side else 0)
        z, y = self.owner(n)
        if n == 0:
            src, dst = self.own, self.at(z, y, core, 0, self.rows)
        else:
            start, size = (self.side_start(1 - p.x), self.side) if side else (self.main_start, self.main)
            src = dst = self.at(z, y, core, start, size)
        return remote(src, dst, self.c_send.at[slot], self.c_recv.at[slot], p.across_core)

    def copy_own(self):
        p = self.p
        return pltpu.make_async_copy(self.own, self.at(p.z, p.y, p.core, 0, self.rows), self.main_send.at[4 * p.depth])

    def each_z(self, other, act):
        p = self.p
        for step in range(1, p.depth):
            if step == 2:
                act(self.z_copy(step, other))
            else:
                end = 0 if step == 3 else 3

                @pl.when(p.z != end)
                def _():
                    act(self.z_copy(step, other))

    def each_relay(self, other, act):
        p = self.p

        @pl.when(p.z == 2)
        def _():
            act(self.relay_copy(other, True))

        @pl.when(p.z == 1)
        def _():
            act(self.relay_copy(other, False))

    def begin(self):
        self.copy_own().start()
        self.y_copy(0).start()
        self.each_z(0, lambda copy: copy.start())
        self.c_copy(0, self.p.core, False).start()

    def order(self):
        depth = self.p.depth
        if self.y_first:
            return [depth, 2, 2 + depth, 1, 3, 1 + depth, 3 + depth]
        return [2, 1, 3, depth, depth + 2, depth + 1, depth + 3]

    def take(self, n):
        p = self.p
        depth = p.depth
        self.arriving(n).wait_recv()
        other = n // depth
        if n % depth == 2 and (self.y_first or other == 0):
            self.each_relay(other, lambda copy: copy.start())
        if self.y_first:
            if n == depth:
                self.each_z(1, lambda copy: copy.start())
        elif other == 0:
            self.y_copy(n).start()
        if self.side:
            self.x_copy(n, p.x).start()
        self.c_copy(n, p.core, False).start()

    def take_x(self, n):
        p = self.p
        if self.side:
            self.x_copy(n, 1 - p.x).wait_recv()
            self.c_copy(n, p.core, True).start()

    def complete(self):
        p = self.p
        self.copy_own().wait()
        for n in range(2 * p.depth):
            self.c_copy(n, 1 - p.core, False).wait_recv()
            if self.side and n:
                self.c_copy(n, 1 - p.core, True).wait_recv()

    def end(self):
        p = self.p

        def wait(copy):
            copy.wait_send()

        for n in range(1 if self.y_first else p.depth):
            self.y_copy(n).wait_send()
        for other in range(2 if self.y_first else 1):
            self.each_z(other, wait)
            self.each_relay(other, wait)
        for n in range(2 * p.depth):
            self.c_copy(n, p.core, False).wait_send()
            if self.side and n:
                self.x_copy(n, p.x).wait_send()
                self.c_copy(n, p.core, True).wait_send()


def gather_sems(count, depth):
    sizes = (4 * depth + 1, 2 * depth, 2 * depth, 2 * depth, 4 * depth, 4 * depth)
    return [pltpu.SemaphoreType.DMA((count, size)) for size in sizes]


LOW = jnp.bfloat16


def dot(a, b, ca=1, cb=0):
    return lax.dot_general(a, b, (((ca,), (cb,)), ((), ())), preferred_element_type=jnp.float32)


def norm_rows(source, gain, target):
    rows = source.shape[0]
    chunk = 64

    @pl.loop(0, rows // chunk)
    def _(i):
        span = pl.ds(pl.multiple_of(i * chunk, chunk), chunk)
        v = source[span].astype(jnp.float32)
        scale = lax.rsqrt(jnp.mean(v * v, axis=-1, keepdims=True) + EPSILON)
        target[span] = (v * scale * gain).astype(LOW)


def norm_back_rows(source, gain, grad, dout, target, gain_grad):
    rows, width = source.shape
    chunk = 64
    gain_grad[...] = jnp.zeros_like(gain_grad)

    @pl.loop(0, rows // chunk)
    def _(i):
        span = pl.ds(pl.multiple_of(i * chunk, chunk), chunk)
        v = source[span].astype(jnp.float32)
        dh = grad[span]
        scale = lax.rsqrt(jnp.mean(v * v, axis=-1, keepdims=True) + EPSILON)
        unit = v * scale
        gain_grad[...] += jnp.sum(dh * unit, axis=0, keepdims=True)
        scaled = dh * gain
        along = jnp.mean(scaled * unit, axis=-1, keepdims=True)
        target[span] = (dout[span].astype(jnp.float32) + scale * (scaled - unit * along)).astype(target.dtype)


def pair_span(pair):
    return pl.ds(pl.multiple_of(pair * 2 * HEAD_DIM, 2 * HEAD_DIM), 2 * HEAD_DIM)


def attend_pair(pair, q, k, v, bias, mixed, lse):
    span = pair_span(pair)
    q_two, k_two, v_two = q[:, span], k[:, span], v[:, span]
    rows = q_two.shape[0]
    low_half = lax.broadcasted_iota(jnp.int32, q_two.shape, 1) < HEAD_DIM
    lane = lax.broadcasted_iota(jnp.int32, (rows, 128), 1)
    outs = []
    sums = lse[...]
    for half in range(2):
        mine = low_half if half == 0 else ~low_half
        scores = dot(jnp.where(mine, q_two, jnp.zeros_like(q_two)), k_two, 1, 1) * HEAD_DIM ** (-0.5)
        if bias is not None:
            scores = scores + bias[...]
        highest = jnp.max(scores, axis=-1, keepdims=True)
        powers = jnp.exp(scores - highest)
        summed = jnp.sum(powers, axis=-1, keepdims=True)
        shares = (powers / summed).astype(LOW)
        outs.append(dot(shares, v_two))
        sums = jnp.where(lane == 2 * pair + half, highest + jnp.log(summed), sums)
    mixed[:, span] = jnp.where(low_half, outs[0], outs[1]).astype(LOW)
    lse[...] = sums


def gelu_parts(gate):
    inner = (2.0 / 3.141592653589793) ** 0.5
    square = gate * gate
    bent = jnp.tanh(inner * gate * (1.0 + 0.044715 * square))
    half = 0.5 * (1.0 + bent)
    slope = half + 0.5 * gate * (1.0 - bent * bent) * inner * (1.0 + 3 * 0.044715 * square)
    return gate * half, slope


class Rows:
    def __init__(self, place, count):
        self.p = place
        self.count = count
        self.row = place.wide * 2 + place.x

    def device(self, row):
        return (row // 2, row % 2)

    def when(self, distance, act):
        @pl.when((self.row + distance >= 0) & (self.row + distance < self.count))
        def _():
            act(self.device(self.row + distance))

    def near(self):
        return (-2, -1, 1, 2)

    def present(self):
        below = jnp.minimum(self.row, 2)
        above = jnp.minimum(self.count - 1 - self.row, 2)
        return below + above


def greet_all(place, rows):
    barrier = pltpu.get_barrier_semaphore()
    others = [place.across_x, place.across_y, place.across_core]
    others += [place.z_ahead(step) for step in range(1, place.depth)]

    def hello(device):
        pl.semaphore_signal(barrier, inc=1, device_id=device, device_id_type=MESH)

    for other in others:
        hello(other)
    for distance in rows.near():
        rows.when(distance, hello)
    pl.semaphore_wait(barrier, len(others) + rows.present())


def pass_rows(rows, source, target, distance, sems):
    send, recv = sems

    def copy(device):
        return remote(source, target, send, recv, device)

    def start():
        rows.when(distance, lambda device: copy(device).start())

    def arrive():
        rows.when(-distance, lambda device: copy(device).wait_recv())

    def end():
        rows.when(distance, lambda device: copy(device).wait_send())

    return start, arrive, end


MLP_CUTS = (0, 512, 1024, 1536, 1792, 2048)
GATHER_LAYOUT = (
    (4, 0, 1, 0, 128, 0),
    (0, 0, 3, 0, 768, 16),
    (0, 3, 4, 0, 768, 16),
    (1, 0, 2, 0, 768, 16),
    (1, 2, 4, 0, 768, 16),
    (3, 0, 1, 0, 768, 48),
    *((2, 0, 2, first, last, 16) for first, last in zip(MLP_CUTS, MLP_CUTS[1:])),
)
WIDTH, HIDDEN, TOKENS, PATCHES = 768, 2048, 384, 256

class Spec:
    def __init__(self, *shape, dtype=LOW):
        self.shape = shape
        self.dtype = dtype

    def array(self):
        return jax.ShapeDtypeStruct(self.shape, self.dtype)

    def scratch(self):
        return pltpu.VMEM(self.shape, self.dtype)


def specs(table):
    return [spec for spec in vars(table).values() if isinstance(spec, Spec)]


class K:
    gain = Spec(8, WIDTH, dtype=jnp.float32)
    h1t = Spec(WIDTH, TOKENS)
    q1 = Spec(TOKENS, WIDTH)
    k1 = Spec(TOKENS, WIDTH)
    v1 = Spec(TOKENS, WIDTH)
    o1t = Spec(WIDTH, TOKENS)
    lse1 = Spec(128, TOKENS, dtype=jnp.float32)
    x1 = Spec(TOKENS, WIDTH, dtype=jnp.float32)
    h2t = Spec(WIDTH, TOKENS)
    memt = Spec(WIDTH, PATCHES)
    q2 = Spec(TOKENS, WIDTH)
    k2 = Spec(PATCHES, WIDTH)
    v2 = Spec(PATCHES, WIDTH)
    o2t = Spec(WIDTH, TOKENS)
    lse2 = Spec(128, TOKENS, dtype=jnp.float32)
    h3t = Spec(WIDTH, TOKENS)
    hiddent = Spec(HIDDEN, TOKENS)
    dgate = Spec(TOKENS, HIDDEN)
    dup = Spec(TOKENS, HIDDEN)
    dx2 = Spec(TOKENS, WIDTH, dtype=jnp.float32)
    gain3 = Spec(1, WIDTH, dtype=jnp.float32)


class W:
    w_self = Spec(4, WIDTH, WIDTH)
    w_cross = Spec(4, WIDTH, WIDTH)
    w_in = Spec(2, WIDTH, HIDDEN)
    w_out = Spec(1, HIDDEN, WIDTH)
    w_gain = Spec(1, 256, 128)


class F:
    bias = Spec(TOKENS, TOKENS, dtype=jnp.float32)
    h = Spec(TOKENS, WIDTH)
    mix = Spec(TOKENS, WIDTH)
    lse = Spec(TOKENS, 128, dtype=jnp.float32)
    mem_one = Spec(PATCHES, WIDTH)
    mem = Spec(PATCHES, WIDTH)
    mem_got = Spec(2, PATCHES, WIDTH)
    x2 = Spec(TOKENS, WIDTH, dtype=jnp.float32)
    gate = Spec(TOKENS, 512, dtype=jnp.float32)
    up = Spec(TOKENS, 512, dtype=jnp.float32)
    dhid = Spec(TOKENS, 512, dtype=jnp.float32)
    hidden = Spec(TOKENS, HIDDEN)
    gain_own = Spec(1, 16, 128)
    total = Spec(TOKENS, WIDTH, dtype=jnp.float32)
    dh = Spec(TOKENS, WIDTH, dtype=jnp.float32)


PASSED = specs(K) + [W.w_self, W.w_cross]


def as_column(row):
    return jnp.broadcast_to(row.astype(jnp.float32), (128, row.shape[1])).T


def row_offset(images, row, count):
    image = images[jnp.minimum(row, count - 1)]
    start = sum((images[other] < image).astype(jnp.int32) for other in range(count))
    return jnp.where(row < count, row - start, 0)


def forward_kernel(depth, row_count, refs):
    (x0, dy, memory, segments, padding, images, gains) = refs[:7]
    owns = refs[7:11]
    out = refs[11]
    rest = refs[12:]
    kept_out, rest = dict(zip(PASSED, rest)), rest[len(PASSED) :]
    kept, rest = dict(zip(specs(K), rest)), rest[len(specs(K)) :]
    weights, rest = dict(zip(specs(W), rest)), rest[len(specs(W)) :]
    local, rest = dict(zip(specs(F), rest)), rest[len(specs(F)) :]
    gather_sem, row_sem, keep_sem, mlp_sem = rest[:6], rest[6], rest[7], rest[8]
    owns = (*owns, local[F.gain_own])
    kept_numbers = {name: number for number, name in enumerate(kept_out)}

    def keep_copy(name):
        source = weights[name] if name in weights else kept[name]
        return pltpu.make_async_copy(source, kept_out[name], keep_sem.at[kept_numbers[name]])

    def keep(*names):
        for name in names:
            keep_copy(name).start()

    place = Place(depth)
    rows = Rows(place, row_count)
    fulls = [weights[spec] for spec in specs(W)]
    blocks = []
    for number, (array, first, last, c0, c1, side) in enumerate(GATHER_LAYOUT):
        own, full = owns[array], fulls[array]
        blocks.append(
            Gather(
                place,
                own.at[first:last, :, c0:c1],
                full.at[first:last, :, c0:c1],
                own.shape[1],
                side,
                False,
                [sem.at[number] for sem in gather_sem],
            )
        )
    near_start, near_arrive, near_end = pass_rows(
        rows, memory, local[F.mem_got].at[0], 1, (row_sem.at[0], row_sem.at[1])
    )
    far_start, far_arrive, far_end = pass_rows(
        rows, local[F.mem_one], local[F.mem_got].at[1], 2, (row_sem.at[2], row_sem.at[3])
    )
    gain = kept[K.gain]
    offset = row_offset(images, rows.row, row_count)
    local[F.gain_own][...] = jnp.zeros_like(local[F.gain_own])
    local[F.gain_own][0, 0 : gains.shape[0], 0 : gains.shape[1]] = gains[...]

    def make_bias():
        seg_q, seg_k = as_column(segments[...])[:, 0:1], segments[...].astype(jnp.float32)
        query = lax.broadcasted_iota(jnp.int32, (TOKENS, TOKENS), 0)
        key = lax.broadcasted_iota(jnp.int32, (TOKENS, TOKENS), 1)
        allowed = (seg_q == seg_k) & (key <= query) & ((padding[...] == 1) | (key == query))
        local[F.bias][...] = jnp.where(allowed, 0.0, -1e30)

    def make_gain():
        total = jnp.zeros((16, WIDTH), jnp.float32)
        count = row_count // 2
        share = WIDTH // count
        for number in range(count):
            row = lax.broadcasted_iota(jnp.int32, (128, WIDTH), 0)
            column = lax.broadcasted_iota(jnp.int32, (128, WIDTH), 1)
            pick = ((column - number * share) == row) & (row < share)
            total += dot(weights[W.w_gain][0, number * 16 : number * 16 + 16, :], pick.astype(LOW))
        gain[...] = total[:8]

    def first_norm():
        norm_rows(x0, gain[0:1], local[F.h])
        kept[K.h1t][...] = local[F.h][...].T
        keep(K.gain, K.h1t)

    def project(name, w, index):
        def run():
            kept[name][...] = dot(local[F.h][...], weights[w][index]).astype(LOW)
            keep(name)

        return run

    def self_pair(pair):
        return lambda: attend_pair(pair, kept[K.q1], kept[K.k1], kept[K.v1], local[F.bias], local[F.mix], local[F.lse])

    def clear_lse():
        local[F.lse][...] = jnp.zeros_like(local[F.lse])

    def self_out():
        kept[K.lse1][...] = local[F.lse][...].T
        kept[K.o1t][...] = local[F.mix][...].T
        kept[K.x1][...] = x0[...].astype(jnp.float32) + dot(local[F.mix][...], weights[W.w_self][3])
        keep(K.lse1, K.o1t, K.x1)

    def second_norm():
        norm_rows(kept[K.x1], gain[1:2], local[F.h])
        kept[K.h2t][...] = local[F.h][...].T
        keep(K.h2t)

    def memory_near():
        near_arrive()
        local[F.mem_one][...] = jnp.where(offset >= 1, local[F.mem_got][0], memory[...])
        far_start()

    def memory_far():
        far_arrive()
        local[F.mem][...] = jnp.where(offset >= 2, local[F.mem_got][1], local[F.mem_one][...])
        kept[K.memt][...] = local[F.mem][...].T
        keep(K.memt)

    def project_memory(name, index):
        def run():
            kept[name][...] = dot(local[F.mem][...], weights[W.w_cross][index]).astype(LOW)
            keep(name)

        return run

    def cross_pair(pair):
        return lambda: attend_pair(pair, kept[K.q2], kept[K.k2], kept[K.v2], None, local[F.mix], local[F.lse])

    def cross_out():
        kept[K.lse2][...] = local[F.lse][...].T
        kept[K.o2t][...] = local[F.mix][...].T
        local[F.x2][...] = kept[K.x1][...] + dot(local[F.mix][...], weights[W.w_cross][3])
        keep(K.lse2, K.o2t)

    def third_norm():
        norm_rows(local[F.x2], gain[2:3], local[F.h])
        kept[K.h3t][...] = local[F.h][...].T
        keep(K.h3t)

    def mlp_dots(number):
        c0, c1 = MLP_CUTS[number], MLP_CUTS[number + 1]

        def run():
            h = local[F.h][...]
            local[F.dhid][:, : c1 - c0] = dot(dy[...], weights[W.w_out][0, c0:c1, :], 1, 1)
            local[F.gate][:, : c1 - c0] = dot(h, weights[W.w_in][0, :, c0:c1])
            local[F.up][:, : c1 - c0] = dot(h, weights[W.w_in][1, :, c0:c1])

        return run

    def mlp_copies(number):
        c0, c1 = MLP_CUTS[number], MLP_CUTS[number + 1]
        cuts = ((K.hiddent, (slice(c0, c1), slice(None))), (K.dgate, (slice(None), slice(c0, c1))))
        cuts += ((K.dup, (slice(None), slice(c0, c1))),)
        return [
            pltpu.make_async_copy(kept[name].at[cut], kept_out[name].at[cut], mlp_sem.at[number, place_of])
            for place_of, (name, cut) in enumerate(cuts)
        ]

    def mlp_point(number):
        c0, c1 = MLP_CUTS[number], MLP_CUTS[number + 1]
        width = c1 - c0

        def run():
            @pl.loop(0, TOKENS // 16)
            def _(i):
                span = pl.ds(pl.multiple_of(i * 16, 16), 16)
                act, slope = gelu_parts(local[F.gate][span, :width])
                up, dhid = local[F.up][span, :width], local[F.dhid][span, :width]
                local[F.hidden][span, c0:c1] = (act * up).astype(LOW)
                kept[K.dgate][span, c0:c1] = (dhid * up * slope).astype(LOW)
                kept[K.dup][span, c0:c1] = (dhid * act).astype(LOW)

            kept[K.hiddent][c0:c1, :] = local[F.hidden][:, c0:c1].T
            for copy in mlp_copies(number):
                copy.start()

        return run

    def mlp_back(number):
        c0, c1 = MLP_CUTS[number], MLP_CUTS[number + 1]

        def run():
            value = dot(kept[K.dgate][:, c0:c1], weights[W.w_in][0, :, c0:c1], 1, 1)
            value += dot(kept[K.dup][:, c0:c1], weights[W.w_in][1, :, c0:c1], 1, 1)
            local[F.dh][...] = value if number == 0 else local[F.dh][...] + value

        return run

    def mlp_sum(number):
        c0, c1 = MLP_CUTS[number], MLP_CUTS[number + 1]

        def run():
            before = local[F.x2] if number == 0 else local[F.total]
            value = before[...] + dot(local[F.hidden][:, c0:c1], weights[W.w_out][0, c0:c1, :])
            if c1 == HIDDEN:
                out[...] = value.astype(LOW)
            else:
                local[F.total][...] = value

        return run

    def mlp_norm():
        norm_back_rows(local[F.x2], gain[2:3], local[F.dh], dy, kept[K.dx2], kept[K.gain3])
        keep(K.dx2, K.gain3)

    work = [
        (None, 0.5, make_bias),
        (None, 0.1, clear_lse),
        (0, 2.0, make_gain),
        (0, 1.5, first_norm),
        (1, 0.7, project(K.q1, W.w_self, 0)),
        (1, 0.7, project(K.k1, W.w_self, 1)),
        (1, 0.7, project(K.v1, W.w_self, 2)),
    ]
    work += [(1, 1.2, self_pair(pair)) for pair in range(6)]
    work += [
        (2, 0.1, lambda: keep(W.w_self)),
        (2, 1.5, self_out),
        (2, 1.2, second_norm),
        (2, 0.5, memory_near),
        (3, 0.7, project(K.q2, W.w_cross, 0)),
        (3, 0.6, memory_far),
        (3, 0.6, project_memory(K.k2, 1)),
        (4, 0.6, project_memory(K.v2, 2)),
        (4, 0.1, lambda: keep(W.w_cross)),
    ]
    work += [(4, 0.9, cross_pair(pair)) for pair in range(6)]
    work += [(4, 1.5, cross_out), (4, 1.2, third_norm)]
    for number in range(len(MLP_CUTS) - 1):
        share = (MLP_CUTS[number + 1] - MLP_CUTS[number]) / 512
        need = 6 + number
        work += [(need, 1.7 * share, mlp_dots(number)), (need, 1.8 * share, mlp_point(number))]
        work += [(need, 1.2 * share, mlp_back(number)), (need, 0.7 * share, mlp_sum(number))]
    work += [(None, 1.2, mlp_norm)]

    count = len(blocks)
    events = []
    for turn in range(count + 3):
        if turn + 2 < count:
            events.append((blocks[turn + 2].begin, None))
        if turn < count:
            for n in blocks[turn].order()[:3]:
                events.append((functools.partial(blocks[turn].take, n), None))
        if 0 <= turn - 1 < count:
            for n in blocks[turn - 1].order()[3:]:
                events.append((functools.partial(blocks[turn - 1].take, n), None))
        if 0 <= turn - 2 < count and blocks[turn - 2].side:
            for n in blocks[turn - 2].order():
                events.append((functools.partial(blocks[turn - 2].take_x, n), None))
        if 0 <= turn - 3 < count:
            events.append((blocks[turn - 3].complete, turn - 3))

    greet_all(place, rows)
    blocks[0].begin()
    blocks[1].begin()
    near_start()
    ready = -1
    done = 0

    def can():
        return done < len(work) and (work[done][0] is None or work[done][0] <= ready)

    for act, completes in events:
        act()
        if completes is not None:
            ready = completes
        if can():
            work[done][2]()
            done += 1
    while can():
        work[done][2]()
        done += 1
    for block in blocks:
        block.end()
    near_end()
    far_end()
    for number in range(len(MLP_CUTS) - 1):
        for copy in mlp_copies(number):
            copy.wait()
    for name in kept_out:
        if name not in (K.hiddent, K.dgate, K.dup):
            keep_copy(name).wait()


def forward(
    layer_input,
    cotangent,
    memory,
    segments,
    padding,
    image_of_row,
    gains,
    self_weights,
    cross_weights,
    mlp_in,
    mlp_out,
):
    wide = lax.axis_size("wide")
    depth = wide // 4
    owns = (self_weights, cross_weights, mlp_in, mlp_out[None])
    vmem, anywhere, smem = (pl.BlockSpec(memory_space=space) for space in (pltpu.VMEM, pl.ANY, pltpu.SMEM))
    kept = [spec.array() for spec in PASSED]
    outs = pl.pallas_call(
        lambda *refs: forward_kernel(depth, 2 * wide, refs),
        out_shape=[jax.ShapeDtypeStruct(layer_input.shape, LOW)] + kept,
        in_specs=[vmem] * 5 + [smem, vmem] + [anywhere] * 4,
        out_specs=[vmem] + [anywhere] * len(kept),
        scratch_shapes=[spec.scratch() for table in (K, W, F) for spec in specs(table)]
        + gather_sems(len(GATHER_LAYOUT), depth)
        + [
            pltpu.SemaphoreType.DMA((4,)),
            pltpu.SemaphoreType.DMA((len(kept),)),
            pltpu.SemaphoreType.DMA((len(MLP_CUTS) - 1, 3)),
        ],
        compiler_params=pltpu.CompilerParams(
            collective_id=0, has_side_effects=True, vmem_limit_bytes=60 * 2**20
        ),
        name="forward",
    )(layer_input, cotangent, memory, segments, padding, image_of_row, gains, *owns)
    return outs[0], dict(zip(PASSED, outs[1:]))


class Scatter:
    def __init__(self, place, bufs, outs, block, sems):
        self.p = place
        rows, side = block.rows, block.side
        self.width = block.width
        self.relay = block.relay
        self.staged, self.held, self.from_x, self.from_y, self.from_z, self.relayed, self.done, self.other = bufs
        self.outs = outs
        self.rows = rows
        self.side = side
        self.main = rows - side
        self.send, self.recv = sems

    def span(self, start, size):
        return pl.ds(pl.multiple_of(start, 16), size)

    @property
    def main_span(self):
        return self.span(self.side * self.p.x, self.main)

    def side_span(self, x):
        return self.span(self.main * x, self.side)

    def c_copy(self):
        return remote(self.staged, self.held, self.send.at[0], self.recv.at[0], self.p.across_core)

    def x_copy(self):
        p = self.p
        return remote(
            self.held.at[:, :, :, self.side_span(1 - p.x)],
            self.from_x,
            self.send.at[1],
            self.recv.at[1],
            p.across_x,
        )

    def y_copy(self):
        p = self.p
        return remote(
            self.held.at[:, :, 1 - p.y, self.main_span], self.from_y, self.send.at[2], self.recv.at[2], p.across_y
        )

    def z_piece(self, z):
        return self.held.at[:, z, self.p.y, self.main_span]

    def z_copy(self, step):
        p = self.p
        return remote(
            self.z_piece((p.z + step) % p.depth),
            self.from_z.at[step - 1],
            self.send.at[2 + step],
            self.recv.at[2 + step],
            p.z_ahead(step),
        )

    def relay_copy(self, up):
        p = self.p
        target, between = (3, 1) if up else (0, 2)
        device = (p.shard(between, p.y, p.core), p.x)
        return remote(self.z_piece(target), self.relayed, self.send.at[6], self.recv.at[6], device)

    def last_copy(self):
        return remote(self.done, self.other, self.send.at[7], self.recv.at[7], self.p.across_x)

    def blank(self):
        p = self.p
        if not self.relay:
            return

        @pl.when(p.z == 0)
        def _():
            self.from_z[0] = jnp.zeros_like(self.from_z[0])

        @pl.when(p.z == 3)
        def _():
            self.from_z[2] = jnp.zeros_like(self.from_z[2])

    def each_z(self, act_direct, act_late, act_relay):
        p = self.p
        if not self.relay:
            if act_direct is not None:
                for step in range(1, p.depth):
                    act_direct(self.z_copy(step))
            return
        if act_direct is not None:

            @pl.when(p.z != 0)
            def _():
                act_direct(self.z_copy(3))

            @pl.when(p.z != 3)
            def _():
                act_direct(self.z_copy(1))

            @pl.when((p.z == 0) | (p.z == 3))
            def _():
                act_direct(self.z_copy(2))

        if act_late is not None:

            @pl.when(p.z == 1)
            def _():
                act_late(self.z_copy(2), 3)

            @pl.when(p.z == 2)
            def _():
                act_late(self.z_copy(2), 0)

        if act_relay is not None:

            @pl.when(p.z == 0)
            def _():
                act_relay(self.relay_copy(True))

            @pl.when(p.z == 3)
            def _():
                act_relay(self.relay_copy(False))

    def start_c(self):
        self.c_copy().start()

    def take_x(self):
        self.x_copy().wait_recv()
        span = self.side_span(self.p.x)
        self.held[:, :, :, span] = self.held[:, :, :, span] + self.from_x[...]

    def take_y(self):
        p = self.p
        self.y_copy().wait_recv()
        span = self.main_span
        self.held[:, :, p.y, span] = self.held[:, :, p.y, span] + self.from_y[...]

    def start_z(self):
        self.each_z(lambda copy: copy.start(), None, lambda copy: copy.start())

    def take_relay(self):
        def late(copy, target):
            self.relay_copy(True).wait_recv()
            p = self.p
            span = self.main_span
            self.held[:, target, p.y, span] = self.held[:, target, p.y, span] + self.relayed[...]
            copy.start()

        self.each_z(None, late, None)

    def take_z(self):
        p = self.p
        self.z_copy(2).wait_recv()
        if self.relay:

            @pl.when(p.z != 0)
            def _():
                self.z_copy(1).wait_recv()

            @pl.when(p.z != 3)
            def _():
                self.z_copy(3).wait_recv()

        else:
            self.z_copy(1).wait_recv()
            self.z_copy(3).wait_recv()

        total = self.held[:, p.z, p.y, self.main_span].astype(jnp.float32)
        for step in range(1, p.depth):
            total += self.from_z[step - 1].astype(jnp.float32)
        self.done[...] = total.astype(LOW)

    def take_last(self):
        p = self.p
        self.last_copy().wait_recv()
        side, both = self.side, self.main - self.side
        for number, (out, mat, column) in enumerate(self.outs):
            columns = slice(column, column + self.width)
            if side:
                out[mat, self.side_span(p.x), columns] = self.done[number, self.span(both * p.x, side)].astype(
                    jnp.float32
                )
                out[mat, self.side_span(1 - p.x), columns] = self.other[
                    number, self.span(both * (1 - p.x), side)
                ].astype(jnp.float32)
            out[mat, side : side + both, columns] = self.done[number, self.span(side * (1 - p.x), both)].astype(
                jnp.float32
            ) + self.other[number, self.span(side * p.x, both)].astype(jnp.float32)

    def end(self):
        def wait(copy, target=None):
            copy.wait_send()

        if self.side:
            self.x_copy().wait_send()
        self.y_copy().wait_send()
        self.each_z(wait, wait, wait)
        self.last_copy().wait_send()


class Block:
    def __init__(self, out, pieces, rows, side, width=256, relay=True):
        self.out, self.pieces, self.rows, self.side = out, tuple(pieces), rows, side
        self.width, self.relay = width, relay

    @property
    def ring(self):
        return self.rows, self.width


def block_list():
    found = [Block(3, [(0, 0)], 128, 0, 256, False)] + [Block(3, [(0, c)], 128, 32, 256, False) for c in (256, 512)]
    found += [Block(2, [(m, first + c) for c in range(0, 1024, 256)], 48, 16) for m in (0, 1) for first in (0, 1024)]
    found += [Block(1, [(3, c) for c in range(0, 768, 256)], 48, 0)]
    found += [Block(1, [(m, c) for m in range(3)], 48, 16) for c in (0, 256, 512)]
    found += [Block(0, [(3, c) for c in range(0, 768, 256)], 48, 0)]
    found += [Block(0, [(m, c) for m in range(3)], 48, 16, 128, False) for c in range(0, 768, 128)]
    return found


SCATTER_LAYOUT = block_list()
RINGS = {(128, 256): (2, 1), (48, 256): (3, 4), (48, 128): (2, 3)}


def scatter_buffers(depth):
    bufs = []
    for block in SCATTER_LAYOUT:
        subs, rows, side, width = len(block.pieces), block.rows, block.side, block.width
        main = rows - side
        bufs += [
            pltpu.VMEM((subs, depth, 2, rows, width), LOW),
            pltpu.VMEM((subs, depth, 2, side, width) if side else (16, 128), LOW),
            pltpu.VMEM((subs, depth, main, width), LOW),
            pltpu.VMEM((depth - 1, subs, main, width), LOW),
            pltpu.VMEM((subs, main, width), LOW),
            pltpu.VMEM((subs, main, width), LOW),
            pltpu.VMEM((subs, main, width), LOW),
        ]
    return bufs


def staging_buffers(depth):
    return [
        pltpu.VMEM((slots, subs, depth, 2, rows, width), LOW) for (rows, width), (slots, subs) in RINGS.items()
    ]


class K0:
    x0 = Spec(TOKENS, WIDTH)


class B:
    biast = Spec(TOKENS, TOKENS, dtype=jnp.float32)
    dlow = Spec(TOKENS, WIDTH)
    do = Spec(TOKENS, WIDTH)
    dq = Spec(TOKENS, WIDTH)
    dk = Spec(TOKENS, WIDTH)
    dv = Spec(TOKENS, WIDTH)
    dh = Spec(TOKENS, WIDTH, dtype=jnp.float32)
    mem_sum = Spec(PATCHES, WIDTH, dtype=jnp.float32)
    mem_low = Spec(2, PATCHES, WIDTH)
    mem_got = Spec(2, PATCHES, WIDTH)
    gains = Spec(8, WIDTH, dtype=jnp.float32)
    gain_got = Spec(6, 8, WIDTH, dtype=jnp.float32)
    gain_row = Spec(1, WIDTH, dtype=jnp.float32)


def attend_back_pair(pair, q, k, v, do, lse, bias, dq, dk, dv):
    span = pair_span(pair)
    q_two, k_two, v_two, do_two = q[:, span], k[:, span], v[:, span], do[:, span]
    low_q = lax.broadcasted_iota(jnp.int32, q_two.shape, 1) < HEAD_DIM
    low_k = lax.broadcasted_iota(jnp.int32, k_two.shape, 1) < HEAD_DIM
    scale = HEAD_DIM ** (-0.5)
    grads = []
    for half in range(2):
        mine = low_q if half == 0 else ~low_q
        scores = dot(k_two, jnp.where(mine, q_two, jnp.zeros_like(q_two)), 1, 1) * scale
        if bias is not None:
            scores = scores + bias[...]
        head = 2 * pair + half
        shares = jnp.exp(scores - lse[head : head + 1, :])
        p_grad = dot(v_two, jnp.where(mine, do_two, jnp.zeros_like(do_two)), 1, 1)
        along = jnp.sum(shares * p_grad, axis=0, keepdims=True)
        s_low = (shares * (p_grad - along)).astype(LOW)
        v_grad = dot(shares.astype(LOW), do_two)
        k_grad = dot(s_low, q_two) * scale
        q_grad = dot(s_low, k_two, 0, 0) * scale
        grads.append((q_grad, k_grad, v_grad))
    dq[:, span] = jnp.where(low_q, grads[0][0], grads[1][0]).astype(LOW)
    count = k_two.shape[0]
    dk[:count, span] = jnp.where(low_k, grads[0][1], grads[1][1]).astype(LOW)
    dv[:count, span] = jnp.where(low_k, grads[0][2], grads[1][2]).astype(LOW)


class Total:
    def __init__(self, place, value, got, send, recv):
        self.p, self.value, self.got, self.send, self.recv = place, value, got, send, recv

    def copy(self, slot):
        p = self.p
        device = (p.across_core, p.across_x, p.across_y, *(p.z_ahead(step) for step in (1, 2, 3)))[slot]
        return remote(self.value, self.got.at[slot], self.send.at[slot], self.recv.at[slot], device)

    def start(self, slots):
        for slot in slots:
            self.copy(slot).start()

    def take(self, slots):
        for slot in slots:
            self.copy(slot).wait()
        total = self.value[...]
        for slot in slots:
            total = total + self.got[slot]
        self.value[...] = total


def backward_kernel(depth, row_count, refs):
    (dy, segments, padding, images) = refs[:4]
    names = PASSED + [K0.x0]
    given = dict(zip(names, refs[4:]))
    rest = refs[4 + len(names) :]
    outs, (x_grad, mem_grad, gain_grad) = rest[:4], rest[4:7]
    rest = rest[7:]
    kept = dict(zip(names, rest))
    rest = rest[len(names) :]
    local, rest = dict(zip(specs(B), rest)), rest[len(specs(B)) :]
    staging, rest = dict(zip(RINGS, rest)), rest[len(RINGS) :]
    count = len(SCATTER_LAYOUT)
    bufs, sems = rest[: 7 * count], rest[7 * count :]
    load_sem, send_sem, recv_sem, row_sem, total_send, total_recv, out_sem = sems
    place = Place(depth)
    rows = Rows(place, row_count)
    core = place.core
    plan = Plan(6, 2.5)

    def load(*chosen):
        for name in chosen:
            number = names.index(name)
            pltpu.make_async_copy(given[name], kept[name], load_sem.at[number]).start()

    def loaded(*chosen):
        for name in chosen:
            number = names.index(name)
            pltpu.make_async_copy(given[name], kept[name], load_sem.at[number]).wait()

    blocks, rings = [], {key: [] for key in RINGS}
    for number, spec in enumerate(SCATTER_LAYOUT):
        ring, slots = rings[spec.ring], RINGS[spec.ring][0]
        staged = staging[spec.ring].at[len(ring) % slots, 0 : len(spec.pieces)]
        block = Scatter(
            place,
            (staged,) + tuple(bufs[7 * number : 7 * number + 7]),
            [(outs[spec.out], mat, column) for mat, column in spec.pieces],
            spec,
            [send_sem.at[number], recv_sem.at[number]],
        )
        block.before = ring[-slots] if len(ring) >= slots else None
        ring.append(block)
        blocks.append(block)

    near_start, near_arrive, near_end = pass_rows(
        rows, local[B.mem_low].at[1], local[B.mem_got].at[1], -1, (row_sem.at[0], row_sem.at[1])
    )
    far_start, far_arrive, far_end = pass_rows(
        rows, local[B.mem_low].at[0], local[B.mem_got].at[0], -2, (row_sem.at[2], row_sem.at[3])
    )
    total = Total(place, local[B.gains], local[B.gain_got], total_send, total_recv)

    def half(left, which):
        part = kept[left][:, :, which]
        return part.reshape(-1, part.shape[-1])

    def products(block, terms, which):
        found = []
        for left, right, first, width in terms:
            value = dot(half(left, which), right[: kept[left].shape[-1], first : first + width])
            value = value.reshape(depth, 2, -1, width)
            found += [value[..., c : c + block.width] for c in range(0, width, block.width)]
        return found

    def size(block, what):
        each = {
            "c": 8 * block.rows,
            "x": 8 * block.side,
            "y": 4 * block.main,
            "z": (2.5 if block.relay else 4) * block.main,
            "r": block.main,
            "l": block.main,
        }
        return len(block.outs) * block.width * 2 * each[what]

    def give(number, terms):
        block = blocks[number]

        def run():
            if block.before is not None:
                block.before.c_copy().wait_send()
                block.before.sent = True
            for sub, value in enumerate(products(block, terms, 1 - core)):
                block.staged[sub] = value.astype(LOW)
            block.start_c()

        return run

    def hold(number, terms):
        block = blocks[number]

        def run():
            block.c_copy().wait_recv()
            for sub, value in enumerate(products(block, terms, core)):
                block.held[sub] = (value + block.held[sub].astype(jnp.float32)).astype(LOW)

            def to_y():
                if block.side:
                    block.take_x()
                plan.send("y", number, size(block, "y"), lambda: block.y_copy().start(), to_z)

            def to_z():
                block.take_y()
                plan.send("z", number, size(block, "z"), block.start_z, to_relay)

            def to_relay():
                if not block.relay:
                    to_last()
                    return
                block.take_relay()
                plan.later(size(block, "r") / plan.rate["z"] + plan.latency, to_last)

            def to_last():
                block.take_z()
                plan.send("x", number, size(block, "l"), lambda: block.last_copy().start(), block.take_last)

            if block.side:
                plan.send("x", number, size(block, "x"), lambda: block.x_copy().start(), to_y)
            else:
                to_y()

        return run

    def make_bias():
        seg_k, seg_q = as_column(segments[...])[:, 0:1], segments[...].astype(jnp.float32)
        real = as_column(padding[...])[:, 0:1] == 1.0
        key = lax.broadcasted_iota(jnp.int32, (TOKENS, TOKENS), 0)
        query = lax.broadcasted_iota(jnp.int32, (TOKENS, TOKENS), 1)
        allowed = (seg_q == seg_k) & (key <= query) & (real | (key == query))
        local[B.biast][...] = jnp.where(allowed, 0.0, -1e30)

    def cross_begin():
        local[B.dlow][...] = kept[K.dx2][...].astype(LOW)

    def cross_do():
        local[B.do][...] = dot(local[B.dlow][...], kept[W.w_cross][3], 1, 1).astype(LOW)

    def cross_pair(pair):
        def run():
            attend_back_pair(
                pair,
                kept[K.q2],
                kept[K.k2],
                kept[K.v2],
                local[B.do],
                kept[K.lse2],
                None,
                local[B.dq],
                local[B.dk],
                local[B.dv],
            )

        return run

    def self_pair(pair):
        def run():
            attend_back_pair(
                pair,
                kept[K.q1],
                kept[K.k1],
                kept[K.v1],
                local[B.do],
                kept[K.lse1],
                local[B.biast],
                local[B.dq],
                local[B.dk],
                local[B.dv],
            )

        return run

    def mem_out():
        return pltpu.make_async_copy(local[B.mem_sum], mem_grad, out_sem.at[0])

    def x_out():
        return pltpu.make_async_copy(kept[K.dx2], x_grad, out_sem.at[1])

    def mem_back():
        value = dot(local[B.dk][:PATCHES], kept[W.w_cross][1], 1, 1)
        value += dot(local[B.dv][:PATCHES], kept[W.w_cross][2], 1, 1)
        local[B.mem_sum][...] = value
        local[B.mem_low][0] = value.astype(LOW)
        far_start()

    def mem_far():
        far_arrive()
        got = jnp.where(row_offset(images, rows.row + 2, row_count) >= 2, local[B.mem_got][0].astype(jnp.float32), 0.0)
        value = local[B.mem_sum][...] + got
        local[B.mem_sum][...] = value
        local[B.mem_low][1] = value.astype(LOW)
        near_start()

    def mem_near():
        near_arrive()
        got = jnp.where(row_offset(images, rows.row + 1, row_count) == 1, local[B.mem_got][1].astype(jnp.float32), 0.0)
        first = row_offset(images, rows.row, row_count) == 0
        local[B.mem_sum][...] = jnp.where(first, local[B.mem_sum][...] + got, 0.0)
        mem_out().start()

    def cross_dh():
        local[B.dh][...] = dot(local[B.dq][...], kept[W.w_cross][0], 1, 1)

    def cross_norm():
        norm_back_rows(kept[K.x1], kept[K.gain][1:2], local[B.dh], kept[K.dx2], kept[K.dx2], local[B.gain_row])
        local[B.gains][1:2, :] = local[B.gain_row][...]
        local[B.dlow][...] = kept[K.dx2][...].astype(LOW)

    def self_do():
        local[B.do][...] = dot(local[B.dlow][...], kept[W.w_self][3], 1, 1).astype(LOW)

    def self_dh_first():
        local[B.dh][...] = dot(local[B.dq][...], kept[W.w_self][0], 1, 1)

    def self_dh_second():
        local[B.dh][...] += dot(local[B.dk][...], kept[W.w_self][1], 1, 1)

    def self_dh_third():
        local[B.dh][...] += dot(local[B.dv][...], kept[W.w_self][2], 1, 1)

    def self_norm():
        norm_back_rows(kept[K0.x0], kept[K.gain][0:1], local[B.dh], kept[K.dx2], kept[K.dx2], local[B.gain_row])
        x_out().start()
        local[B.gains][0:1, :] = local[B.gain_row][...]
        local[B.gains][2:3, :] = kept[K.gain3][...]
        total.start((0,))

    def load_cross():
        load(K.dx2, W.w_cross, K.o2t, K.q2, K.k2, K.v2, K.lse2, K.h2t, K.memt, K.x1, K.gain, K.gain3)

    def load_self():
        load(W.w_self, K.o1t, K.q1, K.k1, K.v1, K.lse1, K.h1t, K0.x0)

    do_low, dq, dk, dv = local[B.dlow], local[B.dq], local[B.dk], local[B.dv]
    out_terms = [[(K.hiddent, dy, 256 * j, 256)] for j in range(3)]
    in_terms = [[(K.h3t, kept[name], first, 1024)] for name in (K.dgate, K.dup) for first in (0, 1024)]

    load(K.hiddent, K.h3t, K.dgate, K.dup)
    local[B.gains][...] = jnp.zeros_like(local[B.gains])
    for block in blocks:
        block.sent = False
        block.blank()
    greet_all(place, rows)
    load_cross()
    loaded(K.hiddent)
    plan.work(0.8, give(0, out_terms[0]))
    plan.work(0.8, give(1, out_terms[1]))
    plan.work(0.9, hold(0, out_terms[0]))
    plan.work(0.8, give(2, out_terms[2]))
    plan.work(0.9, hold(1, out_terms[1]))
    loaded(K.h3t, K.dgate, K.dup)
    load_self()
    plan.work(1.0, give(3, in_terms[0]))
    plan.work(0.9, hold(2, out_terms[2]))
    for j in range(1, 4):
        plan.work(1.0, give(3 + j, in_terms[j]))
        plan.work(1.1, hold(2 + j, in_terms[j - 1]))
    loaded(K.dx2, W.w_cross, K.o2t, K.q2, K.k2, K.v2, K.lse2, K.h2t, K.memt, K.x1, K.gain, K.gain3)
    plan.work(0.3, cross_begin)
    o_terms = [(K.o2t, do_low, 0, 768)]
    plan.work(0.8, give(7, o_terms))
    plan.work(1.1, hold(6, in_terms[3]))
    plan.work(0.8, cross_do)
    plan.work(0.9, hold(7, o_terms))

    def attention(pair_work, first, lefts, pairs):
        previous = None
        width = 128 * pairs
        for group in range(6 // pairs):
            for pair in range(pairs * group, pairs * group + pairs):
                plan.work(1.4, pair_work(pair))
            terms = [(left, right, width * group, width) for left, right in zip(lefts, (dq, dk, dv))]
            plan.work(0.5 * pairs, give(first + group, terms))
            if previous is not None:
                plan.work(0.5 * pairs, hold(*previous))
            previous = (first + group, terms)
        return previous

    previous = attention(cross_pair, 8, (K.h2t, K.memt, K.memt), 2)
    plan.work(1.5, mem_back)
    plan.work(1.0, hold(*previous))
    plan.work(0.8, cross_dh)
    plan.work(1.2, cross_norm)
    loaded(W.w_self, K.o1t, K.q1, K.k1, K.v1, K.lse1, K.h1t, K0.x0)
    o_terms = [(K.o1t, do_low, 0, 768)]
    plan.work(0.8, give(11, o_terms))
    plan.work(0.3, mem_far)
    plan.work(0.8, self_do)
    plan.work(0.5, make_bias)
    plan.work(0.9, hold(11, o_terms))
    previous = attention(self_pair, 12, (K.h1t, K.h1t, K.h1t), 1)
    plan.work(0.8, self_dh_first)
    plan.work(1.0, hold(*previous))
    plan.work(0.8, self_dh_second)
    plan.work(0.8, self_dh_third)
    plan.work(0.5, mem_near)
    plan.work(1.5, self_norm)

    def total_step(slots, after):
        def run():
            total.take(slots)
            if after:
                total.start(after[0])
                plan.later(2.5, total_step(after[0], after[1:]))
            else:
                share = gain_grad.shape[1]
                turned = pltpu.roll(local[B.gains][...], (row_count // 2 - place.wide) * share, 1)
                gain_grad[...] = turned[0 : gain_grad.shape[0], 0:share]

        return run

    plan.later(2.5, total_step((0,), ((1,), (2,), (3, 4, 5))))
    while plan.busy():
        plan.step()
    for block in blocks:
        if not block.sent:
            block.c_copy().wait_send()
        block.end()
    near_end()
    far_end()
    mem_out().wait()
    x_out().wait()


def backward(kept, layer_input, cotangent, segments, padding, image_of_row, share):
    wide = lax.axis_size("wide")
    depth = wide // 4

    def owners(array):
        return array.reshape(depth, 2, 2, -1, array.shape[-1])

    names = PASSED + [K0.x0]
    given = {**kept, K0.x0: layer_input}
    for name in (K.h1t, K.o1t, K.h2t, K.o2t, K.memt, K.h3t, K.hiddent):
        given[name] = owners(given[name])
    arrays = [given[name] for name in names]
    vmem, anywhere, smem = (pl.BlockSpec(memory_space=space) for space in (pltpu.VMEM, pl.ANY, pltpu.SMEM))
    outs = [
        ((4, WIDTH // wide, WIDTH), jnp.float32),
        ((4, WIDTH // wide, WIDTH), jnp.float32),
        ((2, WIDTH // wide, HIDDEN), jnp.float32),
        ((1, HIDDEN // wide, WIDTH), jnp.float32),
        ((TOKENS, WIDTH), jnp.float32),
        ((PATCHES, WIDTH), jnp.float32),
        ((3, share), jnp.float32),
    ]
    count = len(SCATTER_LAYOUT)
    return pl.pallas_call(
        lambda *refs: backward_kernel(depth, 2 * wide, refs),
        out_shape=[jax.ShapeDtypeStruct(*o) for o in outs],
        in_specs=[vmem] * 3 + [smem] + [anywhere] * len(arrays),
        out_specs=[vmem] * 4 + [anywhere] * 2 + [vmem],
        scratch_shapes=[pltpu.VMEM(a.shape, a.dtype) for a in arrays]
        + [spec.scratch() for spec in specs(B)]
        + staging_buffers(depth)
        + scatter_buffers(depth)
        + [
            pltpu.SemaphoreType.DMA((len(arrays),)),
            pltpu.SemaphoreType.DMA((count, 8)),
            pltpu.SemaphoreType.DMA((count, 8)),
            pltpu.SemaphoreType.DMA((4,)),
            pltpu.SemaphoreType.DMA((6,)),
            pltpu.SemaphoreType.DMA((6,)),
            pltpu.SemaphoreType.DMA((2,)),
        ],
        compiler_params=pltpu.CompilerParams(
            collective_id=1, has_side_effects=True, vmem_limit_bytes=63 * 2**20
        ),
        name="backward",
    )(cotangent, segments, padding, image_of_row, *arrays)


def finish(*arrays):
    count = len(arrays)

    def kernel(*refs):
        sems = refs[-1]
        loads = [pltpu.make_async_copy(refs[n], refs[2 * count + n], sems.at[0, n]) for n in range(count)]
        stores = [pltpu.make_async_copy(refs[2 * count + n], refs[count + n], sems.at[1, n]) for n in range(count)]
        for load in loads:
            load.start()
        for load, store in zip(loads, stores):
            load.wait()
            store.start()
        for store in stores:
            store.wait()

    anywhere = pl.BlockSpec(memory_space=pl.ANY)
    return pl.pallas_call(
        kernel,
        out_shape=[jax.ShapeDtypeStruct(a.shape, a.dtype) for a in arrays],
        in_specs=[anywhere] * count,
        out_specs=[anywhere] * count,
        scratch_shapes=[pltpu.VMEM(a.shape, a.dtype) for a in arrays] + [pltpu.SemaphoreType.DMA((2, count))],
        compiler_params=pltpu.CompilerParams(vmem_limit_bytes=60 * 2**20),
        name="finish",
    )(*arrays)


def plain_gather(self_weights, cross_weights, mlp_in, mlp_out, gains):
    return (
        lax.all_gather(self_weights, "wide", axis=1, tiled=True),
        lax.all_gather(cross_weights, "wide", axis=1, tiled=True),
        lax.all_gather(mlp_in, "wide", axis=1, tiled=True),
        lax.all_gather(mlp_out, "wide", axis=0, tiled=True),
        lax.all_gather(gains, "wide", axis=1, tiled=True),
    )


def plain_scatter(*grads):
    outs = []
    for grad, axis in zip(grads, (1, 1, 1, 0, 1)):
        piece = lax.psum_scatter(grad, ("wide", "narrow"), scatter_dimension=axis, tiled=True)
        outs.append(lax.all_gather(piece.astype(jnp.bfloat16), "narrow", axis=axis, tiled=True).astype(jnp.float32))
    return tuple(outs)


def by_kernel(self_weights):
    return lax.axis_size("wide") == 16 and lax.axis_size("narrow") == 2 and self_weights.shape[1] % 48 == 0


def plain_device(
    layer_input,
    memory,
    cotangent,
    segment_ids,
    padding,
    image_of_row,
    self_weights,
    cross_weights,
    mlp_in,
    mlp_out,
    gains,
):
    self_full, cross_full, in_full, out_full, gain_full = plain_gather(
        self_weights, cross_weights, mlp_in, mlp_out, gains
    )
    gain_float = gain_full.astype(jnp.float32)
    x_zero = layer_input[0].astype(jnp.float32)
    seg_row = segment_ids[0]
    pad_row = padding[0]
    seq_len = x_zero.shape[0]
    position = jnp.arange(seq_len)
    allowed = (
        (seg_row[:, None] == seg_row[None, :])
        & (position[None, :] <= position[:, None])
        & ((pad_row[None, :] == 1) | (position[:, None] == position[None, :]))
    )
    h_one = rms_norm(x_zero, gain_float[0]).astype(jnp.bfloat16)
    q_self = linear(h_one, self_full[0]).astype(jnp.bfloat16)
    k_self = linear(h_one, self_full[1]).astype(jnp.bfloat16)
    v_self = linear(h_one, self_full[2]).astype(jnp.bfloat16)
    self_mix, self_lse = forward_heads(q_self, k_self, v_self, allowed)
    x_one = x_zero + linear(self_mix, self_full[3])
    row_ids = jnp.arange(image_of_row.shape[0])
    starts = jnp.sum(image_of_row[None, :] < image_of_row[:, None], axis=1)
    offsets = row_ids - starts
    my_index = lax.axis_index(("wide", "narrow"))
    my_offset = jnp.sum(jnp.where(row_ids == my_index, offsets, 0))
    own_patches = memory[0]
    memory_use = own_patches
    for distance in (1, 2, 3):
        arrived = shifted(own_patches, ("wide", "narrow"), distance)
        memory_use = jnp.where(my_offset == distance, arrived, memory_use)
    h_two = rms_norm(x_one, gain_float[1]).astype(jnp.bfloat16)
    q_cross = linear(h_two, cross_full[0]).astype(jnp.bfloat16)
    k_cross = linear(memory_use, cross_full[1]).astype(jnp.bfloat16)
    v_cross = linear(memory_use, cross_full[2]).astype(jnp.bfloat16)
    cross_mix, cross_lse = forward_heads(q_cross, k_cross, v_cross, None)
    x_two = x_one + linear(cross_mix, cross_full[3])
    h_three = rms_norm(x_two, gain_float[2]).astype(jnp.bfloat16)
    gate_act = linear(h_three, in_full[0])
    up_act = linear(h_three, in_full[1])
    hidden = gated_product(gate_act, up_act).astype(jnp.bfloat16)
    result = x_two + linear(hidden, out_full)
    out_low = cotangent[0]
    out_grad_w = contract_rows(hidden, out_low)
    hidden_grad = times_transposed(out_low, out_full)
    _, pullback = jax.vjp(gated_product, gate_act, up_act)
    gate_grad, up_grad = pullback(hidden_grad)
    gate_low = gate_grad.astype(jnp.bfloat16)
    up_low = up_grad.astype(jnp.bfloat16)
    in_grad = jnp.stack([contract_rows(h_three, gate_low), contract_rows(h_three, up_low)])
    h_three_grad = times_transposed(gate_low, in_full[0]) + times_transposed(up_low, in_full[1])
    _, pullback = jax.vjp(rms_norm, x_two, gain_float[2])
    x_two_norm, gain_three = pullback(h_three_grad)
    x_two_grad = out_low.astype(jnp.float32) + x_two_norm
    cross_out_low = x_two_grad.astype(jnp.bfloat16)
    cross_o_grad = contract_rows(cross_mix, cross_out_low)
    cross_mix_grad = times_transposed(cross_out_low, cross_full[3]).astype(jnp.bfloat16)
    q_cross_grad, k_cross_grad, v_cross_grad = backward_heads(
        q_cross, k_cross, v_cross, cross_mix_grad, cross_lse, None
    )
    cross_grad = jnp.stack(
        [
            contract_rows(h_two, q_cross_grad),
            contract_rows(memory_use, k_cross_grad),
            contract_rows(memory_use, v_cross_grad),
            cross_o_grad,
        ]
    )
    mem_grad = times_transposed(k_cross_grad, cross_full[1]) + times_transposed(
        v_cross_grad, cross_full[2]
    )
    h_two_grad = times_transposed(q_cross_grad, cross_full[0])
    _, pullback = jax.vjp(rms_norm, x_one, gain_float[1])
    x_one_norm, gain_two = pullback(h_two_grad)
    x_one_grad = x_two_grad + x_one_norm
    self_out_low = x_one_grad.astype(jnp.bfloat16)
    self_o_grad = contract_rows(self_mix, self_out_low)
    self_mix_grad = times_transposed(self_out_low, self_full[3]).astype(jnp.bfloat16)
    q_self_grad, k_self_grad, v_self_grad = backward_heads(
        q_self, k_self, v_self, self_mix_grad, self_lse, allowed
    )
    self_grad = jnp.stack(
        [
            contract_rows(h_one, q_self_grad),
            contract_rows(h_one, k_self_grad),
            contract_rows(h_one, v_self_grad),
            self_o_grad,
        ]
    )
    h_one_grad = (
        times_transposed(q_self_grad, self_full[0])
        + times_transposed(k_self_grad, self_full[1])
        + times_transposed(v_self_grad, self_full[2])
    )
    _, pullback = jax.vjp(rms_norm, x_zero, gain_float[0])
    x_zero_norm, gain_one = pullback(h_one_grad)
    x_grad = x_one_grad + x_zero_norm
    mem_summed = jnp.where(my_offset == 0, mem_grad, 0.0)
    for distance in (1, 2, 3):
        arrived = shifted(mem_grad.astype(jnp.bfloat16), ("wide", "narrow"), -distance).astype(
            mem_grad.dtype
        )
        neighbour = jnp.sum(jnp.where(row_ids == my_index + distance, offsets, 0))
        mem_summed = mem_summed + jnp.where(neighbour == distance, arrived, 0.0)
    gain_grad = jnp.stack([gain_one, gain_two, gain_three])
    reduced = plain_scatter(self_grad, cross_grad, in_grad, out_grad_w, gain_grad)
    return (
        result.astype(jnp.bfloat16)[None],
        x_grad[None],
        mem_summed[None],
        reduced[0],
        reduced[1],
        reduced[2],
        reduced[3],
        reduced[4],
    )


def kernel_device(
    layer_input,
    memory,
    cotangent,
    segment_ids,
    padding,
    image_of_row,
    self_weights,
    cross_weights,
    mlp_in,
    mlp_out,
    gains,
):
    result, kept = forward(
        layer_input[0],
        cotangent[0],
        memory[0],
        segment_ids,
        padding,
        image_of_row,
        gains,
        self_weights,
        cross_weights,
        mlp_in,
        mlp_out,
    )
    self_grad, cross_grad, in_grad, out_grad, x_grad, mem_grad, gain_grad, result = finish(
        *backward(kept, layer_input[0], cotangent[0], segment_ids, padding, image_of_row, gains.shape[1]),
        result,
    )
    return (result[None], x_grad[None], mem_grad[None], self_grad, cross_grad, in_grad, out_grad[0], gain_grad)


def on_device(
    layer_input,
    memory,
    cotangent,
    segment_ids,
    padding,
    image_of_row,
    self_weights,
    cross_weights,
    mlp_in,
    mlp_out,
    gains,
):
    run = kernel_device if by_kernel(self_weights) else plain_device
    return run(
        layer_input,
        memory,
        cotangent,
        segment_ids,
        padding,
        image_of_row,
        self_weights,
        cross_weights,
        mlp_in,
        mlp_out,
        gains,
    )


def solution(mesh):
    in_specs = (
        P(("wide", "narrow"), None, None),
        P(("wide", "narrow"), None, None),
        P(("wide", "narrow"), None, None),
        P(("wide", "narrow"), None),
        P(("wide", "narrow"), None),
        P(),
        P(None, "wide", None),
        P(None, "wide", None),
        P(None, "wide", None),
        P("wide", None),
        P(None, "wide"),
    )
    out_specs = (
        P(("wide", "narrow"), None, None),
        P(("wide", "narrow"), None, None),
        P(("wide", "narrow"), None, None),
        P(None, "wide", None),
        P(None, "wide", None),
        P(None, "wide", None),
        P("wide", None),
        P(None, "wide"),
    )
    return jax.shard_map(
        on_device, mesh=mesh, in_specs=in_specs, out_specs=out_specs, check_vma=False
    )
```
